32 devices in a mesh: pix: 8 (over z, y), ch: 4 (over x, core).
Axes of the slice: x: 2, y: 2, z: 4, core: 2. Of those that a mesh axis runs over, the one named last changes fastest.
Arguments:
- features: bfloat16 [25088, 1024], P('pix', 'ch'), may hold values from -6 to 6
- pad_mask: int32 [25088], P('pix'), may hold values from 0 to 1, as said below
- reduce_weight: bfloat16 [1024, 256], P(None, 'ch'), may hold values from -0.1875 to 0.1875
- spatial_weight: bfloat16 [3, 3, 256, 256], P(None, None, None, 'ch'), may hold values from -0.125 to 0.125
- expand_weight: bfloat16 [256, 1024], P('ch'), may hold values from -0.375 to 0.375
- gain_first: bfloat16 [256], P('ch'), may hold values from 0.25 to 1.75
- shift_first: bfloat16 [256], P('ch'), may hold values from -3 to 3
- gain_second: bfloat16 [256], P('ch'), may hold values from 0.25 to 1.75
- shift_second: bfloat16 [256], P('ch'), may hold values from -3 to 3
- gain_third: bfloat16 [1024], P('ch'), may hold values from 0.25 to 1.75
- shift_third: bfloat16 [1024], P('ch'), may hold values from -3 to 3
- out_cotangent: bfloat16 [25088, 1024], P('pix', 'ch'), may hold values from -6 to 6
Outputs:
- result: bfloat16 [25088, 1024], P('pix', 'ch')
- input_grad: bfloat16 [25088, 1024], P('pix', 'ch')
- reduce_grad: float32 [1024, 256], P(None, 'ch')
- spatial_grad: float32 [3, 3, 256, 256], P(None, None, None, 'ch')
- expand_grad: float32 [256, 1024], P('ch')
- gain_first_grad: float32 [256], P('ch')
- shift_first_grad: float32 [256], P('ch')
- gain_second_grad: float32 [256], P('ch')
- shift_second_grad: float32 [256], P('ch')
- gain_third_grad: float32 [1024], P('ch')
- shift_third_grad: float32 [1024], P('ch')
The draws below stay inside these ranges and needn't reach their ends.
Inputs may be any that keep to these rules, and one draw needn't show every extreme that they name: `pad_mask`: 1 marks a pixel that holds picture, 0 one of padding; the share of padding differs from image to image.
All inputs are finite; a program needn't handle non-finite values.
Results may differ from the reference program's by a relative error of at most 0.0081.
Values may be sent and summed in bfloat16 or wider, within the bound.
A program may use at most 128 MiB of HBM per device.

```python
import jax
import jax.numpy as jnp
from jax import lax

C_IN = 1024
C_MID = 256
SIDE = 14
IMAGES = 128
PIXELS = 25088


def draw_pad_mask(key, part):
    key = jax.random.fold_in(key, 11)
    image = jnp.arange(PIXELS, dtype=jnp.int32) // (SIDE * SIDE)
    threshold = 300 + 650 * image // max(IMAGES - 1, 1)
    rolls = jax.random.randint(key, (PIXELS,), 0, 1000, dtype=jnp.int32)
    return (rolls < threshold).astype(jnp.int32)


def steps_of(rng, shape, split, low, largest):
    factor_of = 1.0
    for position, blocks in split:
        draws = jax.random.uniform(jax.random.fold_in(jax.random.fold_in(rng, 6), position), (blocks,), jnp.float32, low / len(split), largest / len(split))
        factor_of = factor_of * jnp.repeat(jnp.exp(draws), shape[position] // blocks).reshape((-1,) + (1,) * (len(shape) - 1 - position))
    return factor_of


def gaussian(rng, extent, deviation, bound, pieces=(), kind=jnp.bfloat16):
    loudness = steps_of(rng, extent, pieces, -0.22, 0.18) if pieces else 1.0
    result = jax.random.normal(rng, extent, jnp.float32) * deviation * loudness
    return jnp.minimum(jnp.maximum(result, -bound), bound).astype(kind)


def setup_inputs(seed: int = 0) -> dict:
    key_of = jax.random.split(jax.random.key(seed), 13)
    return {
        "features": gaussian(key_of[0], (PIXELS, C_IN), 1.0, 6.0, ((0, 8), (1, 4))),
        "pad_mask": draw_pad_mask(jax.random.fold_in(key_of[12], 71), 0),
        "reduce_weight": gaussian(key_of[2], (C_IN, C_MID), C_IN ** -0.5, 0.1875, ((1, 4),)),
        "spatial_weight": gaussian(key_of[3], (3, 3, C_MID, C_MID), (9 * C_MID) ** -0.5, 0.125, ((3, 4),)),
        "expand_weight": gaussian(key_of[4], (C_MID, C_IN), C_MID ** -0.5, 0.375, ((0, 4),)),
        "gain_first": jnp.clip(1.0 + 0.15 * jax.random.normal(key_of[5], (C_MID,), jnp.float32), 0.25, 1.75).astype(jnp.bfloat16),
        "shift_first": gaussian(key_of[6], (C_MID,), 0.5, 3.0, ((0, 4),)),
        "gain_second": jnp.clip(1.0 + 0.15 * jax.random.normal(key_of[7], (C_MID,), jnp.float32), 0.25, 1.75).astype(jnp.bfloat16),
        "shift_second": gaussian(key_of[8], (C_MID,), 0.5, 3.0, ((0, 4),)),
        "gain_third": jnp.clip(1.0 + 0.15 * jax.random.normal(key_of[9], (C_IN,), jnp.float32), 0.25, 1.75).astype(jnp.bfloat16),
        "shift_third": gaussian(key_of[10], (C_IN,), 0.5, 3.0, ((0, 4),)),
        "out_cotangent": gaussian(key_of[11], (PIXELS, C_IN), 1.0, 6.0, ((0, 8), (1, 4))),
    }


EPS = 1e-05
HIGH = lax.Precision.HIGHEST

@jax.custom_vjp
def low(v):
    return lax.optimization_barrier(v.astype(jnp.bfloat16)).astype(jnp.float32)

@jax.custom_vjp
def low_back(v):
    return v

def low_keep(v):
    return (low(v), None)

def low_pass(kept, grad):
    return (grad,)

def back_keep(v):
    return (v, None)

def back_low(kept, grad):
    return (low(grad),)
low.defvjp(low_keep, low_pass)
low_back.defvjp(back_keep, back_low)

def grid_conv(activations, kernel):
    images = activations.shape[0] // (SIDE * SIDE)
    grid = activations.reshape(images, SIDE, SIDE, activations.shape[1])
    output = lax.conv_general_dilated(grid, kernel, (1, 1), 'SAME', dimension_numbers=('NHWC', 'HWIO', 'NHWC'), precision=HIGH)
    return output.reshape(activations.shape[0], kernel.shape[3])

def reference(features, pad_mask, reduce_weight, spatial_weight, expand_weight, gain_first, shift_first, gain_second, shift_second, gain_third, shift_third, out_cotangent):
    valid = pad_mask.astype(jnp.float32)[:, None]
    counted = jnp.sum(valid)

    def normalize(hidden, gain, shift):
        average = lax.optimization_barrier(jnp.sum(valid * hidden, axis=0)) / counted
        variance = lax.optimization_barrier(jnp.sum(valid * hidden * hidden, axis=0)) / counted - average * average
        return valid * (gain * (hidden - average) * lax.rsqrt(variance + EPS) + shift)

    def forward(inputs, reducer, spatial, expander, gain_one, shift_one, gain_two, shift_two, gain_three, shift_three):
        hidden_one = low_back(jnp.dot(inputs, reducer, precision=HIGH))
        active_one = low(jax.nn.silu(normalize(hidden_one, gain_one, shift_one)))
        hidden_two = low_back(grid_conv(active_one, spatial))
        active_two = low(jax.nn.silu(normalize(hidden_two, gain_two, shift_two)))
        hidden_three = low_back(jnp.dot(active_two, expander, precision=HIGH))
        return jax.nn.silu(normalize(hidden_three, gain_three, shift_three) + inputs)
    floats = tuple((entry.astype(jnp.float32) for entry in (features, reduce_weight, spatial_weight, expand_weight, gain_first, shift_first, gain_second, shift_second, gain_third, shift_third)))
    output, pullback = jax.vjp(forward, *floats)
    grads = pullback(out_cotangent.astype(jnp.float32))
    return (output.astype(jnp.bfloat16), grads[0].astype(jnp.bfloat16), grads[1], grads[2], grads[3], grads[4], grads[5], grads[6], grads[7], grads[8], grads[9])
```

```python
import functools

import jax
import jax.numpy as jnp
from jax import lax
from jax.experimental import pallas as pl
from jax.experimental.pallas import tpu as pltpu
from jax.sharding import PartitionSpec as P

SIDE = 14
EPS = 1e-05
MESH = pl.DeviceIdType.MESH
F32 = jnp.float32
BF16 = jnp.bfloat16

ROWS = 112
OWN = 7
BOTH = 14
IMAGES = 4
PAD = 16
FLAT = IMAGES * PAD * PAD
EDGE = 8


def mm(a, b):
    return jnp.dot(a, b, preferred_element_type=F32)


def mm_nt(a, b):
    return lax.dot_general(a, b, (((1,), (1,)), ((), ())), preferred_element_type=F32)


def mm_tn(a, b):
    return lax.dot_general(a, b, (((0,), (0,)), ((), ())), preferred_element_type=F32)


def logistic(v):
    return 0.5 * jnp.tanh(0.5 * v) + 0.5


def fold8(v):
    return jnp.sum(v.reshape(v.shape[0] // 8, 8, v.shape[1]), axis=0)


def fold1(v):
    return jnp.sum(v, axis=0, keepdims=True)


def spread(v, lanes):
    return jnp.concatenate([v] * (lanes // 128), axis=1)


def kernel(
    n_pix,
    n_ch,
    feat,
    cot,
    mask,
    w1_in,
    w2_in,
    w3_in,
    params,
    res_out,
    ig_out,
    rg_out,
    sg_out,
    eg_out,
    st_out,
    F,
    C,
    V,
    w1v,
    w2v,
    w1t_own,
    W1T,
    W2T,
    W3,
    pk,
    sbuf,
    rbuf,
    h1s,
    h1r,
    H1,
    h1b,
    h1o,
    D1,
    comp,
    P0,
    PC,
    Q,
    padded,
    H2,
    h2s,
    h2r,
    A2,
    D2,
    H3,
    GS,
    RES,
    G3,
    E2,
    e2s,
    e2r,
    E1,
    e1s,
    e1r,
    G1,
    acc_w,
    acc_s,
    wp,
    wc,
    wa,
    wr,
    wh,
    wf,
    wfin,
    sp,
    sc,
    sa,
    sr,
    sh,
    sf,
    sx,
    sfin,
    ld_sem,
    fx_send,
    fx_recv,
    w_send,
    w_recv,
    ar_send,
    ar_recv,
    x_send,
    x_recv,
    out_sem,
    o_send,
    o_recv,
    g_send,
    g_recv,
):
    me_p, me_c = lax.axis_index("pix"), lax.axis_index("ch")
    hi, lo = me_c // 2, lax.rem(me_c, 2)
    n_lo = min(n_pix, 8)
    n_hi = n_pix // n_lo
    g_hi, g_lo = me_p // n_lo, lax.rem(me_p, n_lo)
    across = (me_p, (1 - hi) * 2 + lo)
    beside = (me_p, hi * 2 + 1 - lo)
    n_all = n_pix * n_ch

    def remote(src, dst, send, recv, device):
        return pltpu.make_async_remote_copy(
            src_ref=src, dst_ref=dst, send_sem=send, recv_sem=recv, device_id=device, device_id_type=MESH
        )

    def local(src, dst, sem):
        return pltpu.make_async_copy(src, dst, sem)

    mine, theirs = lo * BOTH, (1 - lo) * BOTH
    part0, part1 = hi * OWN, (1 - hi) * OWN

    w1_load = local(w1_in, w1v, ld_sem.at[0])
    w2_load = local(w2_in, w2v, ld_sem.at[1])
    f_load = [
        local(feat.at[pl.ds(mine + part, OWN)], F.at[lo, pl.ds(OWN * s, OWN)], ld_sem.at[2 + s])
        for s, part in enumerate((part0, part1))
    ]
    c_load = [
        local(cot.at[pl.ds(mine + part, OWN)], C.at[lo, pl.ds(OWN * s, OWN)], ld_sem.at[4 + s])
        for s, part in enumerate((part0, part1))
    ]
    w3_load = local(w3_in.at[:, pl.ds(pl.multiple_of(hi * 512, 512), 512)], W3.at[me_c], ld_sem.at[6])
    w1_load.start()
    f_load[1].start()
    f_load[0].start()
    w2_load.start()
    w3_load.start()
    c_load[0].start()
    c_load[1].start()

    barrier = pltpu.get_barrier_semaphore()

    def greet(t, carry):
        q = lax.rem(me_p * n_ch + me_c + t, n_all)
        pl.semaphore_signal(barrier, inc=1, device_id=(q // n_ch, lax.rem(q, n_ch)), device_id_type=MESH)
        return carry

    lax.fori_loop(1, n_all, greet, 0)

    eye = (
        lax.broadcasted_iota(jnp.int32, (64, 64), 0) == lax.broadcasted_iota(jnp.int32, (64, 64), 1)
    ).astype(BF16)
    w1_load.wait()
    w1t = mm_nt(eye, w1v[...]).astype(BF16)
    w1t_own[0] = w1t[:, 0:512]
    w1t_own[1] = w1t[:, 512:1024]
    W1T[me_c] = w1t_own[hi]

    vec = params[...]
    vec8 = jnp.broadcast_to(vec[:, 0:256], (8, 256)).astype(BF16)
    row_i = lax.broadcasted_iota(jnp.int32, (256, 256), 0)
    col_i = lax.broadcasted_iota(jnp.int32, (256, 256), 1)
    pk_rows = []
    for k in range(4):
        sel = (row_i - 64 * k == col_i - 64 * me_c) & (row_i >= 64 * k) & (row_i < 64 * k + 64)
        pk_rows.append(mm(vec8, sel.astype(BF16))[0:1])
    pk_rows += [vec[:, 256:512], vec[:, 512:768], jnp.zeros((2, 256), F32)]
    pk[me_c] = jnp.concatenate(pk_rows, axis=0)

    pl.semaphore_wait(barrier, n_all - 1)

    fx = [
        remote(
            feat.at[pl.ds(theirs + part, OWN)], F.at[lo, pl.ds(OWN * s, OWN)], fx_send.at[s], fx_recv.at[s], beside
        )
        for s, part in enumerate((part0, part1))
    ]
    cx = [
        remote(
            cot.at[pl.ds(theirs + part, OWN)], C.at[lo, pl.ds(OWN * s, OWN)], fx_send.at[2 + s], fx_recv.at[2 + s], beside
        )
        for s, part in enumerate((part0, part1))
    ]
    others = []
    for t in range(1, n_ch):
        q = lax.rem(me_c + t, n_ch)
        others.append((t - 1, (me_p, q), q // 2))
    w1x = [remote(w1t_own.at[h], W1T.at[me_c], w_send.at[t], w_recv.at[me_c], dev) for t, dev, h in others]
    pkx = [remote(pk.at[me_c], pk.at[me_c], w_send.at[4 + t], w_recv.at[4 + me_c], dev) for t, dev, h in others]
    w3x = [
        remote(
            w3_in.at[:, pl.ds(pl.multiple_of(h * 512, 512), 512)],
            W3.at[me_c],
            w_send.at[8 + t],
            w_recv.at[8 + me_c],
            dev,
        )
        for t, dev, h in others
    ]
    for cp in w1x:
        cp.start()
    fx[1].start()
    fx[0].start()
    for cp in pkx:
        cp.start()

    diag = lax.broadcasted_iota(jnp.int32, (ROWS, ROWS), 0) == lax.broadcasted_iota(jnp.int32, (ROWS, ROWS), 1)
    ones = jnp.ones((ROWS, 128), BF16)

    def put_mask(t, carry):
        at = mine + jnp.where(t < OWN, part0 + t, part1 + t - OWN)
        row = mask[pl.ds(at, 1), :]
        V[t] = mm(jnp.where(diag, row, 0.0).astype(BF16), ones)
        return carry

    lax.fori_loop(0, BOTH, put_mask, 0)

    w2_load.wait()
    for r in range(3):
        W2T[me_c, :, 768 * r : 768 * (r + 1)] = mm_nt(eye, w2v[768 * r : 768 * (r + 1), :]).astype(BF16)
    P0[...] = jnp.zeros_like(P0)

    def arrived(dst, sem):
        local(dst, dst, sem).wait()

    for t, dev, h in others:
        q = dev[1]
        arrived(W1T.at[q], w_recv.at[q])

    f_load[1].wait()
    fx[1].wait_recv()
    w1_all = W1T[...].reshape(256, 512)

    def first(t):
        wide = jnp.concatenate([F[0, t], F[1, t]], axis=1)
        return mm_nt(wide, w1_all)

    def xcopy(kind, src, dst, t):
        return remote(src.at[t], dst.at[t], x_send.at[kind, t], x_recv.at[kind, t], across)

    def send_first(t, carry):
        h1s[t] = first(t + OWN).astype(BF16)
        xcopy(0, h1s, h1r, t).start()
        return carry

    lax.fori_loop(0, OWN, send_first, 0)
    f_load[0].wait()
    fx[0].wait_recv()

    def keep_first(t, carry):
        H1[t] = first(t)
        return carry

    lax.fori_loop(0, OWN, keep_first, 0)

    w2x_across = remote(W2T.at[me_c], W2T.at[me_c], w_send.at[12], w_recv.at[12], across)
    w2x_beside = remote(W2T.at[me_c], W2T.at[me_c], w_send.at[13], w_recv.at[13], beside)
    far = (1 - hi) * 2 + lo
    w2x_pass = remote(W2T.at[far], W2T.at[far], w_send.at[14], w_recv.at[14], beside)
    w2x_beside.start()
    w2x_across.start()
    cx[0].start()
    cx[1].start()
    for t, dev, h in others:
        arrived(pk.at[dev[1]], w_recv.at[4 + dev[1]])
    gains = pk[0] + pk[1] + pk[2] + pk[3]
    g1, b1, g2, b2 = (gains[k : k + 1] for k in range(4))
    pair0, pair1 = pk[2 * hi], pk[2 * hi + 1]
    g3 = jnp.concatenate([pair0[4:5], pair1[4:5]], axis=1)
    b3 = jnp.concatenate([pair0[5:6], pair1[5:6]], axis=1)

    def ar_start(k, val, half):
        n = n_pix * 2 if half else n_all
        me = me_p * 2 + lo if half else me_p * n_ch + me_c
        sbuf[k] = val
        rbuf[k, me] = val

        def send(t, carry):
            q = lax.rem(me + t, n)
            dev = (q // 2, hi * 2 + lax.rem(q, 2)) if half else (q // n_ch, lax.rem(q, n_ch))
            remote(sbuf.at[k], rbuf.at[k, me], ar_send.at[k], ar_recv.at[k], dev).start()
            return carry

        lax.fori_loop(1, n, send, 0)

    def ar_finish(k, half):
        n = n_pix * 2 if half else n_all
        span = rbuf.at[k, pl.ds(0, n - 1)]
        arrived(span, ar_recv.at[k])
        total = jnp.sum(rbuf[k, 0:n], axis=0)
        return total

    def ar_close(k, half):
        n = n_pix * 2 if half else n_all
        span = rbuf.at[k, pl.ds(0, n - 1)]
        arrived(span, ar_send.at[k])

    def pack2(a, b, extra=None):
        tail = jnp.zeros((1, 128), F32) if extra is None else extra
        return jnp.concatenate(
            [a[:, 0:128], a[:, 128:256], b[:, 0:128], b[:, 128:256], tail, jnp.zeros((3, 128), F32)], axis=0
        )

    def unpack2(v):
        return (
            jnp.concatenate([v[0:1], v[1:2]], axis=1),
            jnp.concatenate([v[2:3], v[3:4]], axis=1),
        )

    def pack3(a, b):
        return jnp.concatenate([a[:, 128 * i : 128 * (i + 1)] for i in range(4)] + [b[:, 128 * i : 128 * (i + 1)] for i in range(4)], axis=0)

    def unpack3(v):
        return (
            jnp.concatenate([v[i : i + 1] for i in range(4)], axis=1),
            jnp.concatenate([v[i : i + 1] for i in range(4, 8)], axis=1),
        )

    zero = jnp.zeros((8, 256), F32)

    def sum_first(t, carry):
        s, q, n = carry
        xcopy(0, h1s, h1r, t).wait_recv()
        h = H1[t] + h1r[t].astype(F32)
        H1[t] = h
        h1b[t] = h.astype(BF16)
        v = V[t]
        vh = spread(v, 256) * h
        return s + fold8(vh), q + fold8(vh * h), n + fold8(v)

    s, q, n = lax.fori_loop(0, OWN, sum_first, (zero, zero, jnp.zeros((8, 128), F32)))
    ar_start(0, pack2(fold1(s), fold1(q), fold1(n)), False)
    arrived(W2T.at[far], w_recv.at[12])
    w2x_pass.start()
    total = ar_finish(0, False)
    s, q = unpack2(total)
    inv_n = 1.0 / spread(total[4:5], 512)
    inv_n2 = inv_n[:, 0:256]
    avg1 = s * inv_n2
    scale1 = lax.rsqrt(q * inv_n2 - avg1 * avg1 + EPS)
    a1_gain = g1 * scale1
    a1_shift = b1 - avg1 * a1_gain

    def act_first(t, carry):
        v = spread(V[t], 256)
        aff = v * (H1[t] * a1_gain + a1_shift)
        sig = logistic(aff)
        act = aff * sig
        comp[pl.ds(pl.multiple_of(t * ROWS, 16), ROWS), :] = act
        D1[t] = v * (sig + act * (1.0 - sig))
        return carry

    lax.fori_loop(0, OWN, act_first, 0)

    def to_padded():
        for i in range(IMAGES):
            for y in range(SIDE):
                P0[EDGE + (i * PAD + y + 1) * PAD : EDGE + (i * PAD + y + 1) * PAD + SIDE, :] = comp[
                    (i * SIDE + y) * SIDE : (i * SIDE + y + 1) * SIDE, :
                ]

    def from_padded(dst):
        for i in range(IMAGES):
            for y in range(SIDE):
                dst[(i * SIDE + y) * SIDE : (i * SIDE + y + 1) * SIDE, :] = padded[
                    (i * SIDE + y) * PAD : (i * SIDE + y) * PAD + SIDE, :
                ]

    to_padded()
    for i in range(IMAGES):
        for c in range(3):
            at = EDGE + i * 256 + c - 1
            PC[i * 256 : (i + 1) * 256, 256 * c : 256 * (c + 1)] = P0[at : at + 256, :].astype(BF16)

    arrived(W2T.at[hi * 2 + 1 - lo], w_recv.at[13])
    arrived(W2T.at[(1 - hi) * 2 + 1 - lo], w_recv.at[14])
    for cp in w3x:
        cp.start()
    h1x = [remote(h1b, h1o, x_send.at[4, 0], x_recv.at[4, 0], across)]

    def conv(i, carry):
        total = None
        for r in range(3):
            rows = PC[pl.ds(pl.multiple_of(i * 256 + 16 * r, 16), SIDE * PAD), :]
            part = mm_nt(rows, W2T[:, :, 768 * r : 768 * (r + 1)].reshape(256, 768))
            total = part if total is None else total + part
        padded[pl.ds(pl.multiple_of(i * SIDE * PAD, 16), SIDE * PAD), :] = total
        return carry

    lax.fori_loop(0, IMAGES, conv, 0)
    from_padded(H2)

    def sum_second(t, carry):
        s, q = carry
        h = H2[pl.ds(pl.multiple_of(t * ROWS, 16), ROWS), :]
        h2s[t] = h.astype(BF16)
        xcopy(1, h2s, h2r, t).start()
        vh = spread(V[t], 256) * h
        return s + fold8(vh), q + fold8(vh * h)

    s, q = lax.fori_loop(0, OWN, sum_second, (zero, zero))
    ar_start(1, pack2(fold1(s), fold1(q)), False)
    s, q = unpack2(ar_finish(1, False))
    avg2 = s * inv_n2
    scale2 = lax.rsqrt(q * inv_n2 - avg2 * avg2 + EPS)
    a2_gain = g2 * scale2
    a2_shift = b2 - avg2 * a2_gain

    w3_load.wait()
    for t, dev, h in others:
        arrived(W3.at[dev[1]], w_recv.at[8 + dev[1]])

    def act_second(t, h, carry):
        s, q = carry
        v = spread(V[t], 256)
        aff = v * (h * a2_gain + a2_shift)
        sig = logistic(aff)
        act = aff * sig
        D2[t] = v * (sig + act * (1.0 - sig))
        act = act.astype(BF16)
        A2[t] = act
        h3 = mm(act, W3[...].reshape(256, 512))
        H3[t] = h3
        return s + fold8(h3), q + fold8(h3 * h3)

    def own_second(t, carry):
        return act_second(t, H2[pl.ds(pl.multiple_of(t * ROWS, 16), ROWS), :], carry)

    def other_second(t, carry):
        xcopy(1, h2s, h2r, t).wait_recv()
        return act_second(t + OWN, h2r[t].astype(F32), carry)

    wide_zero = jnp.zeros((8, 512), F32)
    carry = lax.fori_loop(0, OWN, own_second, (wide_zero, wide_zero))
    s, q = lax.fori_loop(0, OWN, other_second, carry)
    ar_start(2, pack3(fold1(s), fold1(q)), True)
    for cp in h1x:
        cp.start()
    for cp in c_load:
        cp.wait()
    for cp in cx:
        cp.wait_recv()
    s, q = unpack3(ar_finish(2, True))
    avg3 = s * inv_n
    scale3 = lax.rsqrt(q * inv_n - avg3 * avg3 + EPS)
    a3_gain = g3 * scale3
    a3_shift = b3 - avg3 * a3_gain

    def last(t, carry):
        s, q = carry
        v = spread(V[t], 512)
        h3 = H3[t]
        wide = jnp.concatenate([F[0, t], F[1, t]], axis=1).astype(F32)
        total = v * (h3 * a3_gain + a3_shift) + wide
        sig = logistic(total)
        out = total * sig
        RES[0, t] = out[:, 0:256].astype(BF16)
        RES[1, t] = out[:, 256:512].astype(BF16)
        given = jnp.concatenate([C[0, t], C[1, t]], axis=1).astype(F32)
        gs = given * (sig + out * (1.0 - sig))
        GS[t] = gs
        vg = v * gs
        return s + fold8(vg), q + fold8(vg * (h3 - avg3))

    s, q = lax.fori_loop(0, BOTH, last, (wide_zero, wide_zero))
    ar_start(3, pack3(fold1(s), fold1(q * scale3)), True)
    parts = ((0, part0), (1, part1))
    res_here = [
        local(RES.at[lo, pl.ds(OWN * s, OWN)], res_out.at[pl.ds(mine + part, OWN)], out_sem.at[s]) for s, part in parts
    ]
    res_there = [
        remote(RES.at[1 - lo, pl.ds(OWN * s, OWN)], res_out.at[pl.ds(mine + part, OWN)], o_send.at[s], o_recv.at[s], beside)
        for s, part in parts
    ]
    for cp in res_here + res_there:
        cp.start()
    shift3, gain3 = unpack3(ar_finish(3, True))
    k3_h = -a3_gain * gain3 * scale3 * inv_n
    k3_0 = -a3_gain * shift3 * inv_n - k3_h * avg3

    def back_third(t, carry):
        s, q, h2 = carry[0], carry[1], carry[2]
        v = spread(V[t], 512)
        g = (v * (a3_gain * GS[t] + k3_h * H3[t] + k3_0)).astype(BF16)
        G3[t] = g
        e = mm_nt(g, W3[...].reshape(256, 512)) * D2[t]
        return e, s + fold8(e), q + fold8(e * (h2 - avg2))

    def other_third(t, carry):
        e, s, q = back_third(t + OWN, (carry[0], carry[1], h2r[t].astype(F32)))
        e2s[t] = e.astype(BF16)
        xcopy(2, e2s, e2r, t).start()
        return s, q

    def own_third(t, carry):
        e, s, q = back_third(t, (carry[0], carry[1], H2[pl.ds(pl.multiple_of(t * ROWS, 16), ROWS), :]))
        E2[t] = e
        return s, q

    carry = lax.fori_loop(0, OWN, other_third, (zero, zero))
    s, q = lax.fori_loop(0, OWN, own_third, carry)
    ar_start(4, pack2(fold1(s), fold1(q * scale2)), False)

    piece = 128 // n_lo
    n_sub = n_lo // 2

    def pair_copies(k, part, got):
        return [
            remote(part.at[h, 1 - lo], got.at[h], g_send.at[k, h], g_recv.at[k, h], beside) for h in range(2)
        ]

    def pair_add(k, part, got, acc):
        for h, cp in enumerate(pair_copies(k, part, got)):
            cp.wait_recv()
            both = part[h, lo].astype(F32) + got[h].astype(F32)
            acc[h] = both.astype(BF16).reshape(acc.shape[1:])

    def spread_copies(k, acc, got):
        copies = []
        for t in range(1, n_lo):
            q = lax.rem(g_lo + t, n_lo)
            copies.append(
                remote(
                    acc.at[lax.rem(q, 2), q // 2],
                    got.at[g_lo],
                    g_send.at[k, 2 + t],
                    g_recv.at[k, 2 + t],
                    (g_hi * n_lo + q, me_c),
                )
            )
        return copies

    def spread_add(k, acc, got, level):
        for cp in spread_copies(k, acc, got):
            cp.wait_recv()
        total = acc[lax.rem(g_lo, 2), g_lo // 2].astype(F32)
        for t in range(1, n_lo):
            total = total + got[lax.rem(g_lo + t, n_lo)].astype(F32)
        if n_hi > 1:
            level[g_hi] = total.astype(BF16)

            def swap(t):
                q = lax.rem(g_hi + t, n_hi)
                return remote(
                    level.at[g_hi], level.at[g_hi], g_send.at[k, 27 + t], g_recv.at[k, 27 + t], (q * n_lo + g_lo, me_c)
                )

            for t in range(1, n_hi):
                swap(t).start()
            for t in range(1, n_hi):
                swap(t).wait()
            total = level[0].astype(F32)
            for t in range(1, n_hi):
                total = total + level[t].astype(F32)
        return total

    def give_copies(k, done, fin, to_hi, first=0):
        copies = []
        for t in range(first, n_lo):
            q = lax.rem(g_lo + t, n_lo)
            copies.append(
                remote(
                    done, fin, g_send.at[k, 10 + t], g_recv.at[k, 10 + 8 * hi + t], (g_hi * n_lo + q, to_hi * 2 + lo)
                )
            )
        return copies

    owner_hi = lax.rem(g_lo, 2)
    own_sub = g_lo // 2
    keeps = owner_hi == hi

    def wide_give(k, slot):
        copies = give_copies(k, wf.at[slot], wfin.at[slot, hi, own_sub], owner_hi)
        for t, cp in enumerate(copies):
            if t == 0:

                @pl.when(jnp.logical_not(keeps))
                def _():
                    cp.start()

                @pl.when(keeps)
                def _():
                    wfin[slot, hi, own_sub] = wf[slot]

            else:
                cp.start()

    def wide_take(k, slot, out):
        for sub in range(n_sub):
            q = sub * 2 + hi
            t = lax.rem(g_lo - q + n_lo, n_lo)
            for h in range(2):

                @pl.when(jnp.logical_not((q == g_lo) & (hi == h)))
                def _():
                    arrived(wfin.at[slot, h, sub], g_recv.at[k, 10 + 8 * h + t])

        for h in range(2):
            out[:, 512 * h : 512 * (h + 1)] = wfin[slot, h].astype(F32).reshape(64, 512)

    def wide_close(k, slot):
        for cp in pair_copies(k, wp.at[slot], wc.at[slot]):
            cp.wait_send()
        for cp in spread_copies(k, wa.at[slot], wr.at[slot]):
            cp.wait_send()
        for t, cp in enumerate(give_copies(k, wf.at[slot], wfin.at[slot, hi, own_sub], owner_hi)):
            if t == 0:

                @pl.when(jnp.logical_not(keeps))
                def _():
                    cp.wait_send()

            else:
                cp.wait_send()

    def wide_part(slot, left, right_of):
        acc_w[...] = jnp.zeros_like(acc_w)

        def add(t, carry):
            a = left[pl.ds(2 * t, 2)].reshape(2 * ROWS, 256)
            acc_w[...] += mm_tn(a, right_of(t))
            return carry

        lax.fori_loop(0, OWN, add, 0)
        wp[slot] = acc_w[...].astype(BF16).reshape(2, 2, 64, 512)

    wide_part(0, A2, lambda t: G3[pl.ds(2 * t, 2)].reshape(2 * ROWS, 512))
    for cp in pair_copies(0, wp.at[0], wc.at[0]):
        cp.start()

    shift2, gain2 = unpack2(ar_finish(4, False))
    k2_h = -a2_gain * gain2 * scale2 * inv_n2
    k2_0 = -a2_gain * shift2 * inv_n2 - k2_h * avg2

    def back_second(t, carry):
        xcopy(2, e2s, e2r, t).wait_recv()
        at = pl.ds(pl.multiple_of(t * ROWS, 16), ROWS)
        e = E2[t] + e2r[t].astype(F32)
        comp[at, :] = spread(V[t], 256) * (a2_gain * e + k2_h * H2[at, :] + k2_0)
        return carry

    lax.fori_loop(0, OWN, back_second, 0)
    to_padded()
    for i in range(IMAGES):
        for c in range(3):
            at = EDGE + i * 256 - (c - 1)
            Q[c, i * 256 : (i + 1) * 256, :] = P0[at : at + 256, :].astype(BF16)

    pair_add(0, wp.at[0], wc.at[0], wa.at[0])
    for cp in spread_copies(0, wa.at[0], wr.at[0]):
        cp.start()

    def conv_back(i, carry):
        total = None
        for r in range(3):
            at = pl.ds(pl.multiple_of(i * 256 + 16 * (2 - r), 16), SIDE * PAD)
            for c in range(3):
                w = W2T[:, :, 768 * r + 256 * c : 768 * r + 256 * (c + 1)].reshape(256, 256)
                part = mm(Q[c, at, :], w)
                total = part if total is None else total + part
        padded[pl.ds(pl.multiple_of(i * SIDE * PAD, 16), SIDE * PAD), :] = total
        return carry

    lax.fori_loop(0, IMAGES, conv_back, 0)
    from_padded(comp)

    def sum_back_first(t, carry):
        s, q = carry
        e = comp[pl.ds(pl.multiple_of(t * ROWS, 16), ROWS), :] * D1[t]
        E1[t] = e
        e1s[t] = e.astype(BF16)
        xcopy(3, e1s, e1r, t).start()
        return s + fold8(e), q + fold8(e * (H1[t] - avg1))

    s, q = lax.fori_loop(0, OWN, sum_back_first, (zero, zero))
    ar_start(5, pack2(fold1(s), fold1(q * scale1)), False)

    wf[0] = spread_add(0, wa.at[0], wr.at[0], wh.at[0]).astype(BF16)
    wide_give(0, 0)

    acc_s[...] = jnp.zeros_like(acc_s)

    def taps(i, carry):
        left = Q[1, pl.ds(pl.multiple_of(i * 256 + 16, 16), SIDE * PAD), :]
        for r in range(3):
            right = PC[pl.ds(pl.multiple_of(i * 256 + 16 * r, 16), SIDE * PAD), :]
            acc_s[:, 768 * r : 768 * (r + 1)] += mm_tn(left, right)
        return carry

    lax.fori_loop(0, IMAGES, taps, 0)
    sp[...] = acc_s[...].astype(BF16).reshape(2, 2, 64, 2304)
    for cp in pair_copies(2, sp, sc):
        cp.start()

    shift1, gain1 = unpack2(ar_finish(5, False))
    k1_h = -a1_gain * gain1 * scale1 * inv_n2
    k1_0 = -a1_gain * shift1 * inv_n2 - k1_h * avg1

    def back_first(t, e, h):
        g = (spread(V[t], 256) * (a1_gain * e + k1_h * h + k1_0)).astype(BF16)
        G1[t] = g
        out = (mm(g, W1T[...].reshape(256, 512)) + GS[t]).astype(BF16)
        RES[0, t] = out[:, 0:256]
        RES[1, t] = out[:, 256:512]

    ig_here = [
        local(RES.at[lo, pl.ds(OWN * s, OWN)], ig_out.at[pl.ds(mine + part, OWN)], out_sem.at[2 + s])
        for s, part in parts
    ]
    ig_there = [
        remote(
            RES.at[1 - lo, pl.ds(OWN * s, OWN)], ig_out.at[pl.ds(mine + part, OWN)], o_send.at[2 + s], o_recv.at[2 + s], beside
        )
        for s, part in parts
    ]
    for cp in res_here:
        cp.wait()
    for cp in res_there:
        cp.wait_send()

    def own_back_first(t, carry):
        back_first(t, E1[t], H1[t])
        return carry

    lax.fori_loop(0, OWN, own_back_first, 0)
    ig_here[0].start()
    ig_there[0].start()
    pair_add(2, sp, sc, sa)
    for cp in spread_copies(2, sa, sr):
        cp.start()
    for cp in h1x:
        cp.wait_recv()

    def other_back_first(t, carry):
        xcopy(3, e1s, e1r, t).wait_recv()
        back_first(t + OWN, e1r[t].astype(F32), h1o[t].astype(F32))
        return carry

    lax.fori_loop(0, OWN, other_back_first, 0)
    ig_here[1].start()
    ig_there[1].start()

    def features_of(t):
        left = F[0, pl.ds(2 * t, 2)].reshape(2 * ROWS, 256)
        right = F[1, pl.ds(2 * t, 2)].reshape(2 * ROWS, 256)
        return jnp.concatenate([left, right], axis=1)

    wide_part(1, G1, features_of)
    for cp in pair_copies(1, wp.at[1], wc.at[1]):
        cp.start()

    pair_add(1, wp.at[1], wc.at[1], wa.at[1])
    for cp in spread_copies(1, wa.at[1], wr.at[1]):
        cp.start()
    sf[...] = spread_add(2, sa, sr, sh).astype(BF16)
    cross = remote(sf, sx, g_send.at[2, 26], g_recv.at[2, 26], across)

    @pl.when(jnp.logical_not(keeps))
    def _():
        cross.start()

    wf[1] = spread_add(1, wa.at[1], wr.at[1], wh.at[1]).astype(BF16)
    wide_give(1, 1)

    def s_copies():
        return give_copies(2, sf, sfin.at[own_sub], hi, 1)

    @pl.when(keeps)
    def _():
        cross.wait_recv()
        total = (sf[...].astype(F32) + sx[...].astype(F32)).astype(BF16)
        sf[...] = total
        sfin[own_sub] = total
        for cp in s_copies():
            cp.start()

    def own64(v):
        half = jnp.where(hi == 0, v[:, 0:128], v[:, 128:256])
        swapped = jnp.concatenate([half[:, 64:128], half[:, 0:64]], axis=1)
        return jnp.concatenate([jnp.where(lo == 0, half, swapped), jnp.zeros((1, 128), F32)], axis=1)

    def own256(v):
        return jnp.where(lo == 0, v[:, 0:256], v[:, 256:512])

    st_out[...] = jnp.concatenate(
        [
            own64(gain1),
            own64(shift1),
            own64(gain2),
            own64(shift2),
            own256(gain3),
            own256(shift3),
            jnp.zeros((2, 256), F32),
        ],
        axis=0,
    )

    wide_take(0, 0, eg_out)
    wide_take(1, 1, rg_out)
    for sub in range(n_sub):
        q = sub * 2 + hi
        t = lax.rem(g_lo - q + n_lo, n_lo)

        @pl.when(q != g_lo)
        def _():
            arrived(sfin.at[sub], g_recv.at[2, 10 + 8 * hi + t])

    sg_out[...] = sfin[...].astype(F32).reshape(64, 2304)

    wide_close(0, 0)
    wide_close(1, 1)
    for cp in pair_copies(2, sp, sc) + spread_copies(2, sa, sr):
        cp.wait_send()

    @pl.when(keeps)
    def _():
        for cp in s_copies():
            cp.wait_send()

    @pl.when(jnp.logical_not(keeps))
    def _():
        cross.wait_send()

    for cp in ig_here:
        cp.wait()
    for cp in ig_there:
        cp.wait()
    for cp in res_there:
        cp.wait_recv()
    for cp in fx + cx + w1x + pkx + w3x + h1x + [w2x_across, w2x_beside, w2x_pass]:
        cp.wait_send()
    for kind, src, dst in ((0, h1s, h1r), (1, h2s, h2r), (2, e2s, e2r), (3, e1s, e1r)):
        for t in range(OWN):
            xcopy(kind, src, dst, t).wait_send()
    for k, half in ((0, False), (1, False), (2, True), (3, True), (4, False), (5, False)):
        ar_close(k, half)


def block(n_pix, n_ch, *args):
    (feat, cot, mask, w1, w2, w3, params) = args
    rows, lanes = feat.shape
    n_lo = min(n_pix, 8)
    n_hi = n_pix // n_lo
    piece = 128 // n_lo
    n_sub = n_lo // 2
    chunks = rows // ROWS
    any_space = pl.BlockSpec(memory_space=pl.ANY)
    vmem = pl.BlockSpec(memory_space=pltpu.VMEM)
    V = pltpu.VMEM
    DMA = pltpu.SemaphoreType.DMA
    scratch = [
        V((2, BOTH, ROWS, 256), BF16),
        V((2, BOTH, ROWS, 256), BF16),
        V((BOTH, ROWS, 128), F32),
        V((1024, 64), BF16),
        V((2304, 64), BF16),
        V((2, 64, 512), BF16),
        V((4, 64, 512), BF16),
        V((4, 64, 2304), BF16),
        V((4, 64, 512), BF16),
        V((4, 8, 256), F32),
        V((6, 8, 128), F32),
        V((6, n_pix * n_ch, 8, 128), F32),
        V((OWN, ROWS, 256), BF16),
        V((OWN, ROWS, 256), BF16),
        V((OWN, ROWS, 256), F32),
        V((OWN, ROWS, 256), BF16),
        V((OWN, ROWS, 256), BF16),
        V((OWN, ROWS, 256), F32),
        V((OWN * ROWS, 256), F32),
        V((FLAT + 2 * EDGE, 256), F32),
        V((FLAT, 768), BF16),
        V((3, FLAT, 256), BF16),
        V((IMAGES * SIDE * PAD, 256), F32),
        V((OWN * ROWS, 256), F32),
        V((OWN, ROWS, 256), BF16),
        V((OWN, ROWS, 256), BF16),
        V((BOTH, ROWS, 256), BF16),
        V((BOTH, ROWS, 256), F32),
        V((BOTH, ROWS, 512), F32),
        V((BOTH, ROWS, 512), F32),
        V((2, BOTH, ROWS, 256), BF16),
        V((BOTH, ROWS, 512), BF16),
        V((OWN, ROWS, 256), F32),
        V((OWN, ROWS, 256), BF16),
        V((OWN, ROWS, 256), BF16),
        V((OWN, ROWS, 256), F32),
        V((OWN, ROWS, 256), BF16),
        V((OWN, ROWS, 256), BF16),
        V((BOTH, ROWS, 256), BF16),
        V((256, 512), F32),
        V((256, 2304), F32),
        V((2, 2, 2, 64, 512), BF16),
        V((2, 2, 64, 512), BF16),
        V((2, 2, n_sub, piece, 512), BF16),
        V((2, n_lo, piece, 512), BF16),
        V((2, n_hi, piece, 512), BF16),
        V((2, piece, 512), BF16),
        V((2, 2, n_sub, piece, 512), BF16),
        V((2, 2, 64, 2304), BF16),
        V((2, 64, 2304), BF16),
        V((2, n_sub, piece, 2304), BF16),
        V((n_lo, piece, 2304), BF16),
        V((n_hi, piece, 2304), BF16),
        V((piece, 2304), BF16),
        V((piece, 2304), BF16),
        V((n_sub, piece, 2304), BF16),
        DMA((8,)),
        DMA((4,)),
        DMA((4,)),
        DMA((16,)),
        DMA((16,)),
        DMA((6,)),
        DMA((6,)),
        DMA((5, OWN)),
        DMA((5, OWN)),
        DMA((4,)),
        DMA((4,)),
        DMA((4,)),
        DMA((3, 28 + n_hi)),
        DMA((3, 28 + n_hi)),
    ]
    wide = jax.ShapeDtypeStruct((chunks, ROWS, lanes), BF16)
    return pl.pallas_call(
        functools.partial(kernel, n_pix, n_ch),
        out_shape=(
            wide,
            wide,
            jax.ShapeDtypeStruct((64, 1024), F32),
            jax.ShapeDtypeStruct((64, 2304), F32),
            jax.ShapeDtypeStruct((64, 1024), F32),
            jax.ShapeDtypeStruct((8, 256), F32),
        ),
        in_specs=[any_space, any_space, vmem, any_space, any_space, any_space, vmem],
        out_specs=(any_space, any_space, vmem, vmem, vmem, vmem),
        scratch_shapes=scratch,
        compiler_params=pltpu.CompilerParams(
            collective_id=0, has_side_effects=True, vmem_limit_bytes=56 * 2**20
        ),
        name="bottleneck",
    )(
        feat.reshape(chunks, ROWS, lanes),
        cot.reshape(chunks, ROWS, lanes),
        mask.astype(F32).reshape(chunks, ROWS),
        w1,
        w2.reshape(2304, 64),
        w3,
        params,
    )


def solution(mesh):
    n_pix, n_ch = mesh.shape["pix"], mesh.shape["ch"]

    def body(feat, mask, w1, w2, w3, g1, b1, g2, b2, g3, b3, cot):
        params = jnp.concatenate([v.astype(F32) for v in (g1, b1, g2, b2, g3, b3)]).reshape(1, 768)
        res, ig, rg, sg, eg, st = block(n_pix, n_ch, feat, cot, mask, w1, w2, w3, params)
        return (
            res.reshape(feat.shape),
            ig.reshape(feat.shape),
            rg.T,
            sg.T.reshape(3, 3, 256, 64),
            eg,
            st[0, 0:64],
            st[1, 0:64],
            st[2, 0:64],
            st[3, 0:64],
            st[4],
            st[5],
        )

    wide = P("pix", "ch")
    return jax.shard_map(
        body,
        mesh=mesh,
        in_specs=(wide, P("pix"), P(None, "ch"), P(None, None, None, "ch"), P("ch", None)) + (P("ch"),) * 6 + (wide,),
        out_specs=(wide, wide, P(None, "ch"), P(None, None, None, "ch"), P("ch", None)) + (P("ch"),) * 6,
        check_vma=False,
    )
```

```python
import functools

import jax
import jax.numpy as jnp
from jax import lax
from jax.experimental import pallas as pl
from jax.experimental.pallas import tpu as pltpu
from jax.sharding import PartitionSpec as P

SIDE = 14
EPS = 1e-05
MESH = pl.DeviceIdType.MESH
F32 = jnp.float32
BF16 = jnp.bfloat16

ROWS = 112
OWN = 7
BOTH = 14
IMAGES = 4
PAD = 16
FLAT = IMAGES * PAD * PAD
EDGE = 8


def mm(a, b):
    return jnp.dot(a, b, preferred_element_type=F32)


def mm_nt(a, b):
    return lax.dot_general(a, b, (((1,), (1,)), ((), ())), preferred_element_type=F32)


def mm_tn(a, b):
    return lax.dot_general(a, b, (((0,), (0,)), ((), ())), preferred_element_type=F32)


def logistic(v):
    return 0.5 * jnp.tanh(0.5 * v) + 0.5


def fold8(v):
    return jnp.sum(v.reshape(v.shape[0] // 8, 8, v.shape[1]), axis=0)


def fold1(v):
    return jnp.sum(v, axis=0, keepdims=True)


def spread(v, lanes):
    return jnp.concatenate([v] * (lanes // 128), axis=1)


def kernel(
    n_pix,
    n_ch,
    feat,
    cot,
    mask,
    w1_in,
    w2_in,
    w3_in,
    g1_in,
    b1_in,
    g2_in,
    b2_in,
    g3_in,
    b3_in,
    res_out,
    ig_out,
    rg_out,
    sg_out,
    eg_out,
    st_out,
    F,
    C,
    V,
    W1T,
    W2T,
    W3,
    pk,
    sbuf,
    rbuf,
    h1s,
    h1r,
    H1,
    h1b,
    h1o,
    D1,
    comp,
    P0,
    PC,
    Q,
    padded,
    H2,
    h2s,
    h2r,
    A2,
    D2,
    H3,
    GS,
    RES,
    G3,
    E2,
    e2s,
    e2r,
    E1,
    e1s,
    e1r,
    G1,
    acc_w,
    acc_s,
    wp,
    wc,
    wa,
    wr,
    wh,
    wf,
    wfin,
    sp,
    sc,
    sa,
    sr,
    sh,
    sf,
    sx,
    sfin,
    ld_sem,
    fx_send,
    fx_recv,
    w_send,
    w_recv,
    ar_send,
    ar_recv,
    x_send,
    x_recv,
    out_sem,
    o_send,
    o_recv,
    g_send,
    g_recv,
):
    me_p, me_c = lax.axis_index("pix"), lax.axis_index("ch")
    hi, lo = me_c // 2, lax.rem(me_c, 2)
    n_lo = min(n_pix, 8)
    n_hi = n_pix // n_lo
    g_hi, g_lo = me_p // n_lo, lax.rem(me_p, n_lo)
    across = (me_p, (1 - hi) * 2 + lo)
    beside = (me_p, hi * 2 + 1 - lo)
    n_all = n_pix * n_ch

    def remote(src, dst, send, recv, device):
        return pltpu.make_async_remote_copy(
            src_ref=src, dst_ref=dst, send_sem=send, recv_sem=recv, device_id=device, device_id_type=MESH
        )

    def local(src, dst, sem):
        return pltpu.make_async_copy(src, dst, sem)

    mine, theirs = lo * BOTH, (1 - lo) * BOTH
    part0, part1 = hi * OWN, (1 - hi) * OWN

    w1_load = local(w1_in.at[:, pl.ds(pl.multiple_of(hi * 512, 512), 512)], W1T.at[me_c], ld_sem.at[0])
    w2_load = local(w2_in, W2T.at[me_c], ld_sem.at[1])
    f_load = [
        local(feat.at[pl.ds(mine + part, OWN)], F.at[lo, pl.ds(OWN * s, OWN)], ld_sem.at[2 + s])
        for s, part in enumerate((part0, part1))
    ]
    c_load = [
        local(cot.at[pl.ds(mine + part, OWN)], C.at[lo, pl.ds(OWN * s, OWN)], ld_sem.at[4 + s])
        for s, part in enumerate((part0, part1))
    ]
    w3_load = local(w3_in.at[:, pl.ds(pl.multiple_of(hi * 512, 512), 512)], W3.at[me_c], ld_sem.at[6])
    w1_load.start()
    f_load[1].start()
    f_load[0].start()
    w2_load.start()
    w3_load.start()
    c_load[0].start()
    c_load[1].start()

    barrier = pltpu.get_barrier_semaphore()

    def greet(t, carry):
        q = lax.rem(me_p * n_ch + me_c + t, n_all)
        pl.semaphore_signal(barrier, inc=1, device_id=(q // n_ch, lax.rem(q, n_ch)), device_id_type=MESH)
        return carry

    lax.fori_loop(1, n_all, greet, 0)

    row_i = lax.broadcasted_iota(jnp.int32, (64, 256), 0)
    col_i = lax.broadcasted_iota(jnp.int32, (64, 256), 1)
    place = (row_i == col_i - 64 * me_c).astype(BF16)
    narrow = jnp.concatenate([v[...].astype(F32).reshape(1, 64) for v in (g1_in, b1_in, g2_in, b2_in)] * 2, axis=0)
    pk_rows = [mm(narrow.astype(BF16), place)[0:4]]
    pk_rows += [v[...].astype(F32).reshape(1, 256) for v in (g3_in, b3_in)]
    pk[me_c] = jnp.concatenate(pk_rows + [jnp.zeros((2, 256), F32)], axis=0)

    pl.semaphore_wait(barrier, n_all - 1)

    fx = [
        remote(
            feat.at[pl.ds(theirs + part, OWN)], F.at[lo, pl.ds(OWN * s, OWN)], fx_send.at[s], fx_recv.at[s], beside
        )
        for s, part in enumerate((part0, part1))
    ]
    cx = [
        remote(
            cot.at[pl.ds(theirs + part, OWN)], C.at[lo, pl.ds(OWN * s, OWN)], fx_send.at[2 + s], fx_recv.at[2 + s], beside
        )
        for s, part in enumerate((part0, part1))
    ]
    others = []
    for t in range(1, n_ch):
        q = lax.rem(me_c + t, n_ch)
        others.append((t - 1, (me_p, q), q // 2))
    w1x = [
        remote(
            w1_in.at[:, pl.ds(pl.multiple_of(h * 512, 512), 512)], W1T.at[me_c], w_send.at[t], w_recv.at[me_c], dev
        )
        for t, dev, h in others
    ]
    pkx = [remote(pk.at[me_c], pk.at[me_c], w_send.at[4 + t], w_recv.at[4 + me_c], dev) for t, dev, h in others]
    w3x = [
        remote(
            w3_in.at[:, pl.ds(pl.multiple_of(h * 512, 512), 512)],
            W3.at[me_c],
            w_send.at[8 + t],
            w_recv.at[8 + me_c],
            dev,
        )
        for t, dev, h in others
    ]
    for cp in w1x:
        cp.start()
    fx[1].start()
    fx[0].start()
    for cp in pkx:
        cp.start()

    diag = lax.broadcasted_iota(jnp.int32, (ROWS, ROWS), 0) == lax.broadcasted_iota(jnp.int32, (ROWS, ROWS), 1)
    ones = jnp.ones((ROWS, 128), BF16)

    def put_mask(t, carry):
        at = mine + jnp.where(t < OWN, part0 + t, part1 + t - OWN)
        row = mask[pl.ds(at, 1), :].astype(F32)
        V[t] = mm(jnp.where(diag, row, 0.0).astype(BF16), ones)
        return carry

    lax.fori_loop(0, BOTH, put_mask, 0)

    P0[...] = jnp.zeros_like(P0)

    def arrived(dst, sem):
        local(dst, dst, sem).wait()

    for t, dev, h in others:
        q = dev[1]
        arrived(W1T.at[q], w_recv.at[q])

    w1_load.wait()

    f_load[1].wait()
    fx[1].wait_recv()
    w1_all = W1T[...].reshape(256, 512)

    def first(t):
        wide = jnp.concatenate([F[0, t], F[1, t]], axis=1)
        return mm_nt(wide, w1_all)

    def xcopy(kind, src, dst, t):
        return remote(src.at[t], dst.at[t], x_send.at[kind, t], x_recv.at[kind, t], across)

    def send_first(t, carry):
        h1s[t] = first(t + OWN).astype(BF16)
        xcopy(0, h1s, h1r, t).start()
        return carry

    lax.fori_loop(0, OWN, send_first, 0)
    f_load[0].wait()
    fx[0].wait_recv()

    def keep_first(t, carry):
        H1[t] = first(t)
        return carry

    lax.fori_loop(0, OWN, keep_first, 0)

    w2x_across = remote(W2T.at[me_c], W2T.at[me_c], w_send.at[12], w_recv.at[12], across)
    w2x_beside = remote(W2T.at[me_c], W2T.at[me_c], w_send.at[13], w_recv.at[13], beside)
    far = (1 - hi) * 2 + lo
    w2x_pass = remote(W2T.at[far], W2T.at[far], w_send.at[14], w_recv.at[14], beside)
    w2_load.wait()
    w2x_beside.start()
    w2x_across.start()
    cx[0].start()
    cx[1].start()
    for t, dev, h in others:
        arrived(pk.at[dev[1]], w_recv.at[4 + dev[1]])
    gains = pk[0] + pk[1] + pk[2] + pk[3]
    g1, b1, g2, b2 = (gains[k : k + 1] for k in range(4))
    pair0, pair1 = pk[2 * hi], pk[2 * hi + 1]
    g3 = jnp.concatenate([pair0[4:5], pair1[4:5]], axis=1)
    b3 = jnp.concatenate([pair0[5:6], pair1[5:6]], axis=1)

    def ar_start(k, val, half):
        n = n_pix * 2 if half else n_all
        me = me_p * 2 + lo if half else me_p * n_ch + me_c
        sbuf[k] = val
        rbuf[k, me] = val

        def send(t, carry):
            q = lax.rem(me + t, n)
            dev = (q // 2, hi * 2 + lax.rem(q, 2)) if half else (q // n_ch, lax.rem(q, n_ch))
            remote(sbuf.at[k], rbuf.at[k, me], ar_send.at[k], ar_recv.at[k], dev).start()
            return carry

        lax.fori_loop(1, n, send, 0)

    def ar_finish(k, half):
        n = n_pix * 2 if half else n_all
        span = rbuf.at[k, pl.ds(0, n - 1)]
        arrived(span, ar_recv.at[k])
        total = jnp.sum(rbuf[k, 0:n], axis=0)
        return total

    def ar_close(k, half):
        n = n_pix * 2 if half else n_all
        span = rbuf.at[k, pl.ds(0, n - 1)]
        arrived(span, ar_send.at[k])

    def pack2(a, b, extra=None):
        tail = jnp.zeros((1, 128), F32) if extra is None else extra
        return jnp.concatenate(
            [a[:, 0:128], a[:, 128:256], b[:, 0:128], b[:, 128:256], tail, jnp.zeros((3, 128), F32)], axis=0
        )

    def unpack2(v):
        return (
            jnp.concatenate([v[0:1], v[1:2]], axis=1),
            jnp.concatenate([v[2:3], v[3:4]], axis=1),
        )

    def pack3(a, b):
        return jnp.concatenate([a[:, 128 * i : 128 * (i + 1)] for i in range(4)] + [b[:, 128 * i : 128 * (i + 1)] for i in range(4)], axis=0)

    def unpack3(v):
        return (
            jnp.concatenate([v[i : i + 1] for i in range(4)], axis=1),
            jnp.concatenate([v[i : i + 1] for i in range(4, 8)], axis=1),
        )

    zero = jnp.zeros((8, 256), F32)

    def sum_first(t, carry):
        s, q, n = carry
        xcopy(0, h1s, h1r, t).wait_recv()
        h = H1[t] + h1r[t].astype(F32)
        H1[t] = h
        h1b[t] = h.astype(BF16)
        v = V[t]
        vh = spread(v, 256) * h
        return s + fold8(vh), q + fold8(vh * h), n + fold8(v)

    s, q, n = lax.fori_loop(0, OWN, sum_first, (zero, zero, jnp.zeros((8, 128), F32)))
    ar_start(0, pack2(fold1(s), fold1(q), fold1(n)), False)
    arrived(W2T.at[far], w_recv.at[12])
    w2x_pass.start()
    total = ar_finish(0, False)
    s, q = unpack2(total)
    inv_n = 1.0 / spread(total[4:5], 512)
    inv_n2 = inv_n[:, 0:256]
    avg1 = s * inv_n2
    scale1 = lax.rsqrt(q * inv_n2 - avg1 * avg1 + EPS)
    a1_gain = g1 * scale1
    a1_shift = b1 - avg1 * a1_gain

    def act_first(t, carry):
        v = spread(V[t], 256)
        aff = v * (H1[t] * a1_gain + a1_shift)
        sig = logistic(aff)
        act = aff * sig
        comp[pl.ds(pl.multiple_of(t * ROWS, 16), ROWS), :] = act
        D1[t] = v * (sig + act * (1.0 - sig))
        return carry

    lax.fori_loop(0, OWN, act_first, 0)

    def to_padded():
        for i in range(IMAGES):
            for y in range(SIDE):
                P0[EDGE + (i * PAD + y + 1) * PAD : EDGE + (i * PAD + y + 1) * PAD + SIDE, :] = comp[
                    (i * SIDE + y) * SIDE : (i * SIDE + y + 1) * SIDE, :
                ]

    def from_padded(dst):
        for i in range(IMAGES):
            for y in range(SIDE):
                dst[(i * SIDE + y) * SIDE : (i * SIDE + y + 1) * SIDE, :] = padded[
                    (i * SIDE + y) * PAD : (i * SIDE + y) * PAD + SIDE, :
                ]

    to_padded()
    for i in range(IMAGES):
        for c in range(3):
            at = EDGE + i * 256 + c - 1
            PC[i * 256 : (i + 1) * 256, 256 * c : 256 * (c + 1)] = P0[at : at + 256, :].astype(BF16)

    arrived(W2T.at[hi * 2 + 1 - lo], w_recv.at[13])
    arrived(W2T.at[(1 - hi) * 2 + 1 - lo], w_recv.at[14])
    for cp in w3x:
        cp.start()
    h1x = [remote(h1b, h1o, x_send.at[4, 0], x_recv.at[4, 0], across)]

    def conv(i, carry):
        total = None
        for r in range(3):
            rows = PC[pl.ds(pl.multiple_of(i * 256 + 16 * r, 16), SIDE * PAD), :]
            part = mm_nt(rows, jnp.concatenate([W2T[:, 3 * r + c].reshape(256, 256) for c in range(3)], axis=1))
            total = part if total is None else total + part
        padded[pl.ds(pl.multiple_of(i * SIDE * PAD, 16), SIDE * PAD), :] = total
        return carry

    lax.fori_loop(0, IMAGES, conv, 0)
    from_padded(H2)

    def sum_second(t, carry):
        s, q = carry
        h = H2[pl.ds(pl.multiple_of(t * ROWS, 16), ROWS), :]
        h2s[t] = h.astype(BF16)
        xcopy(1, h2s, h2r, t).start()
        vh = spread(V[t], 256) * h
        return s + fold8(vh), q + fold8(vh * h)

    s, q = lax.fori_loop(0, OWN, sum_second, (zero, zero))
    ar_start(1, pack2(fold1(s), fold1(q)), False)
    s, q = unpack2(ar_finish(1, False))
    avg2 = s * inv_n2
    scale2 = lax.rsqrt(q * inv_n2 - avg2 * avg2 + EPS)
    a2_gain = g2 * scale2
    a2_shift = b2 - avg2 * a2_gain

    w3_load.wait()
    for t, dev, h in others:
        arrived(W3.at[dev[1]], w_recv.at[8 + dev[1]])

    def act_second(t, h, carry):
        s, q = carry
        v = spread(V[t], 256)
        aff = v * (h * a2_gain + a2_shift)
        sig = logistic(aff)
        act = aff * sig
        D2[t] = v * (sig + act * (1.0 - sig))
        act = act.astype(BF16)
        A2[t] = act
        h3 = mm(act, W3[...].reshape(256, 512))
        H3[t] = h3
        return s + fold8(h3), q + fold8(h3 * h3)

    def own_second(t, carry):
        return act_second(t, H2[pl.ds(pl.multiple_of(t * ROWS, 16), ROWS), :], carry)

    def other_second(t, carry):
        xcopy(1, h2s, h2r, t).wait_recv()
        return act_second(t + OWN, h2r[t].astype(F32), carry)

    wide_zero = jnp.zeros((8, 512), F32)
    carry = lax.fori_loop(0, OWN, own_second, (wide_zero, wide_zero))
    s, q = lax.fori_loop(0, OWN, other_second, carry)
    ar_start(2, pack3(fold1(s), fold1(q)), True)
    for cp in h1x:
        cp.start()
    for cp in c_load:
        cp.wait()
    for cp in cx:
        cp.wait_recv()
    s, q = unpack3(ar_finish(2, True))
    avg3 = s * inv_n
    scale3 = lax.rsqrt(q * inv_n - avg3 * avg3 + EPS)
    a3_gain = g3 * scale3
    a3_shift = b3 - avg3 * a3_gain

    def last(t, carry):
        s, q = carry
        v = spread(V[t], 512)
        h3 = H3[t]
        wide = jnp.concatenate([F[0, t], F[1, t]], axis=1).astype(F32)
        total = v * (h3 * a3_gain + a3_shift) + wide
        sig = logistic(total)
        out = total * sig
        RES[0, t] = out[:, 0:256].astype(BF16)
        RES[1, t] = out[:, 256:512].astype(BF16)
        given = jnp.concatenate([C[0, t], C[1, t]], axis=1).astype(F32)
        gs = given * (sig + out * (1.0 - sig))
        GS[t] = gs
        vg = v * gs
        return s + fold8(vg), q + fold8(vg * (h3 - avg3))

    s, q = lax.fori_loop(0, BOTH, last, (wide_zero, wide_zero))
    ar_start(3, pack3(fold1(s), fold1(q * scale3)), True)
    parts = ((0, part0), (1, part1))
    res_here = [
        local(RES.at[lo, pl.ds(OWN * s, OWN)], res_out.at[pl.ds(mine + part, OWN)], out_sem.at[s]) for s, part in parts
    ]
    res_there = [
        remote(RES.at[1 - lo, pl.ds(OWN * s, OWN)], res_out.at[pl.ds(mine + part, OWN)], o_send.at[s], o_recv.at[s], beside)
        for s, part in parts
    ]
    for cp in res_here + res_there:
        cp.start()
    shift3, gain3 = unpack3(ar_finish(3, True))
    k3_h = -a3_gain * gain3 * scale3 * inv_n
    k3_0 = -a3_gain * shift3 * inv_n - k3_h * avg3

    def back_third(t, carry):
        s, q, h2 = carry[0], carry[1], carry[2]
        v = spread(V[t], 512)
        g = (v * (a3_gain * GS[t] + k3_h * H3[t] + k3_0)).astype(BF16)
        G3[t] = g
        e = mm_nt(g, W3[...].reshape(256, 512)) * D2[t]
        return e, s + fold8(e), q + fold8(e * (h2 - avg2))

    def other_third(t, carry):
        e, s, q = back_third(t + OWN, (carry[0], carry[1], h2r[t].astype(F32)))
        e2s[t] = e.astype(BF16)
        xcopy(2, e2s, e2r, t).start()
        return s, q

    def own_third(t, carry):
        e, s, q = back_third(t, (carry[0], carry[1], H2[pl.ds(pl.multiple_of(t * ROWS, 16), ROWS), :]))
        E2[t] = e
        return s, q

    carry = lax.fori_loop(0, OWN, other_third, (zero, zero))
    s, q = lax.fori_loop(0, OWN, own_third, carry)
    ar_start(4, pack2(fold1(s), fold1(q * scale2)), False)

    piece = 128 // n_lo
    n_sub = n_lo // 2

    def pair_copies(k, part, got):
        return [
            remote(part.at[h, 1 - lo], got.at[h], g_send.at[k, h], g_recv.at[k, h], beside) for h in range(2)
        ]

    def pair_add(k, part, got, acc):
        for h, cp in enumerate(pair_copies(k, part, got)):
            cp.wait_recv()
            both = part[h, lo].astype(F32) + got[h].astype(F32)
            acc[h] = both.astype(BF16).reshape(acc.shape[1:])

    def spread_copies(k, acc, got):
        copies = []
        for t in range(1, n_lo):
            q = lax.rem(g_lo + t, n_lo)
            copies.append(
                remote(
                    acc.at[lax.rem(q, 2), q // 2],
                    got.at[g_lo],
                    g_send.at[k, 2 + t],
                    g_recv.at[k, 2 + t],
                    (g_hi * n_lo + q, me_c),
                )
            )
        return copies

    def spread_add(k, acc, got, level):
        for cp in spread_copies(k, acc, got):
            cp.wait_recv()
        total = acc[lax.rem(g_lo, 2), g_lo // 2].astype(F32)
        for t in range(1, n_lo):
            total = total + got[lax.rem(g_lo + t, n_lo)].astype(F32)
        if n_hi > 1:
            level[g_hi] = total.astype(BF16)

            def swap(t):
                q = lax.rem(g_hi + t, n_hi)
                return remote(
                    level.at[g_hi], level.at[g_hi], g_send.at[k, 27 + t], g_recv.at[k, 27 + t], (q * n_lo + g_lo, me_c)
                )

            for t in range(1, n_hi):
                swap(t).start()
            for t in range(1, n_hi):
                swap(t).wait()
            total = level[0].astype(F32)
            for t in range(1, n_hi):
                total = total + level[t].astype(F32)
        return total

    def give_copies(k, done, fin, to_hi, first=0):
        copies = []
        for t in range(first, n_lo):
            q = lax.rem(g_lo + t, n_lo)
            copies.append(
                remote(
                    done, fin, g_send.at[k, 10 + t], g_recv.at[k, 10 + 8 * hi + t], (g_hi * n_lo + q, to_hi * 2 + lo)
                )
            )
        return copies

    owner_hi = lax.rem(g_lo, 2)
    own_sub = g_lo // 2
    keeps = owner_hi == hi

    def wide_give(k, slot):
        copies = give_copies(k, wf.at[slot], wfin.at[slot, hi, own_sub], owner_hi)
        for t, cp in enumerate(copies):
            if t == 0:

                @pl.when(jnp.logical_not(keeps))
                def _():
                    cp.start()

                @pl.when(keeps)
                def _():
                    wfin[slot, hi, own_sub] = wf[slot]

            else:
                cp.start()

    def wide_take(k, slot, out):
        for sub in range(n_sub):
            q = sub * 2 + hi
            t = lax.rem(g_lo - q + n_lo, n_lo)
            for h in range(2):

                @pl.when(jnp.logical_not((q == g_lo) & (hi == h)))
                def _():
                    arrived(wfin.at[slot, h, sub], g_recv.at[k, 10 + 8 * h + t])

        for h in range(2):
            out[:, 512 * h : 512 * (h + 1)] = wfin[slot, h].astype(F32).reshape(64, 512)

    def wide_close(k, slot):
        for cp in pair_copies(k, wp.at[slot], wc.at[slot]):
            cp.wait_send()
        for cp in spread_copies(k, wa.at[slot], wr.at[slot]):
            cp.wait_send()
        for t, cp in enumerate(give_copies(k, wf.at[slot], wfin.at[slot, hi, own_sub], owner_hi)):
            if t == 0:

                @pl.when(jnp.logical_not(keeps))
                def _():
                    cp.wait_send()

            else:
                cp.wait_send()

    def wide_part(slot, left, right_of):
        acc_w[...] = jnp.zeros_like(acc_w)

        def add(t, carry):
            a = left[pl.ds(2 * t, 2)].reshape(2 * ROWS, 256)
            acc_w[...] += mm_tn(a, right_of(t))
            return carry

        lax.fori_loop(0, OWN, add, 0)
        wp[slot] = acc_w[...].astype(BF16).reshape(2, 2, 64, 512)

    wide_part(0, A2, lambda t: G3[pl.ds(2 * t, 2)].reshape(2 * ROWS, 512))
    for cp in pair_copies(0, wp.at[0], wc.at[0]):
        cp.start()

    shift2, gain2 = unpack2(ar_finish(4, False))
    k2_h = -a2_gain * gain2 * scale2 * inv_n2
    k2_0 = -a2_gain * shift2 * inv_n2 - k2_h * avg2

    def back_second(t, carry):
        xcopy(2, e2s, e2r, t).wait_recv()
        at = pl.ds(pl.multiple_of(t * ROWS, 16), ROWS)
        e = E2[t] + e2r[t].astype(F32)
        comp[at, :] = spread(V[t], 256) * (a2_gain * e + k2_h * H2[at, :] + k2_0)
        return carry

    lax.fori_loop(0, OWN, back_second, 0)
    to_padded()
    for i in range(IMAGES):
        for c in range(3):
            at = EDGE + i * 256 - (c - 1)
            Q[c, i * 256 : (i + 1) * 256, :] = P0[at : at + 256, :].astype(BF16)

    pair_add(0, wp.at[0], wc.at[0], wa.at[0])
    for cp in spread_copies(0, wa.at[0], wr.at[0]):
        cp.start()

    def conv_back(i, carry):
        total = None
        for r in range(3):
            at = pl.ds(pl.multiple_of(i * 256 + 16 * (2 - r), 16), SIDE * PAD)
            for c in range(3):
                w = W2T[:, 3 * r + c].reshape(256, 256)
                part = mm(Q[c, at, :], w)
                total = part if total is None else total + part
        padded[pl.ds(pl.multiple_of(i * SIDE * PAD, 16), SIDE * PAD), :] = total
        return carry

    lax.fori_loop(0, IMAGES, conv_back, 0)
    from_padded(comp)

    def sum_back_first(t, carry):
        s, q = carry
        e = comp[pl.ds(pl.multiple_of(t * ROWS, 16), ROWS), :] * D1[t]
        E1[t] = e
        e1s[t] = e.astype(BF16)
        xcopy(3, e1s, e1r, t).start()
        return s + fold8(e), q + fold8(e * (H1[t] - avg1))

    s, q = lax.fori_loop(0, OWN, sum_back_first, (zero, zero))
    ar_start(5, pack2(fold1(s), fold1(q * scale1)), False)

    wf[0] = spread_add(0, wa.at[0], wr.at[0], wh.at[0]).astype(BF16)
    wide_give(0, 0)

    acc_s[...] = jnp.zeros_like(acc_s)

    def taps(i, carry):
        left = Q[1, pl.ds(pl.multiple_of(i * 256 + 16, 16), SIDE * PAD), :]
        for r in range(3):
            right = PC[pl.ds(pl.multiple_of(i * 256 + 16 * r, 16), SIDE * PAD), :]
            acc_s[:, 768 * r : 768 * (r + 1)] += mm_tn(left, right)
        return carry

    lax.fori_loop(0, IMAGES, taps, 0)
    sp[...] = acc_s[...].astype(BF16).reshape(2, 2, 64, 2304)
    for cp in pair_copies(2, sp, sc):
        cp.start()

    shift1, gain1 = unpack2(ar_finish(5, False))
    k1_h = -a1_gain * gain1 * scale1 * inv_n2
    k1_0 = -a1_gain * shift1 * inv_n2 - k1_h * avg1

    def back_first(t, e, h):
        g = (spread(V[t], 256) * (a1_gain * e + k1_h * h + k1_0)).astype(BF16)
        G1[t] = g
        out = (mm(g, W1T[...].reshape(256, 512)) + GS[t]).astype(BF16)
        RES[0, t] = out[:, 0:256]
        RES[1, t] = out[:, 256:512]

    ig_here = [
        local(RES.at[lo, pl.ds(OWN * s, OWN)], ig_out.at[pl.ds(mine + part, OWN)], out_sem.at[2 + s])
        for s, part in parts
    ]
    ig_there = [
        remote(
            RES.at[1 - lo, pl.ds(OWN * s, OWN)], ig_out.at[pl.ds(mine + part, OWN)], o_send.at[2 + s], o_recv.at[2 + s], beside
        )
        for s, part in parts
    ]
    for cp in res_here:
        cp.wait()
    for cp in res_there:
        cp.wait_send()

    def own_back_first(t, carry):
        back_first(t, E1[t], H1[t])
        return carry

    lax.fori_loop(0, OWN, own_back_first, 0)
    ig_here[0].start()
    ig_there[0].start()
    pair_add(2, sp, sc, sa)
    for cp in spread_copies(2, sa, sr):
        cp.start()
    for cp in h1x:
        cp.wait_recv()

    def other_back_first(t, carry):
        xcopy(3, e1s, e1r, t).wait_recv()
        back_first(t + OWN, e1r[t].astype(F32), h1o[t].astype(F32))
        return carry

    lax.fori_loop(0, OWN, other_back_first, 0)
    ig_here[1].start()
    ig_there[1].start()

    def features_of(t):
        left = F[0, pl.ds(2 * t, 2)].reshape(2 * ROWS, 256)
        right = F[1, pl.ds(2 * t, 2)].reshape(2 * ROWS, 256)
        return jnp.concatenate([left, right], axis=1)

    wide_part(1, G1, features_of)
    for cp in pair_copies(1, wp.at[1], wc.at[1]):
        cp.start()

    pair_add(1, wp.at[1], wc.at[1], wa.at[1])
    for cp in spread_copies(1, wa.at[1], wr.at[1]):
        cp.start()
    sf[...] = spread_add(2, sa, sr, sh).astype(BF16)
    cross = remote(sf, sx, g_send.at[2, 26], g_recv.at[2, 26], across)

    @pl.when(jnp.logical_not(keeps))
    def _():
        cross.start()

    wf[1] = spread_add(1, wa.at[1], wr.at[1], wh.at[1]).astype(BF16)
    wide_give(1, 1)

    def s_copies():
        return give_copies(2, sf, sfin.at[own_sub], hi, 1)

    @pl.when(keeps)
    def _():
        cross.wait_recv()
        total = (sf[...].astype(F32) + sx[...].astype(F32)).astype(BF16)
        sf[...] = total
        sfin[own_sub] = total
        for cp in s_copies():
            cp.start()

    def own64(v):
        half = jnp.where(hi == 0, v[:, 0:128], v[:, 128:256])
        swapped = jnp.concatenate([half[:, 64:128], half[:, 0:64]], axis=1)
        return jnp.concatenate([jnp.where(lo == 0, half, swapped), jnp.zeros((1, 128), F32)], axis=1)

    def own256(v):
        return jnp.where(lo == 0, v[:, 0:256], v[:, 256:512])

    st_out[...] = jnp.concatenate(
        [
            own64(gain1),
            own64(shift1),
            own64(gain2),
            own64(shift2),
            own256(gain3),
            own256(shift3),
            jnp.zeros((2, 256), F32),
        ],
        axis=0,
    )

    wide_take(0, 0, eg_out)
    wide_take(1, 1, rg_out)
    for sub in range(n_sub):
        q = sub * 2 + hi
        t = lax.rem(g_lo - q + n_lo, n_lo)

        @pl.when(q != g_lo)
        def _():
            arrived(sfin.at[sub], g_recv.at[2, 10 + 8 * hi + t])

    for k in range(9):
        sg_out[k] = sfin[:, :, 256 * k : 256 * (k + 1)].astype(F32).reshape(64, 256)

    wide_close(0, 0)
    wide_close(1, 1)
    for cp in pair_copies(2, sp, sc) + spread_copies(2, sa, sr):
        cp.wait_send()

    @pl.when(keeps)
    def _():
        for cp in s_copies():
            cp.wait_send()

    @pl.when(jnp.logical_not(keeps))
    def _():
        cross.wait_send()

    for cp in ig_here:
        cp.wait()
    for cp in ig_there:
        cp.wait()
    for cp in res_there:
        cp.wait_recv()
    for cp in fx + cx + w1x + pkx + w3x + h1x + [w2x_across, w2x_beside, w2x_pass]:
        cp.wait_send()
    for kind, src, dst in ((0, h1s, h1r), (1, h2s, h2r), (2, e2s, e2r), (3, e1s, e1r)):
        for t in range(OWN):
            xcopy(kind, src, dst, t).wait_send()
    for k, half in ((0, False), (1, False), (2, True), (3, True), (4, False), (5, False)):
        ar_close(k, half)


def block(n_pix, n_ch, *args):
    feat, cot, mask, w1, w2, w3 = args[:6]
    rows, lanes = feat.shape
    n_lo = min(n_pix, 8)
    n_hi = n_pix // n_lo
    piece = 128 // n_lo
    n_sub = n_lo // 2
    chunks = rows // ROWS
    any_space = pl.BlockSpec(memory_space=pl.ANY)
    vmem = pl.BlockSpec(memory_space=pltpu.VMEM)
    V = pltpu.VMEM
    DMA = pltpu.SemaphoreType.DMA
    scratch = [
        V((2, BOTH, ROWS, 256), BF16),
        V((2, BOTH, ROWS, 256), BF16),
        V((BOTH, ROWS, 128), F32),
        V((4, 64, 512), BF16),
        V((4, 9, 64, 256), BF16),
        V((4, 64, 512), BF16),
        V((4, 8, 256), F32),
        V((6, 8, 128), F32),
        V((6, n_pix * n_ch, 8, 128), F32),
        V((OWN, ROWS, 256), BF16),
        V((OWN, ROWS, 256), BF16),
        V((OWN, ROWS, 256), F32),
        V((OWN, ROWS, 256), BF16),
        V((OWN, ROWS, 256), BF16),
        V((OWN, ROWS, 256), F32),
        V((OWN * ROWS, 256), F32),
        V((FLAT + 2 * EDGE, 256), F32),
        V((FLAT, 768), BF16),
        V((3, FLAT, 256), BF16),
        V((IMAGES * SIDE * PAD, 256), F32),
        V((OWN * ROWS, 256), F32),
        V((OWN, ROWS, 256), BF16),
        V((OWN, ROWS, 256), BF16),
        V((BOTH, ROWS, 256), BF16),
        V((BOTH, ROWS, 256), F32),
        V((BOTH, ROWS, 512), F32),
        V((BOTH, ROWS, 512), F32),
        V((2, BOTH, ROWS, 256), BF16),
        V((BOTH, ROWS, 512), BF16),
        V((OWN, ROWS, 256), F32),
        V((OWN, ROWS, 256), BF16),
        V((OWN, ROWS, 256), BF16),
        V((OWN, ROWS, 256), F32),
        V((OWN, ROWS, 256), BF16),
        V((OWN, ROWS, 256), BF16),
        V((BOTH, ROWS, 256), BF16),
        V((256, 512), F32),
        V((256, 2304), F32),
        V((2, 2, 2, 64, 512), BF16),
        V((2, 2, 64, 512), BF16),
        V((2, 2, n_sub, piece, 512), BF16),
        V((2, n_lo, piece, 512), BF16),
        V((2, n_hi, piece, 512), BF16),
        V((2, piece, 512), BF16),
        V((2, 2, n_sub, piece, 512), BF16),
        V((2, 2, 64, 2304), BF16),
        V((2, 64, 2304), BF16),
        V((2, n_sub, piece, 2304), BF16),
        V((n_lo, piece, 2304), BF16),
        V((n_hi, piece, 2304), BF16),
        V((piece, 2304), BF16),
        V((piece, 2304), BF16),
        V((n_sub, piece, 2304), BF16),
        DMA((8,)),
        DMA((4,)),
        DMA((4,)),
        DMA((16,)),
        DMA((16,)),
        DMA((6,)),
        DMA((6,)),
        DMA((5, OWN)),
        DMA((5, OWN)),
        DMA((4,)),
        DMA((4,)),
        DMA((4,)),
        DMA((3, 28 + n_hi)),
        DMA((3, 28 + n_hi)),
    ]
    wide = jax.ShapeDtypeStruct((chunks, ROWS, lanes), BF16)
    made = pl.pallas_call(
        functools.partial(kernel, n_pix, n_ch),
        out_shape=(
            wide,
            wide,
            jax.ShapeDtypeStruct((64, 1024), F32),
            jax.ShapeDtypeStruct((9, 64, 256), F32),
            jax.ShapeDtypeStruct((64, 1024), F32),
            jax.ShapeDtypeStruct((8, 256), F32),
        ),
        in_specs=[any_space, any_space, vmem, any_space, any_space, any_space] + [vmem] * 6,
        out_specs=(any_space, any_space, vmem, vmem, vmem, vmem),
        scratch_shapes=scratch,
        compiler_params=pltpu.CompilerParams(
            collective_id=0, has_side_effects=True, vmem_limit_bytes=56 * 2**20
        ),
        name="bottleneck",
    )(
        feat.reshape(chunks, ROWS, lanes),
        cot.reshape(chunks, ROWS, lanes),
        mask.reshape(chunks, ROWS),
        w1.T,
        w2.transpose(0, 1, 3, 2).reshape(9, 64, 256),
        w3,
        *args[6:],
    )
    narrow = jax.ShapeDtypeStruct((64,), F32)
    broad = jax.ShapeDtypeStruct((256,), F32)
    return pl.pallas_call(
        finish,
        out_shape=tuple(jax.ShapeDtypeStruct(v.shape, v.dtype) for v in made[:5]) + (narrow,) * 4 + (broad,) * 2,
        in_specs=[vmem] * 6,
        out_specs=(any_space,) * 5 + (vmem,) * 6,
        scratch_shapes=[DMA((5,))],
        name="outputs",
    )(*made)


def finish(*refs):
    made, stats, outs, small, sems = refs[:5], refs[5], refs[6:11], refs[11:17], refs[17]
    copies = [pltpu.make_async_copy(a, b, sems.at[i]) for i, (a, b) in enumerate(zip(made, outs))]
    for cp in copies:
        cp.start()
    for i, out in enumerate(small):
        out[...] = stats[i : i + 1, 0 : out.shape[0]].reshape(out.shape)
    for cp in copies:
        cp.wait()


def solution(mesh):
    n_pix, n_ch = mesh.shape["pix"], mesh.shape["ch"]

    def body(feat, mask, w1, w2, w3, g1, b1, g2, b2, g3, b3, cot):
        made = block(n_pix, n_ch, feat, cot, mask, w1, w2, w3, g1, b1, g2, b2, g3, b3)
        res, ig, rg, sg, eg = made[:5]
        return (
            res.reshape(feat.shape),
            ig.reshape(feat.shape),
            rg.T,
            sg.reshape(3, 3, 64, 256).transpose(0, 1, 3, 2),
            eg,
        ) + tuple(made[5:])

    wide = P("pix", "ch")
    return jax.shard_map(
        body,
        mesh=mesh,
        in_specs=(wide, P("pix"), P(None, "ch"), P(None, None, None, "ch"), P("ch", None)) + (P("ch"),) * 6 + (wide,),
        out_specs=(wide, wide, P(None, "ch"), P(None, None, None, "ch"), P("ch", None)) + (P("ch"),) * 6,
        check_vma=False,
    )
```

```python
import functools

import jax
import jax.numpy as jnp
from jax import lax
from jax.experimental import pallas as pl
from jax.experimental.pallas import tpu as pltpu
from jax.sharding import PartitionSpec as P

SIDE = 14
EPS = 1e-05
MESH = pl.DeviceIdType.MESH
F32 = jnp.float32
BF16 = jnp.bfloat16

ROWS = 112
OWN = 7
BOTH = 14
IMAGES = 4
PAD = 16
FLAT = IMAGES * PAD * PAD
EDGE = 8
BLOCK = PAD * PAD


def mm(a, b):
    return jnp.dot(a, b, preferred_element_type=F32)


def mm_nt(a, b):
    return lax.dot_general(a, b, (((1,), (1,)), ((), ())), preferred_element_type=F32)


def mm_tn(a, b):
    return lax.dot_general(a, b, (((0,), (0,)), ((), ())), preferred_element_type=F32)


def logistic(v):
    return 0.5 * jnp.tanh(0.5 * v) + 0.5


def fold8(v):
    return jnp.sum(v.reshape(v.shape[0] // 8, 8, v.shape[1]), axis=0)


def fold1(v):
    return jnp.sum(v, axis=0, keepdims=True)


def spread(v, lanes):
    return jnp.concatenate([v] * (lanes // 128), axis=1)


def kernel(
    n_pix,
    n_ch,
    feat,
    cot,
    mask,
    w1_in,
    w2_in,
    w3_in,
    g1_in,
    b1_in,
    g2_in,
    b2_in,
    g3_in,
    b3_in,
    res_out,
    ig_out,
    rg_out,
    sg_out,
    eg_out,
    st_out,
    F,
    C,
    V,
    W1T,
    W2T,
    W3,
    pk,
    sbuf,
    rbuf,
    h1s,
    h1r,
    H1,
    h1b,
    h1o,
    D1,
    comp,
    P0,
    PC,
    Q,
    padded,
    H2,
    h2s,
    h2r,
    A2,
    D2,
    H3,
    GS,
    RES,
    G3,
    E2,
    e2s,
    e2r,
    E1,
    e1s,
    e1r,
    G1,
    QT,
    rows28,
    acc_w,
    wp,
    wc,
    wa,
    wb,
    wr,
    wh,
    wf,
    wfin,
    acc_s,
    sp,
    sc,
    s1,
    ys,
    yr,
    s2,
    zs,
    zr,
    s3,
    xs,
    xr,
    sh,
    sfin,
    ld_sem,
    fx_send,
    fx_recv,
    w_send,
    w_recv,
    ar_send,
    ar_recv,
    x_send,
    x_recv,
    out_sem,
    o_send,
    o_recv,
    g_send,
    g_recv,
    s_send,
    s_recv,
    h_send,
    h_recv,
):
    me_p, me_c = lax.axis_index("pix"), lax.axis_index("ch")
    hi, lo = me_c // 2, lax.rem(me_c, 2)
    n_lo = 8
    n_hi = n_pix // n_lo
    g_hi, g_lo = me_p // n_lo, lax.rem(me_p, n_lo)
    across = (me_p, (1 - hi) * 2 + lo)
    beside = (me_p, hi * 2 + 1 - lo)
    n_all = n_pix * n_ch

    def remote(src, dst, send, recv, device):
        return pltpu.make_async_remote_copy(
            src_ref=src, dst_ref=dst, send_sem=send, recv_sem=recv, device_id=device, device_id_type=MESH
        )

    def local(src, dst, sem):
        return pltpu.make_async_copy(src, dst, sem)

    mine, theirs = lo * BOTH, (1 - lo) * BOTH
    part0, part1 = hi * OWN, (1 - hi) * OWN

    w1_load = local(w1_in.at[:, pl.ds(pl.multiple_of(hi * 512, 512), 512)], W1T.at[me_c], ld_sem.at[0])
    w2_load = local(w2_in, W2T.at[me_c], ld_sem.at[1])
    f_load = [
        local(feat.at[pl.ds(mine + part, OWN)], F.at[lo, pl.ds(OWN * s, OWN)], ld_sem.at[2 + s])
        for s, part in enumerate((part0, part1))
    ]
    c_load = [
        local(cot.at[pl.ds(mine + part, OWN)], C.at[lo, pl.ds(OWN * s, OWN)], ld_sem.at[4 + s])
        for s, part in enumerate((part0, part1))
    ]
    w3_load = local(w3_in.at[:, pl.ds(pl.multiple_of(hi * 512, 512), 512)], W3.at[me_c], ld_sem.at[6])
    w1_load.start()
    f_load[1].start()
    f_load[0].start()
    w2_load.start()
    w3_load.start()
    c_load[0].start()
    c_load[1].start()

    barrier = pltpu.get_barrier_semaphore()

    def greet(t, carry):
        q = lax.rem(me_p * n_ch + me_c + t, n_all)
        pl.semaphore_signal(barrier, inc=1, device_id=(q // n_ch, lax.rem(q, n_ch)), device_id_type=MESH)
        return carry

    lax.fori_loop(1, n_all, greet, 0)

    row_i = lax.broadcasted_iota(jnp.int32, (64, 256), 0)
    col_i = lax.broadcasted_iota(jnp.int32, (64, 256), 1)
    place = (row_i == col_i - 64 * me_c).astype(BF16)
    narrow = jnp.concatenate([v[...].astype(F32).reshape(1, 64) for v in (g1_in, b1_in, g2_in, b2_in)] * 2, axis=0)
    pk_rows = [mm(narrow.astype(BF16), place)[0:4]]
    pk_rows += [v[...].astype(F32).reshape(1, 256) for v in (g3_in, b3_in)]
    pk[me_c] = jnp.concatenate(pk_rows + [jnp.zeros((2, 256), F32)], axis=0)

    flat = mask[...].astype(F32).reshape(1, rows28.shape[0] * ROWS)
    for t in range(rows28.shape[0]):
        rows28[t : t + 1, :] = flat[:, t * ROWS : (t + 1) * ROWS]
    diag = lax.broadcasted_iota(jnp.int32, (ROWS, ROWS), 0) == lax.broadcasted_iota(jnp.int32, (ROWS, ROWS), 1)
    ones = jnp.ones((ROWS, 128), BF16)

    def put_mask(t, carry):
        at = mine + jnp.where(t < OWN, part0 + t, part1 + t - OWN)
        row = rows28[pl.ds(at, 1), :]
        V[t] = mm(jnp.where(diag, row, 0.0).astype(BF16), ones)
        return carry

    lax.fori_loop(0, BOTH, put_mask, 0)
    lanes = jnp.broadcast_to(jnp.sum(rows28[...], axis=0, keepdims=True), (8, ROWS))
    local_count = mm(lanes.astype(BF16), ones)
    P0[...] = jnp.zeros_like(P0)
    PC[0:PAD, :] = jnp.zeros((PAD, 768), BF16)
    PC[PAD + FLAT :, :] = jnp.zeros((PAD, 768), BF16)
    w2_load.wait()
    pl.semaphore_wait(barrier, n_all - 1)

    fx = [
        remote(
            feat.at[pl.ds(theirs + part, OWN)], F.at[lo, pl.ds(OWN * s, OWN)], fx_send.at[s], fx_recv.at[s], beside
        )
        for s, part in enumerate((part0, part1))
    ]
    cx = [
        remote(
            cot.at[pl.ds(theirs + part, OWN)], C.at[lo, pl.ds(OWN * s, OWN)], fx_send.at[2 + s], fx_recv.at[2 + s], beside
        )
        for s, part in enumerate((part0, part1))
    ]
    others = []
    for t in range(1, n_ch):
        q = lax.rem(me_c + t, n_ch)
        others.append((t - 1, (me_p, q), q // 2))
    w1x = [
        remote(
            w1_in.at[:, pl.ds(pl.multiple_of(h * 512, 512), 512)], W1T.at[me_c], w_send.at[t], w_recv.at[me_c], dev
        )
        for t, dev, h in others
    ]
    pkx = [remote(pk.at[me_c], pk.at[me_c], w_send.at[4 + t], w_recv.at[4 + me_c], dev) for t, dev, h in others]
    w3x = [
        remote(
            w3_in.at[:, pl.ds(pl.multiple_of(h * 512, 512), 512)],
            W3.at[me_c],
            w_send.at[8 + t],
            w_recv.at[8 + me_c],
            dev,
        )
        for t, dev, h in others
    ]
    for cp in w1x:
        cp.start()
    fx[1].start()
    fx[0].start()
    for cp in pkx:
        cp.start()

    def arrived(dst, sem):
        local(dst, dst, sem).wait()

    def ar_group(kind):
        if kind == "all":
            return n_all, me_p * n_ch + me_c, lambda q: (q // n_ch, lax.rem(q, n_ch))
        if kind == "half":
            return n_pix * 2, me_p * 2 + lo, lambda q: (q // 2, hi * 2 + lax.rem(q, 2))
        return n_pix, me_p, lambda q: (q, me_c)

    def ar_start(k, val, kind):
        n, me, device = ar_group(kind)
        rows = val.shape[0]
        sbuf[k, 0:rows] = val
        rbuf[k, me, 0:rows] = val

        def send(t, carry):
            to = device(lax.rem(me + t, n))
            cut = pl.ds(0, rows)
            remote(sbuf.at[k, cut], rbuf.at[k, me, cut], ar_send.at[k], ar_recv.at[k], to).start()
            return carry

        lax.fori_loop(1, n, send, 0)

    def ar_finish(k, kind, rows):
        n = ar_group(kind)[0]
        arrived(rbuf.at[k, pl.ds(0, n - 1), pl.ds(0, rows)], ar_recv.at[k])
        return jnp.sum(rbuf[k, 0:n, 0:rows], axis=0)

    def ar_close(k, kind, rows):
        n = ar_group(kind)[0]
        arrived(rbuf.at[k, pl.ds(0, n - 1), pl.ds(0, rows)], ar_send.at[k])

    def pack2(a, b):
        return jnp.concatenate([a[:, 0:128], a[:, 128:256], b[:, 0:128], b[:, 128:256]], axis=0)

    def unpack2(v):
        return (
            jnp.concatenate([v[0:1], v[1:2]], axis=1),
            jnp.concatenate([v[2:3], v[3:4]], axis=1),
        )

    def pack3(a, b):
        return jnp.concatenate([a[:, 128 * i : 128 * (i + 1)] for i in range(4)] + [b[:, 128 * i : 128 * (i + 1)] for i in range(4)], axis=0)

    def unpack3(v):
        return (
            jnp.concatenate([v[i : i + 1] for i in range(4)], axis=1),
            jnp.concatenate([v[i : i + 1] for i in range(4, 8)], axis=1),
        )

    ar_start(6, local_count, "pix")

    far = (1 - hi) * 2 + lo

    def w2_piece(slot, q):
        return W2T.at[slot, :, pl.ds(pl.multiple_of(q // 2 * 16, 16), 16), pl.ds(pl.multiple_of(lax.rem(q, 2) * 128, 128), 128)]

    w2x_across = remote(w2_piece(me_c, g_lo), w2_piece(me_c, g_lo), w_send.at[12], w_recv.at[12], across)
    w2x_across.start()
    w2x_beside = remote(W2T.at[me_c], W2T.at[me_c], w_send.at[13], w_recv.at[13], beside)
    w2x_pass = remote(W2T.at[far], W2T.at[far], w_send.at[14], w_recv.at[14], beside)
    w2x_share = []
    for t in range(1, n_lo):
        q = lax.rem(g_lo + t, n_lo)
        w2x_share.append(
            remote(
                w2_piece(far, g_lo), w2_piece(far, g_lo), w_send.at[15 + t], w_recv.at[15 + t], (g_hi * n_lo + q, me_c)
            )
        )

    for t, dev, h in others:
        q = dev[1]
        arrived(W1T.at[q], w_recv.at[q])

    w1_load.wait()

    f_load[1].wait()
    fx[1].wait_recv()
    w1_all = W1T[...].reshape(256, 512)

    def first(t):
        wide = jnp.concatenate([F[0, t], F[1, t]], axis=1)
        return mm_nt(wide, w1_all)

    def xcopy(kind, src, dst, t):
        return remote(src.at[t], dst.at[t], x_send.at[kind, t], x_recv.at[kind, t], across)

    def send_first(t, carry):
        h1s[t] = first(t + OWN).astype(BF16)
        xcopy(0, h1s, h1r, t).start()
        return carry

    lax.fori_loop(0, OWN, send_first, 0)
    f_load[0].wait()
    fx[0].wait_recv()

    def keep_first(t, carry):
        H1[t] = first(t)
        return carry

    lax.fori_loop(0, OWN, keep_first, 0)

    arrived(w2_piece(far, g_lo), w_recv.at[12])
    for cp in w2x_share:
        cp.start()
    w2x_beside.start()
    cx[0].start()
    cx[1].start()
    for t, dev, h in others:
        arrived(pk.at[dev[1]], w_recv.at[4 + dev[1]])
    gains = pk[0] + pk[1] + pk[2] + pk[3]
    g1, b1, g2, b2 = (gains[k : k + 1] for k in range(4))
    pair0, pair1 = pk[2 * hi], pk[2 * hi + 1]
    g3 = jnp.concatenate([pair0[4:5], pair1[4:5]], axis=1)
    b3 = jnp.concatenate([pair0[5:6], pair1[5:6]], axis=1)

    zero = jnp.zeros((8, 256), F32)

    def sum_first(t, carry):
        s, q = carry
        xcopy(0, h1s, h1r, t).wait_recv()
        h = H1[t] + h1r[t].astype(F32)
        H1[t] = h
        h1b[t] = h.astype(BF16)
        vh = spread(V[t], 256) * h
        return s + fold8(vh), q + fold8(vh * h)

    s, q = lax.fori_loop(0, OWN, sum_first, (zero, zero))
    ar_start(0, pack2(fold1(s), fold1(q)), "all")
    for t in range(1, n_lo):
        arrived(w2_piece(far, lax.rem(g_lo - t + n_lo, n_lo)), w_recv.at[15 + t])
    w2x_pass.start()
    inv_n = 1.0 / spread(ar_finish(6, "pix", 8)[0:1], 512)
    inv_n2 = inv_n[:, 0:256]
    s, q = unpack2(ar_finish(0, "all", 4))
    avg1 = s * inv_n2
    scale1 = lax.rsqrt(q * inv_n2 - avg1 * avg1 + EPS)
    a1_gain = g1 * scale1
    a1_shift = b1 - avg1 * a1_gain

    def act_first(t, carry):
        v = spread(V[t], 256)
        aff = v * (H1[t] * a1_gain + a1_shift)
        sig = logistic(aff)
        act = aff * sig
        comp[pl.ds(pl.multiple_of(t * ROWS, 16), ROWS), :] = act
        D1[t] = v * (sig + act * (1.0 - sig))
        return carry

    lax.fori_loop(0, OWN, act_first, 0)

    def to_padded():
        for i in range(IMAGES):
            for y in range(SIDE):
                P0[EDGE + (i * PAD + y + 1) * PAD : EDGE + (i * PAD + y + 1) * PAD + SIDE, :] = comp[
                    (i * SIDE + y) * SIDE : (i * SIDE + y + 1) * SIDE, :
                ]

    def from_padded(dst, images):
        for i in images:
            for y in range(SIDE):
                dst[(i * SIDE + y) * SIDE : (i * SIDE + y + 1) * SIDE, :] = padded[
                    (i * SIDE + y) * PAD : (i * SIDE + y) * PAD + SIDE, :
                ]

    to_padded()
    for i in range(IMAGES):
        for c in range(3):
            at = EDGE + i * 256 + c - 1
            PC[PAD + i * BLOCK : PAD + (i + 1) * BLOCK, 256 * c : 256 * (c + 1)] = P0[at : at + BLOCK, :].astype(BF16)

    arrived(W2T.at[hi * 2 + 1 - lo], w_recv.at[13])
    arrived(W2T.at[(1 - hi) * 2 + 1 - lo], w_recv.at[14])
    for cp in w3x:
        cp.start()
    h1x = [remote(h1b, h1o, x_send.at[4, 0], x_recv.at[4, 0], across)]

    def conv(i, carry):
        total = None
        for r in range(3):
            rows = PC[pl.ds(pl.multiple_of(PAD + i * BLOCK + PAD * r, 16), SIDE * PAD), :]
            part = mm_nt(rows, jnp.concatenate([W2T[:, 3 * r + c].reshape(256, 256) for c in range(3)], axis=1))
            total = part if total is None else total + part
        padded[pl.ds(pl.multiple_of(i * SIDE * PAD, 16), SIDE * PAD), :] = total
        return carry

    def sum_second(t, carry):
        s, q = carry
        h = H2[pl.ds(pl.multiple_of(t * ROWS, 16), ROWS), :]
        h2s[t] = h.astype(BF16)
        vh = spread(V[t], 256) * h
        return s + fold8(vh), q + fold8(vh * h)

    def start_all(kind, src, dst, first, last):
        for t in range(first, last):
            xcopy(kind, src, dst, t).start()

    early = 2
    lax.fori_loop(0, 2, conv, 0)
    from_padded(H2, (0, 1))
    carry = lax.fori_loop(0, 3, sum_second, (zero, zero))
    start_all(1, h2s, h2r, 0, early)
    lax.fori_loop(2, IMAGES, conv, 0)
    from_padded(H2, (2, 3))
    s, q = lax.fori_loop(3, OWN, sum_second, carry)
    ar_start(1, pack2(fold1(s), fold1(q)), "all")
    start_all(1, h2s, h2r, early, OWN)
    s, q = unpack2(ar_finish(1, "all", 4))
    avg2 = s * inv_n2
    scale2 = lax.rsqrt(q * inv_n2 - avg2 * avg2 + EPS)
    a2_gain = g2 * scale2
    a2_shift = b2 - avg2 * a2_gain

    w3_load.wait()
    for t, dev, h in others:
        arrived(W3.at[dev[1]], w_recv.at[8 + dev[1]])

    def act_second(t, h, carry):
        s, q = carry
        v = spread(V[t], 256)
        aff = v * (h * a2_gain + a2_shift)
        sig = logistic(aff)
        act = aff * sig
        D2[t] = v * (sig + act * (1.0 - sig))
        act = act.astype(BF16)
        A2[t] = act
        h3 = mm(act, W3[...].reshape(256, 512))
        H3[t] = h3
        return s + fold8(h3), q + fold8(h3 * h3)

    def own_second(t, carry):
        return act_second(t, H2[pl.ds(pl.multiple_of(t * ROWS, 16), ROWS), :], carry)

    def other_second(t, carry):
        xcopy(1, h2s, h2r, t).wait_recv()
        return act_second(t + OWN, h2r[t].astype(F32), carry)

    wide_zero = jnp.zeros((8, 512), F32)
    carry = lax.fori_loop(0, OWN, own_second, (wide_zero, wide_zero))
    s, q = lax.fori_loop(0, OWN, other_second, carry)
    ar_start(2, pack3(fold1(s), fold1(q)), "half")
    for cp in h1x:
        cp.start()
    for cp in c_load:
        cp.wait()
    for cp in cx:
        cp.wait_recv()
    s, q = unpack3(ar_finish(2, "half", 8))
    avg3 = s * inv_n
    scale3 = lax.rsqrt(q * inv_n - avg3 * avg3 + EPS)
    a3_gain = g3 * scale3
    a3_shift = b3 - avg3 * a3_gain

    def last(t, carry):
        s, q = carry
        v = spread(V[t], 512)
        h3 = H3[t]
        wide = jnp.concatenate([F[0, t], F[1, t]], axis=1).astype(F32)
        total = v * (h3 * a3_gain + a3_shift) + wide
        sig = logistic(total)
        out = total * sig
        RES[0, t] = out[:, 0:256].astype(BF16)
        RES[1, t] = out[:, 256:512].astype(BF16)
        given = jnp.concatenate([C[0, t], C[1, t]], axis=1).astype(F32)
        gs = given * (sig + out * (1.0 - sig))
        GS[t] = gs
        vg = v * gs
        return s + fold8(vg), q + fold8(vg * (h3 - avg3))

    s, q = lax.fori_loop(0, BOTH, last, (wide_zero, wide_zero))
    ar_start(3, pack3(fold1(s), fold1(q * scale3)), "half")
    parts = ((0, part0), (1, part1))
    res_here = [
        local(RES.at[lo, pl.ds(OWN * s, OWN)], res_out.at[pl.ds(mine + part, OWN)], out_sem.at[s]) for s, part in parts
    ]
    res_there = [
        remote(RES.at[1 - lo, pl.ds(OWN * s, OWN)], res_out.at[pl.ds(mine + part, OWN)], o_send.at[s], o_recv.at[s], beside)
        for s, part in parts
    ]
    shift3, gain3 = unpack3(ar_finish(3, "half", 8))
    for cp in res_here + res_there:
        cp.start()
    k3_h = -a3_gain * gain3 * scale3 * inv_n
    k3_0 = -a3_gain * shift3 * inv_n - k3_h * avg3

    def back_third(t, carry):
        s, q, h2 = carry[0], carry[1], carry[2]
        v = spread(V[t], 512)
        g = (v * (a3_gain * GS[t] + k3_h * H3[t] + k3_0)).astype(BF16)
        G3[t] = g
        e = mm_nt(g, W3[...].reshape(256, 512)) * D2[t]
        return e, s + fold8(e), q + fold8(e * (h2 - avg2))

    def other_third(t, carry):
        e, s, q = back_third(t + OWN, (carry[0], carry[1], h2r[t].astype(F32)))
        e2s[t] = e.astype(BF16)

        @pl.when(t < 4)
        def _():
            xcopy(2, e2s, e2r, t).start()

        return s, q

    def own_third(t, carry):
        e, s, q = back_third(t, (carry[0], carry[1], H2[pl.ds(pl.multiple_of(t * ROWS, 16), ROWS), :]))
        E2[t] = e
        return s, q

    carry = lax.fori_loop(0, OWN, other_third, (zero, zero))
    s, q = lax.fori_loop(0, OWN, own_third, carry)
    ar_start(4, pack2(fold1(s), fold1(q * scale2)), "all")
    start_all(2, e2s, e2r, 4, OWN)

    piece = 16
    n_sub = 4

    def pair_copies(k):
        return [remote(wp.at[k, h], wc.at[k, h], g_send.at[k, h], g_recv.at[k, h], beside) for h in range(2)]

    def pair_start(k):
        for h in range(2):
            wp[k, h] = acc_w[k, h, 1 - lo].astype(BF16)
        for cp in pair_copies(k):
            cp.start()

    def pair_add(k):
        for h, cp in enumerate(pair_copies(k)):
            cp.wait_recv()
            both = (acc_w[k, h, lo] + wc[k, h].astype(F32)).reshape(n_sub, piece, 512)
            wa[k, h] = both
            wb[k, h] = both.astype(BF16)
        for cp in spread_copies(k):
            cp.start()

    def spread_copies(k):
        copies = []
        for t in range(1, n_lo):
            q = lax.rem(g_lo + t, n_lo)
            copies.append(
                remote(
                    wb.at[k, lax.rem(q, 2), q // 2],
                    wr.at[k, g_lo],
                    g_send.at[k, 2 + t],
                    g_recv.at[k, 2 + t],
                    (g_hi * n_lo + q, me_c),
                )
            )
        return copies

    def over_groups(total, level, sems):
        if n_hi == 1:
            return total
        level[g_hi] = total.astype(BF16)

        def swap(t):
            q = lax.rem(g_hi + t, n_hi)
            return remote(
                level.at[g_hi], level.at[g_hi], sems[0].at[t], sems[1].at[t], (q * n_lo + g_lo, me_c)
            )

        for t in range(1, n_hi):
            swap(t).start()
        for t in range(1, n_hi):
            swap(t).wait()
        total = level[0].astype(F32)
        for t in range(1, n_hi):
            total = total + level[t].astype(F32)
        return total

    def spread_add(k):
        for cp in spread_copies(k):
            cp.wait_recv()
        total = wa[k, lax.rem(g_lo, 2), g_lo // 2]
        for t in range(1, n_lo):
            total = total + wr[k, lax.rem(g_lo + t, n_lo)].astype(F32)
        return over_groups(total, wh.at[k], (h_send.at[k], h_recv.at[k]))

    def give_copies(k):
        copies = []
        for t in range(n_lo):
            q = lax.rem(g_lo + t, n_lo)
            copies.append(
                remote(
                    wf.at[k],
                    wfin.at[k, hi, own_sub],
                    g_send.at[k, 10 + t],
                    g_recv.at[k, 10 + 8 * hi + t],
                    (g_hi * n_lo + q, owner_hi * 2 + lo),
                )
            )
        return copies

    owner_hi = lax.rem(g_lo, 2)
    own_sub = g_lo // 2
    keeps = owner_hi == hi

    def wide_give(k):
        wf[k] = spread_add(k).astype(BF16)
        for t, cp in enumerate(give_copies(k)):
            if t == 0:

                @pl.when(jnp.logical_not(keeps))
                def _():
                    cp.start()

                @pl.when(keeps)
                def _():
                    wfin[k, hi, own_sub] = wf[k]

            else:
                cp.start()

    def wide_take(k, out):
        for sub in range(n_sub):
            q = sub * 2 + hi
            t = lax.rem(g_lo - q + n_lo, n_lo)
            for h in range(2):

                @pl.when(jnp.logical_not((q == g_lo) & (hi == h)))
                def _():
                    arrived(wfin.at[k, h, sub], g_recv.at[k, 10 + 8 * h + t])

        for h in range(2):
            out[:, 512 * h : 512 * (h + 1)] = wfin[k, h].astype(F32).reshape(64, 512)

    def wide_close(k):
        for cp in pair_copies(k) + spread_copies(k):
            cp.wait_send()
        for t, cp in enumerate(give_copies(k)):
            if t == 0:

                @pl.when(jnp.logical_not(keeps))
                def _():
                    cp.wait_send()

            else:
                cp.wait_send()

    def half_of(ref, part):
        return ref[OWN * part : OWN * (part + 1)].reshape(OWN * ROWS, ref.shape[2])

    acc_w[0] = (mm_tn(half_of(A2, 0), half_of(G3, 0)) + mm_tn(half_of(A2, 1), half_of(G3, 1))).reshape(2, 2, 64, 512)
    pair_start(0)
    pair_add(0)

    shift2, gain2 = unpack2(ar_finish(4, "all", 4))
    k2_h = -a2_gain * gain2 * scale2 * inv_n2
    k2_0 = -a2_gain * shift2 * inv_n2 - k2_h * avg2

    def back_second(t, carry):
        xcopy(2, e2s, e2r, t).wait_recv()
        at = pl.ds(pl.multiple_of(t * ROWS, 16), ROWS)
        e = E2[t] + e2r[t].astype(F32)
        comp[at, :] = spread(V[t], 256) * (a2_gain * e + k2_h * H2[at, :] + k2_0)
        return carry

    lax.fori_loop(0, OWN, back_second, 0)
    to_padded()
    for i in range(IMAGES):
        for c in range(3):
            at = EDGE + i * BLOCK - (c - 1)
            Q[c, i * BLOCK : (i + 1) * BLOCK, :] = P0[at : at + BLOCK, :].astype(BF16)

    def conv_back(i, carry):
        total = None
        for r in range(3):
            at = pl.ds(pl.multiple_of(i * BLOCK + PAD * (2 - r), 16), SIDE * PAD)
            for c in range(3):
                w = W2T[:, 3 * r + c].reshape(256, 256)
                part = mm(Q[c, at, :], w)
                total = part if total is None else total + part
        padded[pl.ds(pl.multiple_of(i * SIDE * PAD, 16), SIDE * PAD), :] = total
        return carry

    def sum_back_first(t, carry):
        s, q = carry
        e = comp[pl.ds(pl.multiple_of(t * ROWS, 16), ROWS), :] * D1[t]
        E1[t] = e
        e1s[t] = e.astype(BF16)
        return s + fold8(e), q + fold8(e * (H1[t] - avg1))

    lax.fori_loop(0, 2, conv_back, 0)
    from_padded(comp, (0, 1))
    carry = lax.fori_loop(0, 3, sum_back_first, (zero, zero))
    start_all(3, e1s, e1r, 0, early)
    lax.fori_loop(2, IMAGES, conv_back, 0)
    from_padded(comp, (2, 3))
    s, q = lax.fori_loop(3, OWN, sum_back_first, carry)
    ar_start(5, pack2(fold1(s), fold1(q * scale1)), "all")
    start_all(3, e1s, e1r, early, OWN)

    bit, quad = lax.rem(g_lo, 2), g_lo // 2
    next_group = (g_hi * n_lo + quad * 2 + 1 - bit, me_c)
    s_owner = lax.rem(quad, 2) == hi

    def s_pair(r):
        return [
            remote(sp.at[r, h], sc.at[r, h], s_send.at[r, h], s_recv.at[r, h], beside) for h in range(2)
        ]

    def s_next(r):
        return remote(ys.at[r], yr.at[r], s_send.at[r, 2], s_recv.at[r, 2], next_group)

    def s_quad(r):
        copies = []
        for t in range(1, 4):
            q = lax.rem(quad + t, 4)
            copies.append(
                remote(
                    zs.at[r, lax.rem(q, 2), q // 2],
                    zr.at[r, t - 1],
                    s_send.at[r, 2 + t],
                    s_recv.at[r, 2 + t],
                    (g_hi * n_lo + q * 2 + bit, me_c),
                )
            )
        return copies

    def s_cross(r):
        return remote(xs.at[r], xr.at[r], s_send.at[r, 6], s_recv.at[r, 6], across)

    def s_give(r):
        copies = []
        for t in range(1, 4):
            q = lax.rem(quad + t, 4)
            spot = sfin.at[r, bit, quad // 2]
            copies.append(
                remote(
                    spot, spot, s_send.at[r, 6 + t], s_recv.at[r, 7 + quad // 2], (g_hi * n_lo + q * 2 + bit, me_c)
                )
            )
        return copies

    def s_back(r):
        return remote(sfin.at[r, bit], sfin.at[r, bit], s_send.at[r, 10], s_recv.at[r, 10], next_group)

    def s_make(r):
        taps = mm(QT[...], PC[PAD * r : PAD * r + FLAT, :])
        acc_s[r] = taps.reshape(2, 2, 64, 768)
        for h in range(2):
            sp[r, h] = acc_s[r, h, 1 - lo].astype(BF16)
        for cp in s_pair(r):
            cp.start()

    def s_pair_add(r):
        for h, cp in enumerate(s_pair(r)):
            cp.wait_recv()
            s1[r, h] = (acc_s[r, h, lo] + sc[r, h].astype(F32)).reshape(2, 32, 768)
            ys[r, h] = s1[r, h, 1 - bit].astype(BF16)
        s_next(r).start()

    def s_next_add(r):
        s_next(r).wait_recv()
        for h in range(2):
            s2[r, h] = (s1[r, h, bit] + yr[r, h].astype(F32)).reshape(2, 16, 768)
            zs[r, h] = s2[r, h].astype(BF16)
        for cp in s_quad(r):
            cp.start()

    def s_quad_add(r):
        for cp in s_quad(r):
            cp.wait_recv()
        total = s2[r, lax.rem(quad, 2), quad // 2]
        for t in range(3):
            total = total + zr[r, t].astype(F32)
        s3[r] = total
        xs[r] = total.astype(BF16)

        @pl.when(jnp.logical_not(s_owner))
        def _():
            s_cross(r).start()

    def s_cross_add(r):
        @pl.when(s_owner)
        def _():
            s_cross(r).wait_recv()
            total = s3[r] + xr[r].astype(F32)
            sfin[r, bit, quad // 2] = over_groups(total, sh.at[r], (h_send.at[2 + r], h_recv.at[2 + r])).astype(BF16)
            for cp in s_give(r):
                cp.start()

    def s_give_back(r):
        for part in range(2):

            @pl.when(quad != 2 * part + hi)
            def _():
                arrived(sfin.at[r, bit, part], s_recv.at[r, 7 + part])

        s_back(r).start()

    def s_take(r):
        arrived(sfin.at[r, 1 - bit], s_recv.at[r, 10])
        rows = sfin[r].astype(F32).reshape(64, 768)
        for c in range(3):
            sg_out[3 * r + c] = rows[:, 256 * c : 256 * (c + 1)]

    def s_close(r):
        for cp in s_pair(r) + [s_next(r)] + s_quad(r) + [s_back(r)]:
            cp.wait_send()

        @pl.when(s_owner)
        def _():
            for cp in s_give(r):
                cp.wait_send()

        @pl.when(jnp.logical_not(s_owner))
        def _():
            s_cross(r).wait_send()

    for i in range(IMAGES):
        QT[:, i * BLOCK : (i + 1) * BLOCK] = P0[EDGE + i * BLOCK : EDGE + (i + 1) * BLOCK, :].T.astype(BF16)
    s_make(0)
    s_make(1)
    s_pair_add(0)
    s_make(2)
    s_pair_add(1)
    s_pair_add(2)

    shift1, gain1 = unpack2(ar_finish(5, "all", 4))
    k1_h = -a1_gain * gain1 * scale1 * inv_n2
    k1_0 = -a1_gain * shift1 * inv_n2 - k1_h * avg1

    def back_first(t, e, h):
        g = (spread(V[t], 256) * (a1_gain * e + k1_h * h + k1_0)).astype(BF16)
        G1[t] = g
        out = (mm(g, W1T[...].reshape(256, 512)) + GS[t]).astype(BF16)
        RES[0, t] = out[:, 0:256]
        RES[1, t] = out[:, 256:512]

    ig_here = [
        local(RES.at[lo, pl.ds(OWN * s, OWN)], ig_out.at[pl.ds(mine + part, OWN)], out_sem.at[2 + s])
        for s, part in parts
    ]
    ig_there = [
        remote(
            RES.at[1 - lo, pl.ds(OWN * s, OWN)], ig_out.at[pl.ds(mine + part, OWN)], o_send.at[2 + s], o_recv.at[2 + s], beside
        )
        for s, part in parts
    ]
    for cp in res_here:
        cp.wait()
    for cp in res_there:
        cp.wait_send()

    def own_back_first(t, carry):
        back_first(t, E1[t], H1[t])
        return carry

    lax.fori_loop(0, OWN, own_back_first, 0)
    ig_here[0].start()
    ig_there[0].start()
    s_next_add(0)

    def features_of(part):
        return jnp.concatenate([half_of(F.at[0], part), half_of(F.at[1], part)], axis=1)

    own_reduce = mm_tn(half_of(G1, 0), features_of(0))
    acc_w[1] = own_reduce.reshape(2, 2, 64, 512)
    s_next_add(1)
    wide_give(0)
    for cp in h1x:
        cp.wait_recv()

    def other_back_first(t, carry):
        xcopy(3, e1s, e1r, t).wait_recv()
        back_first(t + OWN, e1r[t].astype(F32), h1o[t].astype(F32))
        return carry

    lax.fori_loop(0, OWN, other_back_first, 0)
    acc_w[1] += mm_tn(half_of(G1, 1), features_of(1)).reshape(2, 2, 64, 512)
    pair_start(1)
    ig_here[1].start()
    ig_there[1].start()
    s_quad_add(0)
    s_next_add(2)
    pair_add(1)
    s_quad_add(1)
    s_cross_add(0)
    s_quad_add(2)
    s_cross_add(1)
    wide_give(1)
    s_cross_add(2)
    for r in range(3):
        s_give_back(r)

    def own64(v):
        half = jnp.where(hi == 0, v[:, 0:128], v[:, 128:256])
        swapped = jnp.concatenate([half[:, 64:128], half[:, 0:64]], axis=1)
        return jnp.concatenate([jnp.where(lo == 0, half, swapped), jnp.zeros((1, 128), F32)], axis=1)

    def own256(v):
        return jnp.where(lo == 0, v[:, 0:256], v[:, 256:512])

    st_out[...] = jnp.concatenate(
        [
            own64(gain1),
            own64(shift1),
            own64(gain2),
            own64(shift2),
            own256(gain3),
            own256(shift3),
            jnp.zeros((2, 256), F32),
        ],
        axis=0,
    )

    wide_take(0, eg_out)
    for r in range(3):
        s_take(r)
    wide_take(1, rg_out)

    wide_close(0)
    wide_close(1)
    for r in range(3):
        s_close(r)
    for cp in ig_here:
        cp.wait()
    for cp in ig_there:
        cp.wait()
    for cp in res_there:
        cp.wait_recv()
    for cp in fx + cx + w1x + pkx + w3x + h1x + w2x_share + [w2x_across, w2x_beside, w2x_pass]:
        cp.wait_send()
    for kind, src, dst in ((0, h1s, h1r), (1, h2s, h2r), (2, e2s, e2r), (3, e1s, e1r)):
        for t in range(OWN):
            xcopy(kind, src, dst, t).wait_send()
    for k, kind, rows in (
        (0, "all", 4),
        (1, "all", 4),
        (2, "half", 8),
        (3, "half", 8),
        (4, "all", 4),
        (5, "all", 4),
        (6, "pix", 8),
    ):
        ar_close(k, kind, rows)


def block(n_pix, n_ch, *args):
    feat, cot, mask, w1, w2, w3 = args[:6]
    rows, lanes = feat.shape
    n_lo, n_sub, piece = 8, 4, 16
    n_hi = n_pix // n_lo
    chunks = rows // ROWS
    any_space = pl.BlockSpec(memory_space=pl.ANY)
    vmem = pl.BlockSpec(memory_space=pltpu.VMEM)
    V = pltpu.VMEM
    DMA = pltpu.SemaphoreType.DMA
    scratch = [
        V((2, BOTH, ROWS, 256), BF16),
        V((2, BOTH, ROWS, 256), BF16),
        V((BOTH, ROWS, 128), F32),
        V((4, 64, 512), BF16),
        V((4, 9, 64, 256), BF16),
        V((4, 64, 512), BF16),
        V((4, 8, 256), F32),
        V((7, 8, 128), F32),
        V((7, n_pix * n_ch, 8, 128), F32),
        V((OWN, ROWS, 256), BF16),
        V((OWN, ROWS, 256), BF16),
        V((OWN, ROWS, 256), F32),
        V((OWN, ROWS, 256), BF16),
        V((OWN, ROWS, 256), BF16),
        V((OWN, ROWS, 256), F32),
        V((OWN * ROWS, 256), F32),
        V((FLAT + 2 * EDGE, 256), F32),
        V((FLAT + 2 * PAD, 768), BF16),
        V((3, FLAT, 256), BF16),
        V((IMAGES * SIDE * PAD, 256), F32),
        V((OWN * ROWS, 256), F32),
        V((OWN, ROWS, 256), BF16),
        V((OWN, ROWS, 256), BF16),
        V((BOTH, ROWS, 256), BF16),
        V((BOTH, ROWS, 256), F32),
        V((BOTH, ROWS, 512), F32),
        V((BOTH, ROWS, 512), F32),
        V((2, BOTH, ROWS, 256), BF16),
        V((BOTH, ROWS, 512), BF16),
        V((OWN, ROWS, 256), F32),
        V((OWN, ROWS, 256), BF16),
        V((OWN, ROWS, 256), BF16),
        V((OWN, ROWS, 256), F32),
        V((OWN, ROWS, 256), BF16),
        V((OWN, ROWS, 256), BF16),
        V((BOTH, ROWS, 256), BF16),
        V((256, FLAT), BF16),
        V((chunks, ROWS), F32),
        V((2, 2, 2, 64, 512), F32),
        V((2, 2, 64, 512), BF16),
        V((2, 2, 64, 512), BF16),
        V((2, 2, n_sub, piece, 512), F32),
        V((2, 2, n_sub, piece, 512), BF16),
        V((2, n_lo, piece, 512), BF16),
        V((2, n_hi, piece, 512), BF16),
        V((2, piece, 512), BF16),
        V((2, 2, n_sub, piece, 512), BF16),
        V((3, 2, 2, 64, 768), F32),
        V((3, 2, 64, 768), BF16),
        V((3, 2, 64, 768), BF16),
        V((3, 2, 2, 32, 768), F32),
        V((3, 2, 32, 768), BF16),
        V((3, 2, 32, 768), BF16),
        V((3, 2, 2, 16, 768), F32),
        V((3, 2, 2, 16, 768), BF16),
        V((3, 3, 16, 768), BF16),
        V((3, 16, 768), F32),
        V((3, 16, 768), BF16),
        V((3, 16, 768), BF16),
        V((3, n_hi, 16, 768), BF16),
        V((3, 2, 2, 16, 768), BF16),
        DMA((8,)),
        DMA((4,)),
        DMA((4,)),
        DMA((24,)),
        DMA((24,)),
        DMA((7,)),
        DMA((7,)),
        DMA((5, OWN)),
        DMA((5, OWN)),
        DMA((4,)),
        DMA((4,)),
        DMA((4,)),
        DMA((2, 26)),
        DMA((2, 26)),
        DMA((3, 12)),
        DMA((3, 12)),
        DMA((5, n_hi)),
        DMA((5, n_hi)),
    ]
    wide = jax.ShapeDtypeStruct((chunks, ROWS, lanes), BF16)
    made = pl.pallas_call(
        functools.partial(kernel, n_pix, n_ch),
        out_shape=(
            wide,
            wide,
            jax.ShapeDtypeStruct((64, 1024), F32),
            jax.ShapeDtypeStruct((9, 64, 256), F32),
            jax.ShapeDtypeStruct((64, 1024), F32),
            jax.ShapeDtypeStruct((8, 256), F32),
        ),
        in_specs=[any_space, any_space, vmem, any_space, any_space, any_space] + [vmem] * 6,
        out_specs=(any_space, any_space, vmem, vmem, vmem, vmem),
        scratch_shapes=scratch,
        compiler_params=pltpu.CompilerParams(
            collective_id=0, has_side_effects=True, vmem_limit_bytes=56 * 2**20
        ),
        name="bottleneck",
    )(
        feat.reshape(chunks, ROWS, lanes),
        cot.reshape(chunks, ROWS, lanes),
        mask,
        w1.T,
        w2.transpose(0, 1, 3, 2).reshape(9, 64, 256),
        w3,
        *args[6:],
    )
    narrow = jax.ShapeDtypeStruct((64,), F32)
    broad = jax.ShapeDtypeStruct((256,), F32)
    return pl.pallas_call(
        finish,
        out_shape=tuple(jax.ShapeDtypeStruct(v.shape, v.dtype) for v in made[:5]) + (narrow,) * 4 + (broad,) * 2,
        in_specs=[vmem] * 6,
        out_specs=(any_space,) * 5 + (vmem,) * 6,
        scratch_shapes=[DMA((5,))],
        name="outputs",
    )(*made)


def finish(*refs):
    made, stats, outs, small, sems = refs[:5], refs[5], refs[6:11], refs[11:17], refs[17]
    copies = [pltpu.make_async_copy(a, b, sems.at[i]) for i, (a, b) in enumerate(zip(made, outs))]
    for cp in copies:
        cp.start()
    for i, out in enumerate(small):
        out[...] = stats[i : i + 1, 0 : out.shape[0]].reshape(out.shape)
    for cp in copies:
        cp.wait()


def solution(mesh):
    n_pix, n_ch = mesh.shape["pix"], mesh.shape["ch"]

    def body(feat, mask, w1, w2, w3, g1, b1, g2, b2, g3, b3, cot):
        made = block(n_pix, n_ch, feat, cot, mask, w1, w2, w3, g1, b1, g2, b2, g3, b3)
        res, ig, rg, sg, eg = made[:5]
        return (
            res.reshape(feat.shape),
            ig.reshape(feat.shape),
            rg.T,
            sg.reshape(3, 3, 64, 256).transpose(0, 1, 3, 2),
            eg,
        ) + tuple(made[5:])

    wide = P("pix", "ch")
    return jax.shard_map(
        body,
        mesh=mesh,
        in_specs=(wide, P("pix"), P(None, "ch"), P(None, None, None, "ch"), P("ch", None)) + (P("ch"),) * 6 + (wide,),
        out_specs=(wide, wide, P(None, "ch"), P(None, None, None, "ch"), P("ch", None)) + (P("ch"),) * 6,
        check_vma=False,
    )
```

```python
import functools

import jax
import jax.numpy as jnp
from jax import lax
from jax.experimental import pallas as pl
from jax.experimental.pallas import tpu as pltpu
from jax.sharding import PartitionSpec as P

SIDE = 14
EPS = 1e-05
MESH = pl.DeviceIdType.MESH
F32 = jnp.float32
BF16 = jnp.bfloat16

ROWS = 112
OWN = 7
BOTH = 14
IMAGES = 4
PAD = 16
FLAT = IMAGES * PAD * PAD
EDGE = 8
BLOCK = PAD * PAD


def mm(a, b):
    return jnp.dot(a, b, preferred_element_type=F32)


def mm_nt(a, b):
    return lax.dot_general(a, b, (((1,), (1,)), ((), ())), preferred_element_type=F32)


def mm_tn(a, b):
    return lax.dot_general(a, b, (((0,), (0,)), ((), ())), preferred_element_type=F32)


def logistic(v):
    return 0.5 * jnp.tanh(0.5 * v) + 0.5


def fold8(v):
    return jnp.sum(v.reshape(v.shape[0] // 8, 8, v.shape[1]), axis=0)


def fold1(v):
    return jnp.sum(v, axis=0, keepdims=True)


def spread(v, lanes):
    return jnp.concatenate([v] * (lanes // 128), axis=1)


def kernel(
    n_pix,
    n_ch,
    feat,
    cot,
    mask,
    w1_in,
    w2_in,
    w3_in,
    g1_in,
    b1_in,
    g2_in,
    b2_in,
    g3_in,
    b3_in,
    res_out,
    ig_out,
    rg_out,
    sg_out,
    eg_out,
    st_out,
    mask_v,
    g1_v,
    b1_v,
    g2_v,
    b2_v,
    g3_v,
    b3_v,
    F,
    C,
    V,
    W1T,
    W2T,
    W3,
    pk,
    sbuf,
    rbuf,
    h1s,
    h1r,
    H1,
    h1b,
    h1o,
    D1,
    comp,
    P0,
    PC,
    Q,
    padded,
    H2,
    h2s,
    h2r,
    A2,
    D2,
    H3,
    GS,
    RES,
    G3,
    E2,
    e2s,
    e2r,
    E1,
    e1s,
    e1r,
    G1,
    QT,
    rows28,
    acc_w,
    wp,
    wc,
    wa,
    wb,
    wr,
    wh,
    wf,
    wfin,
    acc_s,
    sp,
    sc,
    s1,
    ys,
    yr,
    s2,
    zs,
    zr,
    s3,
    xs,
    xr,
    sh,
    sfin,
    ld_sem,
    fx_send,
    fx_recv,
    w_send,
    w_recv,
    ar_send,
    ar_recv,
    x_send,
    x_recv,
    out_sem,
    o_send,
    o_recv,
    g_send,
    g_recv,
    s_send,
    s_recv,
    h_send,
    h_recv,
):
    me_p, me_c = lax.axis_index("pix"), lax.axis_index("ch")
    hi, lo = me_c // 2, lax.rem(me_c, 2)
    n_lo = 8
    n_hi = n_pix // n_lo
    g_hi, g_lo = me_p // n_lo, lax.rem(me_p, n_lo)
    across = (me_p, (1 - hi) * 2 + lo)
    beside = (me_p, hi * 2 + 1 - lo)
    n_all = n_pix * n_ch

    def remote(src, dst, send, recv, device):
        return pltpu.make_async_remote_copy(
            src_ref=src, dst_ref=dst, send_sem=send, recv_sem=recv, device_id=device, device_id_type=MESH
        )

    def local(src, dst, sem):
        return pltpu.make_async_copy(src, dst, sem)

    mine, theirs = lo * BOTH, (1 - lo) * BOTH
    part0, part1 = hi * OWN, (1 - hi) * OWN

    w1_load = local(w1_in.at[:, pl.ds(pl.multiple_of(hi * 512, 512), 512)], W1T.at[me_c], ld_sem.at[0])
    w2_load = local(w2_in, W2T.at[me_c], ld_sem.at[1])
    f_load = [
        local(feat.at[pl.ds(mine + part, OWN)], F.at[lo, pl.ds(OWN * s, OWN)], ld_sem.at[2 + s])
        for s, part in enumerate((part0, part1))
    ]
    c_load = [
        local(cot.at[pl.ds(mine + part, OWN)], C.at[lo, pl.ds(OWN * s, OWN)], ld_sem.at[4 + s])
        for s, part in enumerate((part0, part1))
    ]
    small_load = [local(mask, mask_v, ld_sem.at[7])]
    pairs = ((g1_in, g1_v), (b1_in, b1_v), (g2_in, g2_v), (b2_in, b2_v), (g3_in, g3_v), (b3_in, b3_v))
    small_load += [local(a, b, ld_sem.at[8 + i]) for i, (a, b) in enumerate(pairs)]
    w3_load = local(w3_in.at[:, pl.ds(pl.multiple_of(hi * 512, 512), 512)], W3.at[me_c], ld_sem.at[6])
    barrier = pltpu.get_barrier_semaphore()

    def greet(t, carry):
        q = lax.rem(me_p * n_ch + me_c + t, n_all)
        pl.semaphore_signal(barrier, inc=1, device_id=(q // n_ch, lax.rem(q, n_ch)), device_id_type=MESH)
        return carry

    lax.fori_loop(1, n_all, greet, 0)
    for cp in small_load:
        cp.start()
    w1_load.start()
    f_load[1].start()
    f_load[0].start()
    w2_load.start()
    w3_load.start()
    c_load[0].start()
    c_load[1].start()

    row_i = lax.broadcasted_iota(jnp.int32, (64, 256), 0)
    col_i = lax.broadcasted_iota(jnp.int32, (64, 256), 1)
    place = (row_i == col_i - 64 * me_c).astype(BF16)
    for cp in small_load:
        cp.wait()
    narrow = jnp.concatenate([v[...].astype(F32).reshape(1, 64) for v in (g1_v, b1_v, g2_v, b2_v)] * 2, axis=0)
    pk_rows = [mm(narrow.astype(BF16), place)[0:4]]
    pk_rows += [v[...].astype(F32).reshape(1, 256) for v in (g3_v, b3_v)]
    pk[me_c] = jnp.concatenate(pk_rows + [jnp.zeros((2, 256), F32)], axis=0)

    flat = mask_v[...].astype(F32).reshape(1, rows28.shape[0] * ROWS)
    for t in range(rows28.shape[0]):
        rows28[t : t + 1, :] = flat[:, t * ROWS : (t + 1) * ROWS]
    diag = lax.broadcasted_iota(jnp.int32, (ROWS, ROWS), 0) == lax.broadcasted_iota(jnp.int32, (ROWS, ROWS), 1)
    ones = jnp.ones((ROWS, 128), BF16)

    def put_mask(t, carry):
        at = mine + jnp.where(t < OWN, part0 + t, part1 + t - OWN)
        row = rows28[pl.ds(at, 1), :]
        V[t] = mm(jnp.where(diag, row, 0.0).astype(BF16), ones)
        return carry

    lax.fori_loop(0, BOTH, put_mask, 0)
    lanes = jnp.broadcast_to(jnp.sum(rows28[...], axis=0, keepdims=True), (8, ROWS))
    local_count = mm(lanes.astype(BF16), ones)
    P0[...] = jnp.zeros_like(P0)
    PC[0:PAD, :] = jnp.zeros((PAD, 768), BF16)
    PC[PAD + FLAT :, :] = jnp.zeros((PAD, 768), BF16)
    w2_load.wait()
    pl.semaphore_wait(barrier, n_all - 1)

    fx = [
        remote(
            feat.at[pl.ds(theirs + part, OWN)], F.at[lo, pl.ds(OWN * s, OWN)], fx_send.at[s], fx_recv.at[s], beside
        )
        for s, part in enumerate((part0, part1))
    ]
    cx = [
        remote(
            cot.at[pl.ds(theirs + part, OWN)], C.at[lo, pl.ds(OWN * s, OWN)], fx_send.at[2 + s], fx_recv.at[2 + s], beside
        )
        for s, part in enumerate((part0, part1))
    ]
    far, near = (1 - hi) * 2 + lo, hi * 2 + 1 - lo

    def columns(ref, h):
        return ref.at[:, pl.ds(pl.multiple_of(h * 512, 512), 512)]

    w1x = [
        remote(columns(w1_in, 1 - hi), W1T.at[me_c], w_send.at[0], w_recv.at[0], across),
        remote(columns(w1_in, hi), W1T.at[me_c], w_send.at[1], w_recv.at[1], beside),
        remote(W1T.at[far], W1T.at[far], w_send.at[2], w_recv.at[2], beside),
    ]
    pkx = [
        remote(pk.at[me_c], pk.at[me_c], w_send.at[3], w_recv.at[3], across),
        remote(pk.at[me_c], pk.at[me_c], w_send.at[4], w_recv.at[4], beside),
        remote(pk.at[far], pk.at[far], w_send.at[5], w_recv.at[5], beside),
    ]

    def w2_piece(slot, q):
        return W2T.at[
            slot, :, pl.ds(pl.multiple_of(q // 2 * 16, 16), 16), pl.ds(pl.multiple_of(lax.rem(q, 2) * 128, 128), 128)
        ]

    def w3_piece(ref, q, first):
        return ref.at[
            pl.ds(pl.multiple_of(q // 2 * 16, 16), 16), pl.ds(pl.multiple_of(first + lax.rem(q, 2) * 256, 256), 256)
        ]

    w2x = [
        remote(w2_piece(me_c, g_lo), w2_piece(me_c, g_lo), w_send.at[6], w_recv.at[6], across),
        remote(W2T.at[me_c], W2T.at[me_c], w_send.at[7], w_recv.at[7], beside),
        remote(W2T.at[far], W2T.at[far], w_send.at[8], w_recv.at[8], beside),
    ]
    w3x = [
        remote(
            w3_piece(w3_in, g_lo, (1 - hi) * 512),
            w3_piece(W3.at[me_c], g_lo, 0),
            w_send.at[9],
            w_recv.at[9],
            across,
        ),
        remote(columns(w3_in, hi), W3.at[me_c], w_send.at[10], w_recv.at[10], beside),
        remote(W3.at[far], W3.at[far], w_send.at[11], w_recv.at[11], beside),
    ]
    shared = []
    for t in range(1, n_lo):
        to = (g_hi * n_lo + lax.rem(g_lo + t, n_lo), me_c)
        for k, piece_of in enumerate((lambda q: w2_piece(far, q), lambda q: w3_piece(W3.at[far], q, 0))):
            at = 12 + 8 * k + t
            shared.append(remote(piece_of(g_lo), piece_of(g_lo), w_send.at[at], w_recv.at[at], to))
    w1x[0].start()
    w1x[1].start()
    fx[1].start()
    fx[0].start()
    for cp in (pkx[0], w3x[0], w2x[0], pkx[1]):
        cp.start()

    def arrived(dst, sem):
        local(dst, dst, sem).wait()

    def ar_group(kind):
        if kind == "all":
            return n_all, me_p * n_ch + me_c, lambda q: (q // n_ch, lax.rem(q, n_ch))
        if kind == "half":
            return n_pix * 2, me_p * 2 + lo, lambda q: (q // 2, hi * 2 + lax.rem(q, 2))
        return n_pix, me_p, lambda q: (q, me_c)

    def ar_start(k, val, kind):
        n, me, device = ar_group(kind)
        rows = val.shape[0]
        sbuf[k, 0:rows] = val
        rbuf[k, me, 0:rows] = val

        def send(t, carry):
            to = device(lax.rem(me + t, n))
            cut = pl.ds(0, rows)
            remote(sbuf.at[k, cut], rbuf.at[k, me, cut], ar_send.at[k], ar_recv.at[k], to).start()
            return carry

        lax.fori_loop(1, n, send, 0)

    def ar_finish(k, kind, rows):
        n = ar_group(kind)[0]
        arrived(rbuf.at[k, pl.ds(0, n - 1), pl.ds(0, rows)], ar_recv.at[k])
        return jnp.sum(rbuf[k, 0:n, 0:rows], axis=0)

    def ar_close(k, kind, rows):
        n = ar_group(kind)[0]
        arrived(rbuf.at[k, pl.ds(0, n - 1), pl.ds(0, rows)], ar_send.at[k])

    def pack2(a, b):
        return jnp.concatenate([a[:, 0:128], a[:, 128:256], b[:, 0:128], b[:, 128:256]], axis=0)

    def unpack2(v):
        return (
            jnp.concatenate([v[0:1], v[1:2]], axis=1),
            jnp.concatenate([v[2:3], v[3:4]], axis=1),
        )

    def pack3(a, b):
        return jnp.concatenate([a[:, 128 * i : 128 * (i + 1)] for i in range(4)] + [b[:, 128 * i : 128 * (i + 1)] for i in range(4)], axis=0)

    def unpack3(v):
        return (
            jnp.concatenate([v[i : i + 1] for i in range(4)], axis=1),
            jnp.concatenate([v[i : i + 1] for i in range(4, 8)], axis=1),
        )

    ar_start(6, local_count, "pix")

    w1_load.wait()
    f_load[1].wait()
    fx[1].wait_recv()
    arrived(W1T.at[near], w_recv.at[1])

    def wide_rows(t):
        return jnp.concatenate([F[0, t], F[1, t]], axis=1)

    def xcopy(kind, src, dst, t):
        return remote(src.at[t], dst.at[t], x_send.at[kind, t], x_recv.at[kind, t], across)

    def send_first(h, kind):
        w = W1T[pl.ds(2 * h, 2)].reshape(128, 512)

        def one(t, carry):
            h1s[h, t] = mm_nt(wide_rows(t + OWN), w).astype(BF16)
            xcopy(kind, h1s.at[h], h1r.at[h], t).start()
            return carry

        lax.fori_loop(0, OWN, one, 0)

    send_first(hi, 0)
    arrived(W1T.at[far], w_recv.at[0])
    w1x[2].start()
    arrived(W1T.at[(1 - hi) * 2 + 1 - lo], w_recv.at[2])
    send_first(1 - hi, 5)
    f_load[0].wait()
    fx[0].wait_recv()

    w1_all = W1T[...].reshape(256, 512)

    def keep_first(t, carry):
        H1[t] = mm_nt(wide_rows(t), w1_all)
        return carry

    lax.fori_loop(0, OWN, keep_first, 0)

    arrived(w2_piece(far, g_lo), w_recv.at[6])
    arrived(w3_piece(W3.at[far], g_lo, 0), w_recv.at[9])
    for cp in shared:
        cp.start()
    arrived(pk.at[far], w_recv.at[3])
    for cp in (pkx[2], w2x[1], w3x[1], cx[0], cx[1]):
        cp.start()
    arrived(pk.at[near], w_recv.at[4])
    arrived(pk.at[(1 - hi) * 2 + 1 - lo], w_recv.at[5])
    gains = pk[0] + pk[1] + pk[2] + pk[3]
    g1, b1, g2, b2 = (gains[k : k + 1] for k in range(4))
    pair0, pair1 = pk[2 * hi], pk[2 * hi + 1]
    g3 = jnp.concatenate([pair0[4:5], pair1[4:5]], axis=1)
    b3 = jnp.concatenate([pair0[5:6], pair1[5:6]], axis=1)

    zero = jnp.zeros((8, 256), F32)

    def sum_first(t, carry):
        s, q = carry
        for kind in (0, 5):
            xcopy(kind, h1s.at[0], h1r.at[0], t).wait_recv()
        h = H1[t] + jnp.concatenate([h1r[0, t], h1r[1, t]], axis=1).astype(F32)
        H1[t] = h
        h1b[t] = h.astype(BF16)
        vh = spread(V[t], 256) * h
        return s + fold8(vh), q + fold8(vh * h)

    s, q = lax.fori_loop(0, OWN, sum_first, (zero, zero))
    ar_start(0, pack2(fold1(s), fold1(q)), "all")
    w3_load.wait()
    for t in range(1, n_lo):
        q = lax.rem(g_lo - t + n_lo, n_lo)
        arrived(w2_piece(far, q), w_recv.at[12 + t])
        arrived(w3_piece(W3.at[far], q, 0), w_recv.at[20 + t])
    w2x[2].start()
    w3x[2].start()
    inv_n = 1.0 / spread(ar_finish(6, "pix", 8)[0:1], 512)
    inv_n2 = inv_n[:, 0:256]
    s, q = unpack2(ar_finish(0, "all", 4))
    avg1 = s * inv_n2
    scale1 = lax.rsqrt(q * inv_n2 - avg1 * avg1 + EPS)
    a1_gain = g1 * scale1
    a1_shift = b1 - avg1 * a1_gain

    def act_first(t, carry):
        v = spread(V[t], 256)
        aff = v * (H1[t] * a1_gain + a1_shift)
        sig = logistic(aff)
        act = aff * sig
        comp[pl.ds(pl.multiple_of(t * ROWS, 16), ROWS), :] = act
        D1[t] = v * (sig + act * (1.0 - sig))
        return carry

    lax.fori_loop(0, OWN, act_first, 0)

    def to_padded():
        for i in range(IMAGES):
            for y in range(SIDE):
                P0[EDGE + (i * PAD + y + 1) * PAD : EDGE + (i * PAD + y + 1) * PAD + SIDE, :] = comp[
                    (i * SIDE + y) * SIDE : (i * SIDE + y + 1) * SIDE, :
                ]

    def from_padded(dst, images):
        for i in images:
            for y in range(SIDE):
                dst[(i * SIDE + y) * SIDE : (i * SIDE + y + 1) * SIDE, :] = padded[
                    (i * SIDE + y) * PAD : (i * SIDE + y) * PAD + SIDE, :
                ]

    to_padded()
    for i in range(IMAGES):
        for c in range(3):
            at = EDGE + i * 256 + c - 1
            PC[PAD + i * BLOCK : PAD + (i + 1) * BLOCK, 256 * c : 256 * (c + 1)] = P0[at : at + BLOCK, :].astype(BF16)

    arrived(W2T.at[near], w_recv.at[7])
    arrived(W2T.at[(1 - hi) * 2 + 1 - lo], w_recv.at[8])
    h1x = [remote(h1b, h1o, x_send.at[4, 0], x_recv.at[4, 0], across)]

    def conv(i, carry):
        total = None
        for r in range(3):
            rows = PC[pl.ds(pl.multiple_of(PAD + i * BLOCK + PAD * r, 16), SIDE * PAD), :]
            part = mm_nt(rows, jnp.concatenate([W2T[:, 3 * r + c].reshape(256, 256) for c in range(3)], axis=1))
            total = part if total is None else total + part
        padded[pl.ds(pl.multiple_of(i * SIDE * PAD, 16), SIDE * PAD), :] = total
        return carry

    def sum_second(t, carry):
        s, q = carry
        h = H2[pl.ds(pl.multiple_of(t * ROWS, 16), ROWS), :]
        h2s[t] = h.astype(BF16)
        vh = spread(V[t], 256) * h
        return s + fold8(vh), q + fold8(vh * h)

    def start_all(kind, src, dst, first, last):
        for t in range(first, last):
            xcopy(kind, src, dst, t).start()

    early = 2
    lax.fori_loop(0, 2, conv, 0)
    from_padded(H2, (0, 1))
    carry = lax.fori_loop(0, 3, sum_second, (zero, zero))
    start_all(1, h2s, h2r, 0, early)
    lax.fori_loop(2, IMAGES, conv, 0)
    from_padded(H2, (2, 3))
    s, q = lax.fori_loop(3, OWN, sum_second, carry)
    ar_start(1, pack2(fold1(s), fold1(q)), "all")
    start_all(1, h2s, h2r, early, OWN)
    s, q = unpack2(ar_finish(1, "all", 4))
    avg2 = s * inv_n2
    scale2 = lax.rsqrt(q * inv_n2 - avg2 * avg2 + EPS)
    a2_gain = g2 * scale2
    a2_shift = b2 - avg2 * a2_gain

    arrived(W3.at[near], w_recv.at[10])
    arrived(W3.at[(1 - hi) * 2 + 1 - lo], w_recv.at[11])

    def act_second(t, h, carry):
        s, q = carry
        v = spread(V[t], 256)
        aff = v * (h * a2_gain + a2_shift)
        sig = logistic(aff)
        act = aff * sig
        D2[t] = v * (sig + act * (1.0 - sig))
        act = act.astype(BF16)
        A2[t] = act
        h3 = mm(act, W3[...].reshape(256, 512))
        H3[t] = h3
        return s + fold8(h3), q + fold8(h3 * h3)

    def own_second(t, carry):
        return act_second(t, H2[pl.ds(pl.multiple_of(t * ROWS, 16), ROWS), :], carry)

    def other_second(t, carry):
        xcopy(1, h2s, h2r, t).wait_recv()
        return act_second(t + OWN, h2r[t].astype(F32), carry)

    wide_zero = jnp.zeros((8, 512), F32)
    carry = lax.fori_loop(0, OWN, own_second, (wide_zero, wide_zero))
    for cp in h1x:
        cp.start()
    s, q = lax.fori_loop(0, OWN, other_second, carry)
    ar_start(2, pack3(fold1(s), fold1(q)), "half")
    for cp in c_load:
        cp.wait()
    for cp in cx:
        cp.wait_recv()
    s, q = unpack3(ar_finish(2, "half", 8))
    avg3 = s * inv_n
    scale3 = lax.rsqrt(q * inv_n - avg3 * avg3 + EPS)
    a3_gain = g3 * scale3
    a3_shift = b3 - avg3 * a3_gain

    def last(t, carry):
        s, q = carry
        v = spread(V[t], 512)
        h3 = H3[t]
        wide = jnp.concatenate([F[0, t], F[1, t]], axis=1).astype(F32)
        total = v * (h3 * a3_gain + a3_shift) + wide
        sig = logistic(total)
        out = total * sig
        RES[0, t] = out[:, 0:256].astype(BF16)
        RES[1, t] = out[:, 256:512].astype(BF16)
        given = jnp.concatenate([C[0, t], C[1, t]], axis=1).astype(F32)
        gs = given * (sig + out * (1.0 - sig))
        GS[t] = gs
        vg = v * gs
        return s + fold8(vg), q + fold8(vg * (h3 - avg3))

    s, q = lax.fori_loop(0, BOTH, last, (wide_zero, wide_zero))
    ar_start(3, pack3(fold1(s), fold1(q * scale3)), "half")
    parts = ((0, part0), (1, part1))
    res_here = [
        local(RES.at[lo, pl.ds(OWN * s, OWN)], res_out.at[pl.ds(mine + part, OWN)], out_sem.at[s]) for s, part in parts
    ]
    res_there = [
        remote(RES.at[1 - lo, pl.ds(OWN * s, OWN)], res_out.at[pl.ds(mine + part, OWN)], o_send.at[s], o_recv.at[s], beside)
        for s, part in parts
    ]
    shift3, gain3 = unpack3(ar_finish(3, "half", 8))
    for cp in res_here + res_there:
        cp.start()
    k3_h = -a3_gain * gain3 * scale3 * inv_n
    k3_0 = -a3_gain * shift3 * inv_n - k3_h * avg3

    def back_third(t, carry):
        s, q, h2 = carry[0], carry[1], carry[2]
        v = spread(V[t], 512)
        g = (v * (a3_gain * GS[t] + k3_h * H3[t] + k3_0)).astype(BF16)
        G3[t] = g
        e = mm_nt(g, W3[...].reshape(256, 512)) * D2[t]
        return e, s + fold8(e), q + fold8(e * (h2 - avg2))

    def other_third(t, carry):
        e, s, q = back_third(t + OWN, (carry[0], carry[1], h2r[t].astype(F32)))
        e2s[t] = e.astype(BF16)

        @pl.when(t < 4)
        def _():
            xcopy(2, e2s, e2r, t).start()

        return s, q

    def own_third(t, carry):
        e, s, q = back_third(t, (carry[0], carry[1], H2[pl.ds(pl.multiple_of(t * ROWS, 16), ROWS), :]))
        E2[t] = e
        return s, q

    carry = lax.fori_loop(0, OWN, other_third, (zero, zero))
    s, q = lax.fori_loop(0, OWN, own_third, carry)
    ar_start(4, pack2(fold1(s), fold1(q * scale2)), "all")
    start_all(2, e2s, e2r, 4, OWN)

    piece = 16
    n_sub = 4

    def pair_copies(k):
        return [remote(wp.at[k, h], wc.at[k, h], g_send.at[k, h], g_recv.at[k, h], beside) for h in range(2)]

    def pair_start(k):
        for h in range(2):
            wp[k, h] = acc_w[k, h, 1 - lo].astype(BF16)
        for cp in pair_copies(k):
            cp.start()

    def pair_add(k):
        for h, cp in enumerate(pair_copies(k)):
            cp.wait_recv()
            both = (acc_w[k, h, lo] + wc[k, h].astype(F32)).reshape(n_sub, piece, 512)
            wa[k, h] = both
            wb[k, h] = both.astype(BF16)
        for cp in spread_copies(k):
            cp.start()

    def spread_copies(k):
        copies = []
        for t in range(1, n_lo):
            q = lax.rem(g_lo + t, n_lo)
            copies.append(
                remote(
                    wb.at[k, lax.rem(q, 2), q // 2],
                    wr.at[k, g_lo],
                    g_send.at[k, 2 + t],
                    g_recv.at[k, 2 + t],
                    (g_hi * n_lo + q, me_c),
                )
            )
        return copies

    def over_groups(total, level, sems):
        if n_hi == 1:
            return total
        level[g_hi] = total.astype(BF16)

        def swap(t):
            q = lax.rem(g_hi + t, n_hi)
            return remote(
                level.at[g_hi], level.at[g_hi], sems[0].at[t], sems[1].at[t], (q * n_lo + g_lo, me_c)
            )

        for t in range(1, n_hi):
            swap(t).start()
        for t in range(1, n_hi):
            swap(t).wait()
        total = level[0].astype(F32)
        for t in range(1, n_hi):
            total = total + level[t].astype(F32)
        return total

    def spread_add(k):
        for cp in spread_copies(k):
            cp.wait_recv()
        total = wa[k, lax.rem(g_lo, 2), g_lo // 2]
        for t in range(1, n_lo):
            total = total + wr[k, lax.rem(g_lo + t, n_lo)].astype(F32)
        return over_groups(total, wh.at[k], (h_send.at[k], h_recv.at[k]))

    def give_copies(k):
        copies = []
        for t in range(n_lo):
            q = lax.rem(g_lo + t, n_lo)
            copies.append(
                remote(
                    wf.at[k],
                    wfin.at[k, hi, own_sub],
                    g_send.at[k, 10 + t],
                    g_recv.at[k, 10 + 8 * hi + t],
                    (g_hi * n_lo + q, owner_hi * 2 + lo),
                )
            )
        return copies

    owner_hi = lax.rem(g_lo, 2)
    own_sub = g_lo // 2
    keeps = owner_hi == hi

    def wide_give(k):
        wf[k] = spread_add(k).astype(BF16)
        for t, cp in enumerate(give_copies(k)):
            if t == 0:

                @pl.when(jnp.logical_not(keeps))
                def _():
                    cp.start()

                @pl.when(keeps)
                def _():
                    wfin[k, hi, own_sub] = wf[k]

            else:
                cp.start()

    def wide_take(k, out):
        for sub in range(n_sub):
            q = sub * 2 + hi
            t = lax.rem(g_lo - q + n_lo, n_lo)
            for h in range(2):

                @pl.when(jnp.logical_not((q == g_lo) & (hi == h)))
                def _():
                    arrived(wfin.at[k, h, sub], g_recv.at[k, 10 + 8 * h + t])

        for h in range(2):
            out[:, 512 * h : 512 * (h + 1)] = wfin[k, h].astype(F32).reshape(64, 512)

    def wide_close(k):
        for cp in pair_copies(k) + spread_copies(k):
            cp.wait_send()
        for t, cp in enumerate(give_copies(k)):
            if t == 0:

                @pl.when(jnp.logical_not(keeps))
                def _():
                    cp.wait_send()

            else:
                cp.wait_send()

    def half_of(ref, part):
        return ref[OWN * part : OWN * (part + 1)].reshape(OWN * ROWS, ref.shape[2])

    acc_w[0] = (mm_tn(half_of(A2, 0), half_of(G3, 0)) + mm_tn(half_of(A2, 1), half_of(G3, 1))).reshape(2, 2, 64, 512)
    pair_start(0)
    pair_add(0)

    shift2, gain2 = unpack2(ar_finish(4, "all", 4))
    k2_h = -a2_gain * gain2 * scale2 * inv_n2
    k2_0 = -a2_gain * shift2 * inv_n2 - k2_h * avg2

    def back_second(t, carry):
        xcopy(2, e2s, e2r, t).wait_recv()
        at = pl.ds(pl.multiple_of(t * ROWS, 16), ROWS)
        e = E2[t] + e2r[t].astype(F32)
        comp[at, :] = spread(V[t], 256) * (a2_gain * e + k2_h * H2[at, :] + k2_0)
        return carry

    lax.fori_loop(0, OWN, back_second, 0)
    to_padded()
    for i in range(IMAGES):
        for c in range(3):
            at = EDGE + i * BLOCK - (c - 1)
            Q[c, i * BLOCK : (i + 1) * BLOCK, :] = P0[at : at + BLOCK, :].astype(BF16)

    def conv_back(i, carry):
        total = None
        for r in range(3):
            at = pl.ds(pl.multiple_of(i * BLOCK + PAD * (2 - r), 16), SIDE * PAD)
            for c in range(3):
                w = W2T[:, 3 * r + c].reshape(256, 256)
                part = mm(Q[c, at, :], w)
                total = part if total is None else total + part
        padded[pl.ds(pl.multiple_of(i * SIDE * PAD, 16), SIDE * PAD), :] = total
        return carry

    def sum_back_first(t, carry):
        s, q = carry
        e = comp[pl.ds(pl.multiple_of(t * ROWS, 16), ROWS), :] * D1[t]
        E1[t] = e
        e1s[t] = e.astype(BF16)
        return s + fold8(e), q + fold8(e * (H1[t] - avg1))

    lax.fori_loop(0, 2, conv_back, 0)
    from_padded(comp, (0, 1))
    carry = lax.fori_loop(0, 3, sum_back_first, (zero, zero))
    start_all(3, e1s, e1r, 0, early)
    lax.fori_loop(2, IMAGES, conv_back, 0)
    from_padded(comp, (2, 3))
    s, q = lax.fori_loop(3, OWN, sum_back_first, carry)
    ar_start(5, pack2(fold1(s), fold1(q * scale1)), "all")
    start_all(3, e1s, e1r, early, OWN)

    bit, quad = lax.rem(g_lo, 2), g_lo // 2
    next_group = (g_hi * n_lo + quad * 2 + 1 - bit, me_c)
    s_owner = lax.rem(quad, 2) == hi

    def s_pair(r):
        return [
            remote(sp.at[r, h], sc.at[r, h], s_send.at[r, h], s_recv.at[r, h], beside) for h in range(2)
        ]

    def s_next(r):
        return remote(ys.at[r], yr.at[r], s_send.at[r, 2], s_recv.at[r, 2], next_group)

    def s_quad(r):
        copies = []
        for t in range(1, 4):
            q = lax.rem(quad + t, 4)
            copies.append(
                remote(
                    zs.at[r, lax.rem(q, 2), q // 2],
                    zr.at[r, t - 1],
                    s_send.at[r, 2 + t],
                    s_recv.at[r, 2 + t],
                    (g_hi * n_lo + q * 2 + bit, me_c),
                )
            )
        return copies

    def s_cross(r):
        return remote(xs.at[r], xr.at[r], s_send.at[r, 6], s_recv.at[r, 6], across)

    def s_give(r):
        copies = []
        for t in range(1, 4):
            q = lax.rem(quad + t, 4)
            spot = sfin.at[r, bit, quad // 2]
            copies.append(
                remote(
                    spot, spot, s_send.at[r, 6 + t], s_recv.at[r, 7 + quad // 2], (g_hi * n_lo + q * 2 + bit, me_c)
                )
            )
        return copies

    def s_back(r):
        return remote(sfin.at[r, bit], sfin.at[r, bit], s_send.at[r, 10], s_recv.at[r, 10], next_group)

    def s_make(r):
        taps = mm(QT[...], PC[PAD * r : PAD * r + FLAT, :])
        acc_s[r] = taps.reshape(2, 2, 64, 768)
        for h in range(2):
            sp[r, h] = acc_s[r, h, 1 - lo].astype(BF16)
        for cp in s_pair(r):
            cp.start()

    def s_pair_add(r):
        for h, cp in enumerate(s_pair(r)):
            cp.wait_recv()
            s1[r, h] = (acc_s[r, h, lo] + sc[r, h].astype(F32)).reshape(2, 32, 768)
            ys[r, h] = s1[r, h, 1 - bit].astype(BF16)
        s_next(r).start()

    def s_next_add(r):
        s_next(r).wait_recv()
        for h in range(2):
            s2[r, h] = (s1[r, h, bit] + yr[r, h].astype(F32)).reshape(2, 16, 768)
            zs[r, h] = s2[r, h].astype(BF16)
        for cp in s_quad(r):
            cp.start()

    def s_quad_add(r):
        for cp in s_quad(r):
            cp.wait_recv()
        total = s2[r, lax.rem(quad, 2), quad // 2]
        for t in range(3):
            total = total + zr[r, t].astype(F32)
        s3[r] = total
        xs[r] = total.astype(BF16)

        @pl.when(jnp.logical_not(s_owner))
        def _():
            s_cross(r).start()

    def s_cross_add(r):
        @pl.when(s_owner)
        def _():
            s_cross(r).wait_recv()
            total = s3[r] + xr[r].astype(F32)
            sfin[r, bit, quad // 2] = over_groups(total, sh.at[r], (h_send.at[2 + r], h_recv.at[2 + r])).astype(BF16)
            for cp in s_give(r):
                cp.start()

    def s_give_back(r):
        for part in range(2):

            @pl.when(quad != 2 * part + hi)
            def _():
                arrived(sfin.at[r, bit, part], s_recv.at[r, 7 + part])

        s_back(r).start()

    def s_take(r):
        arrived(sfin.at[r, 1 - bit], s_recv.at[r, 10])
        rows = sfin[r].astype(F32).reshape(64, 768)
        for c in range(3):
            sg_out[3 * r + c] = rows[:, 256 * c : 256 * (c + 1)]

    def s_close(r):
        for cp in s_pair(r) + [s_next(r)] + s_quad(r) + [s_back(r)]:
            cp.wait_send()

        @pl.when(s_owner)
        def _():
            for cp in s_give(r):
                cp.wait_send()

        @pl.when(jnp.logical_not(s_owner))
        def _():
            s_cross(r).wait_send()

    for i in range(IMAGES):
        QT[:, i * BLOCK : (i + 1) * BLOCK] = P0[EDGE + i * BLOCK : EDGE + (i + 1) * BLOCK, :].T.astype(BF16)
    wide_give(0)
    s_make(0)
    s_make(1)
    s_pair_add(0)
    s_make(2)
    s_pair_add(1)
    s_pair_add(2)

    shift1, gain1 = unpack2(ar_finish(5, "all", 4))
    k1_h = -a1_gain * gain1 * scale1 * inv_n2
    k1_0 = -a1_gain * shift1 * inv_n2 - k1_h * avg1

    def back_first(t, e, h):
        g = (spread(V[t], 256) * (a1_gain * e + k1_h * h + k1_0)).astype(BF16)
        G1[t] = g
        out = (mm(g, W1T[...].reshape(256, 512)) + GS[t]).astype(BF16)
        RES[0, t] = out[:, 0:256]
        RES[1, t] = out[:, 256:512]

    ig_here = [
        local(RES.at[lo, pl.ds(OWN * s, OWN)], ig_out.at[pl.ds(mine + part, OWN)], out_sem.at[2 + s])
        for s, part in parts
    ]
    ig_there = [
        remote(
            RES.at[1 - lo, pl.ds(OWN * s, OWN)], ig_out.at[pl.ds(mine + part, OWN)], o_send.at[2 + s], o_recv.at[2 + s], beside
        )
        for s, part in parts
    ]
    for cp in res_here:
        cp.wait()
    for cp in res_there:
        cp.wait_send()

    def own_back_first(t, carry):
        back_first(t, E1[t], H1[t])
        return carry

    lax.fori_loop(0, OWN, own_back_first, 0)
    ig_here[0].start()
    ig_there[0].start()
    s_next_add(0)

    def features_of(part):
        return jnp.concatenate([half_of(F.at[0], part), half_of(F.at[1], part)], axis=1)

    own_reduce = mm_tn(half_of(G1, 0), features_of(0))
    acc_w[1] = own_reduce.reshape(2, 2, 64, 512)
    for cp in h1x:
        cp.wait_recv()

    def other_back_first(t, carry):
        xcopy(3, e1s, e1r, t).wait_recv()
        back_first(t + OWN, e1r[t].astype(F32), h1o[t].astype(F32))
        return carry

    lax.fori_loop(0, OWN, other_back_first, 0)
    s_next_add(1)
    acc_w[1] += mm_tn(half_of(G1, 1), features_of(1)).reshape(2, 2, 64, 512)
    pair_start(1)
    ig_here[1].start()
    ig_there[1].start()
    s_quad_add(0)
    s_next_add(2)
    pair_add(1)
    s_quad_add(1)
    s_cross_add(0)
    s_quad_add(2)
    s_cross_add(1)
    wide_give(1)
    s_cross_add(2)
    for r in range(3):
        s_give_back(r)

    def own64(v):
        half = jnp.where(hi == 0, v[:, 0:128], v[:, 128:256])
        swapped = jnp.concatenate([half[:, 64:128], half[:, 0:64]], axis=1)
        return jnp.concatenate([jnp.where(lo == 0, half, swapped), jnp.zeros((1, 128), F32)], axis=1)

    def own256(v):
        return jnp.where(lo == 0, v[:, 0:256], v[:, 256:512])

    st_out[...] = jnp.concatenate(
        [
            own64(gain1),
            own64(shift1),
            own64(gain2),
            own64(shift2),
            own256(gain3),
            own256(shift3),
            jnp.zeros((2, 256), F32),
        ],
        axis=0,
    )

    wide_take(0, eg_out)
    for r in range(3):
        s_take(r)
    wide_take(1, rg_out)

    wide_close(0)
    wide_close(1)
    for r in range(3):
        s_close(r)
    for cp in ig_here:
        cp.wait()
    for cp in ig_there:
        cp.wait()
    for cp in res_there:
        cp.wait_recv()
    for cp in fx + cx + w1x + pkx + w2x + w3x + shared + h1x:
        cp.wait_send()
    for kind, src, dst in ((0, h1s.at[hi], h1r.at[hi]), (5, h1s.at[1 - hi], h1r.at[1 - hi]), (1, h2s, h2r), (2, e2s, e2r), (3, e1s, e1r)):
        for t in range(OWN):
            xcopy(kind, src, dst, t).wait_send()
    for k, kind, rows in (
        (0, "all", 4),
        (1, "all", 4),
        (2, "half", 8),
        (3, "half", 8),
        (4, "all", 4),
        (5, "all", 4),
        (6, "pix", 8),
    ):
        ar_close(k, kind, rows)


def block(n_pix, n_ch, *args):
    feat, cot, mask, w1, w2, w3 = args[:6]
    rows, lanes = feat.shape
    n_lo, n_sub, piece = 8, 4, 16
    n_hi = n_pix // n_lo
    chunks = rows // ROWS
    any_space = pl.BlockSpec(memory_space=pl.ANY)
    vmem = pl.BlockSpec(memory_space=pltpu.VMEM)
    V = pltpu.VMEM
    DMA = pltpu.SemaphoreType.DMA
    scratch = [
        V((rows,), jnp.int32),
        *[V((64,), BF16)] * 4,
        *[V((256,), BF16)] * 2,
        V((2, BOTH, ROWS, 256), BF16),
        V((2, BOTH, ROWS, 256), BF16),
        V((BOTH, ROWS, 128), F32),
        V((4, 64, 512), BF16),
        V((4, 9, 64, 256), BF16),
        V((4, 64, 512), BF16),
        V((4, 8, 256), F32),
        V((7, 8, 128), F32),
        V((7, n_pix * n_ch, 8, 128), F32),
        V((2, OWN, ROWS, 128), BF16),
        V((2, OWN, ROWS, 128), BF16),
        V((OWN, ROWS, 256), F32),
        V((OWN, ROWS, 256), BF16),
        V((OWN, ROWS, 256), BF16),
        V((OWN, ROWS, 256), F32),
        V((OWN * ROWS, 256), F32),
        V((FLAT + 2 * EDGE, 256), F32),
        V((FLAT + 2 * PAD, 768), BF16),
        V((3, FLAT, 256), BF16),
        V((IMAGES * SIDE * PAD, 256), F32),
        V((OWN * ROWS, 256), F32),
        V((OWN, ROWS, 256), BF16),
        V((OWN, ROWS, 256), BF16),
        V((BOTH, ROWS, 256), BF16),
        V((BOTH, ROWS, 256), F32),
        V((BOTH, ROWS, 512), F32),
        V((BOTH, ROWS, 512), F32),
        V((2, BOTH, ROWS, 256), BF16),
        V((BOTH, ROWS, 512), BF16),
        V((OWN, ROWS, 256), F32),
        V((OWN, ROWS, 256), BF16),
        V((OWN, ROWS, 256), BF16),
        V((OWN, ROWS, 256), F32),
        V((OWN, ROWS, 256), BF16),
        V((OWN, ROWS, 256), BF16),
        V((BOTH, ROWS, 256), BF16),
        V((256, FLAT), BF16),
        V((chunks, ROWS), F32),
        V((2, 2, 2, 64, 512), F32),
        V((2, 2, 64, 512), BF16),
        V((2, 2, 64, 512), BF16),
        V((2, 2, n_sub, piece, 512), F32),
        V((2, 2, n_sub, piece, 512), BF16),
        V((2, n_lo, piece, 512), BF16),
        V((2, n_hi, piece, 512), BF16),
        V((2, piece, 512), BF16),
        V((2, 2, n_sub, piece, 512), BF16),
        V((3, 2, 2, 64, 768), F32),
        V((3, 2, 64, 768), BF16),
        V((3, 2, 64, 768), BF16),
        V((3, 2, 2, 32, 768), F32),
        V((3, 2, 32, 768), BF16),
        V((3, 2, 32, 768), BF16),
        V((3, 2, 2, 16, 768), F32),
        V((3, 2, 2, 16, 768), BF16),
        V((3, 3, 16, 768), BF16),
        V((3, 16, 768), F32),
        V((3, 16, 768), BF16),
        V((3, 16, 768), BF16),
        V((3, n_hi, 16, 768), BF16),
        V((3, 2, 2, 16, 768), BF16),
        DMA((14,)),
        DMA((4,)),
        DMA((4,)),
        DMA((28,)),
        DMA((28,)),
        DMA((7,)),
        DMA((7,)),
        DMA((6, OWN)),
        DMA((6, OWN)),
        DMA((4,)),
        DMA((4,)),
        DMA((4,)),
        DMA((2, 26)),
        DMA((2, 26)),
        DMA((3, 12)),
        DMA((3, 12)),
        DMA((5, n_hi)),
        DMA((5, n_hi)),
    ]
    wide = V((chunks, ROWS, lanes), BF16)
    made = pl.pallas_call(
        functools.partial(kernel, n_pix, n_ch),
        out_shape=(
            wide,
            wide,
            V((64, 1024), F32),
            V((9, 64, 256), F32),
            V((64, 1024), F32),
            V((8, 256), F32),
        ),
        in_specs=[any_space] * 12,
        out_specs=(any_space, any_space, vmem, vmem, vmem, vmem),
        scratch_shapes=scratch,
        compiler_params=pltpu.CompilerParams(
            collective_id=0, has_side_effects=True, vmem_limit_bytes=56 * 2**20
        ),
        name="bottleneck",
    )(
        feat.reshape(chunks, ROWS, lanes),
        cot.reshape(chunks, ROWS, lanes),
        mask,
        w1.T,
        w2.transpose(0, 1, 3, 2).reshape(9, 64, 256),
        w3,
        *args[6:],
    )
    narrow = jax.ShapeDtypeStruct((64,), F32)
    broad = jax.ShapeDtypeStruct((256,), F32)
    return pl.pallas_call(
        finish,
        out_shape=tuple(jax.ShapeDtypeStruct(v.shape, v.dtype) for v in made[:5]) + (narrow,) * 4 + (broad,) * 2,
        in_specs=[any_space] * 5 + [vmem],
        out_specs=(any_space,) * 5 + (vmem,) * 6,
        scratch_shapes=[DMA((5,))],
        compiler_params=pltpu.CompilerParams(vmem_limit_bytes=2**20),
        name="outputs",
    )(*[pltpu.with_memory_space_constraint(v, pltpu.VMEM) for v in made])


def finish(*refs):
    made, stats, outs, small, sems = refs[:5], refs[5], refs[6:11], refs[11:17], refs[17]
    copies = [pltpu.make_async_copy(a, b, sems.at[i]) for i, (a, b) in enumerate(zip(made, outs))]
    for cp in copies:
        cp.start()
    for i, out in enumerate(small):
        out[...] = stats[i : i + 1, 0 : out.shape[0]].reshape(out.shape)
    for cp in copies:
        cp.wait()


def solution(mesh):
    n_pix, n_ch = mesh.shape["pix"], mesh.shape["ch"]

    def body(feat, mask, w1, w2, w3, g1, b1, g2, b2, g3, b3, cot):
        made = block(n_pix, n_ch, feat, cot, mask, w1, w2, w3, g1, b1, g2, b2, g3, b3)
        res, ig, rg, sg, eg = made[:5]
        return (
            res.reshape(feat.shape),
            ig.reshape(feat.shape),
            rg.T,
            sg.reshape(3, 3, 64, 256).transpose(0, 1, 3, 2),
            eg,
        ) + tuple(made[5:])

    wide = P("pix", "ch")
    return jax.shard_map(
        body,
        mesh=mesh,
        in_specs=(wide, P("pix"), P(None, "ch"), P(None, None, None, "ch"), P("ch", None)) + (P("ch"),) * 6 + (wide,),
        out_specs=(wide, wide, P(None, "ch"), P(None, None, None, "ch"), P("ch", None)) + (P("ch"),) * 6,
        check_vma=False,
    )
```

```python
import functools

import jax
import jax.numpy as jnp
from jax import lax
from jax.experimental import pallas as pl
from jax.experimental.pallas import tpu as pltpu
from jax.sharding import PartitionSpec as P

SIDE = 14
EPS = 1e-05
MESH = pl.DeviceIdType.MESH
F32 = jnp.float32
BF16 = jnp.bfloat16

ROWS = 112
OWN = 7
BOTH = 14
IMAGES = 4
PAD = 16
FLAT = IMAGES * PAD * PAD
EDGE = 8
BLOCK = PAD * PAD


def mm(a, b):
    return jnp.dot(a, b, preferred_element_type=F32)


def mm_nt(a, b):
    return lax.dot_general(a, b, (((1,), (1,)), ((), ())), preferred_element_type=F32)


def mm_tn(a, b):
    return lax.dot_general(a, b, (((0,), (0,)), ((), ())), preferred_element_type=F32)


def logistic(v):
    return 0.5 * jnp.tanh(0.5 * v) + 0.5


def fold8(v):
    return jnp.sum(v.reshape(v.shape[0] // 8, 8, v.shape[1]), axis=0)


def fold1(v):
    return jnp.sum(v, axis=0, keepdims=True)


def spread(v, lanes):
    return jnp.concatenate([v] * (lanes // 128), axis=1)


def kernel(
    n_pix,
    n_ch,
    feat,
    cot,
    mask,
    w1_in,
    w2_in,
    w3_in,
    g1_in,
    b1_in,
    g2_in,
    b2_in,
    g3_in,
    b3_in,
    res_out,
    ig_out,
    rg_out,
    sg_out,
    eg_out,
    st_out,
    mask_v,
    g1_v,
    b1_v,
    g2_v,
    b2_v,
    g3_v,
    b3_v,
    F,
    C,
    V,
    W1T,
    W2T,
    W3,
    pk,
    sbuf,
    rbuf,
    h1s,
    h1r,
    H1,
    h1b,
    h1o,
    D1,
    comp,
    P0,
    PC,
    Q,
    padded,
    H2,
    h2s,
    h2r,
    A2,
    D2,
    H3,
    GS,
    RES,
    G3,
    E2,
    e2s,
    e2r,
    E1,
    e1s,
    e1r,
    G1,
    QT,
    rows28,
    acc_w,
    wp,
    wc,
    wa,
    wb,
    wr,
    wh,
    wf,
    wfin,
    acc_s,
    sp,
    sc,
    s1,
    ys,
    yr,
    s2,
    zs,
    zr,
    s3,
    xs,
    xr,
    sh,
    sfin,
    t1,
    xb,
    xc,
    yb,
    yc,
    t2,
    zb,
    zc,
    th,
    tfin,
    ld_sem,
    fx_send,
    fx_recv,
    w_send,
    w_recv,
    ar_send,
    ar_recv,
    x_send,
    x_recv,
    out_sem,
    o_send,
    o_recv,
    g_send,
    g_recv,
    s_send,
    s_recv,
    h_send,
    h_recv,
):
    me_p, me_c = lax.axis_index("pix"), lax.axis_index("ch")
    hi, lo = me_c // 2, lax.rem(me_c, 2)
    n_lo = 8
    n_hi = n_pix // n_lo
    g_hi, g_lo = me_p // n_lo, lax.rem(me_p, n_lo)
    across = (me_p, (1 - hi) * 2 + lo)
    beside = (me_p, hi * 2 + 1 - lo)
    n_all = n_pix * n_ch

    def remote(src, dst, send, recv, device):
        return pltpu.make_async_remote_copy(
            src_ref=src, dst_ref=dst, send_sem=send, recv_sem=recv, device_id=device, device_id_type=MESH
        )

    def local(src, dst, sem):
        return pltpu.make_async_copy(src, dst, sem)

    mine, theirs = lo * BOTH, (1 - lo) * BOTH
    part0, part1 = hi * OWN, (1 - hi) * OWN

    w1_load = local(w1_in.at[:, pl.ds(pl.multiple_of(hi * 512, 512), 512)], W1T.at[me_c], ld_sem.at[0])
    w2_load = local(w2_in, W2T.at[me_c], ld_sem.at[1])
    f_load = [
        local(feat.at[pl.ds(mine + part, OWN)], F.at[lo, pl.ds(OWN * s, OWN)], ld_sem.at[2 + s])
        for s, part in enumerate((part0, part1))
    ]
    c_load = [
        local(cot.at[pl.ds(mine + part, OWN)], C.at[lo, pl.ds(OWN * s, OWN)], ld_sem.at[4 + s])
        for s, part in enumerate((part0, part1))
    ]
    small_load = [local(mask, mask_v, ld_sem.at[7])]
    pairs = ((g1_in, g1_v), (b1_in, b1_v), (g2_in, g2_v), (b2_in, b2_v), (g3_in, g3_v), (b3_in, b3_v))
    small_load += [local(a, b, ld_sem.at[8 + i]) for i, (a, b) in enumerate(pairs)]
    w3_load = local(w3_in.at[:, pl.ds(pl.multiple_of(hi * 512, 512), 512)], W3.at[me_c], ld_sem.at[6])
    barrier = pltpu.get_barrier_semaphore()

    def greet(t, carry):
        q = lax.rem(me_p * n_ch + me_c + t, n_all)
        pl.semaphore_signal(barrier, inc=1, device_id=(q // n_ch, lax.rem(q, n_ch)), device_id_type=MESH)
        return carry

    lax.fori_loop(1, n_all, greet, 0)
    for cp in small_load:
        cp.start()
    w1_load.start()
    f_load[1].start()
    f_load[0].start()
    w2_load.start()
    w3_load.start()
    c_load[0].start()
    c_load[1].start()

    pl.semaphore_wait(barrier, n_all - 1)

    fx = [
        remote(
            feat.at[pl.ds(theirs + part, OWN)], F.at[lo, pl.ds(OWN * s, OWN)], fx_send.at[s], fx_recv.at[s], beside
        )
        for s, part in enumerate((part0, part1))
    ]
    cx = [
        remote(
            cot.at[pl.ds(theirs + part, OWN)], C.at[lo, pl.ds(OWN * s, OWN)], fx_send.at[2 + s], fx_recv.at[2 + s], beside
        )
        for s, part in enumerate((part0, part1))
    ]
    far, near = (1 - hi) * 2 + lo, hi * 2 + 1 - lo

    def columns(ref, h):
        return ref.at[:, pl.ds(pl.multiple_of(h * 512, 512), 512)]

    w1x = [
        remote(columns(w1_in, 1 - hi), W1T.at[me_c], w_send.at[0], w_recv.at[0], across),
        remote(columns(w1_in, hi), W1T.at[me_c], w_send.at[1], w_recv.at[1], beside),
        remote(W1T.at[far], W1T.at[far], w_send.at[2], w_recv.at[2], beside),
    ]
    pkx = [
        remote(pk.at[me_c], pk.at[me_c], w_send.at[3], w_recv.at[3], across),
        remote(pk.at[me_c], pk.at[me_c], w_send.at[4], w_recv.at[4], beside),
        remote(pk.at[far], pk.at[far], w_send.at[5], w_recv.at[5], beside),
    ]

    def w2_piece(ref, q):
        return ref.at[
            :, pl.ds(pl.multiple_of(q // 2 * 16, 16), 16), pl.ds(pl.multiple_of(lax.rem(q, 2) * 128, 128), 128)
        ]

    def w3_piece(ref, q, first):
        return ref.at[
            pl.ds(pl.multiple_of(q // 2 * 16, 16), 16), pl.ds(pl.multiple_of(first + lax.rem(q, 2) * 256, 256), 256)
        ]

    w2x = [
        remote(w2_piece(w2_in, g_lo), w2_piece(W2T.at[me_c], g_lo), w_send.at[6], w_recv.at[6], across),
        remote(W2T.at[me_c], W2T.at[me_c], w_send.at[7], w_recv.at[7], beside),
        remote(W2T.at[far], W2T.at[far], w_send.at[8], w_recv.at[8], beside),
    ]
    w3x = [
        remote(
            w3_piece(w3_in, g_lo, (1 - hi) * 512),
            w3_piece(W3.at[me_c], g_lo, 0),
            w_send.at[9],
            w_recv.at[9],
            across,
        ),
        remote(columns(w3_in, hi), W3.at[me_c], w_send.at[10], w_recv.at[10], beside),
        remote(W3.at[far], W3.at[far], w_send.at[11], w_recv.at[11], beside),
    ]
    shared = []
    for t in range(1, n_lo):
        to = (g_hi * n_lo + lax.rem(g_lo + t, n_lo), me_c)
        for k, piece_of in enumerate((lambda q: w2_piece(W2T.at[far], q), lambda q: w3_piece(W3.at[far], q, 0))):
            at = 12 + 8 * k + t
            shared.append(remote(piece_of(g_lo), piece_of(g_lo), w_send.at[at], w_recv.at[at], to))
    w1x[0].start()
    w1x[1].start()
    fx[1].start()
    fx[0].start()
    w3x[0].start()
    w2x[0].start()

    row_i = lax.broadcasted_iota(jnp.int32, (64, 256), 0)
    col_i = lax.broadcasted_iota(jnp.int32, (64, 256), 1)
    place = (row_i == col_i - 64 * me_c).astype(BF16)
    for cp in small_load:
        cp.wait()
    narrow = jnp.concatenate([v[...].astype(F32).reshape(1, 64) for v in (g1_v, b1_v, g2_v, b2_v)] * 2, axis=0)
    pk_rows = [mm(narrow.astype(BF16), place)[0:4]]
    pk_rows += [v[...].astype(F32).reshape(1, 256) for v in (g3_v, b3_v)]
    pk[me_c] = jnp.concatenate(pk_rows + [jnp.zeros((2, 256), F32)], axis=0)

    pkx[0].start()
    pkx[1].start()

    def arrived(dst, sem):
        local(dst, dst, sem).wait()

    def ar_group(kind):
        if kind == "all":
            return n_all, me_p * n_ch + me_c, lambda q: (q // n_ch, lax.rem(q, n_ch))
        if kind == "half":
            return n_pix * 2, me_p * 2 + lo, lambda q: (q // 2, hi * 2 + lax.rem(q, 2))
        return n_pix, me_p, lambda q: (q, me_c)

    def ar_start(k, val, kind):
        n, me, device = ar_group(kind)
        rows = val.shape[0]
        sbuf[k, 0:rows] = val
        rbuf[k, me, 0:rows] = val

        def send(t, carry):
            to = device(lax.rem(me + t, n))
            cut = pl.ds(0, rows)
            remote(sbuf.at[k, cut], rbuf.at[k, me, cut], ar_send.at[k], ar_recv.at[k], to).start()
            return carry

        lax.fori_loop(1, n, send, 0)

    def ar_finish(k, kind, rows):
        n = ar_group(kind)[0]
        arrived(rbuf.at[k, pl.ds(0, n - 1), pl.ds(0, rows)], ar_recv.at[k])
        return jnp.sum(rbuf[k, 0:n, 0:rows], axis=0)

    def ar_close(k, kind, rows):
        n = ar_group(kind)[0]
        arrived(rbuf.at[k, pl.ds(0, n - 1), pl.ds(0, rows)], ar_send.at[k])

    def pack2(a, b):
        return jnp.concatenate([a[:, 0:128], a[:, 128:256], b[:, 0:128], b[:, 128:256]], axis=0)

    def unpack2(v):
        return (
            jnp.concatenate([v[0:1], v[1:2]], axis=1),
            jnp.concatenate([v[2:3], v[3:4]], axis=1),
        )

    def pack3(a, b):
        return jnp.concatenate([a[:, 128 * i : 128 * (i + 1)] for i in range(4)] + [b[:, 128 * i : 128 * (i + 1)] for i in range(4)], axis=0)

    def unpack3(v):
        return (
            jnp.concatenate([v[i : i + 1] for i in range(4)], axis=1),
            jnp.concatenate([v[i : i + 1] for i in range(4, 8)], axis=1),
        )


    w1_load.wait()
    w2_load.wait()
    f_load[1].wait()
    fx[1].wait_recv()
    arrived(W1T.at[near], w_recv.at[1])

    def wide_rows(t):
        return jnp.concatenate([F[0, t], F[1, t]], axis=1)

    def xcopy(kind, src, dst, t):
        return remote(src.at[t], dst.at[t], x_send.at[kind, t], x_recv.at[kind, t], across)

    def send_first(h, kind):
        w = W1T[pl.ds(2 * h, 2)].reshape(128, 512)

        def one(t, carry):
            h1s[h, t] = mm_nt(wide_rows(t + OWN), w).astype(BF16)
            xcopy(kind, h1s.at[h], h1r.at[h], t).start()
            return carry

        lax.fori_loop(0, OWN, one, 0)

    send_first(hi, 0)
    arrived(W1T.at[far], w_recv.at[0])
    w1x[2].start()
    arrived(w3_piece(W3.at[far], g_lo, 0), w_recv.at[9])
    arrived(w2_piece(W2T.at[far], g_lo), w_recv.at[6])
    for cp in shared:
        cp.start()
    arrived(W1T.at[(1 - hi) * 2 + 1 - lo], w_recv.at[2])
    send_first(1 - hi, 5)
    f_load[0].wait()
    fx[0].wait_recv()

    w1_all = W1T[...].reshape(256, 512)

    def keep_first(t, carry):
        H1[t] = mm_nt(wide_rows(t), w1_all)
        return carry

    lax.fori_loop(0, OWN, keep_first, 0)

    flat = mask_v[...].astype(F32).reshape(1, rows28.shape[0] * ROWS)
    for t in range(rows28.shape[0]):
        rows28[t : t + 1, :] = flat[:, t * ROWS : (t + 1) * ROWS]
    diag = lax.broadcasted_iota(jnp.int32, (ROWS, ROWS), 0) == lax.broadcasted_iota(jnp.int32, (ROWS, ROWS), 1)
    ones = jnp.ones((ROWS, 128), BF16)

    def put_mask(t, carry):
        at = mine + jnp.where(t < OWN, part0 + t, part1 + t - OWN)
        row = rows28[pl.ds(at, 1), :]
        V[t] = mm(jnp.where(diag, row, 0.0).astype(BF16), ones)
        return carry

    lax.fori_loop(0, BOTH, put_mask, 0)
    lanes = jnp.broadcast_to(jnp.sum(rows28[...], axis=0, keepdims=True), (8, ROWS))
    local_count = mm(lanes.astype(BF16), ones)
    P0[...] = jnp.zeros_like(P0)
    PC[0:PAD, :] = jnp.zeros((PAD, 768), BF16)
    PC[PAD + FLAT :, :] = jnp.zeros((PAD, 768), BF16)
    ar_start(6, local_count, "pix")

    arrived(pk.at[far], w_recv.at[3])
    for cp in (pkx[2], w2x[1], w3x[1], cx[0], cx[1]):
        cp.start()
    arrived(pk.at[near], w_recv.at[4])
    arrived(pk.at[(1 - hi) * 2 + 1 - lo], w_recv.at[5])
    gains = pk[0] + pk[1] + pk[2] + pk[3]
    g1, b1, g2, b2 = (gains[k : k + 1] for k in range(4))
    pair0, pair1 = pk[2 * hi], pk[2 * hi + 1]
    g3 = jnp.concatenate([pair0[4:5], pair1[4:5]], axis=1)
    b3 = jnp.concatenate([pair0[5:6], pair1[5:6]], axis=1)

    zero = jnp.zeros((8, 256), F32)

    def sum_first(t, carry):
        s, q = carry
        for kind in (0, 5):
            xcopy(kind, h1s.at[0], h1r.at[0], t).wait_recv()
        h = H1[t] + jnp.concatenate([h1r[0, t], h1r[1, t]], axis=1).astype(F32)
        H1[t] = h
        h1b[t] = h.astype(BF16)
        vh = spread(V[t], 256) * h
        return s + fold8(vh), q + fold8(vh * h)

    s, q = lax.fori_loop(0, OWN, sum_first, (zero, zero))
    ar_start(0, pack2(fold1(s), fold1(q)), "all")
    w3_load.wait()
    for t in range(1, n_lo):
        q = lax.rem(g_lo - t + n_lo, n_lo)
        arrived(w2_piece(W2T.at[far], q), w_recv.at[12 + t])
        arrived(w3_piece(W3.at[far], q, 0), w_recv.at[20 + t])
    w2x[2].start()
    w3x[2].start()
    inv_n = 1.0 / spread(ar_finish(6, "pix", 8)[0:1], 512)
    inv_n2 = inv_n[:, 0:256]
    s, q = unpack2(ar_finish(0, "all", 4))
    avg1 = s * inv_n2
    scale1 = lax.rsqrt(q * inv_n2 - avg1 * avg1 + EPS)
    a1_gain = g1 * scale1
    a1_shift = b1 - avg1 * a1_gain

    def act_first(t, carry):
        v = spread(V[t], 256)
        aff = v * (H1[t] * a1_gain + a1_shift)
        sig = logistic(aff)
        act = aff * sig
        comp[pl.ds(pl.multiple_of(t * ROWS, 16), ROWS), :] = act
        D1[t] = v * (sig + act * (1.0 - sig))
        return carry

    lax.fori_loop(0, OWN, act_first, 0)

    def to_padded():
        for i in range(IMAGES):
            for y in range(SIDE):
                P0[EDGE + (i * PAD + y + 1) * PAD : EDGE + (i * PAD + y + 1) * PAD + SIDE, :] = comp[
                    (i * SIDE + y) * SIDE : (i * SIDE + y + 1) * SIDE, :
                ]

    def from_padded(dst, images):
        for i in images:
            for y in range(SIDE):
                dst[(i * SIDE + y) * SIDE : (i * SIDE + y + 1) * SIDE, :] = padded[
                    (i * SIDE + y) * PAD : (i * SIDE + y) * PAD + SIDE, :
                ]

    to_padded()
    for i in range(IMAGES):
        for c in range(3):
            at = EDGE + i * 256 + c - 1
            PC[PAD + i * BLOCK : PAD + (i + 1) * BLOCK, 256 * c : 256 * (c + 1)] = P0[at : at + BLOCK, :].astype(BF16)

    arrived(W2T.at[near], w_recv.at[7])
    arrived(W2T.at[(1 - hi) * 2 + 1 - lo], w_recv.at[8])
    h1x = [remote(h1b, h1o, x_send.at[4, 0], x_recv.at[4, 0], across)]

    def conv(i, carry):
        total = None
        for r in range(3):
            rows = PC[pl.ds(pl.multiple_of(PAD + i * BLOCK + PAD * r, 16), SIDE * PAD), :]
            part = mm_nt(rows, jnp.concatenate([W2T[:, 3 * r + c].reshape(256, 256) for c in range(3)], axis=1))
            total = part if total is None else total + part
        padded[pl.ds(pl.multiple_of(i * SIDE * PAD, 16), SIDE * PAD), :] = total
        return carry

    def sum_second(t, carry):
        s, q = carry
        h = H2[pl.ds(pl.multiple_of(t * ROWS, 16), ROWS), :]
        h2s[t] = h.astype(BF16)
        vh = spread(V[t], 256) * h
        return s + fold8(vh), q + fold8(vh * h)

    def start_all(kind, src, dst, first, last):
        for t in range(first, last):
            xcopy(kind, src, dst, t).start()

    early = 3
    whole = [(i + 1) * SIDE * SIDE // ROWS for i in range(IMAGES)]
    carry, done = (zero, zero), 0
    for i, now in enumerate(whole):
        conv(i, 0)
        from_padded(H2, (i,))
        carry = lax.fori_loop(done, now, sum_second, carry)
        start_all(1, h2s, h2r, min(done, early), min(now, early))
        done = now
    s, q = carry
    ar_start(1, pack2(fold1(s), fold1(q)), "all")
    start_all(1, h2s, h2r, early, OWN)
    s, q = unpack2(ar_finish(1, "all", 4))
    avg2 = s * inv_n2
    scale2 = lax.rsqrt(q * inv_n2 - avg2 * avg2 + EPS)
    a2_gain = g2 * scale2
    a2_shift = b2 - avg2 * a2_gain

    arrived(W3.at[near], w_recv.at[10])
    arrived(W3.at[(1 - hi) * 2 + 1 - lo], w_recv.at[11])

    def act_second(t, h, carry):
        s, q = carry
        v = spread(V[t], 256)
        aff = v * (h * a2_gain + a2_shift)
        sig = logistic(aff)
        act = aff * sig
        D2[t] = v * (sig + act * (1.0 - sig))
        act = act.astype(BF16)
        A2[t] = act
        h3 = mm(act, W3[...].reshape(256, 512))
        H3[t] = h3
        return s + fold8(h3), q + fold8(h3 * h3)

    def own_second(t, carry):
        return act_second(t, H2[pl.ds(pl.multiple_of(t * ROWS, 16), ROWS), :], carry)

    def other_second(t, carry):
        xcopy(1, h2s, h2r, t).wait_recv()
        return act_second(t + OWN, h2r[t].astype(F32), carry)

    wide_zero = jnp.zeros((8, 512), F32)
    carry = lax.fori_loop(0, OWN, own_second, (wide_zero, wide_zero))
    for cp in h1x:
        cp.start()
    s, q = lax.fori_loop(0, OWN, other_second, carry)
    ar_start(2, pack3(fold1(s), fold1(q)), "half")
    for cp in c_load:
        cp.wait()
    for cp in cx:
        cp.wait_recv()
    s, q = unpack3(ar_finish(2, "half", 8))
    avg3 = s * inv_n
    scale3 = lax.rsqrt(q * inv_n - avg3 * avg3 + EPS)
    a3_gain = g3 * scale3
    a3_shift = b3 - avg3 * a3_gain

    def last(t, carry):
        s, q = carry
        v = spread(V[t], 512)
        h3 = H3[t]
        wide = jnp.concatenate([F[0, t], F[1, t]], axis=1).astype(F32)
        total = v * (h3 * a3_gain + a3_shift) + wide
        sig = logistic(total)
        out = total * sig
        RES[0, t] = out[:, 0:256].astype(BF16)
        RES[1, t] = out[:, 256:512].astype(BF16)
        given = jnp.concatenate([C[0, t], C[1, t]], axis=1).astype(F32)
        gs = given * (sig + out * (1.0 - sig))
        GS[t] = gs
        vg = v * gs
        return s + fold8(vg), q + fold8(vg * (h3 - avg3))

    s, q = lax.fori_loop(0, BOTH, last, (wide_zero, wide_zero))
    ar_start(3, pack3(fold1(s), fold1(q * scale3)), "half")
    parts = ((0, part0), (1, part1))
    res_here = [
        local(RES.at[lo, pl.ds(OWN * s, OWN)], res_out.at[pl.ds(mine + part, OWN)], out_sem.at[s]) for s, part in parts
    ]
    res_there = [
        remote(RES.at[1 - lo, pl.ds(OWN * s, OWN)], res_out.at[pl.ds(mine + part, OWN)], o_send.at[s], o_recv.at[s], beside)
        for s, part in parts
    ]
    shift3, gain3 = unpack3(ar_finish(3, "half", 8))
    for cp in res_here + res_there:
        cp.start()
    k3_h = -a3_gain * gain3 * scale3 * inv_n
    k3_0 = -a3_gain * shift3 * inv_n - k3_h * avg3

    def back_third(t, carry):
        s, q, h2 = carry[0], carry[1], carry[2]
        v = spread(V[t], 512)
        g = (v * (a3_gain * GS[t] + k3_h * H3[t] + k3_0)).astype(BF16)
        G3[t] = g
        e = mm_nt(g, W3[...].reshape(256, 512)) * D2[t]
        return e, s + fold8(e), q + fold8(e * (h2 - avg2))

    def other_third(t, carry):
        e, s, q = back_third(t + OWN, (carry[0], carry[1], h2r[t].astype(F32)))
        e2s[t] = e.astype(BF16)

        @pl.when(t < 4)
        def _():
            xcopy(2, e2s, e2r, t).start()

        return s, q

    def own_third(t, carry):
        e, s, q = back_third(t, (carry[0], carry[1], H2[pl.ds(pl.multiple_of(t * ROWS, 16), ROWS), :]))
        E2[t] = e
        return s, q

    carry = lax.fori_loop(0, OWN, other_third, (zero, zero))
    s, q = lax.fori_loop(0, OWN, own_third, carry)
    ar_start(4, pack2(fold1(s), fold1(q * scale2)), "all")
    start_all(2, e2s, e2r, 4, OWN)

    piece = 16
    n_sub = 4

    def pair_copies(k):
        return [remote(wp.at[k, h], wc.at[k, h], g_send.at[k, h], g_recv.at[k, h], beside) for h in range(2)]

    def pair_start(k):
        for h in range(2):
            wp[k, h] = acc_w[k, h, 1 - lo].astype(BF16)
        for cp in pair_copies(k):
            cp.start()

    def pair_add(k):
        for h, cp in enumerate(pair_copies(k)):
            cp.wait_recv()
            both = (acc_w[k, h, lo] + wc[k, h].astype(F32)).reshape(n_sub, piece, 512)
            wa[k, h] = both
            wb[k, h] = both.astype(BF16)
        for cp in spread_copies(k):
            cp.start()

    def spread_copies(k):
        copies = []
        for t in range(1, n_lo):
            q = lax.rem(g_lo + t, n_lo)
            copies.append(
                remote(
                    wb.at[k, lax.rem(q, 2), q // 2],
                    wr.at[k, g_lo],
                    g_send.at[k, 2 + t],
                    g_recv.at[k, 2 + t],
                    (g_hi * n_lo + q, me_c),
                )
            )
        return copies

    def over_groups(total, level, sems):
        if n_hi == 1:
            return total
        level[g_hi] = total.astype(BF16)

        def swap(t):
            q = lax.rem(g_hi + t, n_hi)
            return remote(
                level.at[g_hi], level.at[g_hi], sems[0].at[t], sems[1].at[t], (q * n_lo + g_lo, me_c)
            )

        for t in range(1, n_hi):
            swap(t).start()
        for t in range(1, n_hi):
            swap(t).wait()
        total = level[0].astype(F32)
        for t in range(1, n_hi):
            total = total + level[t].astype(F32)
        return total

    def spread_add(k):
        for cp in spread_copies(k):
            cp.wait_recv()
        total = wa[k, lax.rem(g_lo, 2), g_lo // 2]
        for t in range(1, n_lo):
            total = total + wr[k, lax.rem(g_lo + t, n_lo)].astype(F32)
        return over_groups(total, wh.at[k], (h_send.at[k], h_recv.at[k]))

    def give_copies(k):
        copies = []
        for t in range(n_lo):
            q = lax.rem(g_lo + t, n_lo)
            copies.append(
                remote(
                    wf.at[k],
                    wfin.at[k, hi, own_sub],
                    g_send.at[k, 10 + t],
                    g_recv.at[k, 10 + 8 * hi + t],
                    (g_hi * n_lo + q, owner_hi * 2 + lo),
                )
            )
        return copies

    owner_hi = lax.rem(g_lo, 2)
    own_sub = g_lo // 2
    keeps = owner_hi == hi

    def wide_give(k):
        wf[k] = spread_add(k).astype(BF16)
        for t, cp in enumerate(give_copies(k)):
            if t == 0:

                @pl.when(jnp.logical_not(keeps))
                def _():
                    cp.start()

                @pl.when(keeps)
                def _():
                    wfin[k, hi, own_sub] = wf[k]

            else:
                cp.start()

    e_spot = wfin.at[0, hi, own_sub]
    e_cross = remote(wf.at[0], e_spot, g_send.at[0, 10], g_recv.at[0, 10], across)

    def e_share(h, at):
        spot = wfin.at[0, h, own_sub]
        return [
            remote(
                spot, spot, g_send.at[0, at + t], g_recv.at[0, at + t], (g_hi * n_lo + lax.rem(g_lo + t, n_lo), me_c)
            )
            for t in range(1, n_lo)
        ]

    def e_first():
        wf[0] = spread_add(0).astype(BF16)

        @pl.when(jnp.logical_not(keeps))
        def _():
            e_cross.start()

        @pl.when(keeps)
        def _():
            wfin[0, hi, own_sub] = wf[0]
            for cp in e_share(hi, 10):
                cp.start()

    def e_second():
        @pl.when(keeps)
        def _():
            arrived(wfin.at[0, 1 - hi, own_sub], g_recv.at[0, 10])
            for cp in e_share(1 - hi, 17):
                cp.start()

    def e_take(out):
        for sub in range(n_sub):
            q = sub * 2 + hi
            t = lax.rem(g_lo - q + n_lo, n_lo)

            @pl.when(q != g_lo)
            def _():
                arrived(wfin.at[0, hi, sub], g_recv.at[0, 10 + t])
                arrived(wfin.at[0, 1 - hi, sub], g_recv.at[0, 17 + t])

        for h in range(2):
            out[:, 512 * h : 512 * (h + 1)] = wfin[0, h].astype(F32).reshape(64, 512)

    def e_close():
        for cp in pair_copies(0) + spread_copies(0):
            cp.wait_send()

        @pl.when(jnp.logical_not(keeps))
        def _():
            e_cross.wait_send()

        @pl.when(keeps)
        def _():
            for cp in e_share(hi, 10) + e_share(1 - hi, 17):
                cp.wait_send()

    def wide_take(k, out):
        for sub in range(n_sub):
            q = sub * 2 + hi
            t = lax.rem(g_lo - q + n_lo, n_lo)
            for h in range(2):

                @pl.when(jnp.logical_not((q == g_lo) & (hi == h)))
                def _():
                    arrived(wfin.at[k, h, sub], g_recv.at[k, 10 + 8 * h + t])

        for h in range(2):
            out[:, 512 * h : 512 * (h + 1)] = wfin[k, h].astype(F32).reshape(64, 512)

    def wide_close(k):
        for cp in pair_copies(k) + spread_copies(k):
            cp.wait_send()
        for t, cp in enumerate(give_copies(k)):
            if t == 0:

                @pl.when(jnp.logical_not(keeps))
                def _():
                    cp.wait_send()

            else:
                cp.wait_send()

    def half_of(ref, part):
        return ref[OWN * part : OWN * (part + 1)].reshape(OWN * ROWS, ref.shape[2])

    acc_w[0] = (mm_tn(half_of(A2, 0), half_of(G3, 0)) + mm_tn(half_of(A2, 1), half_of(G3, 1))).reshape(2, 2, 64, 512)
    pair_start(0)
    pair_add(0)

    shift2, gain2 = unpack2(ar_finish(4, "all", 4))
    k2_h = -a2_gain * gain2 * scale2 * inv_n2
    k2_0 = -a2_gain * shift2 * inv_n2 - k2_h * avg2

    def back_second(t, carry):
        xcopy(2, e2s, e2r, t).wait_recv()
        at = pl.ds(pl.multiple_of(t * ROWS, 16), ROWS)
        e = E2[t] + e2r[t].astype(F32)
        comp[at, :] = spread(V[t], 256) * (a2_gain * e + k2_h * H2[at, :] + k2_0)
        return carry

    lax.fori_loop(0, OWN, back_second, 0)
    e_first()
    to_padded()
    for i in range(IMAGES):
        for c in range(3):
            at = EDGE + i * BLOCK - (c - 1)
            Q[c, i * BLOCK : (i + 1) * BLOCK, :] = P0[at : at + BLOCK, :].astype(BF16)

    def conv_back(i, carry):
        total = None
        for r in range(3):
            at = pl.ds(pl.multiple_of(i * BLOCK + PAD * (2 - r), 16), SIDE * PAD)
            for c in range(3):
                w = W2T[:, 3 * r + c].reshape(256, 256)
                part = mm(Q[c, at, :], w)
                total = part if total is None else total + part
        padded[pl.ds(pl.multiple_of(i * SIDE * PAD, 16), SIDE * PAD), :] = total
        return carry

    def sum_back_first(t, carry):
        s, q = carry
        e = comp[pl.ds(pl.multiple_of(t * ROWS, 16), ROWS), :] * D1[t]
        E1[t] = e
        e1s[t] = e.astype(BF16)
        return s + fold8(e), q + fold8(e * (H1[t] - avg1))

    carry, done = (zero, zero), 0
    for i, now in enumerate(whole):
        conv_back(i, 0)
        from_padded(comp, (i,))
        carry = lax.fori_loop(done, now, sum_back_first, carry)
        start_all(3, e1s, e1r, min(done, early), min(now, early))
        done = now
    s, q = carry
    ar_start(5, pack2(fold1(s), fold1(q * scale1)), "all")
    start_all(3, e1s, e1r, early, OWN)

    bit, quad = lax.rem(g_lo, 2), g_lo // 2
    next_group = (g_hi * n_lo + quad * 2 + 1 - bit, me_c)
    s_owner = lax.rem(quad, 2) == hi

    def s_pair(r):
        return [
            remote(sp.at[r, h], sc.at[r, h], s_send.at[r, h], s_recv.at[r, h], beside) for h in range(2)
        ]

    def s_make(r):
        taps = mm(QT[...], PC[PAD * r : PAD * r + FLAT, :])
        acc_s[r] = taps.reshape(2, 2, 64, 768)
        for h in range(2):
            sp[r, h] = acc_s[r, h, 1 - lo].astype(BF16)
        for cp in s_pair(r):
            cp.start()

    def s_pair_add(r):
        for h, cp in enumerate(s_pair(r)):
            cp.wait_recv()
            s1[r, h] = (acc_s[r, h, lo] + sc[r, h].astype(F32)).reshape(2, 32, 768)

    def group_at(q):
        return (g_hi * n_lo + q * 2 + bit, me_c)

    y_next = remote(ys, yr, s_send.at[0, 2], s_recv.at[0, 2], next_group)
    y_cross = remote(xs, xr, s_send.at[0, 6], s_recv.at[0, 6], across)

    def y_quad():
        copies = []
        for t in range(1, 4):
            q = lax.rem(quad + t, 4)
            copies.append(
                remote(zs.at[lax.rem(q, 2), q // 2], zr.at[t - 1], s_send.at[0, 2 + t], s_recv.at[0, 2 + t], group_at(q))
            )
        return copies

    def y_give():
        copies = []
        spot = sfin.at[bit, quad // 2]
        for t in range(1, 4):
            to = group_at(lax.rem(quad + t, 4))
            copies.append(remote(spot, spot, s_send.at[0, 6 + t], s_recv.at[0, 7 + quad // 2], to))
        return copies

    y_back = remote(sfin.at[bit], sfin.at[bit], s_send.at[0, 10], s_recv.at[0, 10], next_group)

    def y_start():
        for h in range(2):
            zs[h] = s1[0, h].astype(BF16)
        for cp in y_quad():
            cp.start()

    def y_quad_add():
        for cp in y_quad():
            cp.wait_recv()
        total = s1[0, lax.rem(quad, 2), quad // 2]
        for t in range(3):
            total = total + zr[t].astype(F32)
        s2[...] = total.reshape(2, 16, 768)
        ys[...] = s2[1 - bit].astype(BF16)
        y_next.start()

    def y_next_add():
        y_next.wait_recv()
        total = s2[bit] + yr[...].astype(F32)
        s3[...] = total
        xs[...] = total.astype(BF16)

        @pl.when(jnp.logical_not(s_owner))
        def _():
            y_cross.start()

    def y_cross_add():
        @pl.when(s_owner)
        def _():
            y_cross.wait_recv()
            total = s3[...] + xr[...].astype(F32)
            sfin[bit, quad // 2] = over_groups(total, sh, (h_send.at[2], h_recv.at[2])).astype(BF16)
            for cp in y_give():
                cp.start()

    def y_give_back():
        for part in range(2):

            @pl.when(quad != 2 * part + hi)
            def _():
                arrived(sfin.at[bit, part], s_recv.at[0, 7 + part])

        y_back.start()

    def y_take():
        arrived(sfin.at[1 - bit], s_recv.at[0, 10])
        for b in range(2):
            for h in range(2):
                rows = sfin[b, h].astype(F32)
                for c in range(3):
                    sg_out[c, 32 * h + 16 * b : 32 * h + 16 * (b + 1), :] = rows[:, 256 * c : 256 * (c + 1)]

    def y_close():
        for cp in s_pair(0) + [y_next] + y_quad() + [y_back]:
            cp.wait_send()

        @pl.when(s_owner)
        def _():
            for cp in y_give():
                cp.wait_send()

        @pl.when(jnp.logical_not(s_owner))
        def _():
            y_cross.wait_send()

    def x_cross(r):
        return remote(yb.at[r], yc.at[r], s_send.at[r, 6], s_recv.at[r, 6], across)

    def x_next(r):
        return remote(xb.at[r], xc.at[r], s_send.at[r, 2], s_recv.at[r, 2], next_group)

    def x_quad(r):
        copies = []
        for t in range(1, 4):
            q = lax.rem(quad + t, 4)
            copies.append(
                remote(
                    zb.at[r, q // 2, lax.rem(q, 2)], zc.at[r, t - 1], s_send.at[r, 2 + t], s_recv.at[r, 2 + t], group_at(q)
                )
            )
        return copies

    def x_give(r):
        copies = []
        spot = tfin.at[r, bit, quad // 2, lax.rem(quad, 2)]
        for t in range(1, 4):
            to = group_at(lax.rem(quad + t, 4))
            copies.append(remote(spot, spot, s_send.at[r, 6 + t], s_recv.at[r, 6 + t], to))
        return copies

    def x_back(r):
        return remote(tfin.at[r, bit], tfin.at[r, bit], s_send.at[r, 10], s_recv.at[r, 10], next_group)

    def x_start(r):
        for h in range(2):
            xb[r, h] = s1[r, h, 1 - bit].astype(BF16)
        x_next(r).start()

    def x_next_add(r):
        x_next(r).wait_recv()
        for h in range(2):
            t1[r, h] = s1[r, h, bit] + xc[r, h].astype(F32)
        yb[r] = t1[r, 1 - hi].astype(BF16)
        x_cross(r).start()

    def x_cross_add(r):
        x_cross(r).wait_recv()
        total = t1[r, hi] + yc[r].astype(F32)
        for h in range(2):
            for w in range(2):
                part = total[16 * h : 16 * (h + 1), 384 * w : 384 * (w + 1)]
                t2[r, h, w] = part
                zb[r, h, w] = part.astype(BF16)
        for cp in x_quad(r):
            cp.start()

    def x_quad_add(r):
        for cp in x_quad(r):
            cp.wait_recv()
        total = t2[r, quad // 2, lax.rem(quad, 2)]
        for t in range(3):
            total = total + zc[r, t].astype(F32)
        total = over_groups(total, th.at[r], (h_send.at[2 + r], h_recv.at[2 + r]))
        tfin[r, bit, quad // 2, lax.rem(quad, 2)] = total.astype(BF16)
        for cp in x_give(r):
            cp.start()

    def x_give_back(r):
        for cp in x_give(r):
            cp.wait_recv()
        x_back(r).start()

    def x_take(r):
        arrived(tfin.at[r, 1 - bit], s_recv.at[r, 10])
        halves = [tfin[r, :, :, w].astype(F32).reshape(64, 384) for w in range(2)]
        sg_out[3 * r] = halves[0][:, 0:256]
        sg_out[3 * r + 1] = jnp.concatenate([halves[0][:, 256:384], halves[1][:, 0:128]], axis=1)
        sg_out[3 * r + 2] = halves[1][:, 128:384]

    def x_close(r):
        for cp in s_pair(r) + [x_cross(r), x_next(r)] + x_quad(r) + x_give(r) + [x_back(r)]:
            cp.wait_send()

    for i in range(IMAGES):
        QT[:, i * BLOCK : (i + 1) * BLOCK] = P0[EDGE + i * BLOCK : EDGE + (i + 1) * BLOCK, :].T.astype(BF16)
    s_make(0)
    s_make(1)
    s_pair_add(0)
    y_start()
    s_make(2)
    s_pair_add(1)
    x_start(1)
    s_pair_add(2)
    x_start(2)
    e_second()

    shift1, gain1 = unpack2(ar_finish(5, "all", 4))
    k1_h = -a1_gain * gain1 * scale1 * inv_n2
    k1_0 = -a1_gain * shift1 * inv_n2 - k1_h * avg1

    def back_first(t, e, h):
        g = (spread(V[t], 256) * (a1_gain * e + k1_h * h + k1_0)).astype(BF16)
        G1[t] = g
        out = (mm(g, W1T[...].reshape(256, 512)) + GS[t]).astype(BF16)
        RES[0, t] = out[:, 0:256]
        RES[1, t] = out[:, 256:512]

    ig_here = [
        local(RES.at[lo, pl.ds(OWN * s, OWN)], ig_out.at[pl.ds(mine + part, OWN)], out_sem.at[2 + s])
        for s, part in parts
    ]
    ig_there = [
        remote(
            RES.at[1 - lo, pl.ds(OWN * s, OWN)], ig_out.at[pl.ds(mine + part, OWN)], o_send.at[2 + s], o_recv.at[2 + s], beside
        )
        for s, part in parts
    ]
    for cp in res_here:
        cp.wait()
    for cp in res_there:
        cp.wait_send()

    def own_back_first(t, carry):
        back_first(t, E1[t], H1[t])
        return carry

    lax.fori_loop(0, OWN, own_back_first, 0)
    ig_here[0].start()
    ig_there[0].start()

    def features_of(part):
        return jnp.concatenate([half_of(F.at[0], part), half_of(F.at[1], part)], axis=1)

    own_reduce = mm_tn(half_of(G1, 0), features_of(0))
    acc_w[1] = own_reduce.reshape(2, 2, 64, 512)
    for cp in h1x:
        cp.wait_recv()

    def other_back_first(t, carry):
        xcopy(3, e1s, e1r, t).wait_recv()
        back_first(t + OWN, e1r[t].astype(F32), h1o[t].astype(F32))
        return carry

    lax.fori_loop(0, OWN, other_back_first, 0)
    acc_w[1] += mm_tn(half_of(G1, 1), features_of(1)).reshape(2, 2, 64, 512)
    pair_start(1)
    ig_here[1].start()
    ig_there[1].start()
    x_next_add(1)
    x_next_add(2)
    pair_add(1)
    y_quad_add()
    x_cross_add(1)
    y_next_add()
    x_cross_add(2)
    x_quad_add(1)
    y_cross_add()
    wide_give(1)
    x_quad_add(2)
    x_give_back(1)
    y_give_back()
    x_give_back(2)

    def own64(v):
        half = jnp.where(hi == 0, v[:, 0:128], v[:, 128:256])
        swapped = jnp.concatenate([half[:, 64:128], half[:, 0:64]], axis=1)
        return jnp.concatenate([jnp.where(lo == 0, half, swapped), jnp.zeros((1, 128), F32)], axis=1)

    def own256(v):
        return jnp.where(lo == 0, v[:, 0:256], v[:, 256:512])

    st_out[...] = jnp.concatenate(
        [
            own64(gain1),
            own64(shift1),
            own64(gain2),
            own64(shift2),
            own256(gain3),
            own256(shift3),
            jnp.zeros((2, 256), F32),
        ],
        axis=0,
    )

    e_take(eg_out)
    x_take(1)
    y_take()
    wide_take(1, rg_out)
    x_take(2)

    e_close()
    wide_close(1)
    y_close()
    x_close(1)
    x_close(2)
    for cp in ig_here:
        cp.wait()
    for cp in ig_there:
        cp.wait()
    for cp in res_there:
        cp.wait_recv()
    for cp in fx + cx + w1x + pkx + w2x + w3x + shared + h1x:
        cp.wait_send()
    for kind, src, dst in ((0, h1s.at[hi], h1r.at[hi]), (5, h1s.at[1 - hi], h1r.at[1 - hi]), (1, h2s, h2r), (2, e2s, e2r), (3, e1s, e1r)):
        for t in range(OWN):
            xcopy(kind, src, dst, t).wait_send()
    for k, kind, rows in (
        (0, "all", 4),
        (1, "all", 4),
        (2, "half", 8),
        (3, "half", 8),
        (4, "all", 4),
        (5, "all", 4),
        (6, "pix", 8),
    ):
        ar_close(k, kind, rows)


def block(n_pix, n_ch, *args):
    feat, cot, mask, w1, w2, w3 = args[:6]
    rows, lanes = feat.shape
    n_lo, n_sub, piece = 8, 4, 16
    n_hi = n_pix // n_lo
    chunks = rows // ROWS
    any_space = pl.BlockSpec(memory_space=pl.ANY)
    vmem = pl.BlockSpec(memory_space=pltpu.VMEM)
    V = pltpu.VMEM
    DMA = pltpu.SemaphoreType.DMA
    scratch = [
        V((rows,), jnp.int32),
        *[V((64,), BF16)] * 4,
        *[V((256,), BF16)] * 2,
        V((2, BOTH, ROWS, 256), BF16),
        V((2, BOTH, ROWS, 256), BF16),
        V((BOTH, ROWS, 128), F32),
        V((4, 64, 512), BF16),
        V((4, 9, 64, 256), BF16),
        V((4, 64, 512), BF16),
        V((4, 8, 256), F32),
        V((7, 8, 128), F32),
        V((7, n_pix * n_ch, 8, 128), F32),
        V((2, OWN, ROWS, 128), BF16),
        V((2, OWN, ROWS, 128), BF16),
        V((OWN, ROWS, 256), F32),
        V((OWN, ROWS, 256), BF16),
        V((OWN, ROWS, 256), BF16),
        V((OWN, ROWS, 256), F32),
        V((OWN * ROWS, 256), F32),
        V((FLAT + 2 * EDGE, 256), F32),
        V((FLAT + 2 * PAD, 768), BF16),
        V((3, FLAT, 256), BF16),
        V((IMAGES * SIDE * PAD, 256), F32),
        V((OWN * ROWS, 256), F32),
        V((OWN, ROWS, 256), BF16),
        V((OWN, ROWS, 256), BF16),
        V((BOTH, ROWS, 256), BF16),
        V((BOTH, ROWS, 256), F32),
        V((BOTH, ROWS, 512), F32),
        V((BOTH, ROWS, 512), F32),
        V((2, BOTH, ROWS, 256), BF16),
        V((BOTH, ROWS, 512), BF16),
        V((OWN, ROWS, 256), F32),
        V((OWN, ROWS, 256), BF16),
        V((OWN, ROWS, 256), BF16),
        V((OWN, ROWS, 256), F32),
        V((OWN, ROWS, 256), BF16),
        V((OWN, ROWS, 256), BF16),
        V((BOTH, ROWS, 256), BF16),
        V((256, FLAT), BF16),
        V((chunks, ROWS), F32),
        V((2, 2, 2, 64, 512), F32),
        V((2, 2, 64, 512), BF16),
        V((2, 2, 64, 512), BF16),
        V((2, 2, n_sub, piece, 512), F32),
        V((2, 2, n_sub, piece, 512), BF16),
        V((2, n_lo, piece, 512), BF16),
        V((2, n_hi, piece, 512), BF16),
        V((2, piece, 512), BF16),
        V((2, 2, n_sub, piece, 512), BF16),
        V((3, 2, 2, 64, 768), F32),
        V((3, 2, 64, 768), BF16),
        V((3, 2, 64, 768), BF16),
        V((3, 2, 2, 32, 768), F32),
        V((16, 768), BF16),
        V((16, 768), BF16),
        V((2, 16, 768), F32),
        V((2, 2, 32, 768), BF16),
        V((3, 32, 768), BF16),
        V((16, 768), F32),
        V((16, 768), BF16),
        V((16, 768), BF16),
        V((n_hi, 16, 768), BF16),
        V((2, 2, 16, 768), BF16),
        V((3, 2, 32, 768), F32),
        V((3, 2, 32, 768), BF16),
        V((3, 2, 32, 768), BF16),
        V((3, 32, 768), BF16),
        V((3, 32, 768), BF16),
        V((3, 2, 2, 16, 384), F32),
        V((3, 2, 2, 16, 384), BF16),
        V((3, 3, 16, 384), BF16),
        V((3, n_hi, 16, 384), BF16),
        V((3, 2, 2, 2, 16, 384), BF16),
        DMA((14,)),
        DMA((4,)),
        DMA((4,)),
        DMA((28,)),
        DMA((28,)),
        DMA((7,)),
        DMA((7,)),
        DMA((6, OWN)),
        DMA((6, OWN)),
        DMA((4,)),
        DMA((4,)),
        DMA((4,)),
        DMA((2, 26)),
        DMA((2, 26)),
        DMA((3, 12)),
        DMA((3, 12)),
        DMA((5, n_hi)),
        DMA((5, n_hi)),
    ]
    wide = V((chunks, ROWS, lanes), BF16)
    made = pl.pallas_call(
        functools.partial(kernel, n_pix, n_ch),
        out_shape=(
            wide,
            wide,
            V((64, 1024), F32),
            V((9, 64, 256), F32),
            V((64, 1024), F32),
            V((8, 256), F32),
        ),
        in_specs=[any_space] * 12,
        out_specs=(any_space, any_space, vmem, vmem, vmem, vmem),
        scratch_shapes=scratch,
        compiler_params=pltpu.CompilerParams(
            collective_id=0, has_side_effects=True, vmem_limit_bytes=56 * 2**20
        ),
        name="bottleneck",
    )(
        feat.reshape(chunks, ROWS, lanes),
        cot.reshape(chunks, ROWS, lanes),
        mask,
        w1.T,
        w2.transpose(0, 1, 3, 2).reshape(9, 64, 256),
        w3,
        *args[6:],
    )
    narrow = jax.ShapeDtypeStruct((64,), F32)
    broad = jax.ShapeDtypeStruct((256,), F32)
    return pl.pallas_call(
        finish,
        out_shape=tuple(jax.ShapeDtypeStruct(v.shape, v.dtype) for v in made[:5]) + (narrow,) * 4 + (broad,) * 2,
        in_specs=[any_space] * 5 + [vmem],
        out_specs=(any_space,) * 5 + (vmem,) * 6,
        scratch_shapes=[DMA((20,))],
        compiler_params=pltpu.CompilerParams(vmem_limit_bytes=2**20),
        name="outputs",
    )(*[pltpu.with_memory_space_constraint(v, pltpu.VMEM) for v in made])


def finish(*refs):
    made, stats, outs, small, sems = refs[:5], refs[5], refs[6:11], refs[11:17], refs[17]
    copies = []
    for a, b in zip(made, outs):
        parts = 4 if a.shape[0] % 4 == 0 else 3
        rows = a.shape[0] // parts
        for k in range(parts):
            at = pl.ds(k * rows, rows)
            copies.append(pltpu.make_async_copy(a.at[at], b.at[at], sems.at[len(copies)]))
    for cp in copies:
        cp.start()
    for i, out in enumerate(small):
        out[...] = stats[i : i + 1, 0 : out.shape[0]].reshape(out.shape)
    for cp in copies:
        cp.wait()


def solution(mesh):
    n_pix, n_ch = mesh.shape["pix"], mesh.shape["ch"]

    def body(feat, mask, w1, w2, w3, g1, b1, g2, b2, g3, b3, cot):
        made = block(n_pix, n_ch, feat, cot, mask, w1, w2, w3, g1, b1, g2, b2, g3, b3)
        res, ig, rg, sg, eg = made[:5]
        return (
            res.reshape(feat.shape),
            ig.reshape(feat.shape),
            rg.T,
            sg.reshape(3, 3, 64, 256).transpose(0, 1, 3, 2),
            eg,
        ) + tuple(made[5:])

    wide = P("pix", "ch")
    return jax.shard_map(
        body,
        mesh=mesh,
        in_specs=(wide, P("pix"), P(None, "ch"), P(None, None, None, "ch"), P("ch", None)) + (P("ch"),) * 6 + (wide,),
        out_specs=(wide, wide, P(None, "ch"), P(None, None, None, "ch"), P("ch", None)) + (P("ch"),) * 6,
        check_vma=False,
    )
```

```python
import functools

import jax
import jax.numpy as jnp
from jax import lax
from jax.experimental import pallas as pl
from jax.experimental.pallas import tpu as pltpu
from jax.sharding import PartitionSpec as P

SIDE = 14
EPS = 1e-05
MESH = pl.DeviceIdType.MESH
F32 = jnp.float32
BF16 = jnp.bfloat16

ROWS = 112
OWN = 7
BOTH = 14
IMAGES = 4
PAD = 16
FLAT = IMAGES * PAD * PAD
EDGE = 8
BLOCK = PAD * PAD


def mm(a, b):
    return jnp.dot(a, b, preferred_element_type=F32)


def mm_nt(a, b):
    return lax.dot_general(a, b, (((1,), (1,)), ((), ())), preferred_element_type=F32)


def mm_tn(a, b):
    return lax.dot_general(a, b, (((0,), (0,)), ((), ())), preferred_element_type=F32)


def logistic(v):
    return 0.5 * jnp.tanh(0.5 * v) + 0.5


def fold8(v):
    return jnp.sum(v.reshape(v.shape[0] // 8, 8, v.shape[1]), axis=0)


def fold1(v):
    return jnp.sum(v, axis=0, keepdims=True)


def spread(v, lanes):
    return jnp.concatenate([v] * (lanes // 128), axis=1)


def kernel(
    n_pix,
    n_ch,
    feat,
    cot,
    mask,
    w1_in,
    w2_in,
    w3_in,
    g1_in,
    b1_in,
    g2_in,
    b2_in,
    g3_in,
    b3_in,
    res_out,
    ig_out,
    rg_out,
    sg_out,
    eg_out,
    st_out,
    mask_v,
    g1_v,
    b1_v,
    g2_v,
    b2_v,
    g3_v,
    b3_v,
    F,
    C,
    V,
    W1T,
    W2T,
    W3,
    W3X,
    pk,
    sbuf,
    rbuf,
    h1s,
    h1r,
    H1,
    h1b,
    h1o,
    D1,
    comp,
    P0,
    PC,
    Q,
    padded,
    H2,
    h2s,
    h2r,
    A2,
    D2,
    D2b,
    D2h,
    H3,
    GS,
    RES,
    G3,
    kb,
    kr,
    E2,
    e2s,
    e2r,
    E1,
    e1s,
    e1r,
    G1,
    QT,
    rows28,
    acc_w,
    wp,
    wc,
    wa,
    wb,
    wr,
    wq,
    wu,
    wh,
    wf,
    wfin,
    acc_s,
    sp,
    sc,
    s1,
    sb,
    sr,
    st,
    sz,
    sq,
    sx,
    sh,
    sfin,
    ld_sem,
    fx_send,
    fx_recv,
    w_send,
    w_recv,
    ar_send,
    ar_recv,
    x_send,
    x_recv,
    o_send,
    o_recv,
    g_send,
    g_recv,
    s_send,
    s_recv,
    h_send,
    h_recv,
):
    me_p, me_c = lax.axis_index("pix"), lax.axis_index("ch")
    hi, lo = me_c // 2, lax.rem(me_c, 2)
    n_lo = 8
    n_hi = n_pix // n_lo
    g_hi, g_lo = me_p // n_lo, lax.rem(me_p, n_lo)
    across = (me_p, (1 - hi) * 2 + lo)
    beside = (me_p, hi * 2 + 1 - lo)
    n_all = n_pix * n_ch

    def remote(src, dst, send, recv, device):
        return pltpu.make_async_remote_copy(
            src_ref=src, dst_ref=dst, send_sem=send, recv_sem=recv, device_id=device, device_id_type=MESH
        )

    def local(src, dst, sem):
        return pltpu.make_async_copy(src, dst, sem)

    mine, theirs = lo * BOTH, (1 - lo) * BOTH
    part0, part1 = hi * OWN, (1 - hi) * OWN

    def columns(ref, h):
        return ref.at[:, pl.ds(pl.multiple_of(h * 512, 512), 512)]

    def arrived(dst, sem):
        local(dst, dst, sem).wait()

    w1_load = local(columns(w1_in, hi), W1T.at[me_c], ld_sem.at[0])
    w2_load = local(w2_in, W2T.at[me_c], ld_sem.at[1])
    halves = ((0, part0), (1, part1))
    f_load = [
        local(feat.at[pl.ds(mine + part, OWN)], F.at[lo, pl.ds(OWN * s, OWN)], ld_sem.at[2 + s]) for s, part in halves
    ]
    c_load = [
        local(cot.at[pl.ds(mine + part, OWN)], C.at[lo, pl.ds(OWN * s, OWN)], ld_sem.at[4]) for s, part in halves
    ]
    w3_load = [
        local(columns(w3_in, hi), W3.at[me_c], ld_sem.at[5]),
        local(columns(w3_in, 1 - hi), W3X.at[me_c], ld_sem.at[5]),
    ]
    small_load = [local(mask, mask_v, ld_sem.at[6])]
    pairs = ((g1_in, g1_v), (b1_in, b1_v), (g2_in, g2_v), (b2_in, b2_v), (g3_in, g3_v), (b3_in, b3_v))
    small_load += [local(a, b, ld_sem.at[7 + i]) for i, (a, b) in enumerate(pairs)]

    barrier = pltpu.get_barrier_semaphore()

    def greet(t, carry):
        q = lax.rem(me_p * n_ch + me_c + t, n_all)
        pl.semaphore_signal(barrier, inc=1, device_id=(q // n_ch, lax.rem(q, n_ch)), device_id_type=MESH)
        return carry

    lax.fori_loop(1, n_all, greet, 0)
    for cp in small_load:
        cp.start()
    w1_load.start()
    f_load[1].start()
    f_load[0].start()
    w2_load.start()
    for cp in w3_load + c_load:
        cp.start()

    pl.semaphore_wait(barrier, n_all - 1)

    fx = [
        remote(feat.at[pl.ds(theirs + part, OWN)], F.at[lo, pl.ds(OWN * s, OWN)], fx_send.at[0], fx_recv.at[s], beside)
        for s, part in halves
    ]
    cx = [
        remote(cot.at[pl.ds(theirs + part, OWN)], C.at[lo, pl.ds(OWN * s, OWN)], fx_send.at[1], fx_recv.at[2], beside)
        for s, part in halves
    ]
    far, near, last_one = (1 - hi) * 2 + lo, hi * 2 + 1 - lo, (1 - hi) * 2 + 1 - lo

    quad, top = lax.rem(g_lo, 4), g_lo // 4
    low, high = lax.rem(quad, 2), quad // 2
    next_group = (g_hi * n_lo + top * 4 + high * 2 + 1 - low, me_c)

    w1x = [
        remote(columns(w1_in, 1 - hi), W1T.at[me_c], w_send.at[0], w_recv.at[1], across),
        remote(columns(w1_in, hi), W1T.at[me_c], w_send.at[0], w_recv.at[0], beside),
        remote(W1T.at[far], W1T.at[far], w_send.at[0], w_recv.at[3], beside),
    ]
    pkx = [
        remote(pk.at[me_c], pk.at[me_c], w_send.at[5], w_recv.at[4], across),
        remote(pk.at[me_c], pk.at[me_c], w_send.at[5], w_recv.at[5], beside),
        remote(pk.at[far], pk.at[far], w_send.at[5], w_recv.at[5], beside),
    ]

    def w2_piece(ref, q):
        return ref.at[
            :, pl.ds(pl.multiple_of(q // 2 * 16, 16), 16), pl.ds(pl.multiple_of(lax.rem(q, 2) * 128, 128), 128)
        ]

    def w3_piece(ref, q, first):
        return ref.at[
            pl.ds(pl.multiple_of(q // 2 * 16, 16), 16), pl.ds(pl.multiple_of(first + lax.rem(q, 2) * 256, 256), 256)
        ]

    w2x = [
        remote(w2_piece(w2_in, g_lo), w2_piece(W2T.at[me_c], g_lo), w_send.at[3], w_recv.at[6], across),
        remote(W2T.at[me_c], W2T.at[me_c], w_send.at[1], w_recv.at[8], beside),
        remote(W2T.at[far], W2T.at[far], w_send.at[1], w_recv.at[9], beside),
    ]
    w3x = [
        remote(w3_piece(w3_in, g_lo, (1 - hi) * 512), w3_piece(W3.at[me_c], g_lo, 0), w_send.at[4], w_recv.at[10], across),
        remote(columns(w3_in, hi), W3.at[me_c], w_send.at[2], w_recv.at[12], beside),
        remote(W3.at[far], W3.at[far], w_send.at[2], w_recv.at[13], beside),
    ]
    w3y = [
        remote(w3_piece(w3_in, g_lo, hi * 512), w3_piece(W3X.at[me_c], g_lo, 0), w_send.at[4], w_recv.at[14], across),
        remote(columns(w3_in, 1 - hi), W3X.at[me_c], w_send.at[2], w_recv.at[16], beside),
        remote(W3X.at[far], W3X.at[far], w_send.at[2], w_recv.at[17], beside),
    ]
    shared, shared_y = [], []
    for t in range(1, n_lo):
        to = (g_hi * n_lo + lax.rem(g_lo + t, n_lo), me_c)
        for spot, sent, got, group in (
            (w2_piece(W2T.at[far], g_lo), 3, 7, shared),
            (w3_piece(W3.at[far], g_lo, 0), 4, 11, shared),
            (w3_piece(W3X.at[far], g_lo, 0), 4, 15, shared_y),
        ):
            group.append(remote(spot, spot, w_send.at[sent], w_recv.at[got], to))
    w1x[0].start()
    w1x[1].start()
    fx[1].start()
    fx[0].start()
    w3x[0].start()
    w2x[0].start()

    row_i = lax.broadcasted_iota(jnp.int32, (64, 256), 0)
    col_i = lax.broadcasted_iota(jnp.int32, (64, 256), 1)
    place = (row_i == col_i - 64 * me_c).astype(BF16)
    for cp in small_load:
        cp.wait()
    narrow = jnp.concatenate([v[...].astype(F32).reshape(1, 64) for v in (g1_v, b1_v, g2_v, b2_v)] * 2, axis=0)
    pk_rows = [mm(narrow.astype(BF16), place)[0:4]]
    pk_rows += [v[...].astype(F32).reshape(1, 256) for v in (g3_v, b3_v)]
    pk[me_c] = jnp.concatenate(pk_rows + [jnp.zeros((2, 256), F32)], axis=0)

    pkx[1].start()

    def ar_group(kind):
        if kind == "all":
            return n_all, me_p * n_ch + me_c, lambda q: (q // n_ch, lax.rem(q, n_ch))
        if kind == "half":
            return n_pix * 2, me_p * 2 + lo, lambda q: (q // 2, hi * 2 + lax.rem(q, 2))
        return n_pix, me_p, lambda q: (q, me_c)

    def ar_start(k, val, kind):
        n, me, device = ar_group(kind)
        rows = val.shape[0]
        sbuf[k, 0:rows] = val
        rbuf[k, me, 0:rows] = val

        def send(t, carry):
            to = device(lax.rem(me + t, n))
            cut = pl.ds(0, rows)
            remote(sbuf.at[k, cut], rbuf.at[k, me, cut], ar_send.at[k], ar_recv.at[k], to).start()
            return carry

        lax.fori_loop(1, n, send, 0)

    def ar_finish(k, kind, rows):
        n = ar_group(kind)[0]
        arrived(rbuf.at[k, pl.ds(0, n - 1), pl.ds(0, rows)], ar_recv.at[k])
        return jnp.sum(rbuf[k, 0:n, 0:rows], axis=0)

    def ar_close(k, kind, rows):
        n = ar_group(kind)[0]
        arrived(rbuf.at[k, pl.ds(0, n - 1), pl.ds(0, rows)], ar_send.at[k])

    def pack2(a, b):
        return jnp.concatenate([a[:, 0:128], a[:, 128:256], b[:, 0:128], b[:, 128:256]], axis=0)

    def unpack2(v):
        return (
            jnp.concatenate([v[0:1], v[1:2]], axis=1),
            jnp.concatenate([v[2:3], v[3:4]], axis=1),
        )

    def pack3(a, b):
        return jnp.concatenate([a[:, 128 * i : 128 * (i + 1)] for i in range(4)] + [b[:, 128 * i : 128 * (i + 1)] for i in range(4)], axis=0)

    def unpack3(v):
        return (
            jnp.concatenate([v[i : i + 1] for i in range(4)], axis=1),
            jnp.concatenate([v[i : i + 1] for i in range(4, 8)], axis=1),
        )


    w1_load.wait()
    w2_load.wait()
    f_load[1].wait()
    fx[1].wait_recv()
    arrived(W1T.at[near], w_recv.at[0])

    def wide_rows(t):
        return jnp.concatenate([F[0, t], F[1, t]], axis=1)

    def xcopy(kind, src, dst, t):
        got = (0, 8 + t, 15 + jnp.where(t < 2, 0, 1), 17, None, 1 + t)[kind]
        return remote(src.at[t], dst.at[t], x_send.at[kind], x_recv.at[got], across)

    def send_first(h, kind):
        w = W1T[pl.ds(2 * h, 2)].reshape(128, 512)

        def one(t, carry):
            h1s[h, t] = mm_nt(wide_rows(t + OWN), w).astype(BF16)
            xcopy(kind, h1s.at[h], h1r.at[h], t).start()
            return carry

        lax.fori_loop(0, OWN, one, 0)

    send_first(hi, 0)
    arrived(W1T.at[far], w_recv.at[1])
    w1x[2].start()
    arrived(w3_piece(W3.at[far], g_lo, 0), w_recv.at[10])
    arrived(w2_piece(W2T.at[far], g_lo), w_recv.at[6])
    for cp in shared:
        cp.start()

    flat = mask_v[...].astype(F32).reshape(1, rows28.shape[0] * ROWS)
    for t in range(rows28.shape[0]):
        rows28[t : t + 1, :] = flat[:, t * ROWS : (t + 1) * ROWS]
    diag = lax.broadcasted_iota(jnp.int32, (ROWS, ROWS), 0) == lax.broadcasted_iota(jnp.int32, (ROWS, ROWS), 1)
    ones = jnp.ones((ROWS, 128), BF16)

    lanes = jnp.broadcast_to(jnp.sum(rows28[...], axis=0, keepdims=True), (8, ROWS))
    local_count = mm(lanes.astype(BF16), ones)
    P0[...] = jnp.zeros_like(P0)
    PC[0:PAD, :] = jnp.zeros((PAD, 768), BF16)
    PC[PAD + FLAT :, :] = jnp.zeros((PAD, 768), BF16)
    ar_start(6, local_count, "pix")

    arrived(W1T.at[last_one], w_recv.at[3])
    send_first(1 - hi, 5)
    pkx[0].start()
    f_load[0].wait()
    fx[0].wait_recv()

    w1_all = W1T[...].reshape(256, 512)

    def keep_first(t, carry):
        H1[t] = mm_nt(wide_rows(t), w1_all)
        return carry

    lax.fori_loop(0, OWN, keep_first, 0)

    def put_mask(t, carry):
        at = mine + jnp.where(t < OWN, part0 + t, part1 + t - OWN)
        row = rows28[pl.ds(at, 1), :]
        V[t] = mm(jnp.where(diag, row, 0.0).astype(BF16), ones)
        return carry

    lax.fori_loop(0, BOTH, put_mask, 0)

    for cp in (w2x[1], w3x[1], cx[0], cx[1]):
        cp.start()

    zero = jnp.zeros((8, 256), F32)

    def sum_first(t, carry):
        s, q = carry
        xcopy(5, h1s.at[0], h1r.at[0], t).wait_recv()
        h = H1[t] + jnp.concatenate([h1r[0, t], h1r[1, t]], axis=1).astype(F32)
        H1[t] = h
        h1b[t] = h.astype(BF16)
        vh = spread(V[t], 256) * h
        return s + fold8(vh), q + fold8(vh * h)

    arrived(h1r.at[0], x_recv.at[0])
    s, q = lax.fori_loop(0, OWN, sum_first, (zero, zero))
    ar_start(0, pack2(fold1(s), fold1(q)), "all")
    arrived(pk.at[far], w_recv.at[4])
    pkx[2].start()
    arrived(W3.at[pl.ds(0, 2)], ld_sem.at[5])
    arrived(G3.at[pl.ds(0, 9), :, pl.ds(0, 128)], w_recv.at[7])
    arrived(A2.at[0], w_recv.at[11])
    w2x[2].start()
    w3x[2].start()
    arrived(pk.at[pl.ds(0, 2)], w_recv.at[5])
    gains = pk[0] + pk[1] + pk[2] + pk[3]
    g1, b1, g2, b2 = (gains[k : k + 1] for k in range(4))
    pair0, pair1 = pk[2 * hi], pk[2 * hi + 1]
    g3 = jnp.concatenate([pair0[4:5], pair1[4:5]], axis=1)
    b3 = jnp.concatenate([pair0[5:6], pair1[5:6]], axis=1)
    inv_n = 1.0 / spread(ar_finish(6, "pix", 8)[0:1], 512)
    inv_n2 = inv_n[:, 0:256]
    s, q = unpack2(ar_finish(0, "all", 4))
    w3y[0].start()
    avg1 = s * inv_n2
    scale1 = lax.rsqrt(q * inv_n2 - avg1 * avg1 + EPS)
    a1_gain = g1 * scale1
    a1_shift = b1 - avg1 * a1_gain

    def act_first(t, carry):
        v = spread(V[t], 256)
        aff = v * (H1[t] * a1_gain + a1_shift)
        sig = logistic(aff)
        act = aff * sig
        comp[pl.ds(pl.multiple_of(t * ROWS, 16), ROWS), :] = act
        D1[t] = v * (sig + act * (1.0 - sig))
        return carry

    def to_padded(images):
        for i in images:
            for y in range(SIDE):
                at = EDGE + (i * PAD + y + 1) * PAD
                P0[at : at + SIDE, :] = comp[(i * SIDE + y) * SIDE : (i * SIDE + y + 1) * SIDE, :]

    def from_padded(dst, image, first, last):
        for y in range(first, last):
            at = (image * PAD + y + 1) * PAD
            dst[(image * SIDE + y) * SIDE : (image * SIDE + y + 1) * SIDE, :] = padded[at : at + SIDE, :]

    def columns_forward(images):
        for i in images:
            for c in range(3):
                at = EDGE + i * BLOCK + c - 1
                PC[PAD + i * BLOCK : PAD + (i + 1) * BLOCK, 256 * c : 256 * (c + 1)] = P0[at : at + BLOCK, :].astype(BF16)

    lax.fori_loop(0, 2, act_first, 0)
    to_padded((0,))
    columns_forward((0,))

    arrived(W2T.at[near], w_recv.at[8])
    arrived(W2T.at[last_one], w_recv.at[9])
    h1x = [remote(h1b, h1o, x_send.at[4], x_recv.at[18], across)]

    def conv(first, rows):
        taps = [PC[PAD * r + first : PAD * r + first + rows, :] for r in range(3)]
        weights = [W2T[:, k].reshape(256, 256) for k in range(9)]
        padded[first : first + rows, :] = mm_nt(jnp.concatenate(taps, axis=1), jnp.concatenate(weights, axis=1))

    def sum_second(t, carry):
        s, q = carry
        h = H2[pl.ds(pl.multiple_of(t * ROWS, 16), ROWS), :]
        h2s[t] = h.astype(BF16)
        vh = spread(V[t], 256) * h
        return s + fold8(vh), q + fold8(vh * h)

    def start_all(kind, src, dst, first, last):
        for t in range(first, last):
            xcopy(kind, src, dst, t).start()

    early = 3
    pieces = (
        (PAD, 8 * PAD, ((0, 0, 8),), 1),
        (9 * PAD, 2 * BLOCK - 10 * PAD, ((0, 8, SIDE), (1, 0, SIDE)), 3),
        (2 * BLOCK + PAD, 2 * BLOCK - 2 * PAD, ((2, 0, SIDE), (3, 0, SIDE)), OWN),
    )
    carry, done = (zero, zero), 0
    for first, rows, images, now in pieces:
        conv(first, rows)
        for image, y0, y1 in images:
            from_padded(H2, image, y0, y1)
        carry = lax.fori_loop(done, now, sum_second, carry)
        start_all(1, h2s, h2r, min(done, early), min(now, early))
        if done == 0:
            lax.fori_loop(2, OWN, act_first, 0)
            to_padded((1, 2, 3))
            columns_forward((1, 2, 3))
        done = now
    s, q = carry
    ar_start(1, pack2(fold1(s), fold1(q)), "all")
    start_all(1, h2s, h2r, early, OWN)
    s, q = unpack2(ar_finish(1, "all", 4))
    avg2 = s * inv_n2
    scale2 = lax.rsqrt(q * inv_n2 - avg2 * avg2 + EPS)
    a2_gain = g2 * scale2
    a2_shift = b2 - avg2 * a2_gain

    arrived(w3_piece(W3X.at[far], g_lo, 0), w_recv.at[14])
    for cp in shared_y:
        cp.start()
    w3y[1].start()
    arrived(W3.at[near], w_recv.at[12])
    arrived(W3.at[last_one], w_recv.at[13])

    def act_second(t, h, carry):
        s, q, d, e = carry
        v = spread(V[t], 256)
        aff = v * (h * a2_gain + a2_shift)
        sig = logistic(aff)
        act = aff * sig
        slope = v * (sig + act * (1.0 - sig))
        far_slope = slope * (h - avg2)
        D2[t] = slope
        D2b[t] = slope.astype(BF16)
        D2h[t] = far_slope.astype(BF16)
        act = act.astype(BF16)
        A2[t] = act
        h3 = mm(act, W3[...].reshape(256, 512))
        H3[t] = h3
        return s + fold8(h3), q + fold8(h3 * h3), d + fold8(slope), e + fold8(far_slope)

    def own_second(t, carry):
        return act_second(t, H2[pl.ds(pl.multiple_of(t * ROWS, 16), ROWS), :], carry)

    def other_second(t, carry):
        xcopy(1, h2s, h2r, t).wait_recv()
        return act_second(t + OWN, h2r[t].astype(F32), carry)

    wide_zero = jnp.zeros((8, 512), F32)
    carry = lax.fori_loop(0, OWN, own_second, (wide_zero, wide_zero, zero, zero))
    for cp in h1x:
        cp.start()
    s, q, slopes, far_slopes = lax.fori_loop(0, OWN, other_second, carry)
    ar_start(2, pack3(fold1(s), fold1(q)), "half")
    arrived(C.at[lo], ld_sem.at[4])
    arrived(C.at[1 - lo], fx_recv.at[2])
    def half_of(ref, part):
        return ref[OWN * part : OWN * (part + 1)].reshape(OWN * ROWS, ref.shape[2])

    cross_d = mm_tn(half_of(A2, 0), half_of(D2b, 0)) + mm_tn(half_of(A2, 1), half_of(D2b, 1))
    cross_h = mm_tn(half_of(A2, 0), half_of(D2h, 0)) + mm_tn(half_of(A2, 1), half_of(D2h, 1))
    slopes, far_slopes = fold1(slopes), fold1(far_slopes)
    arrived(A2.at[0], w_recv.at[15])
    w3y[2].start()

    s, q = unpack3(ar_finish(2, "half", 8))
    avg3 = s * inv_n
    scale3 = lax.rsqrt(q * inv_n - avg3 * avg3 + EPS)
    a3_gain = g3 * scale3
    a3_shift = b3 - avg3 * a3_gain

    def put_out(ref, t, out):
        first, second = out[:, 0:256].astype(BF16), out[:, 256:512].astype(BF16)
        ref[mine + jnp.where(t < OWN, part0 + t, part1 + t - OWN)] = jnp.where(lo == 0, first, second)
        RES[t] = jnp.where(lo == 0, second, first)

    def last(t, carry):
        s, q = carry
        v = spread(V[t], 512)
        h3 = H3[t]
        wide = jnp.concatenate([F[0, t], F[1, t]], axis=1).astype(F32)
        total = v * (h3 * a3_gain + a3_shift) + wide
        sig = logistic(total)
        out = total * sig
        put_out(res_out, t, out)
        given = jnp.concatenate([C[0, t], C[1, t]], axis=1).astype(F32)
        gs = given * (sig + out * (1.0 - sig))
        GS[t] = gs
        vg = v * gs
        return s + fold8(vg), q + fold8(vg * (h3 - avg3))

    def product(t, h, carry):
        s, q = carry
        given = (spread(V[t], 512) * (a3_gain * GS[t])).astype(BF16)
        e = mm_nt(given, W3[...].reshape(256, 512)) * D2[t]
        return e, (s + fold8(e), q + fold8(e * (h - avg2)))

    def other_product(t, carry):
        e, carry = product(t + OWN, h2r[t].astype(F32), carry)
        e2s[t] = e.astype(BF16)
        return carry

    def last_and_product(t, carry):
        sums = last(t + OWN, carry[0])
        prods = other_product(t, carry[1])
        xcopy(2, e2s, e2r, t).start()
        return sums, prods

    def own_product(t, carry):
        e, carry = product(t, H2[pl.ds(pl.multiple_of(t * ROWS, 16), ROWS), :], carry)
        E2[t] = e
        return carry

    sums, prods = lax.fori_loop(0, 3, last_and_product, ((wide_zero, wide_zero), (zero, zero)))
    sums = lax.fori_loop(OWN + 3, BOTH, last, sums)
    s, q = lax.fori_loop(0, OWN, last, sums)
    ar_start(3, pack3(fold1(s), fold1(q * scale3)), "half")
    prods = lax.fori_loop(3, OWN, other_product, prods)
    start_all(2, e2s, e2r, 3, 4)
    prods = lax.fori_loop(0, OWN, own_product, prods)
    def beside_out(ref, k):
        return [
            remote(RES.at[pl.ds(OWN * s, OWN)], ref.at[pl.ds(mine + part, OWN)], o_send.at[k], o_recv.at[k], beside)
            for s, part in halves
        ]

    res_there, ig_there = beside_out(res_out, 0), beside_out(ig_out, 1)
    shift3, gain3 = unpack3(ar_finish(3, "half", 8))
    k3_h = -a3_gain * gain3 * scale3 * inv_n
    k3_0 = -a3_gain * shift3 * inv_n - k3_h * avg3

    def low_high(v):
        high = v.astype(BF16)
        return high, (v - high.astype(F32)).astype(BF16)

    def corrections(by_h, by_0, weights):
        flat = weights[...].reshape(256, 512)
        high, low = low_high(flat.astype(F32) * by_h)
        square = mm_nt(high, flat) + mm_nt(low, flat)
        high, low = low_high(by_0)
        rows = mm_nt(jnp.concatenate([high.astype(F32), low.astype(F32)] * 4, axis=0).astype(BF16), flat)
        return square, rows[0:1] + rows[1:2]

    kb[...] = jnp.concatenate([k3_h, k3_0, jnp.zeros((6, 512), F32)], axis=0)
    kx = remote(kb, kr, w_send.at[6], w_recv.at[18], across)
    kx.start()
    start_all(2, e2s, e2r, 4, 5)
    square, line = corrections(k3_h, k3_0, W3)
    s = fold1(prods[0]) + fold1(square * cross_d) + line * slopes
    q = fold1(prods[1]) + fold1(square * cross_h) + line * far_slopes
    ar_start(4, pack2(s, q * scale2), "all")
    start_all(2, e2s, e2r, 5, OWN)
    for cp in res_there:
        cp.start()

    def back_third(t, carry):
        v = spread(V[t], 512)
        G3[t] = (v * (a3_gain * GS[t] + k3_h * H3[t] + k3_0)).astype(BF16)
        return carry

    lax.fori_loop(0, BOTH, back_third, 0)

    def group_at(t, up=False):
        return (g_hi * n_lo + (1 - top if up else top) * 4 + lax.rem(quad + t, 4), me_c)

    def over_groups(total, level, sems):
        if n_hi == 1:
            return total
        level[g_hi] = total.astype(BF16)

        def swap(t):
            q = lax.rem(g_hi + t, n_hi)
            return remote(level.at[g_hi], level.at[g_hi], sems[0].at[t], sems[1].at[t], (q * n_lo + g_lo, me_c))

        for t in range(1, n_hi):
            swap(t).start()
        for t in range(1, n_hi):
            swap(t).wait()
        total = level[0].astype(F32)
        for t in range(1, n_hi):
            total = total + level[t].astype(F32)
        return total

    def pair_copies(k):
        return [remote(wp.at[k, h], wc.at[k, h], g_send.at[k], g_recv.at[k, 0], beside) for h in range(2)]

    def four_copies(k):
        return [
            remote(wb.at[k, lax.rem(quad + t, 4)], wr.at[k, quad], g_send.at[k], g_recv.at[k, 1], group_at(t))
            for t in range(1, 4)
        ]

    def swap_copy(k):
        return remote(wq.at[k], wu.at[k], g_send.at[k], g_recv.at[k, 2], group_at(0, True))

    def give_copies(k):
        spot = wfin.at[k, hi, quad]
        copies = []
        for t in range(4):
            group, place = group_at(t)
            if t > 0:
                copies.append(remote(wf.at[k, hi], spot, g_send.at[k], g_recv.at[k, 3], (group, place)))
            copies.append(
                remote(wf.at[k, 1 - hi], spot, g_send.at[k], g_recv.at[k, 3], (group, (1 - hi) * 2 + lo))
            )
        return copies

    def pair_start(k):
        for h in range(2):
            wp[k, h] = acc_w[k, h, 1 - lo].astype(BF16)
        for cp in pair_copies(k):
            cp.start()

    def pair_add(k):
        arrived(wc.at[k], g_recv.at[k, 0])
        for h in range(2):
            both = (acc_w[k, h, lo] + wc[k, h].astype(F32)).reshape(4, 16, 512)
            wa[k, h] = both
            for q in range(4):
                wb[k, q, h] = both[q].astype(BF16)
        for cp in four_copies(k):
            cp.start()

    def four_add(k):
        arrived(wr.at[k, pl.ds(0, 3)], g_recv.at[k, 1])
        total = wa[k, :, quad]
        for t in range(1, 4):
            total = total + wr[k, lax.rem(quad + t, 4)].astype(F32)
        wq[k] = total.astype(BF16)
        swap_copy(k).start()

    def swap_add(k):
        arrived(wu.at[k], g_recv.at[k, 2])
        total = over_groups(wq[k].astype(F32) + wu[k].astype(F32), wh.at[k], (h_send.at[k], h_recv.at[k]))
        wf[k] = total.astype(BF16)
        wfin[k, hi, quad] = wf[k, hi]
        for cp in give_copies(k):
            cp.start()

    def wide_take(k, out):
        arrived(A2.at[pl.ds(0, 2)], g_recv.at[k, 3])
        for h in range(2):
            out[:, 512 * h : 512 * (h + 1)] = wfin[k, h].astype(F32).reshape(64, 512)

    def wide_close(k):
        arrived(Q.at[0, pl.ds(0, 736)], g_send.at[k])

    acc_w[0] = (mm_tn(half_of(A2, 0), half_of(G3, 0)) + mm_tn(half_of(A2, 1), half_of(G3, 1))).reshape(2, 2, 64, 512)
    pair_start(0)
    arrived(kr, w_recv.at[18])
    arrived(W3X.at[near], w_recv.at[16])
    arrived(W3X.at[last_one], w_recv.at[17])
    square_x, line_x = corrections(kr[0:1], kr[1:2], W3X)
    square_both = jnp.concatenate(low_high(square + square_x), axis=1)
    line = line + line_x

    def correct(t, carry):
        both = mm(A2[t], square_both)
        E2[t] += D2[t] * (both[:, 0:256] + both[:, 256:512] + line)
        return carry

    lax.fori_loop(0, OWN, correct, 0)
    pair_add(0)

    shift2, gain2 = unpack2(ar_finish(4, "all", 4))
    k2_h = -a2_gain * gain2 * scale2 * inv_n2
    k2_0 = -a2_gain * shift2 * inv_n2 - k2_h * avg2

    def s_pair(r):
        return [remote(sp.at[r, h], sc.at[r, h], s_send.at[r], s_recv.at[r, 0], beside) for h in range(2)]

    def s_four(r):
        copies = []
        for t in range(1, 4):
            q = lax.rem(quad + t, 4)
            copies.append(
                remote(
                    sb.at[r, lax.rem(q, 2), q // 2], sr.at[r, low, high], s_send.at[r], s_recv.at[r, 1], group_at(t)
                )
            )
        return copies

    def s_low(r):
        return remote(sb.at[r, 1 - low], sr.at[r, 0], s_send.at[r], s_recv.at[r, 1], next_group)

    def s_high(r):
        to = (g_hi * n_lo + top * 4 + (1 - high) * 2 + low, me_c)
        return remote(sr.at[r, 1, 0], sz.at[r], s_send.at[r], s_recv.at[r, 2], to)

    def s_swap(r):
        up = group_at(0, True)[0]
        aside = (1 - hi) * 2 + lo
        return [
            remote(sq.at[r, 1 - hi], sx.at[r, 0], s_send.at[r], s_recv.at[r, 3], (me_p, aside)),
            remote(sq.at[r, hi], sx.at[r, 1], s_send.at[r], s_recv.at[r, 3], (up, me_c)),
            remote(sq.at[r, 1 - hi], sx.at[r, 2], s_send.at[r], s_recv.at[r, 3], (up, aside)),
        ]

    def s_give(r):
        spot = sfin.at[r, quad]
        return [remote(spot, spot, s_send.at[r], s_recv.at[r, 4], group_at(t)) for t in range(1, 4)]

    def s_make(r):
        taps = mm(QT[...], PC[PAD * r : PAD * r + FLAT, :])
        acc_s[r] = taps.reshape(2, 2, 64, 768)
        for h in range(2):
            sp[r, h] = acc_s[r, h, 1 - lo].astype(BF16)
        for cp in s_pair(r):
            cp.start()

    def s_pair_add(r):
        arrived(sc.at[r], s_recv.at[r, 0])
        for h in range(2):
            both = (acc_s[r, h, lo] + sc[r, h].astype(F32)).reshape(4, 16, 768)
            s1[r, h] = both
            for q in range(4):
                sb[r, q % 2, q // 2, h] = both[q].astype(BF16)
        for cp in s_four(r) if r == 2 else [s_low(r)]:
            cp.start()

    def s_low_add(r):
        arrived(sr.at[r, 0], s_recv.at[r, 1])
        for z in range(2):
            st[r, z] = s1[r, :, 2 * z + low] + sr[r, 0, z].astype(F32)
        sr[r, 1, 0] = st[r, 1 - high].astype(BF16)
        s_high(r).start()

    def s_four_add(r):
        if r == 2:
            arrived(PC.at[pl.ds(0, 96)], s_recv.at[r, 1])
            total = s1[r, :, quad]
            for t in range(1, 4):
                q = lax.rem(quad + t, 4)
                total = total + sr[r, lax.rem(q, 2), q // 2].astype(F32)
        else:
            arrived(sz.at[r], s_recv.at[r, 2])
            total = st[r, high] + sz[r].astype(F32)
        sq[r] = total.astype(BF16)
        for cp in s_swap(r):
            cp.start()

    def s_swap_add(r):
        arrived(sx.at[r], s_recv.at[r, 3])
        here = sq[r, hi].astype(F32) + sx[r, 0].astype(F32)
        there = sx[r, 1].astype(F32) + sx[r, 2].astype(F32)
        total = over_groups(here + there, sh.at[r], (h_send.at[2 + r], h_recv.at[2 + r]))
        sfin[r, quad] = total.astype(BF16)
        for cp in s_give(r):
            cp.start()

    def s_take(r):
        arrived(sfin.at[r, pl.ds(0, 3)], s_recv.at[r, 4])
        rows = sfin[r].astype(F32).reshape(64, 768)
        for c in range(3):
            sg_out[3 * r + c] = rows[:, 256 * c : 256 * (c + 1)]

    def s_close(r):
        arrived(PC.at[pl.ds(0, 320)], s_send.at[r])

    def back_second(t, carry):
        at = pl.ds(pl.multiple_of(t * ROWS, 16), ROWS)
        e = E2[t] + e2r[t].astype(F32)
        comp[at, :] = spread(V[t], 256) * (a2_gain * e + k2_h * H2[at, :] + k2_0)
        return carry

    def columns_back(images):
        for i in images:
            for c in range(3):
                at = EDGE + i * BLOCK - (c - 1)
                Q[c, i * BLOCK : (i + 1) * BLOCK, :] = P0[at : at + BLOCK, :].astype(BF16)

    def conv_back(first, rows):
        taps = []
        for r in range(3):
            at = first + PAD * (1 - r)
            taps += [Q[c, at : at + rows, :] for c in range(3)]
        weights = [W2T[:, k].reshape(256, 256) for k in range(9)]
        padded[first : first + rows, :] = mm(jnp.concatenate(taps, axis=1), jnp.concatenate(weights, axis=0))

    arrived(e2r.at[pl.ds(0, 2)], x_recv.at[15])
    lax.fori_loop(0, 2, back_second, 0)
    to_padded((0,))
    columns_back((0,))

    def sum_back_first(t, carry):
        s, q = carry
        e = comp[pl.ds(pl.multiple_of(t * ROWS, 16), ROWS), :] * D1[t]
        E1[t] = e
        e1s[t] = e.astype(BF16)
        return s + fold8(e), q + fold8(e * (H1[t] - avg1))

    carry, done = (zero, zero), 0
    for first, rows, images, now in pieces:
        if done == 3:
            for i in range(IMAGES):
                QT[:, i * BLOCK : (i + 1) * BLOCK] = P0[EDGE + i * BLOCK : EDGE + (i + 1) * BLOCK, :].T.astype(BF16)
            s_make(0)
        conv_back(first, rows)
        for image, y0, y1 in images:
            from_padded(comp, image, y0, y1)
        carry = lax.fori_loop(done, now, sum_back_first, carry)
        start_all(3, e1s, e1r, min(done, early), min(now, early))
        if done == 0:
            arrived(e2r.at[pl.ds(2, OWN - 2)], x_recv.at[16])
            lax.fori_loop(2, OWN, back_second, 0)
            to_padded((1, 2, 3))
            columns_back((1, 2, 3))
        done = now
    s, q = carry
    ar_start(5, pack2(fold1(s), fold1(q * scale1)), "all")
    start_all(3, e1s, e1r, early, OWN)
    four_add(0)

    s_pair_add(0)
    s_make(1)
    s_make(2)
    s_pair_add(1)
    s_pair_add(2)

    shift1, gain1 = unpack2(ar_finish(5, "all", 4))
    k1_h = -a1_gain * gain1 * scale1 * inv_n2
    k1_0 = -a1_gain * shift1 * inv_n2 - k1_h * avg1

    def back_first(t, e, h):
        G1[t] = (spread(V[t], 256) * (a1_gain * e + k1_h * h + k1_0)).astype(BF16)

    def input_term(t, carry):
        out = mm(G1[t], W1T[...].reshape(256, 512)) + GS[t]
        put_out(ig_out, t, out)
        return carry

    arrived(RES, o_send.at[0])

    def own_back_first(t, carry):
        back_first(t, E1[t], H1[t])
        return carry

    def features_of(part):
        return jnp.concatenate([half_of(F.at[0], part), half_of(F.at[1], part)], axis=1)

    lax.fori_loop(0, OWN, own_back_first, 0)
    own_reduce = mm_tn(half_of(G1, 0), features_of(0))
    acc_w[1] = own_reduce.reshape(2, 2, 64, 512)
    s_low_add(0)
    swap_add(0)
    lax.fori_loop(0, OWN, input_term, 0)
    ig_there[0].start()
    s_low_add(1)
    for cp in h1x:
        cp.wait_recv()

    def other_back_first(t, carry):
        back_first(t + OWN, e1r[t].astype(F32), h1o[t].astype(F32))
        return carry

    arrived(e1r, x_recv.at[17])
    lax.fori_loop(0, OWN, other_back_first, 0)
    acc_w[1] += mm_tn(half_of(G1, 1), features_of(1)).reshape(2, 2, 64, 512)
    pair_start(1)
    s_four_add(0)
    lax.fori_loop(OWN, BOTH, input_term, 0)
    ig_there[1].start()
    pair_add(1)
    s_four_add(1)
    s_four_add(2)
    s_swap_add(0)
    four_add(1)
    s_swap_add(1)
    s_swap_add(2)
    swap_add(1)

    def own64(v):
        half = jnp.where(hi == 0, v[:, 0:128], v[:, 128:256])
        swapped = jnp.concatenate([half[:, 64:128], half[:, 0:64]], axis=1)
        return jnp.concatenate([jnp.where(lo == 0, half, swapped), jnp.zeros((1, 128), F32)], axis=1)

    def own256(v):
        return jnp.where(lo == 0, v[:, 0:256], v[:, 256:512])

    st_out[...] = jnp.concatenate(
        [
            own64(gain1),
            own64(shift1),
            own64(gain2),
            own64(shift2),
            own256(gain3),
            own256(shift3),
            jnp.zeros((2, 256), F32),
        ],
        axis=0,
    )

    wide_take(0, eg_out)
    for r in range(3):
        s_take(r)
    wide_take(1, rg_out)

    wide_close(0)
    wide_close(1)
    for r in range(3):
        s_close(r)
    arrived(RES, o_send.at[1])
    for k, ref in enumerate((res_out, ig_out)):
        arrived(ref.at[pl.ds(theirs, BOTH)], o_recv.at[k])
    arrived(F.at[0], fx_send.at[0])
    arrived(C.at[0], fx_send.at[1])
    for k, ref in enumerate((W1T.at[pl.ds(0, 3)], W2T.at[pl.ds(0, 2)], W3, W2T.at[0], W3.at[pl.ds(0, 2)], pk.at[pl.ds(0, 3)], kb)):
        arrived(ref, w_send.at[k])
    for k, ref in enumerate((h1s.at[0], h2s, e2s, e1s, h1b, h1s.at[1])):
        arrived(ref, x_send.at[k])
    for k, kind, rows in (
        (0, "all", 4),
        (1, "all", 4),
        (2, "half", 8),
        (3, "half", 8),
        (4, "all", 4),
        (5, "all", 4),
        (6, "pix", 8),
    ):
        ar_close(k, kind, rows)


def block(n_pix, n_ch, *args):
    feat, cot, mask, w1, w2, w3 = args[:6]
    rows, lanes = feat.shape
    n_lo = 8
    n_hi = n_pix // n_lo
    chunks = rows // ROWS
    any_space = pl.BlockSpec(memory_space=pl.ANY)
    vmem = pl.BlockSpec(memory_space=pltpu.VMEM)
    V = pltpu.VMEM
    DMA = pltpu.SemaphoreType.DMA
    scratch = [
        V((rows,), jnp.int32),
        *[V((64,), BF16)] * 4,
        *[V((256,), BF16)] * 2,
        V((2, BOTH, ROWS, 256), BF16),
        V((2, BOTH, ROWS, 256), BF16),
        V((BOTH, ROWS, 128), F32),
        V((4, 64, 512), BF16),
        V((4, 9, 64, 256), BF16),
        V((4, 64, 512), BF16),
        V((4, 64, 512), BF16),
        V((4, 8, 256), F32),
        V((7, 8, 128), F32),
        V((7, n_pix * n_ch, 8, 128), F32),
        V((2, OWN, ROWS, 128), BF16),
        V((2, OWN, ROWS, 128), BF16),
        V((OWN, ROWS, 256), F32),
        V((OWN, ROWS, 256), BF16),
        V((OWN, ROWS, 256), BF16),
        V((OWN, ROWS, 256), F32),
        V((OWN * ROWS, 256), F32),
        V((FLAT + 2 * EDGE, 256), F32),
        V((FLAT + 2 * PAD, 768), BF16),
        V((3, FLAT, 256), BF16),
        V((FLAT, 256), F32),
        V((OWN * ROWS, 256), F32),
        V((OWN, ROWS, 256), BF16),
        V((OWN, ROWS, 256), BF16),
        V((BOTH, ROWS, 256), BF16),
        V((BOTH, ROWS, 256), F32),
        V((BOTH, ROWS, 256), BF16),
        V((BOTH, ROWS, 256), BF16),
        V((BOTH, ROWS, 512), F32),
        V((BOTH, ROWS, 512), F32),
        V((BOTH, ROWS, 256), BF16),
        V((BOTH, ROWS, 512), BF16),
        V((8, 512), F32),
        V((8, 512), F32),
        V((OWN, ROWS, 256), F32),
        V((OWN, ROWS, 256), BF16),
        V((OWN, ROWS, 256), BF16),
        V((OWN, ROWS, 256), F32),
        V((OWN, ROWS, 256), BF16),
        V((OWN, ROWS, 256), BF16),
        V((BOTH, ROWS, 256), BF16),
        V((256, FLAT), BF16),
        V((chunks, ROWS), F32),
        V((2, 2, 2, 64, 512), F32),
        V((2, 2, 64, 512), BF16),
        V((2, 2, 64, 512), BF16),
        V((2, 2, 4, 16, 512), F32),
        V((2, 4, 2, 16, 512), BF16),
        V((2, 4, 2, 16, 512), BF16),
        V((2, 2, 16, 512), BF16),
        V((2, 2, 16, 512), BF16),
        V((2, n_hi, 2, 16, 512), BF16),
        V((2, 2, 16, 512), BF16),
        V((2, 2, 4, 16, 512), BF16),
        V((3, 2, 2, 64, 768), F32),
        V((3, 2, 64, 768), BF16),
        V((3, 2, 64, 768), BF16),
        V((3, 2, 4, 16, 768), F32),
        V((3, 2, 2, 2, 16, 768), BF16),
        V((3, 2, 2, 2, 16, 768), BF16),
        V((2, 2, 2, 16, 768), F32),
        V((2, 2, 16, 768), BF16),
        V((3, 2, 16, 768), BF16),
        V((3, 3, 16, 768), BF16),
        V((3, n_hi, 16, 768), BF16),
        V((3, 4, 16, 768), BF16),
        DMA((13,)),
        DMA((2,)),
        DMA((3,)),
        DMA((7,)),
        DMA((19,)),
        DMA((7,)),
        DMA((7,)),
        DMA((6,)),
        DMA((19,)),
        DMA((2,)),
        DMA((2,)),
        DMA((2,)),
        DMA((2, 4)),
        DMA((3,)),
        DMA((3, 5)),
        DMA((5, n_hi) if n_hi > 1 else (1, 1)),
        DMA((5, n_hi) if n_hi > 1 else (1, 1)),
    ]
    wide = V((chunks, ROWS, lanes), BF16)
    made = pl.pallas_call(
        functools.partial(kernel, n_pix, n_ch),
        out_shape=(
            wide,
            wide,
            V((64, 1024), F32),
            V((9, 64, 256), F32),
            V((64, 1024), F32),
            V((8, 256), F32),
        ),
        in_specs=[any_space] * 12,
        out_specs=(vmem,) * 6,
        scratch_shapes=scratch,
        compiler_params=pltpu.CompilerParams(
            collective_id=0, has_side_effects=True, vmem_limit_bytes=56 * 2**20
        ),
        name="bottleneck",
    )(
        feat.reshape(chunks, ROWS, lanes),
        cot.reshape(chunks, ROWS, lanes),
        mask,
        w1.T,
        w2.transpose(0, 1, 3, 2).reshape(9, 64, 256),
        w3,
        *args[6:],
    )
    narrow = jax.ShapeDtypeStruct((64,), F32)
    broad = jax.ShapeDtypeStruct((256,), F32)
    return pl.pallas_call(
        finish,
        out_shape=tuple(jax.ShapeDtypeStruct(v.shape, v.dtype) for v in made[:5]) + (narrow,) * 4 + (broad,) * 2,
        in_specs=[any_space] * 5 + [vmem],
        out_specs=(any_space,) * 5 + (vmem,) * 6,
        scratch_shapes=[DMA((20,))],
        compiler_params=pltpu.CompilerParams(vmem_limit_bytes=2**20),
        name="outputs",
    )(*[pltpu.with_memory_space_constraint(v, pltpu.VMEM) for v in made])


def finish(*refs):
    made, stats, outs, small, sems = refs[:5], refs[5], refs[6:11], refs[11:17], refs[17]
    copies = []
    for a, b in zip(made, outs):
        parts = 4 if a.shape[0] % 4 == 0 else 3
        rows = a.shape[0] // parts
        for k in range(parts):
            at = pl.ds(k * rows, rows)
            copies.append(pltpu.make_async_copy(a.at[at], b.at[at], sems.at[len(copies)]))
    for cp in copies:
        cp.start()
    for i, out in enumerate(small):
        out[...] = stats[i : i + 1, 0 : out.shape[0]].reshape(out.shape)
    for cp in copies:
        cp.wait()


def solution(mesh):
    n_pix, n_ch = mesh.shape["pix"], mesh.shape["ch"]

    def body(feat, mask, w1, w2, w3, g1, b1, g2, b2, g3, b3, cot):
        made = block(n_pix, n_ch, feat, cot, mask, w1, w2, w3, g1, b1, g2, b2, g3, b3)
        res, ig, rg, sg, eg = made[:5]
        return (
            res.reshape(feat.shape),
            ig.reshape(feat.shape),
            rg.T,
            sg.reshape(3, 3, 64, 256).transpose(0, 1, 3, 2),
            eg,
        ) + tuple(made[5:])

    wide = P("pix", "ch")
    return jax.shard_map(
        body,
        mesh=mesh,
        in_specs=(wide, P("pix"), P(None, "ch"), P(None, None, None, "ch"), P("ch", None)) + (P("ch"),) * 6 + (wide,),
        out_specs=(wide, wide, P(None, "ch"), P(None, None, None, "ch"), P("ch", None)) + (P("ch"),) * 6,
        check_vma=False,
    )
```

```python
import functools

import jax
import jax.numpy as jnp
from jax import lax
from jax.experimental import pallas as pl
from jax.experimental.pallas import tpu as pltpu
from jax.sharding import PartitionSpec as P

SIDE = 14
EPS = 1e-05
MESH = pl.DeviceIdType.MESH
F32 = jnp.float32
BF16 = jnp.bfloat16

ROWS = 112
OWN = 7
BOTH = 14
IMAGES = 4
PAD = 16
FLAT = IMAGES * PAD * PAD
EDGE = 8
BLOCK = PAD * PAD


def mm(a, b):
    return jnp.dot(a, b, preferred_element_type=F32)


def mm_nt(a, b):
    return lax.dot_general(a, b, (((1,), (1,)), ((), ())), preferred_element_type=F32)


def mm_tn(a, b):
    return lax.dot_general(a, b, (((0,), (0,)), ((), ())), preferred_element_type=F32)


def logistic(v):
    return 0.5 * jnp.tanh(0.5 * v) + 0.5


def fold8(v):
    return jnp.sum(v.reshape(v.shape[0] // 8, 8, v.shape[1]), axis=0)


def fold1(v):
    return jnp.sum(v, axis=0, keepdims=True)


def spread(v, lanes):
    return jnp.concatenate([v] * (lanes // 128), axis=1)


def kernel(
    n_pix,
    n_ch,
    feat,
    cot,
    mask,
    w1_in,
    w2_in,
    w3_in,
    g1_in,
    b1_in,
    g2_in,
    b2_in,
    g3_in,
    b3_in,
    res_out,
    ig_out,
    rg_out,
    sg_out,
    eg_out,
    st_out,
    mask_v,
    g1_v,
    b1_v,
    g2_v,
    b2_v,
    g3_v,
    b3_v,
    F,
    C,
    V,
    W1T,
    W2T,
    W3,
    W3X,
    pk,
    sbuf,
    rbuf,
    h1s,
    h1r,
    H1,
    h1b,
    h1o,
    D1,
    comp,
    P0,
    PC,
    Q,
    padded,
    H2,
    h2s,
    h2r,
    A2,
    D2,
    D2b,
    D2h,
    H3,
    GS,
    RES,
    G3,
    kb,
    kr,
    E2,
    e2s,
    e2r,
    E1,
    e1s,
    e1r,
    G1,
    QT,
    rows28,
    acc_w,
    wp,
    wc,
    wa,
    wb,
    wr,
    wq,
    wu,
    wh,
    wf,
    wfin,
    acc_s,
    sp,
    sc,
    s1,
    sb,
    sr,
    st,
    sz,
    sq,
    sx,
    sh,
    sfin,
    ld_sem,
    fx_send,
    fx_recv,
    w_send,
    w_recv,
    ar_send,
    ar_recv,
    x_send,
    x_recv,
    o_send,
    o_recv,
    g_send,
    g_recv,
    s_send,
    s_recv,
    h_send,
    h_recv,
):
    me_p, me_c = lax.axis_index("pix"), lax.axis_index("ch")
    hi, lo = me_c // 2, lax.rem(me_c, 2)
    n_lo = 8
    n_hi = n_pix // n_lo
    g_hi, g_lo = me_p // n_lo, lax.rem(me_p, n_lo)
    across = (me_p, (1 - hi) * 2 + lo)
    beside = (me_p, hi * 2 + 1 - lo)
    n_all = n_pix * n_ch

    def remote(src, dst, send, recv, device):
        return pltpu.make_async_remote_copy(
            src_ref=src, dst_ref=dst, send_sem=send, recv_sem=recv, device_id=device, device_id_type=MESH
        )

    def local(src, dst, sem):
        return pltpu.make_async_copy(src, dst, sem)

    mine, theirs = lo * BOTH, (1 - lo) * BOTH
    part0, part1 = hi * OWN, (1 - hi) * OWN

    def columns(ref, h):
        return ref.at[:, pl.ds(pl.multiple_of(h * 512, 512), 512)]

    def arrived(dst, sem):
        local(dst, dst, sem).wait()

    w1_load = local(columns(w1_in, hi), W1T.at[me_c], ld_sem.at[0])
    w2_load = local(w2_in, W2T.at[me_c], ld_sem.at[1])
    halves = ((0, part0), (1, part1))
    f_load = [
        local(feat.at[pl.ds(mine + part, OWN)], F.at[lo, pl.ds(OWN * s, OWN)], ld_sem.at[2 + s]) for s, part in halves
    ]
    c_load = [
        local(cot.at[pl.ds(mine + part, OWN)], C.at[lo, pl.ds(OWN * s, OWN)], ld_sem.at[4]) for s, part in halves
    ]
    w3_load = [
        local(columns(w3_in, hi), W3.at[me_c], ld_sem.at[5]),
        local(columns(w3_in, 1 - hi), W3X.at[me_c], ld_sem.at[5]),
    ]
    small_load = [local(mask, mask_v, ld_sem.at[6])]
    pairs = ((g1_in, g1_v), (b1_in, b1_v), (g2_in, g2_v), (b2_in, b2_v), (g3_in, g3_v), (b3_in, b3_v))
    small_load += [local(a, b, ld_sem.at[7 + i]) for i, (a, b) in enumerate(pairs)]

    barrier = pltpu.get_barrier_semaphore()

    few = n_pix <= 8
    pix_at = [me_p] + [lax.rem(me_p + i, n_pix) for i in range(1, n_pix)] if few else []
    ch_at = [me_c] + [lax.rem(me_c + i, n_ch) for i in range(1, n_ch)]
    place_beside = hi * 2 + 1 - lo

    def everybody(kind):
        places = {"all": ch_at, "half": [me_c, place_beside], "pix": [me_c]}[kind]
        return [(p, c) for i, p in enumerate(pix_at) for j, c in enumerate(places) if i + j > 0]

    def greet(t, carry):
        q = lax.rem(me_p * n_ch + me_c + t, n_all)
        pl.semaphore_signal(barrier, inc=1, device_id=(q // n_ch, lax.rem(q, n_ch)), device_id_type=MESH)
        return carry

    if few:
        for device in everybody("all"):
            pl.semaphore_signal(barrier, inc=1, device_id=device, device_id_type=MESH)
    else:
        lax.fori_loop(1, n_all, greet, 0)
    for cp in small_load:
        cp.start()
    w1_load.start()
    f_load[1].start()
    f_load[0].start()
    w2_load.start()
    for cp in w3_load + c_load:
        cp.start()

    pl.semaphore_wait(barrier, n_all - 1)

    fx = [
        remote(feat.at[pl.ds(theirs + part, OWN)], F.at[lo, pl.ds(OWN * s, OWN)], fx_send.at[0], fx_recv.at[s], beside)
        for s, part in halves
    ]
    cx = [
        remote(cot.at[pl.ds(theirs + part, OWN)], C.at[lo, pl.ds(OWN * s, OWN)], fx_send.at[1], fx_recv.at[2], beside)
        for s, part in halves
    ]
    far, near, last_one = (1 - hi) * 2 + lo, hi * 2 + 1 - lo, (1 - hi) * 2 + 1 - lo

    quad, top = lax.rem(g_lo, 4), g_lo // 4
    low, high = lax.rem(quad, 2), quad // 2
    next_group = (g_hi * n_lo + top * 4 + high * 2 + 1 - low, me_c)

    w1x = [
        remote(columns(w1_in, 1 - hi), W1T.at[me_c], w_send.at[0], w_recv.at[1], across),
        remote(columns(w1_in, hi), W1T.at[me_c], w_send.at[0], w_recv.at[0], beside),
        remote(W1T.at[far], W1T.at[far], w_send.at[0], w_recv.at[3], beside),
    ]
    pkx = [
        remote(pk.at[me_c], pk.at[me_c], w_send.at[5], w_recv.at[4], across),
        remote(pk.at[me_c], pk.at[me_c], w_send.at[5], w_recv.at[5], beside),
        remote(pk.at[far], pk.at[far], w_send.at[5], w_recv.at[5], beside),
    ]

    def w2_piece(ref, q):
        return ref.at[
            :, pl.ds(pl.multiple_of(q // 2 * 16, 16), 16), pl.ds(pl.multiple_of(lax.rem(q, 2) * 128, 128), 128)
        ]

    def w3_piece(ref, q, first):
        return ref.at[
            pl.ds(pl.multiple_of(q // 2 * 16, 16), 16), pl.ds(pl.multiple_of(first + lax.rem(q, 2) * 256, 256), 256)
        ]

    w2x = [
        remote(w2_piece(w2_in, g_lo), w2_piece(W2T.at[me_c], g_lo), w_send.at[3], w_recv.at[6], across),
        remote(W2T.at[me_c], W2T.at[me_c], w_send.at[1], w_recv.at[8], beside),
        remote(W2T.at[far], W2T.at[far], w_send.at[1], w_recv.at[9], beside),
    ]
    w3x = [
        remote(w3_piece(w3_in, g_lo, (1 - hi) * 512), w3_piece(W3.at[me_c], g_lo, 0), w_send.at[4], w_recv.at[10], across),
        remote(columns(w3_in, hi), W3.at[me_c], w_send.at[2], w_recv.at[12], beside),
        remote(W3.at[far], W3.at[far], w_send.at[2], w_recv.at[13], beside),
    ]
    w3y = [
        remote(w3_piece(w3_in, g_lo, hi * 512), w3_piece(W3X.at[me_c], g_lo, 0), w_send.at[4], w_recv.at[14], across),
        remote(columns(w3_in, 1 - hi), W3X.at[me_c], w_send.at[2], w_recv.at[16], beside),
        remote(W3X.at[far], W3X.at[far], w_send.at[2], w_recv.at[17], beside),
    ]
    flip = (1 - top) * 4 + quad
    to_flip, to_four = (g_hi * n_lo + flip, me_c), []
    for t in range(1, 4):
        to_four.append((g_hi * n_lo + top * 4 + lax.rem(quad + t, 4), me_c))

    def pass_pieces(piece_of, sent, got):
        one = [remote(piece_of(g_lo), piece_of(g_lo), w_send.at[sent], w_recv.at[got], to_flip)]
        two = [
            remote(piece_of(q), piece_of(q), w_send.at[sent], w_recv.at[18 + got // 4], to)
            for to in to_four
            for q in (g_lo, flip)
        ]
        return one, two

    w2_flip, w2_four = pass_pieces(lambda q: w2_piece(W2T.at[far], q), 3, 7)
    w3_flip, w3_four = pass_pieces(lambda q: w3_piece(W3.at[far], q, 0), 4, 11)
    w3y_flip, w3y_four = pass_pieces(lambda q: w3_piece(W3X.at[far], q, 0), 4, 15)
    w1x[0].start()
    w1x[1].start()
    fx[1].start()
    fx[0].start()
    w3x[0].start()
    w2x[0].start()

    row_i = lax.broadcasted_iota(jnp.int32, (64, 256), 0)
    col_i = lax.broadcasted_iota(jnp.int32, (64, 256), 1)
    place = (row_i == col_i - 64 * me_c).astype(BF16)
    for cp in small_load:
        cp.wait()
    narrow = jnp.concatenate([v[...].astype(F32).reshape(1, 64) for v in (g1_v, b1_v, g2_v, b2_v)] * 2, axis=0)
    pk_rows = [mm(narrow.astype(BF16), place)[0:4]]
    pk_rows += [v[...].astype(F32).reshape(1, 256) for v in (g3_v, b3_v)]
    pk[me_c] = jnp.concatenate(pk_rows + [jnp.zeros((2, 256), F32)], axis=0)

    pkx[1].start()

    def ar_group(kind):
        if kind == "all":
            return n_all, me_p * n_ch + me_c, lambda q: (q // n_ch, lax.rem(q, n_ch))
        if kind == "half":
            return n_pix * 2, me_p * 2 + lo, lambda q: (q // 2, hi * 2 + lax.rem(q, 2))
        return n_pix, me_p, lambda q: (q, me_c)

    def ar_start(k, val, kind):
        n, me, device = ar_group(kind)
        rows = val.shape[0]
        sbuf[k, 0:rows] = val
        rbuf[k, me, 0:rows] = val

        cut = pl.ds(0, rows)

        def send(to):
            remote(sbuf.at[k, cut], rbuf.at[k, me, cut], ar_send.at[k], ar_recv.at[k], to).start()

        def send_next(t, carry):
            send(device(lax.rem(me + t, n)))
            return carry

        if few:
            for to in everybody(kind):
                send(to)
        else:
            lax.fori_loop(1, n, send_next, 0)

    def ar_finish(k, kind, rows):
        n = ar_group(kind)[0]
        arrived(rbuf.at[k, pl.ds(0, n - 1), pl.ds(0, rows)], ar_recv.at[k])
        return jnp.sum(rbuf[k, 0:n, 0:rows], axis=0)

    def ar_close(k, kind, rows):
        n = ar_group(kind)[0]
        arrived(rbuf.at[k, pl.ds(0, n - 1), pl.ds(0, rows)], ar_send.at[k])

    def pack2(a, b):
        return jnp.concatenate([a[:, 0:128], a[:, 128:256], b[:, 0:128], b[:, 128:256]], axis=0)

    def unpack2(v):
        return (
            jnp.concatenate([v[0:1], v[1:2]], axis=1),
            jnp.concatenate([v[2:3], v[3:4]], axis=1),
        )

    def pack3(a, b):
        return jnp.concatenate([a[:, 128 * i : 128 * (i + 1)] for i in range(4)] + [b[:, 128 * i : 128 * (i + 1)] for i in range(4)], axis=0)

    def unpack3(v):
        return (
            jnp.concatenate([v[i : i + 1] for i in range(4)], axis=1),
            jnp.concatenate([v[i : i + 1] for i in range(4, 8)], axis=1),
        )


    w1_load.wait()
    w2_load.wait()
    f_load[1].wait()
    fx[1].wait_recv()
    arrived(W1T.at[near], w_recv.at[0])

    def wide_rows(t):
        return jnp.concatenate([F[0, t], F[1, t]], axis=1)

    def xcopy(kind, src, dst, t):
        got = (0, 8 + t, 15 + jnp.where(t < 2, 0, 1), 17, None, 1 + t)[kind]
        return remote(src.at[t], dst.at[t], x_send.at[kind], x_recv.at[got], across)

    def send_first(h, kind):
        w = W1T[pl.ds(2 * h, 2)].reshape(128, 512)

        def one(t, carry):
            h1s[h, t] = mm_nt(wide_rows(t + OWN), w).astype(BF16)
            xcopy(kind, h1s.at[h], h1r.at[h], t).start()
            return carry

        lax.fori_loop(0, OWN, one, 0)

    send_first(hi, 0)
    arrived(W1T.at[far], w_recv.at[1])
    w1x[2].start()
    arrived(w3_piece(W3.at[far], g_lo, 0), w_recv.at[10])
    arrived(w2_piece(W2T.at[far], g_lo), w_recv.at[6])
    for cp in w2_flip + w3_flip:
        cp.start()

    flat = mask_v[...].astype(F32).reshape(1, rows28.shape[0] * ROWS)
    for t in range(rows28.shape[0]):
        rows28[t : t + 1, :] = flat[:, t * ROWS : (t + 1) * ROWS]
    diag = lax.broadcasted_iota(jnp.int32, (ROWS, ROWS), 0) == lax.broadcasted_iota(jnp.int32, (ROWS, ROWS), 1)
    ones = jnp.ones((ROWS, 128), BF16)

    lanes = jnp.broadcast_to(jnp.sum(rows28[...], axis=0, keepdims=True), (8, ROWS))
    local_count = mm(lanes.astype(BF16), ones)
    P0[...] = jnp.zeros_like(P0)
    PC[0:PAD, :] = jnp.zeros((PAD, 768), BF16)
    PC[PAD + FLAT :, :] = jnp.zeros((PAD, 768), BF16)
    ar_start(6, local_count, "pix")

    arrived(W1T.at[last_one], w_recv.at[3])
    send_first(1 - hi, 5)
    pkx[0].start()
    f_load[0].wait()
    fx[0].wait_recv()

    w1_all = W1T[...].reshape(256, 512)

    def keep_first(t, carry):
        H1[t] = mm_nt(wide_rows(t), w1_all)
        return carry

    lax.fori_loop(0, OWN, keep_first, 0)
    arrived(w2_piece(W2T.at[far], flip), w_recv.at[7])
    arrived(w3_piece(W3.at[far], flip, 0), w_recv.at[11])
    for cp in w2_four + w3_four:
        cp.start()

    def put_mask(t, carry):
        at = mine + jnp.where(t < OWN, part0 + t, part1 + t - OWN)
        row = rows28[pl.ds(at, 1), :]
        V[t] = mm(jnp.where(diag, row, 0.0).astype(BF16), ones)
        return carry

    lax.fori_loop(0, BOTH, put_mask, 0)

    for cp in (w2x[1], w3x[1], cx[0], cx[1]):
        cp.start()

    zero = jnp.zeros((8, 256), F32)

    def sum_first(t, carry):
        s, q = carry
        xcopy(5, h1s.at[0], h1r.at[0], t).wait_recv()
        h = H1[t] + jnp.concatenate([h1r[0, t], h1r[1, t]], axis=1).astype(F32)
        H1[t] = h
        h1b[t] = h.astype(BF16)
        vh = spread(V[t], 256) * h
        return s + fold8(vh), q + fold8(vh * h)

    arrived(h1r.at[0], x_recv.at[0])
    s, q = lax.fori_loop(0, OWN, sum_first, (zero, zero))
    ar_start(0, pack2(fold1(s), fold1(q)), "all")
    arrived(pk.at[far], w_recv.at[4])
    pkx[2].start()
    arrived(W3.at[pl.ds(0, 2)], ld_sem.at[5])
    arrived(G3.at[pl.ds(0, 9), pl.ds(0, 96), pl.ds(0, 128)], w_recv.at[19])
    arrived(A2.at[0, pl.ds(0, 96)], w_recv.at[20])
    w2x[2].start()
    w3x[2].start()
    arrived(pk.at[pl.ds(0, 2)], w_recv.at[5])
    gains = pk[0] + pk[1] + pk[2] + pk[3]
    g1, b1, g2, b2 = (gains[k : k + 1] for k in range(4))
    pair0, pair1 = pk[2 * hi], pk[2 * hi + 1]
    g3 = jnp.concatenate([pair0[4:5], pair1[4:5]], axis=1)
    b3 = jnp.concatenate([pair0[5:6], pair1[5:6]], axis=1)
    inv_n = 1.0 / spread(ar_finish(6, "pix", 8)[0:1], 512)
    inv_n2 = inv_n[:, 0:256]
    s, q = unpack2(ar_finish(0, "all", 4))
    w3y[0].start()
    avg1 = s * inv_n2
    scale1 = lax.rsqrt(q * inv_n2 - avg1 * avg1 + EPS)
    a1_gain = g1 * scale1
    a1_shift = b1 - avg1 * a1_gain

    def act_first(t, carry):
        v = spread(V[t], 256)
        aff = v * (H1[t] * a1_gain + a1_shift)
        sig = logistic(aff)
        act = aff * sig
        comp[pl.ds(pl.multiple_of(t * ROWS, 16), ROWS), :] = act
        D1[t] = v * (sig + act * (1.0 - sig))
        return carry

    def to_padded(images):
        for i in images:
            for y in range(SIDE):
                at = EDGE + (i * PAD + y + 1) * PAD
                P0[at : at + SIDE, :] = comp[(i * SIDE + y) * SIDE : (i * SIDE + y + 1) * SIDE, :]

    def from_padded(dst, image, first, last):
        for y in range(first, last):
            at = (image * PAD + y + 1) * PAD
            dst[(image * SIDE + y) * SIDE : (image * SIDE + y + 1) * SIDE, :] = padded[at : at + SIDE, :]

    def columns_forward(images):
        for i in images:
            for c in range(3):
                at = EDGE + i * BLOCK + c - 1
                PC[PAD + i * BLOCK : PAD + (i + 1) * BLOCK, 256 * c : 256 * (c + 1)] = P0[at : at + BLOCK, :].astype(BF16)

    lax.fori_loop(0, 2, act_first, 0)
    to_padded((0,))
    columns_forward((0,))

    arrived(W2T.at[near], w_recv.at[8])
    arrived(W2T.at[last_one], w_recv.at[9])
    h1x = [remote(h1b, h1o, x_send.at[4], x_recv.at[18], across)]

    def conv(first, rows):
        taps = [PC[PAD * r + first : PAD * r + first + rows, :] for r in range(3)]
        weights = [W2T[:, k].reshape(256, 256) for k in range(9)]
        padded[first : first + rows, :] = mm_nt(jnp.concatenate(taps, axis=1), jnp.concatenate(weights, axis=1))

    def sum_second(t, carry):
        s, q = carry
        h = H2[pl.ds(pl.multiple_of(t * ROWS, 16), ROWS), :]
        h2s[t] = h.astype(BF16)
        vh = spread(V[t], 256) * h
        return s + fold8(vh), q + fold8(vh * h)

    def start_all(kind, src, dst, first, last):
        for t in range(first, last):
            xcopy(kind, src, dst, t).start()

    early = 3
    pieces = (
        (PAD, 8 * PAD, ((0, 0, 8),), 1),
        (9 * PAD, 2 * BLOCK - 10 * PAD, ((0, 8, SIDE), (1, 0, SIDE)), 3),
        (2 * BLOCK + PAD, 2 * BLOCK - 2 * PAD, ((2, 0, SIDE), (3, 0, SIDE)), OWN),
    )
    carry, done = (zero, zero), 0
    for first, rows, images, now in pieces:
        conv(first, rows)
        for image, y0, y1 in images:
            from_padded(H2, image, y0, y1)
        carry = lax.fori_loop(done, now, sum_second, carry)
        start_all(1, h2s, h2r, min(done, early), min(now, early))
        if done == 0:
            lax.fori_loop(2, OWN, act_first, 0)
            to_padded((1, 2, 3))
            columns_forward((1, 2, 3))
        done = now
    s, q = carry
    ar_start(1, pack2(fold1(s), fold1(q)), "all")
    start_all(1, h2s, h2r, early, OWN)
    arrived(w3_piece(W3X.at[far], g_lo, 0), w_recv.at[14])
    w3y_flip[0].start()
    s, q = unpack2(ar_finish(1, "all", 4))
    avg2 = s * inv_n2
    scale2 = lax.rsqrt(q * inv_n2 - avg2 * avg2 + EPS)
    a2_gain = g2 * scale2
    a2_shift = b2 - avg2 * a2_gain

    arrived(w3_piece(W3X.at[far], flip, 0), w_recv.at[15])
    for cp in w3y_four:
        cp.start()
    w3y[1].start()
    arrived(W3.at[near], w_recv.at[12])
    arrived(W3.at[last_one], w_recv.at[13])

    def act_second(t, h, carry):
        s, q, d, e = carry
        v = spread(V[t], 256)
        aff = v * (h * a2_gain + a2_shift)
        sig = logistic(aff)
        act = aff * sig
        slope = v * (sig + act * (1.0 - sig))
        far_slope = slope * (h - avg2)
        D2[t] = slope
        D2b[t] = slope.astype(BF16)
        D2h[t] = far_slope.astype(BF16)
        act = act.astype(BF16)
        A2[t] = act
        h3 = mm(act, W3[...].reshape(256, 512))
        H3[t] = h3
        return s + fold8(h3), q + fold8(h3 * h3), d + fold8(slope), e + fold8(far_slope)

    def own_second(t, carry):
        return act_second(t, H2[pl.ds(pl.multiple_of(t * ROWS, 16), ROWS), :], carry)

    def other_second(t, carry):
        xcopy(1, h2s, h2r, t).wait_recv()
        return act_second(t + OWN, h2r[t].astype(F32), carry)

    wide_zero = jnp.zeros((8, 512), F32)
    carry = lax.fori_loop(0, OWN, own_second, (wide_zero, wide_zero, zero, zero))
    for cp in h1x:
        cp.start()
    s, q, slopes, far_slopes = lax.fori_loop(0, OWN, other_second, carry)
    ar_start(2, pack3(fold1(s), fold1(q)), "half")
    arrived(C.at[lo], ld_sem.at[4])
    arrived(C.at[1 - lo], fx_recv.at[2])
    def half_of(ref, part):
        return ref[OWN * part : OWN * (part + 1)].reshape(OWN * ROWS, ref.shape[2])

    cross_d = mm_tn(half_of(A2, 0), half_of(D2b, 0)) + mm_tn(half_of(A2, 1), half_of(D2b, 1))
    cross_h = mm_tn(half_of(A2, 0), half_of(D2h, 0)) + mm_tn(half_of(A2, 1), half_of(D2h, 1))
    slopes, far_slopes = fold1(slopes), fold1(far_slopes)
    arrived(A2.at[0, pl.ds(0, 96)], w_recv.at[21])
    w3y[2].start()

    s, q = unpack3(ar_finish(2, "half", 8))
    avg3 = s * inv_n
    scale3 = lax.rsqrt(q * inv_n - avg3 * avg3 + EPS)
    a3_gain = g3 * scale3
    a3_shift = b3 - avg3 * a3_gain

    def put_out(ref, t, out):
        first, second = out[:, 0:256].astype(BF16), out[:, 256:512].astype(BF16)
        ref[mine + jnp.where(t < OWN, part0 + t, part1 + t - OWN)] = jnp.where(lo == 0, first, second)
        RES[t] = jnp.where(lo == 0, second, first)

    def last(t, carry):
        s, q = carry
        v = spread(V[t], 512)
        h3 = H3[t]
        wide = jnp.concatenate([F[0, t], F[1, t]], axis=1).astype(F32)
        total = v * (h3 * a3_gain + a3_shift) + wide
        sig = logistic(total)
        out = total * sig
        put_out(res_out, t, out)
        given = jnp.concatenate([C[0, t], C[1, t]], axis=1).astype(F32)
        gs = given * (sig + out * (1.0 - sig))
        GS[t] = gs
        vg = v * gs
        return s + fold8(vg), q + fold8(vg * (h3 - avg3))

    def product(t, h, carry):
        s, q = carry
        given = (spread(V[t], 512) * (a3_gain * GS[t])).astype(BF16)
        e = mm_nt(given, W3[...].reshape(256, 512)) * D2[t]
        return e, (s + fold8(e), q + fold8(e * (h - avg2)))

    def other_product(t, carry):
        e, carry = product(t + OWN, h2r[t].astype(F32), carry)
        e2s[t] = e.astype(BF16)
        return carry

    def last_and_product(t, carry):
        sums = last(t + OWN, carry[0])
        prods = other_product(t, carry[1])
        xcopy(2, e2s, e2r, t).start()
        return sums, prods

    def own_product(t, carry):
        e, carry = product(t, H2[pl.ds(pl.multiple_of(t * ROWS, 16), ROWS), :], carry)
        E2[t] = e
        return carry

    sums, prods = lax.fori_loop(0, 3, last_and_product, ((wide_zero, wide_zero), (zero, zero)))
    sums = lax.fori_loop(OWN + 3, BOTH, last, sums)
    s, q = lax.fori_loop(0, OWN, last, sums)
    ar_start(3, pack3(fold1(s), fold1(q * scale3)), "half")
    prods = lax.fori_loop(3, OWN, other_product, prods)
    start_all(2, e2s, e2r, 3, 5)
    prods = lax.fori_loop(0, OWN, own_product, prods)
    def beside_out(ref, k):
        return [
            remote(RES.at[pl.ds(OWN * s, OWN)], ref.at[pl.ds(mine + part, OWN)], o_send.at[k], o_recv.at[k], beside)
            for s, part in halves
        ]

    res_there, ig_there = beside_out(res_out, 0), beside_out(ig_out, 1)
    shift3, gain3 = unpack3(ar_finish(3, "half", 8))
    k3_h = -a3_gain * gain3 * scale3 * inv_n
    k3_0 = -a3_gain * shift3 * inv_n - k3_h * avg3

    def low_high(v):
        high = v.astype(BF16)
        return high, (v - high.astype(F32)).astype(BF16)

    def corrections(by_h, by_0, weights):
        flat = weights[...].reshape(256, 512)
        high, low = low_high(flat.astype(F32) * by_h)
        square = mm_nt(high, flat) + mm_nt(low, flat)
        high, low = low_high(by_0)
        rows = mm_nt(jnp.concatenate([high.astype(F32), low.astype(F32)] * 4, axis=0).astype(BF16), flat)
        return square, rows[0:1] + rows[1:2]

    kb[...] = jnp.concatenate([k3_h, k3_0, jnp.zeros((6, 512), F32)], axis=0)
    kx = remote(kb, kr, w_send.at[6], w_recv.at[18], across)
    kx.start()
    square, line = corrections(k3_h, k3_0, W3)
    s = fold1(prods[0]) + fold1(square * cross_d) + line * slopes
    q = fold1(prods[1]) + fold1(square * cross_h) + line * far_slopes
    ar_start(4, pack2(s, q * scale2), "all")
    start_all(2, e2s, e2r, 5, OWN)
    for cp in res_there:
        cp.start()

    def back_third(t, carry):
        v = spread(V[t], 512)
        G3[t] = (v * (a3_gain * GS[t] + k3_h * H3[t] + k3_0)).astype(BF16)
        return carry

    lax.fori_loop(0, BOTH, back_third, 0)

    def group_at(t, up=False):
        return (g_hi * n_lo + (1 - top if up else top) * 4 + lax.rem(quad + t, 4), me_c)

    def over_groups(total, level, sems):
        if n_hi == 1:
            return total
        level[g_hi] = total.astype(BF16)

        def swap(t):
            q = lax.rem(g_hi + t, n_hi)
            return remote(level.at[g_hi], level.at[g_hi], sems[0].at[t], sems[1].at[t], (q * n_lo + g_lo, me_c))

        for t in range(1, n_hi):
            swap(t).start()
        for t in range(1, n_hi):
            swap(t).wait()
        total = level[0].astype(F32)
        for t in range(1, n_hi):
            total = total + level[t].astype(F32)
        return total

    def pair_copies(k):
        return [remote(wp.at[k, h], wc.at[k, h], g_send.at[k], g_recv.at[k, 0], beside) for h in range(2)]

    def four_copies(k):
        return [
            remote(wb.at[k, lax.rem(quad + t, 4)], wr.at[k, quad], g_send.at[k], g_recv.at[k, 1], group_at(t))
            for t in range(1, 4)
        ]

    def swap_copy(k):
        return remote(wq.at[k], wu.at[k], g_send.at[k], g_recv.at[k, 2], group_at(0, True))

    def give_copies(k):
        spot = wfin.at[k, hi, quad]
        copies = []
        for t in range(4):
            group, place = group_at(t)
            if t > 0:
                copies.append(remote(wf.at[k, hi], spot, g_send.at[k], g_recv.at[k, 3], (group, place)))
            copies.append(
                remote(wf.at[k, 1 - hi], spot, g_send.at[k], g_recv.at[k, 3], (group, (1 - hi) * 2 + lo))
            )
        return copies

    def pair_start(k):
        for h in range(2):
            wp[k, h] = acc_w[k, h, 1 - lo].astype(BF16)
        for cp in pair_copies(k):
            cp.start()

    def pair_add(k):
        arrived(wc.at[k], g_recv.at[k, 0])
        for h in range(2):
            both = (acc_w[k, h, lo] + wc[k, h].astype(F32)).reshape(4, 16, 512)
            wa[k, h] = both
            for q in range(4):
                wb[k, q, h] = both[q].astype(BF16)
        for cp in four_copies(k):
            cp.start()

    def four_add(k):
        arrived(wr.at[k, pl.ds(0, 3)], g_recv.at[k, 1])
        total = wa[k, :, quad]
        for t in range(1, 4):
            total = total + wr[k, lax.rem(quad + t, 4)].astype(F32)
        wq[k] = total.astype(BF16)
        swap_copy(k).start()

    def swap_add(k):
        arrived(wu.at[k], g_recv.at[k, 2])
        total = over_groups(wq[k].astype(F32) + wu[k].astype(F32), wh.at[k], (h_send.at[k], h_recv.at[k]))
        wf[k] = total.astype(BF16)
        wfin[k, hi, quad] = wf[k, hi]
        for cp in give_copies(k):
            cp.start()

    def wide_take(k, out):
        arrived(A2.at[pl.ds(0, 2)], g_recv.at[k, 3])
        for h in range(2):
            out[:, 512 * h : 512 * (h + 1)] = wfin[k, h].astype(F32).reshape(64, 512)

    def wide_close(k):
        arrived(Q.at[0, pl.ds(0, 736)], g_send.at[k])

    acc_w[0] = (mm_tn(half_of(A2, 0), half_of(G3, 0)) + mm_tn(half_of(A2, 1), half_of(G3, 1))).reshape(2, 2, 64, 512)
    pair_start(0)
    arrived(kr, w_recv.at[18])
    arrived(W3X.at[near], w_recv.at[16])
    arrived(W3X.at[last_one], w_recv.at[17])
    square_x, line_x = corrections(kr[0:1], kr[1:2], W3X)
    square_both = jnp.concatenate(low_high(square + square_x), axis=1)
    line = line + line_x

    def correct(t, carry):
        both = mm(A2[t], square_both)
        E2[t] += D2[t] * (both[:, 0:256] + both[:, 256:512] + line)
        return carry

    lax.fori_loop(0, OWN, correct, 0)
    pair_add(0)

    shift2, gain2 = unpack2(ar_finish(4, "all", 4))
    k2_h = -a2_gain * gain2 * scale2 * inv_n2
    k2_0 = -a2_gain * shift2 * inv_n2 - k2_h * avg2

    def s_pair(r):
        return [remote(sp.at[r, h], sc.at[r, h], s_send.at[r], s_recv.at[r, 0], beside) for h in range(2)]

    def s_four(r):
        copies = []
        for t in range(1, 4):
            q = lax.rem(quad + t, 4)
            copies.append(
                remote(
                    sb.at[r, lax.rem(q, 2), q // 2], sr.at[r, low, high], s_send.at[r], s_recv.at[r, 1], group_at(t)
                )
            )
        return copies

    def s_low(r):
        return remote(sb.at[r, 1 - low], sr.at[r, 0], s_send.at[r], s_recv.at[r, 1], next_group)

    def s_high(r):
        to = (g_hi * n_lo + top * 4 + (1 - high) * 2 + low, me_c)
        return remote(sr.at[r, 1, 0], sz.at[r], s_send.at[r], s_recv.at[r, 2], to)

    def s_swap(r):
        up = group_at(0, True)[0]
        aside = (1 - hi) * 2 + lo
        return [
            remote(sq.at[r, 1 - hi], sx.at[r, 0], s_send.at[r], s_recv.at[r, 3], (me_p, aside)),
            remote(sq.at[r, hi], sx.at[r, 1], s_send.at[r], s_recv.at[r, 3], (up, me_c)),
            remote(sq.at[r, 1 - hi], sx.at[r, 2], s_send.at[r], s_recv.at[r, 3], (up, aside)),
        ]

    def s_give(r):
        spot = sfin.at[r, quad]
        return [remote(spot, spot, s_send.at[r], s_recv.at[r, 4], group_at(t)) for t in range(1, 4)]

    def s_make(r):
        taps = mm(QT[...], PC[PAD * r : PAD * r + FLAT, :])
        acc_s[r] = taps.reshape(2, 2, 64, 768)
        for h in range(2):
            sp[r, h] = acc_s[r, h, 1 - lo].astype(BF16)
        for cp in s_pair(r):
            cp.start()

    def s_pair_add(r):
        arrived(sc.at[r], s_recv.at[r, 0])
        for h in range(2):
            both = (acc_s[r, h, lo] + sc[r, h].astype(F32)).reshape(4, 16, 768)
            s1[r, h] = both
            for q in range(4):
                sb[r, q % 2, q // 2, h] = both[q].astype(BF16)
        for cp in s_four(r) if r in (0, 1, 2) else [s_low(r)]:
            cp.start()

    def s_low_add(r):
        arrived(sr.at[r, 0], s_recv.at[r, 1])
        for z in range(2):
            st[r, z] = s1[r, :, 2 * z + low] + sr[r, 0, z].astype(F32)
        sr[r, 1, 0] = st[r, 1 - high].astype(BF16)
        s_high(r).start()

    def s_four_add(r):
        if r in (0, 1, 2):
            arrived(PC.at[pl.ds(0, 96)], s_recv.at[r, 1])
            total = s1[r, :, quad]
            for t in range(1, 4):
                q = lax.rem(quad + t, 4)
                total = total + sr[r, lax.rem(q, 2), q // 2].astype(F32)
        else:
            arrived(sz.at[r], s_recv.at[r, 2])
            total = st[r, high] + sz[r].astype(F32)
        sq[r] = total.astype(BF16)
        for cp in s_swap(r):
            cp.start()

    def s_swap_add(r):
        arrived(sx.at[r], s_recv.at[r, 3])
        here = sq[r, hi].astype(F32) + sx[r, 0].astype(F32)
        there = sx[r, 1].astype(F32) + sx[r, 2].astype(F32)
        total = over_groups(here + there, sh.at[r], (h_send.at[2 + r], h_recv.at[2 + r]))
        sfin[r, quad] = total.astype(BF16)
        for cp in s_give(r):
            cp.start()

    def s_take(r):
        arrived(sfin.at[r, pl.ds(0, 3)], s_recv.at[r, 4])
        rows = sfin[r].astype(F32).reshape(64, 768)
        for c in range(3):
            sg_out[3 * r + c] = rows[:, 256 * c : 256 * (c + 1)]

    def s_close(r):
        arrived(PC.at[pl.ds(0, 320)], s_send.at[r])

    def back_second(t, carry):
        at = pl.ds(pl.multiple_of(t * ROWS, 16), ROWS)
        e = E2[t] + e2r[t].astype(F32)
        comp[at, :] = spread(V[t], 256) * (a2_gain * e + k2_h * H2[at, :] + k2_0)
        return carry

    def columns_back(images):
        for i in images:
            for c in range(3):
                at = EDGE + i * BLOCK - (c - 1)
                Q[c, i * BLOCK : (i + 1) * BLOCK, :] = P0[at : at + BLOCK, :].astype(BF16)

    def conv_back(first, rows):
        taps = []
        for r in range(3):
            at = first + PAD * (1 - r)
            taps += [Q[c, at : at + rows, :] for c in range(3)]
        weights = [W2T[:, k].reshape(256, 256) for k in range(9)]
        padded[first : first + rows, :] = mm(jnp.concatenate(taps, axis=1), jnp.concatenate(weights, axis=0))

    arrived(e2r.at[pl.ds(0, 2)], x_recv.at[15])
    lax.fori_loop(0, 2, back_second, 0)
    to_padded((0,))
    columns_back((0,))

    def sum_back_first(t, carry):
        s, q = carry
        e = comp[pl.ds(pl.multiple_of(t * ROWS, 16), ROWS), :] * D1[t]
        E1[t] = e
        e1s[t] = e.astype(BF16)
        return s + fold8(e), q + fold8(e * (H1[t] - avg1))

    carry, done = (zero, zero), 0
    for first, rows, images, now in pieces:
        if done == 3:
            for i in range(IMAGES):
                QT[:, i * BLOCK : (i + 1) * BLOCK] = P0[EDGE + i * BLOCK : EDGE + (i + 1) * BLOCK, :].T.astype(BF16)
            s_make(0)
        conv_back(first, rows)
        for image, y0, y1 in images:
            from_padded(comp, image, y0, y1)
        carry = lax.fori_loop(done, now, sum_back_first, carry)
        start_all(3, e1s, e1r, min(done, early), min(now, early))
        if done == 0:
            arrived(e2r.at[pl.ds(2, OWN - 2)], x_recv.at[16])
            lax.fori_loop(2, OWN, back_second, 0)
            to_padded((1, 2, 3))
            columns_back((1, 2, 3))
        done = now
    s, q = carry
    ar_start(5, pack2(fold1(s), fold1(q * scale1)), "all")
    start_all(3, e1s, e1r, early, OWN)
    four_add(0)

    s_pair_add(0)
    s_make(1)
    s_make(2)
    s_pair_add(1)
    s_pair_add(2)

    shift1, gain1 = unpack2(ar_finish(5, "all", 4))
    k1_h = -a1_gain * gain1 * scale1 * inv_n2
    k1_0 = -a1_gain * shift1 * inv_n2 - k1_h * avg1

    def back_first(t, e, h):
        G1[t] = (spread(V[t], 256) * (a1_gain * e + k1_h * h + k1_0)).astype(BF16)

    def input_term(t, carry):
        out = mm(G1[t], W1T[...].reshape(256, 512)) + GS[t]
        put_out(ig_out, t, out)
        return carry

    arrived(RES, o_send.at[0])

    def own_back_first(t, carry):
        back_first(t, E1[t], H1[t])
        return carry

    def features_of(part):
        return jnp.concatenate([half_of(F.at[0], part), half_of(F.at[1], part)], axis=1)

    lax.fori_loop(0, OWN, own_back_first, 0)
    own_reduce = mm_tn(half_of(G1, 0), features_of(0))
    acc_w[1] = own_reduce.reshape(2, 2, 64, 512)
    swap_add(0)
    lax.fori_loop(0, OWN, input_term, 0)
    ig_there[0].start()
    for cp in h1x:
        cp.wait_recv()

    def other_back_first(t, carry):
        back_first(t + OWN, e1r[t].astype(F32), h1o[t].astype(F32))
        return carry

    arrived(e1r, x_recv.at[17])
    lax.fori_loop(0, OWN, other_back_first, 0)
    acc_w[1] += mm_tn(half_of(G1, 1), features_of(1)).reshape(2, 2, 64, 512)
    pair_start(1)
    s_four_add(0)
    lax.fori_loop(OWN, BOTH, input_term, 0)
    ig_there[1].start()
    pair_add(1)
    s_four_add(1)
    s_four_add(2)
    s_swap_add(0)
    four_add(1)
    s_swap_add(1)
    s_swap_add(2)
    swap_add(1)

    def own64(v):
        half = jnp.where(hi == 0, v[:, 0:128], v[:, 128:256])
        swapped = jnp.concatenate([half[:, 64:128], half[:, 0:64]], axis=1)
        return jnp.concatenate([jnp.where(lo == 0, half, swapped), jnp.zeros((1, 128), F32)], axis=1)

    def own256(v):
        return jnp.where(lo == 0, v[:, 0:256], v[:, 256:512])

    st_out[...] = jnp.concatenate(
        [
            own64(gain1),
            own64(shift1),
            own64(gain2),
            own64(shift2),
            own256(gain3),
            own256(shift3),
            jnp.zeros((2, 256), F32),
        ],
        axis=0,
    )

    wide_take(0, eg_out)
    for r in range(3):
        s_take(r)
    wide_take(1, rg_out)

    wide_close(0)
    wide_close(1)
    for r in range(3):
        s_close(r)
    arrived(RES, o_send.at[1])
    for k, ref in enumerate((res_out, ig_out)):
        arrived(ref.at[pl.ds(theirs, BOTH)], o_recv.at[k])
    arrived(F.at[0], fx_send.at[0])
    arrived(C.at[0], fx_send.at[1])
    for k, ref in enumerate((W1T.at[pl.ds(0, 3)], W2T.at[pl.ds(0, 2)], W3, W2T.at[0], W3.at[pl.ds(0, 2)], pk.at[pl.ds(0, 3)], kb)):
        arrived(ref, w_send.at[k])
    for k, ref in enumerate((h1s.at[0], h2s, e2s, e1s, h1b, h1s.at[1])):
        arrived(ref, x_send.at[k])
    for k, kind, rows in (
        (0, "all", 4),
        (1, "all", 4),
        (2, "half", 8),
        (3, "half", 8),
        (4, "all", 4),
        (5, "all", 4),
        (6, "pix", 8),
    ):
        ar_close(k, kind, rows)


def block(n_pix, n_ch, *args):
    feat, cot, mask, w1, w2, w3 = args[:6]
    rows, lanes = feat.shape
    n_lo = 8
    n_hi = n_pix // n_lo
    chunks = rows // ROWS
    any_space = pl.BlockSpec(memory_space=pl.ANY)
    vmem = pl.BlockSpec(memory_space=pltpu.VMEM)
    V = pltpu.VMEM
    DMA = pltpu.SemaphoreType.DMA
    scratch = [
        V((rows,), jnp.int32),
        *[V((64,), BF16)] * 4,
        *[V((256,), BF16)] * 2,
        V((2, BOTH, ROWS, 256), BF16),
        V((2, BOTH, ROWS, 256), BF16),
        V((BOTH, ROWS, 128), F32),
        V((4, 64, 512), BF16),
        V((4, 9, 64, 256), BF16),
        V((4, 64, 512), BF16),
        V((4, 64, 512), BF16),
        V((4, 8, 256), F32),
        V((7, 8, 128), F32),
        V((7, n_pix * n_ch, 8, 128), F32),
        V((2, OWN, ROWS, 128), BF16),
        V((2, OWN, ROWS, 128), BF16),
        V((OWN, ROWS, 256), F32),
        V((OWN, ROWS, 256), BF16),
        V((OWN, ROWS, 256), BF16),
        V((OWN, ROWS, 256), F32),
        V((OWN * ROWS, 256), F32),
        V((FLAT + 2 * EDGE, 256), F32),
        V((FLAT + 2 * PAD, 768), BF16),
        V((3, FLAT, 256), BF16),
        V((FLAT, 256), F32),
        V((OWN * ROWS, 256), F32),
        V((OWN, ROWS, 256), BF16),
        V((OWN, ROWS, 256), BF16),
        V((BOTH, ROWS, 256), BF16),
        V((BOTH, ROWS, 256), F32),
        V((BOTH, ROWS, 256), BF16),
        V((BOTH, ROWS, 256), BF16),
        V((BOTH, ROWS, 512), F32),
        V((BOTH, ROWS, 512), F32),
        V((BOTH, ROWS, 256), BF16),
        V((BOTH, ROWS, 512), BF16),
        V((8, 512), F32),
        V((8, 512), F32),
        V((OWN, ROWS, 256), F32),
        V((OWN, ROWS, 256), BF16),
        V((OWN, ROWS, 256), BF16),
        V((OWN, ROWS, 256), F32),
        V((OWN, ROWS, 256), BF16),
        V((OWN, ROWS, 256), BF16),
        V((BOTH, ROWS, 256), BF16),
        V((256, FLAT), BF16),
        V((chunks, ROWS), F32),
        V((2, 2, 2, 64, 512), F32),
        V((2, 2, 64, 512), BF16),
        V((2, 2, 64, 512), BF16),
        V((2, 2, 4, 16, 512), F32),
        V((2, 4, 2, 16, 512), BF16),
        V((2, 4, 2, 16, 512), BF16),
        V((2, 2, 16, 512), BF16),
        V((2, 2, 16, 512), BF16),
        V((2, n_hi, 2, 16, 512), BF16),
        V((2, 2, 16, 512), BF16),
        V((2, 2, 4, 16, 512), BF16),
        V((3, 2, 2, 64, 768), F32),
        V((3, 2, 64, 768), BF16),
        V((3, 2, 64, 768), BF16),
        V((3, 2, 4, 16, 768), F32),
        V((3, 2, 2, 2, 16, 768), BF16),
        V((3, 2, 2, 2, 16, 768), BF16),
        V((2, 2, 2, 16, 768), F32),
        V((2, 2, 16, 768), BF16),
        V((3, 2, 16, 768), BF16),
        V((3, 3, 16, 768), BF16),
        V((3, n_hi, 16, 768), BF16),
        V((3, 4, 16, 768), BF16),
        DMA((13,)),
        DMA((2,)),
        DMA((3,)),
        DMA((7,)),
        DMA((22,)),
        DMA((7,)),
        DMA((7,)),
        DMA((6,)),
        DMA((19,)),
        DMA((2,)),
        DMA((2,)),
        DMA((2,)),
        DMA((2, 4)),
        DMA((3,)),
        DMA((3, 5)),
        DMA((5, n_hi) if n_hi > 1 else (1, 1)),
        DMA((5, n_hi) if n_hi > 1 else (1, 1)),
    ]
    wide = V((chunks, ROWS, lanes), BF16)
    made = pl.pallas_call(
        functools.partial(kernel, n_pix, n_ch),
        out_shape=(
            wide,
            wide,
            V((64, 1024), F32),
            V((9, 64, 256), F32),
            V((64, 1024), F32),
            V((8, 256), F32),
        ),
        in_specs=[any_space] * 12,
        out_specs=(vmem,) * 6,
        scratch_shapes=scratch,
        compiler_params=pltpu.CompilerParams(
            collective_id=0, has_side_effects=True, vmem_limit_bytes=56 * 2**20
        ),
        name="bottleneck",
    )(
        feat.reshape(chunks, ROWS, lanes),
        cot.reshape(chunks, ROWS, lanes),
        mask,
        w1.T,
        w2.transpose(0, 1, 3, 2).reshape(9, 64, 256),
        w3,
        *args[6:],
    )
    narrow = jax.ShapeDtypeStruct((64,), F32)
    broad = jax.ShapeDtypeStruct((256,), F32)
    return pl.pallas_call(
        finish,
        out_shape=tuple(jax.ShapeDtypeStruct(v.shape, v.dtype) for v in made[:5]) + (narrow,) * 4 + (broad,) * 2,
        in_specs=[any_space] * 5 + [vmem],
        out_specs=(any_space,) * 5 + (vmem,) * 6,
        scratch_shapes=[DMA((20,))],
        compiler_params=pltpu.CompilerParams(vmem_limit_bytes=2**20),
        name="outputs",
    )(*[pltpu.with_memory_space_constraint(v, pltpu.VMEM) for v in made])


def finish(*refs):
    made, stats, outs, small, sems = refs[:5], refs[5], refs[6:11], refs[11:17], refs[17]
    copies = []
    for a, b in zip(made, outs):
        parts = 4 if a.shape[0] % 4 == 0 else 3
        rows = a.shape[0] // parts
        for k in range(parts):
            at = pl.ds(k * rows, rows)
            copies.append(pltpu.make_async_copy(a.at[at], b.at[at], sems.at[len(copies)]))
    for cp in copies:
        cp.start()
    for i, out in enumerate(small):
        out[...] = stats[i : i + 1, 0 : out.shape[0]].reshape(out.shape)
    for cp in copies:
        cp.wait()


def solution(mesh):
    n_pix, n_ch = mesh.shape["pix"], mesh.shape["ch"]

    def body(feat, mask, w1, w2, w3, g1, b1, g2, b2, g3, b3, cot):
        made = block(n_pix, n_ch, feat, cot, mask, w1, w2, w3, g1, b1, g2, b2, g3, b3)
        res, ig, rg, sg, eg = made[:5]
        return (
            res.reshape(feat.shape),
            ig.reshape(feat.shape),
            rg.T,
            sg.reshape(3, 3, 64, 256).transpose(0, 1, 3, 2),
            eg,
        ) + tuple(made[5:])

    wide = P("pix", "ch")
    return jax.shard_map(
        body,
        mesh=mesh,
        in_specs=(wide, P("pix"), P(None, "ch"), P(None, None, None, "ch"), P("ch", None)) + (P("ch"),) * 6 + (wide,),
        out_specs=(wide, wide, P(None, "ch"), P(None, None, None, "ch"), P("ch", None)) + (P("ch"),) * 6,
        check_vma=False,
    )
```

```python
import functools

import jax
import jax.numpy as jnp
from jax import lax
from jax.experimental import pallas as pl
from jax.experimental.pallas import tpu as pltpu
from jax.sharding import PartitionSpec as P

SIDE = 14
EPS = 1e-05
MESH = pl.DeviceIdType.MESH
F32 = jnp.float32
BF16 = jnp.bfloat16

ROWS = 112
OWN = 7
BOTH = 14
IMAGES = 4
PAD = 16
FLAT = IMAGES * PAD * PAD
EDGE = 8
BLOCK = PAD * PAD


def mm(a, b):
    return jnp.dot(a, b, preferred_element_type=F32)


def mm_nt(a, b):
    return lax.dot_general(a, b, (((1,), (1,)), ((), ())), preferred_element_type=F32)


def mm_tn(a, b):
    return lax.dot_general(a, b, (((0,), (0,)), ((), ())), preferred_element_type=F32)


def silu_and_slope(half):
    t = jnp.tanh(half)
    up = 1.0 + t
    out = half * up
    return out, up + out * (1.0 - t)


def fold8(v):
    return jnp.sum(v.reshape(v.shape[0] // 8, 8, v.shape[1]), axis=0)


def fold1(v):
    return jnp.sum(v, axis=0, keepdims=True)


def spread(v, lanes):
    return jnp.concatenate([v] * (lanes // 128), axis=1)


def kernel(
    n_pix,
    n_ch,
    feat,
    cot,
    mask,
    w1_in,
    w2_in,
    w3_in,
    g1_in,
    b1_in,
    g2_in,
    b2_in,
    g3_in,
    b3_in,
    res_out,
    ig_out,
    rg_out,
    sg_out,
    eg_out,
    st_out,
    mask_v,
    g1_v,
    b1_v,
    g2_v,
    b2_v,
    g3_v,
    b3_v,
    F,
    C,
    V,
    W1T,
    W2T,
    W3,
    W3X,
    pk,
    sbuf,
    rbuf,
    pbuf,
    h1s,
    h1r,
    H1,
    h1b,
    h1o,
    D1,
    comp,
    P0,
    PC,
    Q,
    padded,
    H2,
    h2s,
    h2r,
    A2,
    D2,
    D2b,
    D2h,
    H3,
    GS,
    RES,
    G3,
    kb,
    kr,
    E2,
    e2s,
    e2r,
    E1,
    e1s,
    e1r,
    G1,
    QT,
    rows28,
    acc_w,
    wp,
    wc,
    wa,
    wb,
    wr,
    wq,
    wu,
    wh,
    wf,
    wfin,
    acc_s,
    sp,
    sc,
    s1,
    sb,
    sr,
    st,
    sz,
    sq,
    sx,
    sh,
    sfin,
    ld_sem,
    fx_send,
    fx_recv,
    w_send,
    w_recv,
    ar_send,
    ar_recv,
    pair_send,
    pair_recv,
    x_send,
    x_recv,
    o_send,
    o_recv,
    g_send,
    g_recv,
    s_send,
    s_recv,
    h_send,
    h_recv,
):
    me_p, me_c = lax.axis_index("pix"), lax.axis_index("ch")
    hi, lo = me_c // 2, lax.rem(me_c, 2)
    n_lo = 8
    n_hi = n_pix // n_lo
    g_hi, g_lo = me_p // n_lo, lax.rem(me_p, n_lo)
    across = (me_p, (1 - hi) * 2 + lo)
    beside = (me_p, hi * 2 + 1 - lo)
    n_all = n_pix * n_ch

    def remote(src, dst, send, recv, device):
        return pltpu.make_async_remote_copy(
            src_ref=src, dst_ref=dst, send_sem=send, recv_sem=recv, device_id=device, device_id_type=MESH
        )

    def local(src, dst, sem):
        return pltpu.make_async_copy(src, dst, sem)

    mine, theirs = lo * BOTH, (1 - lo) * BOTH
    part0, part1 = hi * OWN, (1 - hi) * OWN

    def columns(ref, h):
        return ref.at[:, pl.ds(pl.multiple_of(h * 512, 512), 512)]

    def arrived(dst, sem):
        local(dst, dst, sem).wait()

    w1_load = local(columns(w1_in, hi), W1T.at[me_c], ld_sem.at[0])
    w2_load = local(w2_in, W2T.at[me_c], ld_sem.at[1])
    halves = ((0, part0), (1, part1))
    f_load = [
        local(feat.at[pl.ds(mine + part, OWN)], F.at[lo, pl.ds(OWN * s, OWN)], ld_sem.at[2 + s]) for s, part in halves
    ]
    c_load = [
        local(cot.at[pl.ds(mine + part, OWN)], C.at[lo, pl.ds(OWN * s, OWN)], ld_sem.at[4]) for s, part in halves
    ]
    w3_load = [
        local(columns(w3_in, hi), W3.at[me_c], ld_sem.at[5]),
        local(columns(w3_in, 1 - hi), W3X.at[me_c], ld_sem.at[5]),
    ]
    small_load = [local(mask, mask_v, ld_sem.at[6])]
    pairs = ((g1_in, g1_v), (b1_in, b1_v), (g2_in, g2_v), (b2_in, b2_v), (g3_in, g3_v), (b3_in, b3_v))
    small_load += [local(a, b, ld_sem.at[7 + i]) for i, (a, b) in enumerate(pairs)]

    barrier = pltpu.get_barrier_semaphore()

    few = n_pix <= 8
    pix_at = [me_p] + [lax.rem(me_p + i, n_pix) for i in range(1, n_pix)] if few else []
    ch_at = [me_c] + [lax.rem(me_c + i, n_ch) for i in range(1, n_ch)]
    place_beside = hi * 2 + 1 - lo

    def everybody(kind):
        places = {"all": ch_at, "half": [me_c, place_beside], "pix": [me_c], "core": [me_c, (1 - hi) * 2 + lo]}[kind]
        return [(p, c) for i, p in enumerate(pix_at) for j, c in enumerate(places) if i + j > 0]

    def greet(t, carry):
        q = lax.rem(me_p * n_ch + me_c + t, n_all)
        pl.semaphore_signal(barrier, inc=1, device_id=(q // n_ch, lax.rem(q, n_ch)), device_id_type=MESH)
        return carry

    if few:
        for device in everybody("all"):
            pl.semaphore_signal(barrier, inc=1, device_id=device, device_id_type=MESH)
    else:
        lax.fori_loop(1, n_all, greet, 0)
    for cp in small_load:
        cp.start()
    w1_load.start()
    f_load[1].start()
    f_load[0].start()
    w2_load.start()
    for cp in w3_load + c_load:
        cp.start()

    pl.semaphore_wait(barrier, n_all - 1)

    fx = [
        remote(feat.at[pl.ds(theirs + part, OWN)], F.at[lo, pl.ds(OWN * s, OWN)], fx_send.at[0], fx_recv.at[s], beside)
        for s, part in halves
    ]
    cx = [
        remote(cot.at[pl.ds(theirs + part, OWN)], C.at[lo, pl.ds(OWN * s, OWN)], fx_send.at[1], fx_recv.at[2], beside)
        for s, part in halves
    ]
    far, near, last_one = (1 - hi) * 2 + lo, hi * 2 + 1 - lo, (1 - hi) * 2 + 1 - lo

    quad, top = lax.rem(g_lo, 4), g_lo // 4
    low, high = lax.rem(quad, 2), quad // 2
    next_group = (g_hi * n_lo + top * 4 + high * 2 + 1 - low, me_c)

    w1x = [
        remote(columns(w1_in, 1 - hi), W1T.at[me_c], w_send.at[0], w_recv.at[1], across),
        remote(columns(w1_in, hi), W1T.at[me_c], w_send.at[0], w_recv.at[0], beside),
        remote(W1T.at[far], W1T.at[far], w_send.at[0], w_recv.at[3], beside),
    ]
    pkx = [
        remote(pk.at[me_c], pk.at[me_c], w_send.at[5], w_recv.at[4], across),
        remote(pk.at[me_c], pk.at[me_c], w_send.at[5], w_recv.at[5], beside),
        remote(pk.at[far], pk.at[far], w_send.at[5], w_recv.at[5], beside),
    ]

    def w2_piece(ref, q):
        return ref.at[
            :, pl.ds(pl.multiple_of(q // 2 * 16, 16), 16), pl.ds(pl.multiple_of(lax.rem(q, 2) * 128, 128), 128)
        ]

    def w3_piece(ref, q, first):
        return ref.at[
            pl.ds(pl.multiple_of(q // 2 * 16, 16), 16), pl.ds(pl.multiple_of(first + lax.rem(q, 2) * 256, 256), 256)
        ]

    w2x = [
        remote(w2_piece(w2_in, g_lo), w2_piece(W2T.at[me_c], g_lo), w_send.at[3], w_recv.at[6], across),
        remote(W2T.at[me_c], W2T.at[me_c], w_send.at[1], w_recv.at[8], beside),
        remote(W2T.at[far], W2T.at[far], w_send.at[1], w_recv.at[9], beside),
    ]
    w3x = [
        remote(w3_piece(w3_in, g_lo, (1 - hi) * 512), w3_piece(W3.at[me_c], g_lo, 0), w_send.at[4], w_recv.at[10], across),
        remote(columns(w3_in, hi), W3.at[me_c], w_send.at[2], w_recv.at[12], beside),
        remote(W3.at[far], W3.at[far], w_send.at[2], w_recv.at[13], beside),
    ]
    w3y = [
        remote(w3_piece(w3_in, g_lo, hi * 512), w3_piece(W3X.at[me_c], g_lo, 0), w_send.at[4], w_recv.at[14], across),
        remote(columns(w3_in, 1 - hi), W3X.at[me_c], w_send.at[2], w_recv.at[16], beside),
        remote(W3X.at[far], W3X.at[far], w_send.at[2], w_recv.at[17], beside),
    ]
    flip = (1 - top) * 4 + quad
    to_flip, to_four = (g_hi * n_lo + flip, me_c), []
    for t in range(1, 4):
        to_four.append((g_hi * n_lo + top * 4 + lax.rem(quad + t, 4), me_c))

    def pass_pieces(piece_of, sent, got):
        one = [remote(piece_of(g_lo), piece_of(g_lo), w_send.at[sent], w_recv.at[got], to_flip)]
        two = [
            remote(piece_of(q), piece_of(q), w_send.at[sent], w_recv.at[18 + got // 4], to)
            for to in to_four
            for q in (g_lo, flip)
        ]
        return one, two

    w2_flip, w2_four = pass_pieces(lambda q: w2_piece(W2T.at[far], q), 3, 7)
    w3_flip, w3_four = pass_pieces(lambda q: w3_piece(W3.at[far], q, 0), 4, 11)
    w3y_flip, w3y_four = pass_pieces(lambda q: w3_piece(W3X.at[far], q, 0), 4, 15)
    w1x[0].start()
    w1x[1].start()
    fx[1].start()
    fx[0].start()
    w3x[0].start()
    w2x[0].start()

    row_i = lax.broadcasted_iota(jnp.int32, (64, 256), 0)
    col_i = lax.broadcasted_iota(jnp.int32, (64, 256), 1)
    place = (row_i == col_i - 64 * me_c).astype(BF16)
    for cp in small_load:
        cp.wait()
    narrow = jnp.concatenate([v[...].astype(F32).reshape(1, 64) for v in (g1_v, b1_v, g2_v, b2_v)] * 2, axis=0)
    pk_rows = [mm(narrow.astype(BF16), place)[0:4]]
    pk_rows += [v[...].astype(F32).reshape(1, 256) for v in (g3_v, b3_v)]
    pk[me_c] = jnp.concatenate(pk_rows + [jnp.zeros((2, 256), F32)], axis=0)

    pkx[1].start()

    def ar_group(kind):
        if kind == "all":
            return n_all, me_p * n_ch + me_c, lambda q: (q // n_ch, lax.rem(q, n_ch))
        if kind == "half":
            return n_pix * 2, me_p * 2 + lo, lambda q: (q // 2, hi * 2 + lax.rem(q, 2))
        if kind == "core":
            return n_pix * 2, me_p * 2 + hi, lambda q: (q // 2, lax.rem(q, 2) * 2 + lo)
        return n_pix, me_p, lambda q: (q, me_c)

    def ar_start(k, val, kind):
        n, me, device = ar_group(kind)
        rows = val.shape[0]
        sbuf[k, 0:rows] = val
        rbuf[k, me, 0:rows] = val

        cut = pl.ds(0, rows)

        def send(to):
            remote(sbuf.at[k, cut], rbuf.at[k, me, cut], ar_send.at[k], ar_recv.at[k], to).start()

        def send_next(t, carry):
            send(device(lax.rem(me + t, n)))
            return carry

        if few:
            for to in everybody(kind):
                send(to)
        else:
            lax.fori_loop(1, n, send_next, 0)

    def pair_first(k, val):
        pbuf[k, 0] = val
        swap = remote(pbuf.at[k, 0], pbuf.at[k, 1], pair_send.at[k], pair_recv.at[k], beside)
        swap.start()
        swap.wait()
        return pbuf[k, 0] + pbuf[k, 1]

    def ar_finish(k, kind, rows):
        n = ar_group(kind)[0]
        arrived(rbuf.at[k, pl.ds(0, n - 1), pl.ds(0, rows)], ar_recv.at[k])
        return jnp.sum(rbuf[k, 0:n, 0:rows], axis=0)

    def ar_close(k, kind, rows):
        n = ar_group(kind)[0]
        arrived(rbuf.at[k, pl.ds(0, n - 1), pl.ds(0, rows)], ar_send.at[k])

    def pack2(a, b):
        return jnp.concatenate([a[:, 0:128], a[:, 128:256], b[:, 0:128], b[:, 128:256]], axis=0)

    def unpack2(v):
        return (
            jnp.concatenate([v[0:1], v[1:2]], axis=1),
            jnp.concatenate([v[2:3], v[3:4]], axis=1),
        )

    def pack3(a, b):
        return jnp.concatenate([a[:, 128 * i : 128 * (i + 1)] for i in range(4)] + [b[:, 128 * i : 128 * (i + 1)] for i in range(4)], axis=0)

    def unpack3(v):
        return (
            jnp.concatenate([v[i : i + 1] for i in range(4)], axis=1),
            jnp.concatenate([v[i : i + 1] for i in range(4, 8)], axis=1),
        )


    w1_load.wait()
    w2_load.wait()
    f_load[1].wait()
    fx[1].wait_recv()
    arrived(W1T.at[near], w_recv.at[0])

    def wide_rows(t):
        return jnp.concatenate([F[0, t], F[1, t]], axis=1)

    def xcopy(kind, src, dst, t):
        got = (
            0,
            3 + jnp.where(t < 3, 0, jnp.where(t < 5, 1, 2)),
            6 + jnp.where(t < 2, 0, 1),
            8 + jnp.where(t < 4, 0, 1),
            None,
            1 + jnp.where(t < 5, 0, 1),
        )[kind]
        return remote(src.at[t], dst.at[t], x_send.at[kind], x_recv.at[got], across)

    def send_first(h, kind):
        w = W1T[pl.ds(2 * h, 2)].reshape(128, 512)

        def one(t, carry):
            h1s[h, t] = mm_nt(wide_rows(t + OWN), w).astype(BF16)
            xcopy(kind, h1s.at[h], h1r.at[h], t).start()
            return carry

        lax.fori_loop(0, OWN, one, 0)

    send_first(hi, 0)
    arrived(W1T.at[far], w_recv.at[1])
    w1x[2].start()
    arrived(w3_piece(W3.at[far], g_lo, 0), w_recv.at[10])
    arrived(w2_piece(W2T.at[far], g_lo), w_recv.at[6])
    for cp in w2_flip + w3_flip:
        cp.start()

    flat = mask_v[...].astype(F32).reshape(1, rows28.shape[0] * ROWS)
    for t in range(rows28.shape[0]):
        rows28[t : t + 1, :] = flat[:, t * ROWS : (t + 1) * ROWS]
    diag = lax.broadcasted_iota(jnp.int32, (ROWS, ROWS), 0) == lax.broadcasted_iota(jnp.int32, (ROWS, ROWS), 1)
    ones = jnp.ones((ROWS, 128), BF16)

    lanes = jnp.broadcast_to(jnp.sum(rows28[...], axis=0, keepdims=True), (8, ROWS))
    local_count = mm(lanes.astype(BF16), ones)
    P0[...] = jnp.zeros_like(P0)
    PC[0:PAD, :] = jnp.zeros((PAD, 768), BF16)
    PC[PAD + FLAT :, :] = jnp.zeros((PAD, 768), BF16)
    ar_start(6, local_count, "pix")

    arrived(W1T.at[last_one], w_recv.at[3])
    send_first(1 - hi, 5)
    pkx[0].start()
    f_load[0].wait()
    fx[0].wait_recv()

    w1_all = W1T[...].reshape(256, 512)

    def keep_first(t, carry):
        H1[t] = mm_nt(wide_rows(t), w1_all)
        return carry

    lax.fori_loop(0, OWN, keep_first, 0)
    arrived(w2_piece(W2T.at[far], flip), w_recv.at[7])
    arrived(w3_piece(W3.at[far], flip, 0), w_recv.at[11])
    for cp in w2_four + w3_four:
        cp.start()

    def put_mask(t, carry):
        at = mine + jnp.where(t < OWN, part0 + t, part1 + t - OWN)
        row = rows28[pl.ds(at, 1), :]
        V[t] = mm(jnp.where(diag, row, 0.0).astype(BF16), ones)
        return carry

    lax.fori_loop(0, BOTH, put_mask, 0)

    for cp in (w2x[1], w3x[1], cx[0], cx[1]):
        cp.start()

    zero = jnp.zeros((8, 256), F32)

    def sum_first(t, carry):
        s, q = carry
        h = H1[t] + jnp.concatenate([h1r[0, t], h1r[1, t]], axis=1).astype(F32)
        H1[t] = h
        h1b[t] = h.astype(BF16)
        vh = spread(V[t], 256) * h
        return s + fold8(vh), q + fold8(vh * h)

    arrived(h1r.at[0], x_recv.at[0])
    arrived(h1r.at[0, pl.ds(0, 5)], x_recv.at[1])
    carry = lax.fori_loop(0, 5, sum_first, (zero, zero))
    arrived(h1r.at[0, pl.ds(5, OWN - 5)], x_recv.at[2])
    s, q = lax.fori_loop(5, OWN, sum_first, carry)
    ar_start(0, pack2(fold1(s), fold1(q)), "all")
    arrived(pk.at[far], w_recv.at[4])
    pkx[2].start()
    arrived(W3.at[pl.ds(0, 2)], ld_sem.at[5])
    arrived(G3.at[pl.ds(0, 9), pl.ds(0, 96), pl.ds(0, 128)], w_recv.at[19])
    arrived(A2.at[0, pl.ds(0, 96)], w_recv.at[20])
    w2x[2].start()
    w3x[2].start()
    arrived(pk.at[pl.ds(0, 2)], w_recv.at[5])
    gains = pk[0] + pk[1] + pk[2] + pk[3]
    g1, b1, g2, b2 = (gains[k : k + 1] for k in range(4))
    pair0, pair1 = pk[2 * hi], pk[2 * hi + 1]
    g3 = jnp.concatenate([pair0[4:5], pair1[4:5]], axis=1)
    b3 = jnp.concatenate([pair0[5:6], pair1[5:6]], axis=1)
    inv_n = 1.0 / spread(ar_finish(6, "pix", 8)[0:1], 512)
    inv_n2 = inv_n[:, 0:256]
    s, q = unpack2(ar_finish(0, "all", 4))
    w3y[0].start()
    avg1 = s * inv_n2
    scale1 = lax.rsqrt(q * inv_n2 - avg1 * avg1 + EPS)
    a1_gain = g1 * scale1
    a1_shift = b1 - avg1 * a1_gain

    def act_first(t, carry):
        v = spread(V[t], 256)
        act, slope = silu_and_slope(v * (H1[t] * (0.5 * a1_gain) + 0.5 * a1_shift))
        comp[pl.ds(pl.multiple_of(t * ROWS, 16), ROWS), :] = act
        D1[t] = spread(0.5 * V[t], 256) * slope
        return carry

    def to_padded(images):
        for i in images:
            for y in range(SIDE):
                at = EDGE + (i * PAD + y + 1) * PAD
                P0[at : at + SIDE, :] = comp[(i * SIDE + y) * SIDE : (i * SIDE + y + 1) * SIDE, :]

    def from_padded(dst, image, first, last):
        for y in range(first, last):
            at = (image * PAD + y + 1) * PAD
            dst[(image * SIDE + y) * SIDE : (image * SIDE + y + 1) * SIDE, :] = padded[at : at + SIDE, :]

    def columns_forward(images):
        for i in images:
            for c in range(3):
                at = EDGE + i * BLOCK + c - 1
                PC[PAD + i * BLOCK : PAD + (i + 1) * BLOCK, 256 * c : 256 * (c + 1)] = P0[at : at + BLOCK, :].astype(BF16)

    lax.fori_loop(0, 2, act_first, 0)
    to_padded((0,))
    columns_forward((0,))

    arrived(W2T.at[near], w_recv.at[8])
    arrived(W2T.at[last_one], w_recv.at[9])
    h1x = [remote(h1b, h1o, x_send.at[4], x_recv.at[10], across)]

    def conv(first, rows):
        taps = [PC[PAD * r + first : PAD * r + first + rows, :] for r in range(3)]
        weights = [W2T[:, k].reshape(256, 256) for k in range(9)]
        padded[first : first + rows, :] = mm_nt(jnp.concatenate(taps, axis=1), jnp.concatenate(weights, axis=1))

    def sum_second(t, carry):
        s, q = carry
        h = H2[pl.ds(pl.multiple_of(t * ROWS, 16), ROWS), :]
        h2s[t] = h.astype(BF16)
        vh = spread(V[t], 256) * h
        return s + fold8(vh), q + fold8(vh * h)

    def start_all(kind, src, dst, first, last):
        for t in range(first, last):
            xcopy(kind, src, dst, t).start()

    early = 3
    pieces = (
        (PAD, 8 * PAD, ((0, 0, 8),), 1),
        (9 * PAD, 2 * BLOCK - 10 * PAD, ((0, 8, SIDE), (1, 0, SIDE)), 3),
        (2 * BLOCK + PAD, 2 * BLOCK - 2 * PAD, ((2, 0, SIDE), (3, 0, SIDE)), OWN),
    )
    carry, done = (zero, zero), 0
    for first, rows, images, now in pieces:
        conv(first, rows)
        for image, y0, y1 in images:
            from_padded(H2, image, y0, y1)
        carry = lax.fori_loop(done, now, sum_second, carry)
        start_all(1, h2s, h2r, min(done, early), min(now, early))
        if done == 0:
            lax.fori_loop(2, OWN, act_first, 0)
            to_padded((1, 2, 3))
            columns_forward((1, 2, 3))
        done = now
    s, q = carry
    ar_start(1, pair_first(0, pack2(fold1(s), fold1(q))), "core")
    start_all(1, h2s, h2r, early, OWN)
    arrived(w3_piece(W3X.at[far], g_lo, 0), w_recv.at[14])
    w3y_flip[0].start()
    s, q = unpack2(ar_finish(1, "core", 4))
    avg2 = s * inv_n2
    scale2 = lax.rsqrt(q * inv_n2 - avg2 * avg2 + EPS)
    a2_gain = g2 * scale2
    a2_shift = b2 - avg2 * a2_gain

    arrived(w3_piece(W3X.at[far], flip, 0), w_recv.at[15])
    for cp in w3y_four:
        cp.start()
    w3y[1].start()
    arrived(W3.at[near], w_recv.at[12])
    arrived(W3.at[last_one], w_recv.at[13])

    def act_second(t, h, carry):
        s, q, d, e = carry
        v = spread(V[t], 256)
        act, slope = silu_and_slope(v * (h * (0.5 * a2_gain) + 0.5 * a2_shift))
        slope = spread(0.5 * V[t], 256) * slope
        far_slope = slope * (h - avg2)
        D2[t] = slope
        D2b[t] = slope.astype(BF16)
        D2h[t] = far_slope.astype(BF16)
        act = act.astype(BF16)
        A2[t] = act
        h3 = mm(act, W3[...].reshape(256, 512))
        H3[t] = h3
        return s + fold8(h3), q + fold8(h3 * h3), d + fold8(slope), e + fold8(far_slope)

    def own_second(t, carry):
        return act_second(t, H2[pl.ds(pl.multiple_of(t * ROWS, 16), ROWS), :], carry)

    def other_second(t, carry):
        return act_second(t + OWN, h2r[t].astype(F32), carry)

    wide_zero = jnp.zeros((8, 512), F32)
    carry = lax.fori_loop(0, OWN, own_second, (wide_zero, wide_zero, zero, zero))
    for cp in h1x:
        cp.start()
    for k, (first, last) in enumerate(((0, 3), (3, 5), (5, OWN))):
        arrived(h2r.at[pl.ds(first, last - first)], x_recv.at[3 + k])
        carry = lax.fori_loop(first, last, other_second, carry)
    s, q, slopes, far_slopes = carry
    ar_start(2, pack3(fold1(s), fold1(q)), "half")
    arrived(C.at[lo], ld_sem.at[4])
    arrived(C.at[1 - lo], fx_recv.at[2])
    def half_of(ref, part):
        return ref[OWN * part : OWN * (part + 1)].reshape(OWN * ROWS, ref.shape[2])

    cross_d = mm_tn(half_of(A2, 0), half_of(D2b, 0)) + mm_tn(half_of(A2, 1), half_of(D2b, 1))
    cross_h = mm_tn(half_of(A2, 0), half_of(D2h, 0)) + mm_tn(half_of(A2, 1), half_of(D2h, 1))
    slopes, far_slopes = fold1(slopes), fold1(far_slopes)
    arrived(A2.at[0, pl.ds(0, 96)], w_recv.at[21])
    w3y[2].start()

    s, q = unpack3(ar_finish(2, "half", 8))
    avg3 = s * inv_n
    scale3 = lax.rsqrt(q * inv_n - avg3 * avg3 + EPS)
    a3_gain = g3 * scale3
    a3_shift = b3 - avg3 * a3_gain
    half_gain, half_shift = 0.5 * a3_gain, 0.5 * a3_shift

    def put_out(ref, t, out):
        first, second = out[:, 0:256].astype(BF16), out[:, 256:512].astype(BF16)
        ref[mine + jnp.where(t < OWN, part0 + t, part1 + t - OWN)] = jnp.where(lo == 0, first, second)
        RES[t] = jnp.where(lo == 0, second, first)

    def last(t, carry):
        s, q = carry
        v = spread(V[t], 512)
        h3 = H3[t]
        wide = jnp.concatenate([F[0, t], F[1, t]], axis=1).astype(F32)
        out, slope = silu_and_slope(v * (h3 * half_gain + half_shift) + 0.5 * wide)
        put_out(res_out, t, out)
        given = jnp.concatenate([C[0, t], C[1, t]], axis=1).astype(F32)
        gs = given * slope
        GS[t] = gs
        return s + fold8(v * gs), q + fold8(gs * h3)

    def product(t, h, carry):
        s, q = carry
        given = (spread(V[t], 512) * (half_gain * GS[t])).astype(BF16)
        e = mm_nt(given, W3[...].reshape(256, 512)) * D2[t]
        return e, (s + fold8(e), q + fold8(e * (h - avg2)))

    def other_product(t, carry):
        e, carry = product(t + OWN, h2r[t].astype(F32), carry)
        e2s[t] = e.astype(BF16)
        return carry

    def last_and_product(t, carry):
        sums = last(t + OWN, carry[0])
        prods = other_product(t, carry[1])
        xcopy(2, e2s, e2r, t).start()
        return sums, prods

    def own_product(t, carry):
        e, carry = product(t, H2[pl.ds(pl.multiple_of(t * ROWS, 16), ROWS), :], carry)
        E2[t] = e
        return carry

    sums, prods = lax.fori_loop(0, 3, last_and_product, ((wide_zero, wide_zero), (zero, zero)))
    sums = lax.fori_loop(OWN + 3, BOTH, last, sums)
    s, q = lax.fori_loop(0, OWN, last, sums)
    s, q = 0.5 * fold1(s), 0.5 * fold1(q)
    ar_start(3, pack3(s, (q - avg3 * s) * scale3), "half")
    prods = lax.fori_loop(3, OWN, other_product, prods)
    start_all(2, e2s, e2r, 3, 5)
    prods = lax.fori_loop(0, OWN, own_product, prods)
    def beside_out(ref, k):
        return [
            remote(RES.at[pl.ds(OWN * s, OWN)], ref.at[pl.ds(mine + part, OWN)], o_send.at[k], o_recv.at[k], beside)
            for s, part in halves
        ]

    res_there, ig_there = beside_out(res_out, 0), beside_out(ig_out, 1)
    shift3, gain3 = unpack3(ar_finish(3, "half", 8))
    k3_h = -a3_gain * gain3 * scale3 * inv_n
    k3_0 = -a3_gain * shift3 * inv_n - k3_h * avg3

    def low_high(v):
        high = v.astype(BF16)
        return high, (v - high.astype(F32)).astype(BF16)

    def corrections(by_h, by_0, weights):
        flat = weights[...].reshape(256, 512)
        high, low = low_high(flat.astype(F32) * by_h)
        square = mm_nt(high, flat) + mm_nt(low, flat)
        high, low = low_high(by_0)
        rows = mm_nt(jnp.concatenate([high.astype(F32), low.astype(F32)] * 4, axis=0).astype(BF16), flat)
        return square, rows[0:1] + rows[1:2]

    kb[...] = jnp.concatenate([k3_h, k3_0, jnp.zeros((6, 512), F32)], axis=0)
    kx = remote(kb, kr, w_send.at[6], w_recv.at[18], across)
    kx.start()
    square, line = corrections(k3_h, k3_0, W3)
    s = fold1(prods[0]) + fold1(square * cross_d) + line * slopes
    q = fold1(prods[1]) + fold1(square * cross_h) + line * far_slopes
    ar_start(4, pack2(s, q * scale2), "all")
    start_all(2, e2s, e2r, 5, OWN)
    for cp in res_there:
        cp.start()

    def back_third(t, carry):
        v = spread(V[t], 512)
        G3[t] = (v * (half_gain * GS[t] + k3_h * H3[t] + k3_0)).astype(BF16)
        return carry

    lax.fori_loop(0, BOTH, back_third, 0)

    def group_at(t, up=False):
        return (g_hi * n_lo + (1 - top if up else top) * 4 + lax.rem(quad + t, 4), me_c)

    def over_groups(total, level, sems):
        if n_hi == 1:
            return total
        level[g_hi] = total.astype(BF16)

        def swap(t):
            q = lax.rem(g_hi + t, n_hi)
            return remote(level.at[g_hi], level.at[g_hi], sems[0].at[t], sems[1].at[t], (q * n_lo + g_lo, me_c))

        for t in range(1, n_hi):
            swap(t).start()
        for t in range(1, n_hi):
            swap(t).wait()
        total = level[0].astype(F32)
        for t in range(1, n_hi):
            total = total + level[t].astype(F32)
        return total

    def pair_copies(k):
        return [remote(wp.at[k, h], wc.at[k, h], g_send.at[k], g_recv.at[k, 0], beside) for h in range(2)]

    def four_copies(k):
        return [
            remote(wb.at[k, lax.rem(quad + t, 4)], wr.at[k, quad], g_send.at[k], g_recv.at[k, 1], group_at(t))
            for t in range(1, 4)
        ]

    def swap_copy(k):
        return remote(wq.at[k], wu.at[k], g_send.at[k], g_recv.at[k, 2], group_at(0, True))

    def give_copies(k):
        spot = wfin.at[k, hi, quad]
        copies = []
        for t in range(4):
            group, place = group_at(t)
            if t > 0:
                copies.append(remote(wf.at[k, hi], spot, g_send.at[k], g_recv.at[k, 3], (group, place)))
            copies.append(
                remote(wf.at[k, 1 - hi], spot, g_send.at[k], g_recv.at[k, 3], (group, (1 - hi) * 2 + lo))
            )
        return copies

    def pair_start(k):
        for h in range(2):
            wp[k, h] = acc_w[k, h, 1 - lo].astype(BF16)
        for cp in pair_copies(k):
            cp.start()

    def pair_add(k):
        arrived(wc.at[k], g_recv.at[k, 0])
        for h in range(2):
            both = (acc_w[k, h, lo] + wc[k, h].astype(F32)).reshape(4, 16, 512)
            wa[k, h] = both
            for q in range(4):
                wb[k, q, h] = both[q].astype(BF16)
        for cp in four_copies(k):
            cp.start()

    def four_add(k):
        arrived(wr.at[k, pl.ds(0, 3)], g_recv.at[k, 1])
        total = wa[k, :, quad]
        for t in range(1, 4):
            total = total + wr[k, lax.rem(quad + t, 4)].astype(F32)
        wq[k] = total.astype(BF16)
        swap_copy(k).start()

    def swap_add(k):
        arrived(wu.at[k], g_recv.at[k, 2])
        total = over_groups(wq[k].astype(F32) + wu[k].astype(F32), wh.at[k], (h_send.at[k], h_recv.at[k]))
        wf[k] = total.astype(BF16)
        wfin[k, hi, quad] = wf[k, hi]
        for cp in give_copies(k):
            cp.start()

    def wide_take(k, out):
        arrived(A2.at[pl.ds(0, 2)], g_recv.at[k, 3])
        for h in range(2):
            out[:, 512 * h : 512 * (h + 1)] = wfin[k, h].astype(F32).reshape(64, 512)

    def wide_close(k):
        arrived(Q.at[0, pl.ds(0, 736)], g_send.at[k])

    acc_w[0] = (mm_tn(half_of(A2, 0), half_of(G3, 0)) + mm_tn(half_of(A2, 1), half_of(G3, 1))).reshape(2, 2, 64, 512)
    pair_start(0)
    arrived(kr, w_recv.at[18])
    arrived(W3X.at[near], w_recv.at[16])
    arrived(W3X.at[last_one], w_recv.at[17])
    square_x, line_x = corrections(kr[0:1], kr[1:2], W3X)
    square_both = jnp.concatenate(low_high(square + square_x), axis=1)
    line = line + line_x

    def correct(t, carry):
        both = mm(A2[t], square_both)
        E2[t] += D2[t] * (both[:, 0:256] + both[:, 256:512] + line)
        return carry

    lax.fori_loop(0, OWN, correct, 0)
    pair_add(0)

    shift2, gain2 = unpack2(ar_finish(4, "all", 4))
    k2_h = -a2_gain * gain2 * scale2 * inv_n2
    k2_0 = -a2_gain * shift2 * inv_n2 - k2_h * avg2

    def s_pair(r):
        return [remote(sp.at[r, h], sc.at[r, h], s_send.at[r], s_recv.at[r, 0], beside) for h in range(2)]

    def s_four(r):
        copies = []
        for t in range(1, 4):
            q = lax.rem(quad + t, 4)
            copies.append(
                remote(
                    sb.at[r, lax.rem(q, 2), q // 2], sr.at[r, low, high], s_send.at[r], s_recv.at[r, 1], group_at(t)
                )
            )
        return copies

    def s_low(r):
        return remote(sb.at[r, 1 - low], sr.at[r, 0], s_send.at[r], s_recv.at[r, 1], next_group)

    def s_high(r):
        to = (g_hi * n_lo + top * 4 + (1 - high) * 2 + low, me_c)
        return remote(sr.at[r, 1, 0], sz.at[r], s_send.at[r], s_recv.at[r, 2], to)

    def s_swap(r):
        up = group_at(0, True)[0]
        aside = (1 - hi) * 2 + lo
        return [
            remote(sq.at[r, 1 - hi], sx.at[r, 0], s_send.at[r], s_recv.at[r, 3], (me_p, aside)),
            remote(sq.at[r, hi], sx.at[r, 1], s_send.at[r], s_recv.at[r, 3], (up, me_c)),
            remote(sq.at[r, 1 - hi], sx.at[r, 2], s_send.at[r], s_recv.at[r, 3], (up, aside)),
        ]

    def s_give(r):
        spot = sfin.at[r, quad]
        return [remote(spot, spot, s_send.at[r], s_recv.at[r, 4], group_at(t)) for t in range(1, 4)]

    def s_make(r):
        taps = mm(QT[...], PC[PAD * r : PAD * r + FLAT, :])
        acc_s[r] = taps.reshape(2, 2, 64, 768)
        for h in range(2):
            sp[r, h] = acc_s[r, h, 1 - lo].astype(BF16)
        for cp in s_pair(r):
            cp.start()

    def s_pair_add(r):
        arrived(sc.at[r], s_recv.at[r, 0])
        for h in range(2):
            both = (acc_s[r, h, lo] + sc[r, h].astype(F32)).reshape(4, 16, 768)
            s1[r, h] = both
            for q in range(4):
                sb[r, q % 2, q // 2, h] = both[q].astype(BF16)
        for cp in s_four(r) if r in (0, 1, 2) else [s_low(r)]:
            cp.start()

    def s_low_add(r):
        arrived(sr.at[r, 0], s_recv.at[r, 1])
        for z in range(2):
            st[r, z] = s1[r, :, 2 * z + low] + sr[r, 0, z].astype(F32)
        sr[r, 1, 0] = st[r, 1 - high].astype(BF16)
        s_high(r).start()

    def s_four_add(r):
        if r in (0, 1, 2):
            arrived(PC.at[pl.ds(0, 96)], s_recv.at[r, 1])
            total = s1[r, :, quad]
            for t in range(1, 4):
                q = lax.rem(quad + t, 4)
                total = total + sr[r, lax.rem(q, 2), q // 2].astype(F32)
        else:
            arrived(sz.at[r], s_recv.at[r, 2])
            total = st[r, high] + sz[r].astype(F32)
        sq[r] = total.astype(BF16)
        for cp in s_swap(r):
            cp.start()

    def s_swap_add(r):
        arrived(sx.at[r], s_recv.at[r, 3])
        here = sq[r, hi].astype(F32) + sx[r, 0].astype(F32)
        there = sx[r, 1].astype(F32) + sx[r, 2].astype(F32)
        total = over_groups(here + there, sh.at[r], (h_send.at[2 + r], h_recv.at[2 + r]))
        sfin[r, quad] = total.astype(BF16)
        for cp in s_give(r):
            cp.start()

    def s_take(r):
        arrived(sfin.at[r, pl.ds(0, 3)], s_recv.at[r, 4])
        rows = sfin[r].astype(F32).reshape(64, 768)
        for c in range(3):
            sg_out[3 * r + c] = rows[:, 256 * c : 256 * (c + 1)]

    def s_close(r):
        arrived(PC.at[pl.ds(0, 320)], s_send.at[r])

    def back_second(t, carry):
        at = pl.ds(pl.multiple_of(t * ROWS, 16), ROWS)
        e = E2[t] + e2r[t].astype(F32)
        comp[at, :] = spread(V[t], 256) * (a2_gain * e + k2_h * H2[at, :] + k2_0)
        return carry

    def columns_back(images):
        for i in images:
            for c in range(3):
                at = EDGE + i * BLOCK - (c - 1)
                Q[c, i * BLOCK : (i + 1) * BLOCK, :] = P0[at : at + BLOCK, :].astype(BF16)

    def conv_back(first, rows):
        taps = []
        for r in range(3):
            at = first + PAD * (1 - r)
            taps += [Q[c, at : at + rows, :] for c in range(3)]
        weights = [W2T[:, k].reshape(256, 256) for k in range(9)]
        padded[first : first + rows, :] = mm(jnp.concatenate(taps, axis=1), jnp.concatenate(weights, axis=0))

    arrived(e2r.at[pl.ds(0, 2)], x_recv.at[6])
    lax.fori_loop(0, 2, back_second, 0)
    to_padded((0,))
    columns_back((0,))

    def sum_back_first(t, carry):
        s, q = carry
        e = comp[pl.ds(pl.multiple_of(t * ROWS, 16), ROWS), :] * D1[t]
        E1[t] = e
        e1s[t] = e.astype(BF16)
        return s + fold8(e), q + fold8(e * (H1[t] - avg1))

    carry, done = (zero, zero), 0
    for first, rows, images, now in pieces:
        if done == 3:
            for i in range(IMAGES):
                QT[:, i * BLOCK : (i + 1) * BLOCK] = P0[EDGE + i * BLOCK : EDGE + (i + 1) * BLOCK, :].T.astype(BF16)
            s_make(0)
        conv_back(first, rows)
        for image, y0, y1 in images:
            from_padded(comp, image, y0, y1)
        carry = lax.fori_loop(done, now, sum_back_first, carry)
        start_all(3, e1s, e1r, min(done, early), min(now, early))
        if done == 0:
            arrived(e2r.at[pl.ds(2, OWN - 2)], x_recv.at[7])
            lax.fori_loop(2, OWN, back_second, 0)
            to_padded((1, 2, 3))
            columns_back((1, 2, 3))
        done = now
    s, q = carry
    ar_start(5, pack2(fold1(s), fold1(q * scale1)), "all")
    start_all(3, e1s, e1r, early, OWN)
    four_add(0)

    s_pair_add(0)
    s_make(1)
    s_make(2)
    s_pair_add(1)
    s_pair_add(2)

    shift1, gain1 = unpack2(ar_finish(5, "all", 4))
    k1_h = -a1_gain * gain1 * scale1 * inv_n2
    k1_0 = -a1_gain * shift1 * inv_n2 - k1_h * avg1

    def back_first(t, e, h):
        G1[t] = (spread(V[t], 256) * (a1_gain * e + k1_h * h + k1_0)).astype(BF16)

    def input_term(t, carry):
        out = mm(G1[t], W1T[...].reshape(256, 512)) + 0.5 * GS[t]
        put_out(ig_out, t, out)
        return carry

    arrived(RES, o_send.at[0])

    def own_back_first(t, carry):
        back_first(t, E1[t], H1[t])
        return carry

    def reduce_rows(first, chunks):
        parts = [v[first : first + chunks].reshape(chunks * ROWS, 256) for v in (G1, F.at[0], F.at[1])]
        return mm_tn(parts[0], jnp.concatenate(parts[1:], axis=1)).reshape(2, 2, 64, 512)

    lax.fori_loop(0, OWN, own_back_first, 0)
    acc_w[1] = reduce_rows(0, OWN)
    swap_add(0)
    lax.fori_loop(0, OWN, input_term, 0)
    ig_there[0].start()
    for cp in h1x:
        cp.wait_recv()

    def other_back_first(t, carry):
        back_first(t + OWN, e1r[t].astype(F32), h1o[t].astype(F32))
        return carry

    arrived(e1r.at[pl.ds(0, 4)], x_recv.at[8])
    arrived(e1r.at[pl.ds(4, OWN - 4)], x_recv.at[9])
    lax.fori_loop(0, OWN, other_back_first, 0)
    acc_w[1] += reduce_rows(OWN, OWN)
    pair_start(1)
    s_four_add(0)
    lax.fori_loop(OWN, BOTH, input_term, 0)
    ig_there[1].start()
    pair_add(1)
    s_four_add(1)
    s_four_add(2)
    s_swap_add(0)
    four_add(1)
    s_swap_add(1)
    s_swap_add(2)
    swap_add(1)

    def own64(v):
        half = jnp.where(hi == 0, v[:, 0:128], v[:, 128:256])
        swapped = jnp.concatenate([half[:, 64:128], half[:, 0:64]], axis=1)
        return jnp.concatenate([jnp.where(lo == 0, half, swapped), jnp.zeros((1, 128), F32)], axis=1)

    def own256(v):
        return jnp.where(lo == 0, v[:, 0:256], v[:, 256:512])

    st_out[...] = jnp.concatenate(
        [
            own64(gain1),
            own64(shift1),
            own64(gain2),
            own64(shift2),
            own256(gain3),
            own256(shift3),
            jnp.zeros((2, 256), F32),
        ],
        axis=0,
    )

    wide_take(0, eg_out)
    for r in range(3):
        s_take(r)
    wide_take(1, rg_out)

    wide_close(0)
    wide_close(1)
    for r in range(3):
        s_close(r)
    arrived(RES, o_send.at[1])
    for k, ref in enumerate((res_out, ig_out)):
        arrived(ref.at[pl.ds(theirs, BOTH)], o_recv.at[k])
    arrived(F.at[0], fx_send.at[0])
    arrived(C.at[0], fx_send.at[1])
    for k, ref in enumerate((W1T.at[pl.ds(0, 3)], W2T.at[pl.ds(0, 2)], W3, W2T.at[0], W3.at[pl.ds(0, 2)], pk.at[pl.ds(0, 3)], kb)):
        arrived(ref, w_send.at[k])
    for k, ref in enumerate((h1s.at[0], h2s, e2s, e1s, h1b, h1s.at[1])):
        arrived(ref, x_send.at[k])
    for k, kind, rows in (
        (0, "all", 4),
        (1, "core", 4),
        (2, "half", 8),
        (3, "half", 8),
        (4, "all", 4),
        (5, "all", 4),
        (6, "pix", 8),
    ):
        ar_close(k, kind, rows)


def block(n_pix, n_ch, *args):
    feat, cot, mask, w1, w2, w3 = args[:6]
    rows, lanes = feat.shape
    n_lo = 8
    n_hi = n_pix // n_lo
    chunks = rows // ROWS
    any_space = pl.BlockSpec(memory_space=pl.ANY)
    vmem = pl.BlockSpec(memory_space=pltpu.VMEM)
    V = pltpu.VMEM
    DMA = pltpu.SemaphoreType.DMA
    scratch = [
        V((rows,), jnp.int32),
        *[V((64,), BF16)] * 4,
        *[V((256,), BF16)] * 2,
        V((2, BOTH, ROWS, 256), BF16),
        V((2, BOTH, ROWS, 256), BF16),
        V((BOTH, ROWS, 128), F32),
        V((4, 64, 512), BF16),
        V((4, 9, 64, 256), BF16),
        V((4, 64, 512), BF16),
        V((4, 64, 512), BF16),
        V((4, 8, 256), F32),
        V((7, 8, 128), F32),
        V((7, n_pix * n_ch, 8, 128), F32),
        V((2, 2, 4, 128), F32),
        V((2, OWN, ROWS, 128), BF16),
        V((2, OWN, ROWS, 128), BF16),
        V((OWN, ROWS, 256), F32),
        V((OWN, ROWS, 256), BF16),
        V((OWN, ROWS, 256), BF16),
        V((OWN, ROWS, 256), F32),
        V((OWN * ROWS, 256), F32),
        V((FLAT + 2 * EDGE, 256), F32),
        V((FLAT + 2 * PAD, 768), BF16),
        V((3, FLAT, 256), BF16),
        V((FLAT, 256), F32),
        V((OWN * ROWS, 256), F32),
        V((OWN, ROWS, 256), BF16),
        V((OWN, ROWS, 256), BF16),
        V((BOTH, ROWS, 256), BF16),
        V((BOTH, ROWS, 256), F32),
        V((BOTH, ROWS, 256), BF16),
        V((BOTH, ROWS, 256), BF16),
        V((BOTH, ROWS, 512), F32),
        V((BOTH, ROWS, 512), F32),
        V((BOTH, ROWS, 256), BF16),
        V((BOTH, ROWS, 512), BF16),
        V((8, 512), F32),
        V((8, 512), F32),
        V((OWN, ROWS, 256), F32),
        V((OWN, ROWS, 256), BF16),
        V((OWN, ROWS, 256), BF16),
        V((OWN, ROWS, 256), F32),
        V((OWN, ROWS, 256), BF16),
        V((OWN, ROWS, 256), BF16),
        V((BOTH, ROWS, 256), BF16),
        V((256, FLAT), BF16),
        V((chunks, ROWS), F32),
        V((2, 2, 2, 64, 512), F32),
        V((2, 2, 64, 512), BF16),
        V((2, 2, 64, 512), BF16),
        V((2, 2, 4, 16, 512), F32),
        V((2, 4, 2, 16, 512), BF16),
        V((2, 4, 2, 16, 512), BF16),
        V((2, 2, 16, 512), BF16),
        V((2, 2, 16, 512), BF16),
        V((2, n_hi, 2, 16, 512), BF16),
        V((2, 2, 16, 512), BF16),
        V((2, 2, 4, 16, 512), BF16),
        V((3, 2, 2, 64, 768), F32),
        V((3, 2, 64, 768), BF16),
        V((3, 2, 64, 768), BF16),
        V((3, 2, 4, 16, 768), F32),
        V((3, 2, 2, 2, 16, 768), BF16),
        V((3, 2, 2, 2, 16, 768), BF16),
        V((2, 2, 2, 16, 768), F32),
        V((2, 2, 16, 768), BF16),
        V((3, 2, 16, 768), BF16),
        V((3, 3, 16, 768), BF16),
        V((3, n_hi, 16, 768), BF16),
        V((3, 4, 16, 768), BF16),
        DMA((13,)),
        DMA((2,)),
        DMA((3,)),
        DMA((7,)),
        DMA((22,)),
        DMA((7,)),
        DMA((7,)),
        DMA((2,)),
        DMA((2,)),
        DMA((6,)),
        DMA((11,)),
        DMA((2,)),
        DMA((2,)),
        DMA((2,)),
        DMA((2, 4)),
        DMA((3,)),
        DMA((3, 5)),
        DMA((5, n_hi) if n_hi > 1 else (1, 1)),
        DMA((5, n_hi) if n_hi > 1 else (1, 1)),
    ]
    wide = V((chunks, ROWS, lanes), BF16)
    made = pl.pallas_call(
        functools.partial(kernel, n_pix, n_ch),
        out_shape=(
            wide,
            wide,
            V((64, 1024), F32),
            V((9, 64, 256), F32),
            V((64, 1024), F32),
            V((8, 256), F32),
        ),
        in_specs=[any_space] * 12,
        out_specs=(vmem,) * 6,
        scratch_shapes=scratch,
        compiler_params=pltpu.CompilerParams(
            collective_id=0, has_side_effects=True, vmem_limit_bytes=56 * 2**20
        ),
        name="bottleneck",
    )(
        feat.reshape(chunks, ROWS, lanes),
        cot.reshape(chunks, ROWS, lanes),
        mask,
        w1.T,
        w2.transpose(0, 1, 3, 2).reshape(9, 64, 256),
        w3,
        *args[6:],
    )
    narrow = jax.ShapeDtypeStruct((64,), F32)
    broad = jax.ShapeDtypeStruct((256,), F32)
    return pl.pallas_call(
        finish,
        out_shape=tuple(jax.ShapeDtypeStruct(v.shape, v.dtype) for v in made[:5]) + (narrow,) * 4 + (broad,) * 2,
        in_specs=[any_space] * 6,
        out_specs=(any_space,) * 11,
        scratch_shapes=[V((8, 256), F32)] + [V(v.shape, F32) for v in (narrow,) * 4 + (broad,) * 2] + [DMA((12,))],
        compiler_params=pltpu.CompilerParams(vmem_limit_bytes=2**20),
        name="outputs",
    )(*[pltpu.with_memory_space_constraint(v, pltpu.VMEM) for v in made])


def finish(*refs):
    made, outs, stats, small, sems = refs[:6], refs[6:17], refs[17], refs[18:24], refs[24]
    copies = [pltpu.make_async_copy(a, b, sems.at[i]) for i, (a, b) in enumerate(zip(made[:5], outs[:5]))]
    got = pltpu.make_async_copy(made[5], stats, sems.at[5])
    got.start()
    for cp in copies:
        cp.start()
    got.wait()
    for i, (one, out) in enumerate(zip(small, outs[5:])):
        one[...] = stats[i : i + 1, 0 : one.shape[0]].reshape(one.shape)
        copies.append(pltpu.make_async_copy(one, out, sems.at[6 + i]))
        copies[-1].start()
    for cp in copies:
        cp.wait()


def solution(mesh):
    n_pix, n_ch = mesh.shape["pix"], mesh.shape["ch"]

    def body(feat, mask, w1, w2, w3, g1, b1, g2, b2, g3, b3, cot):
        made = block(n_pix, n_ch, feat, cot, mask, w1, w2, w3, g1, b1, g2, b2, g3, b3)
        res, ig, rg, sg, eg = made[:5]
        return (
            res.reshape(feat.shape),
            ig.reshape(feat.shape),
            rg.T,
            sg.reshape(3, 3, 64, 256).transpose(0, 1, 3, 2),
            eg,
        ) + tuple(made[5:])

    wide = P("pix", "ch")
    return jax.shard_map(
        body,
        mesh=mesh,
        in_specs=(wide, P("pix"), P(None, "ch"), P(None, None, None, "ch"), P("ch", None)) + (P("ch"),) * 6 + (wide,),
        out_specs=(wide, wide, P(None, "ch"), P(None, None, None, "ch"), P("ch", None)) + (P("ch"),) * 6,
        check_vma=False,
    )
```

```python
import functools

import jax
import jax.numpy as jnp
from jax import lax
from jax.experimental import pallas as pl
from jax.experimental.pallas import tpu as pltpu
from jax.sharding import PartitionSpec as P

SIDE = 14
EPS = 1e-05
MESH = pl.DeviceIdType.MESH
F32 = jnp.float32
BF16 = jnp.bfloat16

ROWS = 112
OWN = 7
BOTH = 14
IMAGES = 4
PAD = 16
FLAT = IMAGES * PAD * PAD
EDGE = 8
BLOCK = PAD * PAD


def mm(a, b):
    return jnp.dot(a, b, preferred_element_type=F32)


def mm_nt(a, b):
    return lax.dot_general(a, b, (((1,), (1,)), ((), ())), preferred_element_type=F32)


def mm_tn(a, b):
    return lax.dot_general(a, b, (((0,), (0,)), ((), ())), preferred_element_type=F32)


def silu_and_slope(half):
    t = jnp.tanh(half)
    up = 1.0 + t
    out = half * up
    return out, up + out * (1.0 - t)


def fold8(v):
    return jnp.sum(v.reshape(v.shape[0] // 8, 8, v.shape[1]), axis=0)


def fold1(v):
    return jnp.sum(v, axis=0, keepdims=True)


def spread(v, lanes):
    return jnp.concatenate([v] * (lanes // 128), axis=1)


def kernel(
    n_pix,
    n_ch,
    feat,
    cot,
    mask,
    w1_in,
    w2_in,
    w3_in,
    g1_in,
    b1_in,
    g2_in,
    b2_in,
    g3_in,
    b3_in,
    res_out,
    ig_out,
    rg_out,
    sg_out,
    eg_out,
    st_out,
    mask_v,
    g1_v,
    b1_v,
    g2_v,
    b2_v,
    g3_v,
    b3_v,
    F,
    C,
    V,
    W1T,
    W2T,
    W3,
    W3X,
    pk,
    sbuf,
    rbuf,
    pbuf,
    h1s,
    h1r,
    H1,
    h1b,
    h1o,
    D1,
    comp,
    P0,
    PC,
    Q,
    padded,
    H2,
    h2s,
    h2r,
    A2,
    D2,
    D2b,
    D2h,
    H3,
    GS,
    RES,
    G3,
    kb,
    kr,
    E2,
    e2s,
    e2r,
    E1,
    e1s,
    e1r,
    G1,
    QT,
    rows28,
    acc_w,
    wp,
    wc,
    wa,
    wb,
    wr,
    wq,
    wu,
    wh,
    wf,
    wfin,
    acc_s,
    sp,
    sc,
    s1,
    sb,
    sr,
    st,
    sz,
    sq,
    sx,
    sh,
    sfin,
    ld_sem,
    fx_send,
    fx_recv,
    w_send,
    w_recv,
    ar_send,
    ar_recv,
    pair_send,
    pair_recv,
    x_send,
    x_recv,
    o_send,
    o_recv,
    g_send,
    g_recv,
    s_send,
    s_recv,
    h_send,
    h_recv,
):
    me_p, me_c = lax.axis_index("pix"), lax.axis_index("ch")
    hi, lo = me_c // 2, lax.rem(me_c, 2)
    n_lo = 8
    n_hi = n_pix // n_lo
    g_hi, g_lo = me_p // n_lo, lax.rem(me_p, n_lo)
    across = (me_p, (1 - hi) * 2 + lo)
    beside = (me_p, hi * 2 + 1 - lo)
    n_all = n_pix * n_ch

    def remote(src, dst, send, recv, device):
        return pltpu.make_async_remote_copy(
            src_ref=src, dst_ref=dst, send_sem=send, recv_sem=recv, device_id=device, device_id_type=MESH
        )

    def local(src, dst, sem):
        return pltpu.make_async_copy(src, dst, sem)

    mine, theirs = lo * BOTH, (1 - lo) * BOTH
    part0, part1 = hi * OWN, (1 - hi) * OWN

    def columns(ref, h):
        return ref.at[:, pl.ds(pl.multiple_of(h * 512, 512), 512)]

    def arrived(dst, sem):
        local(dst, dst, sem).wait()

    w1_load = local(columns(w1_in, hi), W1T.at[me_c], ld_sem.at[0])
    w2_load = local(w2_in, W2T.at[me_c], ld_sem.at[1])
    halves = ((0, part0), (1, part1))
    f_load = [
        local(feat.at[pl.ds(mine + part, OWN)], F.at[lo, pl.ds(OWN * s, OWN)], ld_sem.at[2 + s]) for s, part in halves
    ]
    c_load = [
        local(cot.at[pl.ds(mine + part, OWN)], C.at[lo, pl.ds(OWN * s, OWN)], ld_sem.at[4]) for s, part in halves
    ]
    w3_load = [
        local(columns(w3_in, hi), W3.at[me_c], ld_sem.at[5]),
        local(columns(w3_in, 1 - hi), W3X.at[me_c], ld_sem.at[5]),
    ]
    small_load = [local(mask, mask_v, ld_sem.at[6])]
    pairs = ((g1_in, g1_v), (b1_in, b1_v), (g2_in, g2_v), (b2_in, b2_v), (g3_in, g3_v), (b3_in, b3_v))
    small_load += [local(a, b, ld_sem.at[7 + i]) for i, (a, b) in enumerate(pairs)]

    barrier = pltpu.get_barrier_semaphore()

    few = n_pix <= 8
    pix_at = [me_p] + [lax.rem(me_p + i, n_pix) for i in range(1, n_pix)] if few else []
    ch_at = [me_c] + [lax.rem(me_c + i, n_ch) for i in range(1, n_ch)]
    place_beside = hi * 2 + 1 - lo

    def everybody(kind):
        places = {"all": ch_at, "half": [me_c, place_beside], "pix": [me_c], "core": [me_c, (1 - hi) * 2 + lo]}[kind]
        return [(p, c) for i, p in enumerate(pix_at) for j, c in enumerate(places) if i + j > 0]

    def greet(t, carry):
        q = lax.rem(me_p * n_ch + me_c + t, n_all)
        pl.semaphore_signal(barrier, inc=1, device_id=(q // n_ch, lax.rem(q, n_ch)), device_id_type=MESH)
        return carry

    if few:
        for device in everybody("all"):
            pl.semaphore_signal(barrier, inc=1, device_id=device, device_id_type=MESH)
    else:
        lax.fori_loop(1, n_all, greet, 0)
    for cp in small_load:
        cp.start()
    w1_load.start()
    f_load[1].start()
    f_load[0].start()
    w2_load.start()
    for cp in w3_load + c_load:
        cp.start()

    pl.semaphore_wait(barrier, n_all - 1)

    fx = [
        remote(feat.at[pl.ds(theirs + part, OWN)], F.at[lo, pl.ds(OWN * s, OWN)], fx_send.at[0], fx_recv.at[s], beside)
        for s, part in halves
    ]
    cx = [
        remote(cot.at[pl.ds(theirs + part, OWN)], C.at[lo, pl.ds(OWN * s, OWN)], fx_send.at[1], fx_recv.at[2], beside)
        for s, part in halves
    ]
    far, near, last_one = (1 - hi) * 2 + lo, hi * 2 + 1 - lo, (1 - hi) * 2 + 1 - lo

    quad, top = lax.rem(g_lo, 4), g_lo // 4
    low, high = lax.rem(quad, 2), quad // 2
    next_group = (g_hi * n_lo + top * 4 + high * 2 + 1 - low, me_c)

    w1x = [
        remote(columns(w1_in, 1 - hi), W1T.at[me_c], w_send.at[0], w_recv.at[1], across),
        remote(columns(w1_in, hi), W1T.at[me_c], w_send.at[0], w_recv.at[0], beside),
        remote(W1T.at[far], W1T.at[far], w_send.at[0], w_recv.at[3], beside),
    ]
    pkx = [
        remote(pk.at[me_c], pk.at[me_c], w_send.at[5], w_recv.at[4], across),
        remote(pk.at[me_c], pk.at[me_c], w_send.at[5], w_recv.at[5], beside),
        remote(pk.at[far], pk.at[far], w_send.at[5], w_recv.at[5], beside),
    ]

    def w2_piece(ref, q):
        return ref.at[
            :, pl.ds(pl.multiple_of(q // 2 * 16, 16), 16), pl.ds(pl.multiple_of(lax.rem(q, 2) * 128, 128), 128)
        ]

    def w3_piece(ref, q, first):
        return ref.at[
            pl.ds(pl.multiple_of(q // 2 * 16, 16), 16), pl.ds(pl.multiple_of(first + lax.rem(q, 2) * 256, 256), 256)
        ]

    w2x = [
        remote(w2_piece(w2_in, g_lo), w2_piece(W2T.at[me_c], g_lo), w_send.at[3], w_recv.at[6], across),
        remote(W2T.at[me_c], W2T.at[me_c], w_send.at[1], w_recv.at[8], beside),
        remote(W2T.at[far], W2T.at[far], w_send.at[1], w_recv.at[9], beside),
    ]
    w3x = [
        remote(w3_piece(w3_in, g_lo, (1 - hi) * 512), w3_piece(W3.at[me_c], g_lo, 0), w_send.at[4], w_recv.at[10], across),
        remote(columns(w3_in, hi), W3.at[me_c], w_send.at[2], w_recv.at[12], beside),
        remote(W3.at[far], W3.at[far], w_send.at[2], w_recv.at[13], beside),
    ]
    w3y = [
        remote(w3_piece(w3_in, g_lo, hi * 512), w3_piece(W3X.at[me_c], g_lo, 0), w_send.at[4], w_recv.at[14], across),
        remote(columns(w3_in, 1 - hi), W3X.at[me_c], w_send.at[2], w_recv.at[16], beside),
        remote(W3X.at[far], W3X.at[far], w_send.at[2], w_recv.at[17], beside),
    ]
    flip = (1 - top) * 4 + quad
    to_flip, to_four = (g_hi * n_lo + flip, me_c), []
    for t in range(1, 4):
        to_four.append((g_hi * n_lo + top * 4 + lax.rem(quad + t, 4), me_c))

    def pass_pieces(piece_of, sent, got):
        one = [remote(piece_of(g_lo), piece_of(g_lo), w_send.at[sent], w_recv.at[got], to_flip)]
        two = [
            remote(piece_of(q), piece_of(q), w_send.at[sent], w_recv.at[18 + got // 4], to)
            for to in to_four
            for q in (g_lo, flip)
        ]
        return one, two

    w2_flip, w2_four = pass_pieces(lambda q: w2_piece(W2T.at[far], q), 3, 7)
    w3_flip, w3_four = pass_pieces(lambda q: w3_piece(W3.at[far], q, 0), 4, 11)
    w3y_flip, w3y_four = pass_pieces(lambda q: w3_piece(W3X.at[far], q, 0), 4, 15)
    w1x[0].start()
    w1x[1].start()
    fx[1].start()
    fx[0].start()
    w3x[0].start()
    w2x[0].start()

    row_i = lax.broadcasted_iota(jnp.int32, (64, 256), 0)
    col_i = lax.broadcasted_iota(jnp.int32, (64, 256), 1)
    place = (row_i == col_i - 64 * me_c).astype(BF16)
    for cp in small_load:
        cp.wait()
    narrow = jnp.concatenate([v[...].astype(F32).reshape(1, 64) for v in (g1_v, b1_v, g2_v, b2_v)] * 2, axis=0)
    pk_rows = [mm(narrow.astype(BF16), place)[0:4]]
    pk_rows += [v[...].astype(F32).reshape(1, 256) for v in (g3_v, b3_v)]
    pk[me_c] = jnp.concatenate(pk_rows + [jnp.zeros((2, 256), F32)], axis=0)

    pkx[1].start()

    def ar_group(kind):
        if kind == "all":
            return n_all, me_p * n_ch + me_c, lambda q: (q // n_ch, lax.rem(q, n_ch))
        if kind == "half":
            return n_pix * 2, me_p * 2 + lo, lambda q: (q // 2, hi * 2 + lax.rem(q, 2))
        if kind == "core":
            return n_pix * 2, me_p * 2 + hi, lambda q: (q // 2, lax.rem(q, 2) * 2 + lo)
        return n_pix, me_p, lambda q: (q, me_c)

    def ar_start(k, val, kind):
        n, me, device = ar_group(kind)
        rows = val.shape[0]
        sbuf[k, 0:rows] = val
        rbuf[k, me, 0:rows] = val

        cut = pl.ds(0, rows)

        def send(to):
            remote(sbuf.at[k, cut], rbuf.at[k, me, cut], ar_send.at[k], ar_recv.at[k], to).start()

        def send_next(t, carry):
            send(device(lax.rem(me + t, n)))
            return carry

        if few:
            for to in everybody(kind):
                send(to)
        else:
            lax.fori_loop(1, n, send_next, 0)

    def pair_first(k, val):
        pbuf[k, 0] = val
        swap = remote(pbuf.at[k, 0], pbuf.at[k, 1], pair_send.at[k], pair_recv.at[k], beside)
        swap.start()
        swap.wait()
        return pbuf[k, 0] + pbuf[k, 1]

    def ar_finish(k, kind, rows):
        n = ar_group(kind)[0]
        arrived(rbuf.at[k, pl.ds(0, n - 1), pl.ds(0, rows)], ar_recv.at[k])
        return jnp.sum(rbuf[k, 0:n, 0:rows], axis=0)

    def ar_close(k, kind, rows):
        n = ar_group(kind)[0]
        arrived(rbuf.at[k, pl.ds(0, n - 1), pl.ds(0, rows)], ar_send.at[k])

    def pack2(a, b):
        return jnp.concatenate([a[:, 0:128], a[:, 128:256], b[:, 0:128], b[:, 128:256]], axis=0)

    def unpack2(v):
        return (
            jnp.concatenate([v[0:1], v[1:2]], axis=1),
            jnp.concatenate([v[2:3], v[3:4]], axis=1),
        )

    def pack3(a, b):
        return jnp.concatenate([a[:, 128 * i : 128 * (i + 1)] for i in range(4)] + [b[:, 128 * i : 128 * (i + 1)] for i in range(4)], axis=0)

    def unpack3(v):
        return (
            jnp.concatenate([v[i : i + 1] for i in range(4)], axis=1),
            jnp.concatenate([v[i : i + 1] for i in range(4, 8)], axis=1),
        )


    w1_load.wait()
    w2_load.wait()
    f_load[1].wait()
    fx[1].wait_recv()
    arrived(W1T.at[near], w_recv.at[0])

    def wide_rows(t):
        return jnp.concatenate([F[0, t], F[1, t]], axis=1)

    def xcopy(kind, src, dst, t):
        got = (
            0,
            3 + jnp.where(t < 3, 0, jnp.where(t < 5, 1, 2)),
            6 + jnp.where(t < 2, 0, 1),
            8 + jnp.where(t < 4, 0, 1),
            None,
            1 + jnp.where(t < 5, 0, 1),
        )[kind]
        return remote(src.at[t], dst.at[t], x_send.at[kind], x_recv.at[got], across)

    def send_first(h, kind):
        w = W1T[pl.ds(2 * h, 2)].reshape(128, 512)

        def one(t, carry):
            h1s[h, t] = mm_nt(wide_rows(t + OWN), w).astype(BF16)
            xcopy(kind, h1s.at[h], h1r.at[h], t).start()
            return carry

        lax.fori_loop(0, OWN, one, 0)

    send_first(hi, 0)
    arrived(W1T.at[far], w_recv.at[1])
    w1x[2].start()
    arrived(w3_piece(W3.at[far], g_lo, 0), w_recv.at[10])
    arrived(w2_piece(W2T.at[far], g_lo), w_recv.at[6])
    for cp in w2_flip + w3_flip:
        cp.start()

    flat = mask_v[...].astype(F32).reshape(1, rows28.shape[0] * ROWS)
    for t in range(rows28.shape[0]):
        rows28[t : t + 1, :] = flat[:, t * ROWS : (t + 1) * ROWS]
    diag = lax.broadcasted_iota(jnp.int32, (ROWS, ROWS), 0) == lax.broadcasted_iota(jnp.int32, (ROWS, ROWS), 1)
    ones = jnp.ones((ROWS, 128), BF16)

    lanes = jnp.broadcast_to(jnp.sum(rows28[...], axis=0, keepdims=True), (8, ROWS))
    local_count = mm(lanes.astype(BF16), ones)
    P0[...] = jnp.zeros_like(P0)
    PC[0:PAD, :] = jnp.zeros((PAD, 768), BF16)
    PC[PAD + FLAT :, :] = jnp.zeros((PAD, 768), BF16)
    ar_start(6, local_count, "pix")

    arrived(W1T.at[last_one], w_recv.at[3])
    send_first(1 - hi, 5)
    pkx[0].start()
    f_load[0].wait()
    fx[0].wait_recv()

    w1_all = W1T[...].reshape(256, 512)

    def keep_first(t, carry):
        H1[t] = mm_nt(wide_rows(t), w1_all)
        return carry

    lax.fori_loop(0, OWN, keep_first, 0)
    arrived(w2_piece(W2T.at[far], flip), w_recv.at[7])
    arrived(w3_piece(W3.at[far], flip, 0), w_recv.at[11])
    for cp in w2_four + w3_four:
        cp.start()

    def put_mask(t, carry):
        at = mine + jnp.where(t < OWN, part0 + t, part1 + t - OWN)
        row = rows28[pl.ds(at, 1), :]
        V[t] = mm(jnp.where(diag, row, 0.0).astype(BF16), ones)
        return carry

    lax.fori_loop(0, BOTH, put_mask, 0)

    for cp in (w2x[1], w3x[1], cx[0], cx[1]):
        cp.start()

    zero = jnp.zeros((8, 256), F32)

    def sum_first(t, carry):
        s, q = carry
        h = H1[t] + jnp.concatenate([h1r[0, t], h1r[1, t]], axis=1).astype(F32)
        H1[t] = h
        h1b[t] = h.astype(BF16)
        vh = spread(V[t], 256) * h
        return s + fold8(vh), q + fold8(vh * h)

    arrived(h1r.at[0], x_recv.at[0])
    arrived(h1r.at[0, pl.ds(0, 5)], x_recv.at[1])
    carry = lax.fori_loop(0, 5, sum_first, (zero, zero))
    arrived(h1r.at[0, pl.ds(5, OWN - 5)], x_recv.at[2])
    s, q = lax.fori_loop(5, OWN, sum_first, carry)
    ar_start(0, pack2(fold1(s), fold1(q)), "all")
    arrived(pk.at[far], w_recv.at[4])
    pkx[2].start()
    arrived(W3.at[pl.ds(0, 2)], ld_sem.at[5])
    arrived(G3.at[pl.ds(0, 9), pl.ds(0, 96), pl.ds(0, 128)], w_recv.at[19])
    arrived(A2.at[0, pl.ds(0, 96)], w_recv.at[20])
    w2x[2].start()
    w3x[2].start()
    arrived(pk.at[pl.ds(0, 2)], w_recv.at[5])
    gains = pk[0] + pk[1] + pk[2] + pk[3]
    g1, b1, g2, b2 = (gains[k : k + 1] for k in range(4))
    pair0, pair1 = pk[2 * hi], pk[2 * hi + 1]
    g3 = jnp.concatenate([pair0[4:5], pair1[4:5]], axis=1)
    b3 = jnp.concatenate([pair0[5:6], pair1[5:6]], axis=1)
    inv_n = 1.0 / spread(ar_finish(6, "pix", 8)[0:1], 512)
    inv_n2 = inv_n[:, 0:256]
    s, q = unpack2(ar_finish(0, "all", 4))
    w3y[0].start()
    avg1 = s * inv_n2
    scale1 = lax.rsqrt(q * inv_n2 - avg1 * avg1 + EPS)
    a1_gain = g1 * scale1
    a1_shift = b1 - avg1 * a1_gain

    def act_first(t, carry):
        v = spread(V[t], 256)
        act, slope = silu_and_slope(v * (H1[t] * (0.5 * a1_gain) + 0.5 * a1_shift))
        comp[pl.ds(pl.multiple_of(t * ROWS, 16), ROWS), :] = act
        D1[t] = spread(0.5 * V[t], 256) * slope
        return carry

    def to_padded(images):
        for i in images:
            for y in range(SIDE):
                at = EDGE + (i * PAD + y + 1) * PAD
                P0[at : at + SIDE, :] = comp[(i * SIDE + y) * SIDE : (i * SIDE + y + 1) * SIDE, :]

    def from_padded(dst, image, first, last):
        for y in range(first, last):
            at = (image * PAD + y + 1) * PAD
            dst[(image * SIDE + y) * SIDE : (image * SIDE + y + 1) * SIDE, :] = padded[at : at + SIDE, :]

    def columns_forward(images):
        for i in images:
            for c in range(3):
                at = EDGE + i * BLOCK + c - 1
                PC[PAD + i * BLOCK : PAD + (i + 1) * BLOCK, 256 * c : 256 * (c + 1)] = P0[at : at + BLOCK, :].astype(BF16)

    lax.fori_loop(0, 2, act_first, 0)
    to_padded((0,))
    columns_forward((0,))

    arrived(W2T.at[near], w_recv.at[8])
    arrived(W2T.at[last_one], w_recv.at[9])
    h1x = [remote(h1b, h1o, x_send.at[4], x_recv.at[10], across)]

    def conv(first, rows):
        taps = [PC[PAD * r + first : PAD * r + first + rows, :] for r in range(3)]
        weights = [W2T[:, k].reshape(256, 256) for k in range(9)]
        padded[first : first + rows, :] = mm_nt(jnp.concatenate(taps, axis=1), jnp.concatenate(weights, axis=1))

    def sum_second(t, carry):
        s, q = carry
        h = H2[pl.ds(pl.multiple_of(t * ROWS, 16), ROWS), :]
        h2s[t] = h.astype(BF16)
        vh = spread(V[t], 256) * h
        return s + fold8(vh), q + fold8(vh * h)

    def start_all(kind, src, dst, first, last):
        for t in range(first, last):
            xcopy(kind, src, dst, t).start()

    early = 3
    pieces = (
        (PAD, 8 * PAD, ((0, 0, 8),), 1),
        (9 * PAD, 2 * BLOCK - 10 * PAD, ((0, 8, SIDE), (1, 0, SIDE)), 3),
        (2 * BLOCK + PAD, 2 * BLOCK - 2 * PAD, ((2, 0, SIDE), (3, 0, SIDE)), OWN),
    )
    carry, done = (zero, zero), 0
    for first, rows, images, now in pieces:
        conv(first, rows)
        for image, y0, y1 in images:
            from_padded(H2, image, y0, y1)
        carry = lax.fori_loop(done, now, sum_second, carry)
        start_all(1, h2s, h2r, min(done, early), min(now, early))
        if done == 0:
            lax.fori_loop(2, OWN, act_first, 0)
            to_padded((1, 2, 3))
            columns_forward((1, 2, 3))
        done = now
    s, q = carry
    ar_start(1, pair_first(0, pack2(fold1(s), fold1(q))), "core")
    start_all(1, h2s, h2r, early, OWN)
    arrived(w3_piece(W3X.at[far], g_lo, 0), w_recv.at[14])
    w3y_flip[0].start()
    s, q = unpack2(ar_finish(1, "core", 4))
    avg2 = s * inv_n2
    scale2 = lax.rsqrt(q * inv_n2 - avg2 * avg2 + EPS)
    a2_gain = g2 * scale2
    a2_shift = b2 - avg2 * a2_gain

    arrived(w3_piece(W3X.at[far], flip, 0), w_recv.at[15])
    for cp in w3y_four:
        cp.start()
    w3y[1].start()
    arrived(W3.at[near], w_recv.at[12])
    arrived(W3.at[last_one], w_recv.at[13])

    def act_second(t, h, carry):
        s, q, d, e = carry
        v = spread(V[t], 256)
        act, slope = silu_and_slope(v * (h * (0.5 * a2_gain) + 0.5 * a2_shift))
        slope = spread(0.5 * V[t], 256) * slope
        far_slope = slope * (h - avg2)
        D2[t] = slope
        D2b[t] = slope.astype(BF16)
        D2h[t] = far_slope.astype(BF16)
        act = act.astype(BF16)
        A2[t] = act
        h3 = mm(act, W3[...].reshape(256, 512))
        H3[t] = h3
        return s + fold8(h3), q + fold8(h3 * h3), d + fold8(slope), e + fold8(far_slope)

    def own_second(t, carry):
        return act_second(t, H2[pl.ds(pl.multiple_of(t * ROWS, 16), ROWS), :], carry)

    def other_second(t, carry):
        return act_second(t + OWN, h2r[t].astype(F32), carry)

    wide_zero = jnp.zeros((8, 512), F32)
    carry = lax.fori_loop(0, OWN, own_second, (wide_zero, wide_zero, zero, zero))
    for cp in h1x:
        cp.start()
    for k, (first, last) in enumerate(((0, 3), (3, 5), (5, OWN))):
        arrived(h2r.at[pl.ds(first, last - first)], x_recv.at[3 + k])
        carry = lax.fori_loop(first, last, other_second, carry)
    s, q, slopes, far_slopes = carry
    ar_start(2, pack3(fold1(s), fold1(q)), "half")
    arrived(C.at[lo], ld_sem.at[4])
    arrived(C.at[1 - lo], fx_recv.at[2])
    def half_of(ref, part):
        return ref[OWN * part : OWN * (part + 1)].reshape(OWN * ROWS, ref.shape[2])

    cross_d = mm_tn(half_of(A2, 0), half_of(D2b, 0)) + mm_tn(half_of(A2, 1), half_of(D2b, 1))
    cross_h = mm_tn(half_of(A2, 0), half_of(D2h, 0)) + mm_tn(half_of(A2, 1), half_of(D2h, 1))
    slopes, far_slopes = fold1(slopes), fold1(far_slopes)
    arrived(A2.at[0, pl.ds(0, 96)], w_recv.at[21])
    w3y[2].start()

    s, q = unpack3(ar_finish(2, "half", 8))
    avg3 = s * inv_n
    scale3 = lax.rsqrt(q * inv_n - avg3 * avg3 + EPS)
    a3_gain = g3 * scale3
    a3_shift = b3 - avg3 * a3_gain
    half_gain, half_shift = 0.5 * a3_gain, 0.5 * a3_shift

    def put_out(ref, t, out):
        first, second = out[:, 0:256].astype(BF16), out[:, 256:512].astype(BF16)
        ref[mine + jnp.where(t < OWN, part0 + t, part1 + t - OWN)] = jnp.where(lo == 0, first, second)
        RES[t] = jnp.where(lo == 0, second, first)

    def last(t, carry):
        s, q = carry
        v = spread(V[t], 512)
        h3 = H3[t]
        wide = jnp.concatenate([F[0, t], F[1, t]], axis=1).astype(F32)
        out, slope = silu_and_slope(v * (h3 * half_gain + half_shift) + 0.5 * wide)
        put_out(res_out, t, out)
        given = jnp.concatenate([C[0, t], C[1, t]], axis=1).astype(F32)
        gs = given * slope
        GS[t] = gs
        return s + fold8(v * gs), q + fold8(gs * h3)

    def product(t, h, carry):
        s, q = carry
        given = (spread(V[t], 512) * (half_gain * GS[t])).astype(BF16)
        e = mm_nt(given, W3[...].reshape(256, 512)) * D2[t]
        return e, (s + fold8(e), q + fold8(e * (h - avg2)))

    def other_product(t, carry):
        e, carry = product(t + OWN, h2r[t].astype(F32), carry)
        e2s[t] = e.astype(BF16)
        return carry

    def last_and_product(t, carry):
        sums = last(t + OWN, carry[0])
        prods = other_product(t, carry[1])
        xcopy(2, e2s, e2r, t).start()
        return sums, prods

    def own_product(t, carry):
        e, carry = product(t, H2[pl.ds(pl.multiple_of(t * ROWS, 16), ROWS), :], carry)
        E2[t] = e
        return carry

    sums, prods = lax.fori_loop(0, 3, last_and_product, ((wide_zero, wide_zero), (zero, zero)))
    sums = lax.fori_loop(OWN + 3, BOTH, last, sums)
    s, q = lax.fori_loop(0, OWN, last, sums)
    s, q = 0.5 * fold1(s), 0.5 * fold1(q)
    ar_start(3, pack3(s, (q - avg3 * s) * scale3), "half")
    prods = lax.fori_loop(3, OWN, other_product, prods)
    start_all(2, e2s, e2r, 3, 5)
    prods = lax.fori_loop(0, OWN, own_product, prods)
    def beside_out(ref, k):
        return [
            remote(RES.at[pl.ds(OWN * s, OWN)], ref.at[pl.ds(mine + part, OWN)], o_send.at[k], o_recv.at[k], beside)
            for s, part in halves
        ]

    res_there, ig_there = beside_out(res_out, 0), beside_out(ig_out, 1)
    shift3, gain3 = unpack3(ar_finish(3, "half", 8))
    k3_h = -a3_gain * gain3 * scale3 * inv_n
    k3_0 = -a3_gain * shift3 * inv_n - k3_h * avg3

    def low_high(v):
        high = v.astype(BF16)
        return high, (v - high.astype(F32)).astype(BF16)

    def corrections(by_h, by_0, weights):
        flat = weights[...].reshape(256, 512)
        high, low = low_high(flat.astype(F32) * by_h)
        square = mm_nt(high, flat) + mm_nt(low, flat)
        high, low = low_high(by_0)
        rows = mm_nt(jnp.concatenate([high.astype(F32), low.astype(F32)] * 4, axis=0).astype(BF16), flat)
        return square, rows[0:1] + rows[1:2]

    kb[...] = jnp.concatenate([k3_h, k3_0, jnp.zeros((6, 512), F32)], axis=0)
    kx = remote(kb, kr, w_send.at[6], w_recv.at[18], across)
    kx.start()
    square, line = corrections(k3_h, k3_0, W3)
    s = fold1(prods[0]) + fold1(square * cross_d) + line * slopes
    q = fold1(prods[1]) + fold1(square * cross_h) + line * far_slopes
    ar_start(4, pack2(s, q * scale2), "all")
    start_all(2, e2s, e2r, 5, OWN)
    for cp in res_there:
        cp.start()

    def back_third(t, carry):
        v = spread(V[t], 512)
        G3[t] = (v * (half_gain * GS[t] + k3_h * H3[t] + k3_0)).astype(BF16)
        return carry

    lax.fori_loop(0, BOTH, back_third, 0)

    def group_at(t, up=False):
        return (g_hi * n_lo + (1 - top if up else top) * 4 + lax.rem(quad + t, 4), me_c)

    def over_groups(total, level, sems):
        if n_hi == 1:
            return total
        level[g_hi] = total.astype(BF16)

        def swap(t):
            q = lax.rem(g_hi + t, n_hi)
            return remote(level.at[g_hi], level.at[g_hi], sems[0].at[t], sems[1].at[t], (q * n_lo + g_lo, me_c))

        for t in range(1, n_hi):
            swap(t).start()
        for t in range(1, n_hi):
            swap(t).wait()
        total = level[0].astype(F32)
        for t in range(1, n_hi):
            total = total + level[t].astype(F32)
        return total

    def lanes_of(k):
        return pl.ds(0, 512 if k == 0 else 256)

    def pair_copies(k):
        at = lanes_of(k)
        return [remote(wp.at[k, h, :, at], wc.at[k, h, :, at], g_send.at[k], g_recv.at[k, 0], beside) for h in range(2)]

    def four_copies(k):
        return [
            remote(
                wb.at[k, lax.rem(quad + t, 4), :, :, lanes_of(k)],
                wr.at[k, quad, :, :, lanes_of(k)],
                g_send.at[k],
                g_recv.at[k, 1],
                group_at(t),
            )
            for t in range(1, 4)
        ]

    def swap_copy(k):
        at = lanes_of(k)
        return remote(wq.at[k, :, :, at], wu.at[k, :, :, at], g_send.at[k], g_recv.at[k, 2], group_at(0, True))

    def give_copies(k):
        at = lanes_of(k)
        spot = wfin.at[k, hi, quad, :, at]
        copies = []
        for t in range(4):
            group, place = group_at(t)
            if t > 0:
                copies.append(remote(wf.at[k, hi, :, at], spot, g_send.at[k], g_recv.at[k, 3], (group, place)))
            copies.append(
                remote(wf.at[k, 1 - hi, :, at], spot, g_send.at[k], g_recv.at[k, 3], (group, (1 - hi) * 2 + lo))
            )
        return copies

    def pair_start(k):
        width = 512 if k == 0 else 256
        for h in range(2):
            wp[k, h, :, 0:width] = acc_w[k, h, 1 - lo, :, 0:width].astype(BF16)
        for cp in pair_copies(k):
            cp.start()

    def pair_add(k):
        width = 512 if k == 0 else 256
        arrived(wc.at[k, :, :, lanes_of(k)], g_recv.at[k, 0])
        for h in range(2):
            both = acc_w[k, h, lo, :, 0:width] + wc[k, h, :, 0:width].astype(F32)
            both = both.reshape(4, 16, width)
            wa[k, h, :, :, 0:width] = both
            for q in range(4):
                wb[k, q, h, :, 0:width] = both[q].astype(BF16)
        for cp in four_copies(k):
            cp.start()

    def four_add(k):
        width = 512 if k == 0 else 256
        arrived(wr.at[k, pl.ds(0, 3), :, :, lanes_of(k)], g_recv.at[k, 1])
        total = wa[k, :, quad, :, 0:width]
        for t in range(1, 4):
            total = total + wr[k, lax.rem(quad + t, 4), :, :, 0:width].astype(F32)
        wq[k, :, :, 0:width] = total.astype(BF16)
        swap_copy(k).start()

    def swap_add(k):
        width = 512 if k == 0 else 256
        arrived(wu.at[k, :, :, lanes_of(k)], g_recv.at[k, 2])
        total = wq[k, :, :, 0:width].astype(F32) + wu[k, :, :, 0:width].astype(F32)
        total = over_groups(total, wh.at[k, :, :, :, lanes_of(k)], (h_send.at[k], h_recv.at[k])).astype(BF16)
        wf[k, :, :, 0:width] = total
        wfin[k, hi, quad, :, 0:width] = wf[k, hi, :, 0:width]
        for cp in give_copies(k):
            cp.start()

    def wide_take(k, out):
        arrived(A2.at[pl.ds(0, 2)] if k == 0 else A2.at[0], g_recv.at[k, 3])
        width, first = (512, 0) if k == 0 else (256, 256 * (k - 1))
        for h in range(2):
            out[:, 512 * h + first : 512 * h + first + width] = wfin[k, h, :, :, 0:width].astype(F32).reshape(64, width)

    def wide_close(k):
        arrived(Q.at[0, pl.ds(0, 736 if k == 0 else 368)], g_send.at[k])

    acc_w[0] = (mm_tn(half_of(A2, 0), half_of(G3, 0)) + mm_tn(half_of(A2, 1), half_of(G3, 1))).reshape(2, 2, 64, 512)
    pair_start(0)
    arrived(kr, w_recv.at[18])
    arrived(W3X.at[near], w_recv.at[16])
    arrived(W3X.at[last_one], w_recv.at[17])
    square_x, line_x = corrections(kr[0:1], kr[1:2], W3X)
    square_both = jnp.concatenate(low_high(square + square_x), axis=1)
    line = line + line_x

    def correct(t, carry):
        both = mm(A2[t], square_both)
        E2[t] += D2[t] * (both[:, 0:256] + both[:, 256:512] + line)
        return carry

    lax.fori_loop(0, OWN, correct, 0)
    pair_add(0)

    shift2, gain2 = unpack2(ar_finish(4, "all", 4))
    k2_h = -a2_gain * gain2 * scale2 * inv_n2
    k2_0 = -a2_gain * shift2 * inv_n2 - k2_h * avg2

    def s_pair(r):
        return [remote(sp.at[r, h], sc.at[r, h], s_send.at[r], s_recv.at[r, 0], beside) for h in range(2)]

    def s_four(r):
        copies = []
        for t in range(1, 4):
            q = lax.rem(quad + t, 4)
            copies.append(
                remote(
                    sb.at[r, lax.rem(q, 2), q // 2], sr.at[r, low, high], s_send.at[r], s_recv.at[r, 1], group_at(t)
                )
            )
        return copies

    def s_low(r):
        return remote(sb.at[r, 1 - low], sr.at[r, 0], s_send.at[r], s_recv.at[r, 1], next_group)

    def s_high(r):
        to = (g_hi * n_lo + top * 4 + (1 - high) * 2 + low, me_c)
        return remote(sr.at[r, 1, 0], sz.at[r], s_send.at[r], s_recv.at[r, 2], to)

    def s_swap(r):
        up = group_at(0, True)[0]
        aside = (1 - hi) * 2 + lo
        return [
            remote(sq.at[r, 1 - hi], sx.at[r, 0], s_send.at[r], s_recv.at[r, 3], (me_p, aside)),
            remote(sq.at[r, hi], sx.at[r, 1], s_send.at[r], s_recv.at[r, 3], (up, me_c)),
            remote(sq.at[r, 1 - hi], sx.at[r, 2], s_send.at[r], s_recv.at[r, 3], (up, aside)),
        ]

    def s_give(r):
        spot = sfin.at[r, quad]
        return [remote(spot, spot, s_send.at[r], s_recv.at[r, 4], group_at(t)) for t in range(1, 4)]

    def s_make(r):
        taps = mm(QT[...], PC[PAD * r : PAD * r + FLAT, :])
        acc_s[r] = taps.reshape(2, 2, 64, 768)
        for h in range(2):
            sp[r, h] = acc_s[r, h, 1 - lo].astype(BF16)
        for cp in s_pair(r):
            cp.start()

    def s_pair_add(r):
        arrived(sc.at[r], s_recv.at[r, 0])
        for h in range(2):
            both = (acc_s[r, h, lo] + sc[r, h].astype(F32)).reshape(4, 16, 768)
            s1[r, h] = both
            for q in range(4):
                sb[r, q % 2, q // 2, h] = both[q].astype(BF16)
        for cp in s_four(r) if r in (0, 1, 2) else [s_low(r)]:
            cp.start()

    def s_low_add(r):
        arrived(sr.at[r, 0], s_recv.at[r, 1])
        for z in range(2):
            st[r, z] = s1[r, :, 2 * z + low] + sr[r, 0, z].astype(F32)
        sr[r, 1, 0] = st[r, 1 - high].astype(BF16)
        s_high(r).start()

    def s_four_add(r):
        if r in (0, 1, 2):
            arrived(PC.at[pl.ds(0, 96)], s_recv.at[r, 1])
            total = s1[r, :, quad]
            for t in range(1, 4):
                q = lax.rem(quad + t, 4)
                total = total + sr[r, lax.rem(q, 2), q // 2].astype(F32)
        else:
            arrived(sz.at[r], s_recv.at[r, 2])
            total = st[r, high] + sz[r].astype(F32)
        sq[r] = total.astype(BF16)
        for cp in s_swap(r):
            cp.start()

    def s_swap_add(r):
        arrived(sx.at[r], s_recv.at[r, 3])
        here = sq[r, hi].astype(F32) + sx[r, 0].astype(F32)
        there = sx[r, 1].astype(F32) + sx[r, 2].astype(F32)
        total = over_groups(here + there, sh.at[r], (h_send.at[3 + r], h_recv.at[3 + r]))
        sfin[r, quad] = total.astype(BF16)
        for cp in s_give(r):
            cp.start()

    def s_take(r):
        arrived(sfin.at[r, pl.ds(0, 3)], s_recv.at[r, 4])
        rows = sfin[r].astype(F32).reshape(64, 768)
        for c in range(3):
            sg_out[3 * r + c] = rows[:, 256 * c : 256 * (c + 1)]

    def s_close(r):
        arrived(PC.at[pl.ds(0, 320)], s_send.at[r])

    def back_second(t, carry):
        at = pl.ds(pl.multiple_of(t * ROWS, 16), ROWS)
        e = E2[t] + e2r[t].astype(F32)
        comp[at, :] = spread(V[t], 256) * (a2_gain * e + k2_h * H2[at, :] + k2_0)
        return carry

    def columns_back(images):
        for i in images:
            for c in range(3):
                at = EDGE + i * BLOCK - (c - 1)
                Q[c, i * BLOCK : (i + 1) * BLOCK, :] = P0[at : at + BLOCK, :].astype(BF16)

    def conv_back(first, rows):
        taps = []
        for r in range(3):
            at = first + PAD * (1 - r)
            taps += [Q[c, at : at + rows, :] for c in range(3)]
        weights = [W2T[:, k].reshape(256, 256) for k in range(9)]
        padded[first : first + rows, :] = mm(jnp.concatenate(taps, axis=1), jnp.concatenate(weights, axis=0))

    arrived(e2r.at[pl.ds(0, 2)], x_recv.at[6])
    lax.fori_loop(0, 2, back_second, 0)
    to_padded((0,))
    columns_back((0,))

    def sum_back_first(t, carry):
        s, q = carry
        e = comp[pl.ds(pl.multiple_of(t * ROWS, 16), ROWS), :] * D1[t]
        E1[t] = e
        e1s[t] = e.astype(BF16)
        return s + fold8(e), q + fold8(e * (H1[t] - avg1))

    carry, done = (zero, zero), 0
    for first, rows, images, now in pieces:
        if done == 3:
            for i in range(IMAGES):
                QT[:, i * BLOCK : (i + 1) * BLOCK] = P0[EDGE + i * BLOCK : EDGE + (i + 1) * BLOCK, :].T.astype(BF16)
            s_make(0)
        conv_back(first, rows)
        for image, y0, y1 in images:
            from_padded(comp, image, y0, y1)
        carry = lax.fori_loop(done, now, sum_back_first, carry)
        start_all(3, e1s, e1r, min(done, early), min(now, early))
        if done == 0:
            arrived(e2r.at[pl.ds(2, OWN - 2)], x_recv.at[7])
            lax.fori_loop(2, OWN, back_second, 0)
            to_padded((1, 2, 3))
            columns_back((1, 2, 3))
        done = now
    s, q = carry
    ar_start(5, pack2(fold1(s), fold1(q * scale1)), "all")
    start_all(3, e1s, e1r, early, OWN)
    four_add(0)

    s_pair_add(0)
    s_make(1)
    s_make(2)
    s_pair_add(1)
    s_pair_add(2)

    shift1, gain1 = unpack2(ar_finish(5, "all", 4))
    k1_h = -a1_gain * gain1 * scale1 * inv_n2
    k1_0 = -a1_gain * shift1 * inv_n2 - k1_h * avg1

    def back_first(t, e, h):
        G1[t] = (spread(V[t], 256) * (a1_gain * e + k1_h * h + k1_0)).astype(BF16)

    def input_term(t, carry):
        out = mm(G1[t], W1T[...].reshape(256, 512)) + 0.5 * GS[t]
        put_out(ig_out, t, out)
        return carry

    arrived(RES, o_send.at[0])

    def own_back_first(t, carry):
        back_first(t, E1[t], H1[t])
        return carry

    def reduce_rows(first, chunks, w):
        left = G1[first : first + chunks].reshape(chunks * ROWS, 256)
        right = F[w, first : first + chunks].reshape(chunks * ROWS, 256)
        return mm_tn(left, right).reshape(2, 2, 64, 256)

    lax.fori_loop(0, OWN, own_back_first, 0)
    for w in range(2):
        acc_w[1 + w, :, :, :, 0:256] = reduce_rows(0, OWN, w)
    swap_add(0)
    lax.fori_loop(0, OWN, input_term, 0)
    ig_there[0].start()
    for cp in h1x:
        cp.wait_recv()

    def other_back_first(t, carry):
        back_first(t + OWN, e1r[t].astype(F32), h1o[t].astype(F32))
        return carry

    arrived(e1r.at[pl.ds(0, 4)], x_recv.at[8])
    arrived(e1r.at[pl.ds(4, OWN - 4)], x_recv.at[9])
    lax.fori_loop(0, OWN, other_back_first, 0)
    for w in range(2):
        acc_w[1 + w, :, :, :, 0:256] += reduce_rows(OWN, OWN, w)
        pair_start(1 + w)
    s_four_add(0)
    lax.fori_loop(OWN, BOTH, input_term, 0)
    ig_there[1].start()
    pair_add(1)
    pair_add(2)
    s_four_add(1)
    s_four_add(2)
    s_swap_add(0)
    four_add(1)
    four_add(2)
    s_swap_add(1)
    s_swap_add(2)
    swap_add(1)
    swap_add(2)

    def own64(v):
        half = jnp.where(hi == 0, v[:, 0:128], v[:, 128:256])
        swapped = jnp.concatenate([half[:, 64:128], half[:, 0:64]], axis=1)
        return jnp.concatenate([jnp.where(lo == 0, half, swapped), jnp.zeros((1, 128), F32)], axis=1)

    def own256(v):
        return jnp.where(lo == 0, v[:, 0:256], v[:, 256:512])

    st_out[...] = jnp.concatenate(
        [
            own64(gain1),
            own64(shift1),
            own64(gain2),
            own64(shift2),
            own256(gain3),
            own256(shift3),
            jnp.zeros((2, 256), F32),
        ],
        axis=0,
    )

    wide_take(0, eg_out)
    for r in range(3):
        s_take(r)
    wide_take(1, rg_out)
    wide_take(2, rg_out)

    wide_close(0)
    wide_close(1)
    wide_close(2)
    for r in range(3):
        s_close(r)
    arrived(RES, o_send.at[1])
    for k, ref in enumerate((res_out, ig_out)):
        arrived(ref.at[pl.ds(theirs, BOTH)], o_recv.at[k])
    arrived(F.at[0], fx_send.at[0])
    arrived(C.at[0], fx_send.at[1])
    for k, ref in enumerate((W1T.at[pl.ds(0, 3)], W2T.at[pl.ds(0, 2)], W3, W2T.at[0], W3.at[pl.ds(0, 2)], pk.at[pl.ds(0, 3)], kb)):
        arrived(ref, w_send.at[k])
    for k, ref in enumerate((h1s.at[0], h2s, e2s, e1s, h1b, h1s.at[1])):
        arrived(ref, x_send.at[k])
    for k, kind, rows in (
        (0, "all", 4),
        (1, "core", 4),
        (2, "half", 8),
        (3, "half", 8),
        (4, "all", 4),
        (5, "all", 4),
        (6, "pix", 8),
    ):
        ar_close(k, kind, rows)


def block(n_pix, n_ch, *args):
    feat, cot, mask, w1, w2, w3 = args[:6]
    rows, lanes = feat.shape
    n_lo = 8
    n_hi = n_pix // n_lo
    chunks = rows // ROWS
    any_space = pl.BlockSpec(memory_space=pl.ANY)
    vmem = pl.BlockSpec(memory_space=pltpu.VMEM)
    V = pltpu.VMEM
    DMA = pltpu.SemaphoreType.DMA
    scratch = [
        V((rows,), jnp.int32),
        *[V((64,), BF16)] * 4,
        *[V((256,), BF16)] * 2,
        V((2, BOTH, ROWS, 256), BF16),
        V((2, BOTH, ROWS, 256), BF16),
        V((BOTH, ROWS, 128), F32),
        V((4, 64, 512), BF16),
        V((4, 9, 64, 256), BF16),
        V((4, 64, 512), BF16),
        V((4, 64, 512), BF16),
        V((4, 8, 256), F32),
        V((7, 8, 128), F32),
        V((7, n_pix * n_ch, 8, 128), F32),
        V((2, 2, 4, 128), F32),
        V((2, OWN, ROWS, 128), BF16),
        V((2, OWN, ROWS, 128), BF16),
        V((OWN, ROWS, 256), F32),
        V((OWN, ROWS, 256), BF16),
        V((OWN, ROWS, 256), BF16),
        V((OWN, ROWS, 256), F32),
        V((OWN * ROWS, 256), F32),
        V((FLAT + 2 * EDGE, 256), F32),
        V((FLAT + 2 * PAD, 768), BF16),
        V((3, FLAT, 256), BF16),
        V((FLAT, 256), F32),
        V((OWN * ROWS, 256), F32),
        V((OWN, ROWS, 256), BF16),
        V((OWN, ROWS, 256), BF16),
        V((BOTH, ROWS, 256), BF16),
        V((BOTH, ROWS, 256), F32),
        V((BOTH, ROWS, 256), BF16),
        V((BOTH, ROWS, 256), BF16),
        V((BOTH, ROWS, 512), F32),
        V((BOTH, ROWS, 512), F32),
        V((BOTH, ROWS, 256), BF16),
        V((BOTH, ROWS, 512), BF16),
        V((8, 512), F32),
        V((8, 512), F32),
        V((OWN, ROWS, 256), F32),
        V((OWN, ROWS, 256), BF16),
        V((OWN, ROWS, 256), BF16),
        V((OWN, ROWS, 256), F32),
        V((OWN, ROWS, 256), BF16),
        V((OWN, ROWS, 256), BF16),
        V((BOTH, ROWS, 256), BF16),
        V((256, FLAT), BF16),
        V((chunks, ROWS), F32),
        V((3, 2, 2, 64, 512), F32),
        V((3, 2, 64, 512), BF16),
        V((3, 2, 64, 512), BF16),
        V((3, 2, 4, 16, 512), F32),
        V((3, 4, 2, 16, 512), BF16),
        V((3, 4, 2, 16, 512), BF16),
        V((3, 2, 16, 512), BF16),
        V((3, 2, 16, 512), BF16),
        V((3, n_hi, 2, 16, 512), BF16),
        V((3, 2, 16, 512), BF16),
        V((3, 2, 4, 16, 512), BF16),
        V((3, 2, 2, 64, 768), F32),
        V((3, 2, 64, 768), BF16),
        V((3, 2, 64, 768), BF16),
        V((3, 2, 4, 16, 768), F32),
        V((3, 2, 2, 2, 16, 768), BF16),
        V((3, 2, 2, 2, 16, 768), BF16),
        V((2, 2, 2, 16, 768), F32),
        V((2, 2, 16, 768), BF16),
        V((3, 2, 16, 768), BF16),
        V((3, 3, 16, 768), BF16),
        V((3, n_hi, 16, 768), BF16),
        V((3, 4, 16, 768), BF16),
        DMA((13,)),
        DMA((2,)),
        DMA((3,)),
        DMA((7,)),
        DMA((22,)),
        DMA((7,)),
        DMA((7,)),
        DMA((2,)),
        DMA((2,)),
        DMA((6,)),
        DMA((11,)),
        DMA((2,)),
        DMA((2,)),
        DMA((3,)),
        DMA((3, 4)),
        DMA((3,)),
        DMA((3, 5)),
        DMA((6, n_hi) if n_hi > 1 else (1, 1)),
        DMA((6, n_hi) if n_hi > 1 else (1, 1)),
    ]
    wide = V((chunks, ROWS, lanes), BF16)
    made = pl.pallas_call(
        functools.partial(kernel, n_pix, n_ch),
        out_shape=(
            wide,
            wide,
            V((64, 1024), F32),
            V((9, 64, 256), F32),
            V((64, 1024), F32),
            V((8, 256), F32),
        ),
        in_specs=[any_space] * 12,
        out_specs=(vmem,) * 6,
        scratch_shapes=scratch,
        compiler_params=pltpu.CompilerParams(
            collective_id=0, has_side_effects=True, vmem_limit_bytes=56 * 2**20
        ),
        name="bottleneck",
    )(
        feat.reshape(chunks, ROWS, lanes),
        cot.reshape(chunks, ROWS, lanes),
        mask,
        w1.T,
        w2.transpose(0, 1, 3, 2).reshape(9, 64, 256),
        w3,
        *args[6:],
    )
    narrow = jax.ShapeDtypeStruct((64,), F32)
    broad = jax.ShapeDtypeStruct((256,), F32)
    return pl.pallas_call(
        finish,
        out_shape=tuple(jax.ShapeDtypeStruct(v.shape, v.dtype) for v in made[:5]) + (narrow,) * 4 + (broad,) * 2,
        in_specs=[any_space] * 6,
        out_specs=(any_space,) * 11,
        scratch_shapes=[V((8, 256), F32)] + [V(v.shape, F32) for v in (narrow,) * 4 + (broad,) * 2] + [DMA((12,))],
        compiler_params=pltpu.CompilerParams(vmem_limit_bytes=2**20),
        name="outputs",
    )(*[pltpu.with_memory_space_constraint(v, pltpu.VMEM) for v in made])


def finish(*refs):
    made, outs, stats, small, sems = refs[:6], refs[6:17], refs[17], refs[18:24], refs[24]
    copies = [pltpu.make_async_copy(a, b, sems.at[i]) for i, (a, b) in enumerate(zip(made[:5], outs[:5]))]
    got = pltpu.make_async_copy(made[5], stats, sems.at[5])
    got.start()
    for cp in copies:
        cp.start()
    got.wait()
    for i, (one, out) in enumerate(zip(small, outs[5:])):
        one[...] = stats[i : i + 1, 0 : one.shape[0]].reshape(one.shape)
        copies.append(pltpu.make_async_copy(one, out, sems.at[6 + i]))
        copies[-1].start()
    for cp in copies:
        cp.wait()


def solution(mesh):
    n_pix, n_ch = mesh.shape["pix"], mesh.shape["ch"]

    def body(feat, mask, w1, w2, w3, g1, b1, g2, b2, g3, b3, cot):
        made = block(n_pix, n_ch, feat, cot, mask, w1, w2, w3, g1, b1, g2, b2, g3, b3)
        res, ig, rg, sg, eg = made[:5]
        return (
            res.reshape(feat.shape),
            ig.reshape(feat.shape),
            rg.T,
            sg.reshape(3, 3, 64, 256).transpose(0, 1, 3, 2),
            eg,
        ) + tuple(made[5:])

    wide = P("pix", "ch")
    return jax.shard_map(
        body,
        mesh=mesh,
        in_specs=(wide, P("pix"), P(None, "ch"), P(None, None, None, "ch"), P("ch", None)) + (P("ch"),) * 6 + (wide,),
        out_specs=(wide, wide, P(None, "ch"), P(None, None, None, "ch"), P("ch", None)) + (P("ch"),) * 6,
        check_vma=False,
    )
```

```python
import functools

import jax
import jax.numpy as jnp
from jax import lax
from jax.experimental import pallas as pl
from jax.experimental.pallas import tpu as pltpu
from jax.sharding import PartitionSpec as P

SIDE = 14
EPS = 1e-05
MESH = pl.DeviceIdType.MESH
F32 = jnp.float32
BF16 = jnp.bfloat16

ROWS = 112
OWN = 7
BOTH = 14
IMAGES = 4
PAD = 16
FLAT = IMAGES * PAD * PAD
EDGE = 8
BLOCK = PAD * PAD


def mm(a, b):
    return jnp.dot(a, b, preferred_element_type=F32)


def mm_nt(a, b):
    return lax.dot_general(a, b, (((1,), (1,)), ((), ())), preferred_element_type=F32)


def mm_tn(a, b):
    return lax.dot_general(a, b, (((0,), (0,)), ((), ())), preferred_element_type=F32)


def silu_and_slope(half):
    t = jnp.tanh(half)
    up = 1.0 + t
    out = half * up
    return out, up + out * (1.0 - t)


def fold8(v):
    return jnp.sum(v.reshape(v.shape[0] // 8, 8, v.shape[1]), axis=0)


def fold1(v):
    return jnp.sum(v, axis=0, keepdims=True)


def spread(v, lanes):
    return jnp.concatenate([v] * (lanes // 128), axis=1)


def kernel(
    n_pix,
    n_ch,
    feat,
    cot,
    mask,
    w1_in,
    w2_in,
    w3_in,
    g1_in,
    b1_in,
    g2_in,
    b2_in,
    g3_in,
    b3_in,
    res_out,
    ig_out,
    rg_out,
    sg_out,
    eg_out,
    st_out,
    mask_v,
    g1_v,
    b1_v,
    g2_v,
    b2_v,
    g3_v,
    b3_v,
    F,
    C,
    V,
    W1T,
    W2T,
    W3,
    W3X,
    pk,
    sbuf,
    rbuf,
    pbuf,
    h1s,
    h1r,
    H1,
    h1b,
    h1o,
    D1,
    comp,
    P0,
    PC,
    Q,
    padded,
    H2,
    h2s,
    h2r,
    A2,
    D2,
    D2b,
    D2h,
    H3,
    GS,
    RES,
    G3,
    kb,
    kr,
    E2,
    e2s,
    e2r,
    E1,
    e1s,
    e1r,
    G1,
    QT,
    rows28,
    acc_w,
    wp,
    wc,
    wa,
    wb,
    wr,
    wq,
    wu,
    wh,
    wf,
    wfin,
    acc_s,
    sp,
    sc,
    s1,
    sb,
    sr,
    st,
    sz,
    sq,
    sx,
    sh,
    sfin,
    ld_sem,
    fx_send,
    fx_recv,
    w_send,
    w_recv,
    ar_send,
    ar_recv,
    pair_send,
    pair_recv,
    x_send,
    x_recv,
    o_send,
    o_recv,
    g_send,
    g_recv,
    s_send,
    s_recv,
    h_send,
    h_recv,
):
    me_p, me_c = lax.axis_index("pix"), lax.axis_index("ch")
    hi, lo = me_c // 2, lax.rem(me_c, 2)
    n_lo = 8
    n_hi = n_pix // n_lo
    g_hi, g_lo = me_p // n_lo, lax.rem(me_p, n_lo)
    across = (me_p, (1 - hi) * 2 + lo)
    beside = (me_p, hi * 2 + 1 - lo)
    n_all = n_pix * n_ch

    def remote(src, dst, send, recv, device):
        return pltpu.make_async_remote_copy(
            src_ref=src, dst_ref=dst, send_sem=send, recv_sem=recv, device_id=device, device_id_type=MESH
        )

    def local(src, dst, sem):
        return pltpu.make_async_copy(src, dst, sem)

    mine, theirs = lo * BOTH, (1 - lo) * BOTH
    part0, part1 = hi * OWN, (1 - hi) * OWN

    def columns(ref, h):
        return ref.at[:, pl.ds(pl.multiple_of(h * 512, 512), 512)]

    def arrived(dst, sem):
        local(dst, dst, sem).wait()

    w1_load = local(columns(w1_in, hi), W1T.at[me_c], ld_sem.at[0])
    w2_load = local(w2_in, W2T.at[me_c], ld_sem.at[1])
    halves = ((0, part0), (1, part1))
    f_load = [
        local(feat.at[pl.ds(mine + part, OWN)], F.at[lo, pl.ds(OWN * s, OWN)], ld_sem.at[2 + s]) for s, part in halves
    ]
    c_load = [
        local(cot.at[pl.ds(mine + part, OWN)], C.at[lo, pl.ds(OWN * s, OWN)], ld_sem.at[4]) for s, part in halves
    ]
    w3_load = [
        local(columns(w3_in, hi), W3.at[me_c], ld_sem.at[5]),
        local(columns(w3_in, 1 - hi), W3X.at[me_c], ld_sem.at[5]),
    ]
    small_load = [local(mask, mask_v, ld_sem.at[6])]
    pairs = ((g1_in, g1_v), (b1_in, b1_v), (g2_in, g2_v), (b2_in, b2_v), (g3_in, g3_v), (b3_in, b3_v))
    small_load += [local(a, b, ld_sem.at[7 + i]) for i, (a, b) in enumerate(pairs)]

    barrier = pltpu.get_barrier_semaphore()

    few = n_pix <= 8
    pix_at = [me_p] + [lax.rem(me_p + i, n_pix) for i in range(1, n_pix)] if few else []
    ch_at = [me_c] + [lax.rem(me_c + i, n_ch) for i in range(1, n_ch)]
    place_beside = hi * 2 + 1 - lo

    def everybody(kind):
        places = {"all": ch_at, "half": [me_c, place_beside], "pix": [me_c], "core": [me_c, (1 - hi) * 2 + lo]}[kind]
        return [(p, c) for i, p in enumerate(pix_at) for j, c in enumerate(places) if i + j > 0]

    def greet(t, carry):
        q = lax.rem(me_p * n_ch + me_c + t, n_all)
        pl.semaphore_signal(barrier, inc=1, device_id=(q // n_ch, lax.rem(q, n_ch)), device_id_type=MESH)
        return carry

    if few:
        for device in everybody("all"):
            pl.semaphore_signal(barrier, inc=1, device_id=device, device_id_type=MESH)
    else:
        lax.fori_loop(1, n_all, greet, 0)
    for cp in small_load:
        cp.start()
    w1_load.start()
    f_load[1].start()
    f_load[0].start()
    w2_load.start()
    for cp in w3_load + c_load:
        cp.start()

    pl.semaphore_wait(barrier, n_all - 1)

    fx = [
        remote(feat.at[pl.ds(theirs + part, OWN)], F.at[lo, pl.ds(OWN * s, OWN)], fx_send.at[0], fx_recv.at[s], beside)
        for s, part in halves
    ]
    cx = [
        remote(cot.at[pl.ds(theirs + part, OWN)], C.at[lo, pl.ds(OWN * s, OWN)], fx_send.at[0], fx_recv.at[2], beside)
        for s, part in halves
    ]
    far, near, last_one = (1 - hi) * 2 + lo, hi * 2 + 1 - lo, (1 - hi) * 2 + 1 - lo

    quad, top = lax.rem(g_lo, 4), g_lo // 4
    low, high = lax.rem(quad, 2), quad // 2
    next_group = (g_hi * n_lo + top * 4 + high * 2 + 1 - low, me_c)

    w1x = [
        remote(columns(w1_in, 1 - hi), W1T.at[me_c], w_send.at[0], w_recv.at[1], across),
        remote(columns(w1_in, hi), W1T.at[me_c], w_send.at[0], w_recv.at[0], beside),
        remote(W1T.at[far], W1T.at[far], w_send.at[0], w_recv.at[3], beside),
    ]
    pkx = [
        remote(pk.at[me_c], pk.at[me_c], w_send.at[5], w_recv.at[4], across),
        remote(pk.at[me_c], pk.at[me_c], w_send.at[5], w_recv.at[5], beside),
        remote(pk.at[far], pk.at[far], w_send.at[5], w_recv.at[5], beside),
    ]

    def w2_piece(ref, q):
        return ref.at[
            :, pl.ds(pl.multiple_of(q // 2 * 16, 16), 16), pl.ds(pl.multiple_of(lax.rem(q, 2) * 128, 128), 128)
        ]

    def w3_piece(ref, q, first):
        return ref.at[
            pl.ds(pl.multiple_of(q // 2 * 16, 16), 16), pl.ds(pl.multiple_of(first + lax.rem(q, 2) * 256, 256), 256)
        ]

    w2x = [
        remote(w2_piece(w2_in, g_lo), w2_piece(W2T.at[me_c], g_lo), w_send.at[3], w_recv.at[6], across),
        remote(W2T.at[me_c], W2T.at[me_c], w_send.at[1], w_recv.at[8], beside),
        remote(W2T.at[far], W2T.at[far], w_send.at[1], w_recv.at[9], beside),
    ]
    w3x = [
        remote(w3_piece(w3_in, g_lo, (1 - hi) * 512), w3_piece(W3.at[me_c], g_lo, 0), w_send.at[4], w_recv.at[10], across),
        remote(columns(w3_in, hi), W3.at[me_c], w_send.at[2], w_recv.at[12], beside),
        remote(W3.at[far], W3.at[far], w_send.at[2], w_recv.at[13], beside),
    ]
    w3y = [
        remote(w3_piece(w3_in, g_lo, hi * 512), w3_piece(W3X.at[me_c], g_lo, 0), w_send.at[4], w_recv.at[14], across),
        remote(columns(w3_in, 1 - hi), W3X.at[me_c], w_send.at[2], w_recv.at[16], beside),
        remote(W3X.at[far], W3X.at[far], w_send.at[2], w_recv.at[17], beside),
    ]
    flip = (1 - top) * 4 + quad
    to_flip, to_four = (g_hi * n_lo + flip, me_c), []
    for t in range(1, 4):
        to_four.append((g_hi * n_lo + top * 4 + lax.rem(quad + t, 4), me_c))

    def pass_pieces(piece_of, sent, got):
        one = [remote(piece_of(g_lo), piece_of(g_lo), w_send.at[sent], w_recv.at[got], to_flip)]
        two = [
            remote(piece_of(q), piece_of(q), w_send.at[sent], w_recv.at[18 + got // 4], to)
            for to in to_four
            for q in (g_lo, flip)
        ]
        return one, two

    w2_flip, w2_four = pass_pieces(lambda q: w2_piece(W2T.at[far], q), 3, 7)
    w3_flip, w3_four = pass_pieces(lambda q: w3_piece(W3.at[far], q, 0), 4, 11)
    w3y_flip, w3y_four = pass_pieces(lambda q: w3_piece(W3X.at[far], q, 0), 4, 15)
    w1x[0].start()
    w1x[1].start()
    fx[1].start()
    fx[0].start()
    w3x[0].start()
    w2x[0].start()

    row_i = lax.broadcasted_iota(jnp.int32, (64, 256), 0)
    col_i = lax.broadcasted_iota(jnp.int32, (64, 256), 1)
    place = (row_i == col_i - 64 * me_c).astype(BF16)
    for cp in small_load:
        cp.wait()
    narrow = jnp.concatenate([v[...].astype(F32).reshape(1, 64) for v in (g1_v, b1_v, g2_v, b2_v)] * 2, axis=0)
    pk_rows = [mm(narrow.astype(BF16), place)[0:4]]
    pk_rows += [v[...].astype(F32).reshape(1, 256) for v in (g3_v, b3_v)]
    pk[me_c] = jnp.concatenate(pk_rows + [jnp.zeros((2, 256), F32)], axis=0)

    pkx[1].start()

    def ar_group(kind):
        if kind == "all":
            return n_all, me_p * n_ch + me_c, lambda q: (q // n_ch, lax.rem(q, n_ch))
        if kind == "half":
            return n_pix * 2, me_p * 2 + lo, lambda q: (q // 2, hi * 2 + lax.rem(q, 2))
        if kind == "core":
            return n_pix * 2, me_p * 2 + hi, lambda q: (q // 2, lax.rem(q, 2) * 2 + lo)
        return n_pix, me_p, lambda q: (q, me_c)

    def ar_start(k, val, kind):
        n, me, device = ar_group(kind)
        rows = val.shape[0]
        sbuf[k, 0:rows] = val
        rbuf[k, me, 0:rows] = val

        cut = pl.ds(0, rows)

        def send(to):
            remote(sbuf.at[k, cut], rbuf.at[k, me, cut], ar_send.at[k], ar_recv.at[k], to).start()

        def send_next(t, carry):
            send(device(lax.rem(me + t, n)))
            return carry

        if few:
            for to in everybody(kind):
                send(to)
        else:
            lax.fori_loop(1, n, send_next, 0)

    def pair_first(k, val):
        pbuf[k, 0] = val
        swap = remote(pbuf.at[k, 0], pbuf.at[k, 1], pair_send.at[k], pair_recv.at[k], beside)
        swap.start()
        swap.wait()
        return pbuf[k, 0] + pbuf[k, 1]

    def ar_finish(k, kind, rows):
        n = ar_group(kind)[0]
        arrived(rbuf.at[k, pl.ds(0, n - 1), pl.ds(0, rows)], ar_recv.at[k])
        return jnp.sum(rbuf[k, 0:n, 0:rows], axis=0)

    def ar_close(k, kind, rows):
        n = ar_group(kind)[0]
        arrived(rbuf.at[k, pl.ds(0, n - 1), pl.ds(0, rows)], ar_send.at[k])

    def pack2(a, b):
        return jnp.concatenate([a[:, 0:128], a[:, 128:256], b[:, 0:128], b[:, 128:256]], axis=0)

    def unpack2(v):
        return (
            jnp.concatenate([v[0:1], v[1:2]], axis=1),
            jnp.concatenate([v[2:3], v[3:4]], axis=1),
        )

    def pack3(a, b):
        return jnp.concatenate([a[:, 128 * i : 128 * (i + 1)] for i in range(4)] + [b[:, 128 * i : 128 * (i + 1)] for i in range(4)], axis=0)

    def unpack3(v):
        return (
            jnp.concatenate([v[i : i + 1] for i in range(4)], axis=1),
            jnp.concatenate([v[i : i + 1] for i in range(4, 8)], axis=1),
        )


    w1_load.wait()
    w2_load.wait()
    f_load[1].wait()
    fx[1].wait_recv()
    arrived(W1T.at[near], w_recv.at[0])

    def wide_rows(t):
        return jnp.concatenate([F[0, t], F[1, t]], axis=1)

    def xcopy(kind, src, dst, t):
        got = (
            0,
            3 + jnp.where(t < 3, 0, jnp.where(t < 5, 1, 2)),
            6 + jnp.where(t < 2, 0, 1),
            8 + jnp.where(t < 4, 0, 1),
            None,
            1 + jnp.where(t < 5, 0, 1),
        )[kind]
        return remote(src.at[t], dst.at[t], x_send.at[0], x_recv.at[got], across)

    def send_first(h, kind):
        w = W1T[pl.ds(2 * h, 2)].reshape(128, 512)

        def one(t, carry):
            h1s[h, t] = mm_nt(wide_rows(t + OWN), w).astype(BF16)
            xcopy(kind, h1s.at[h], h1r.at[h], t).start()
            return carry

        lax.fori_loop(0, OWN, one, 0)

    send_first(hi, 0)
    arrived(W1T.at[far], w_recv.at[1])
    w1x[2].start()
    arrived(w3_piece(W3.at[far], g_lo, 0), w_recv.at[10])
    arrived(w2_piece(W2T.at[far], g_lo), w_recv.at[6])
    for cp in w2_flip + w3_flip:
        cp.start()

    flat = mask_v[...].astype(F32).reshape(1, rows28.shape[0] * ROWS)
    for t in range(rows28.shape[0]):
        rows28[t : t + 1, :] = flat[:, t * ROWS : (t + 1) * ROWS]
    diag = lax.broadcasted_iota(jnp.int32, (ROWS, ROWS), 0) == lax.broadcasted_iota(jnp.int32, (ROWS, ROWS), 1)
    ones = jnp.ones((ROWS, 128), BF16)

    lanes = jnp.broadcast_to(jnp.sum(rows28[...], axis=0, keepdims=True), (8, ROWS))
    local_count = mm(lanes.astype(BF16), ones)
    P0[...] = jnp.zeros_like(P0)
    PC[0:PAD, :] = jnp.zeros((PAD, 768), BF16)
    PC[PAD + FLAT :, :] = jnp.zeros((PAD, 768), BF16)
    ar_start(6, local_count, "pix")

    arrived(W1T.at[last_one], w_recv.at[3])
    send_first(1 - hi, 5)
    pkx[0].start()
    f_load[0].wait()
    fx[0].wait_recv()

    w1_all = W1T[...].reshape(256, 512)

    def keep_first(t, carry):
        H1[t] = mm_nt(wide_rows(t), w1_all)
        return carry

    lax.fori_loop(0, OWN, keep_first, 0)
    arrived(w2_piece(W2T.at[far], flip), w_recv.at[7])
    arrived(w3_piece(W3.at[far], flip, 0), w_recv.at[11])
    for cp in w2_four + w3_four:
        cp.start()

    def put_mask(t, carry):
        at = mine + jnp.where(t < OWN, part0 + t, part1 + t - OWN)
        row = rows28[pl.ds(at, 1), :]
        V[t] = mm(jnp.where(diag, row, 0.0).astype(BF16), ones)
        return carry

    lax.fori_loop(0, BOTH, put_mask, 0)

    for cp in (w2x[1], w3x[1], cx[0], cx[1]):
        cp.start()

    zero = jnp.zeros((8, 256), F32)

    def sum_first(t, carry):
        s, q = carry
        h = H1[t] + jnp.concatenate([h1r[0, t], h1r[1, t]], axis=1).astype(F32)
        H1[t] = h
        h1b[t] = h.astype(BF16)
        vh = spread(V[t], 256) * h
        return s + fold8(vh), q + fold8(vh * h)

    arrived(h1r.at[0], x_recv.at[0])
    arrived(h1r.at[0, pl.ds(0, 5)], x_recv.at[1])
    carry = lax.fori_loop(0, 5, sum_first, (zero, zero))
    arrived(h1r.at[0, pl.ds(5, OWN - 5)], x_recv.at[2])
    s, q = lax.fori_loop(5, OWN, sum_first, carry)
    ar_start(0, pack2(fold1(s), fold1(q)), "all")
    arrived(pk.at[far], w_recv.at[4])
    pkx[2].start()
    arrived(W3.at[pl.ds(0, 2)], ld_sem.at[5])
    arrived(G3.at[pl.ds(0, 9), pl.ds(0, 96), pl.ds(0, 128)], w_recv.at[19])
    arrived(A2.at[0, pl.ds(0, 96)], w_recv.at[20])
    w2x[2].start()
    w3x[2].start()
    arrived(pk.at[pl.ds(0, 2)], w_recv.at[5])
    gains = pk[0] + pk[1] + pk[2] + pk[3]
    g1, b1, g2, b2 = (gains[k : k + 1] for k in range(4))
    pair0, pair1 = pk[2 * hi], pk[2 * hi + 1]
    g3 = jnp.concatenate([pair0[4:5], pair1[4:5]], axis=1)
    b3 = jnp.concatenate([pair0[5:6], pair1[5:6]], axis=1)
    inv_n = 1.0 / spread(ar_finish(6, "pix", 8)[0:1], 512)
    inv_n2 = inv_n[:, 0:256]
    s, q = unpack2(ar_finish(0, "all", 4))
    w3y[0].start()
    avg1 = s * inv_n2
    scale1 = lax.rsqrt(q * inv_n2 - avg1 * avg1 + EPS)
    a1_gain = g1 * scale1
    a1_shift = b1 - avg1 * a1_gain

    def act_first(t, carry):
        v = spread(V[t], 256)
        act, slope = silu_and_slope(v * (H1[t] * (0.5 * a1_gain) + 0.5 * a1_shift))
        comp[pl.ds(pl.multiple_of(t * ROWS, 16), ROWS), :] = act
        D1[t] = spread(0.5 * V[t], 256) * slope
        return carry

    def to_padded(images):
        for i in images:
            for y in range(SIDE):
                at = EDGE + (i * PAD + y + 1) * PAD
                P0[at : at + SIDE, :] = comp[(i * SIDE + y) * SIDE : (i * SIDE + y + 1) * SIDE, :]

    def from_padded(dst, image, first, last):
        for y in range(first, last):
            at = (image * PAD + y + 1) * PAD
            dst[(image * SIDE + y) * SIDE : (image * SIDE + y + 1) * SIDE, :] = padded[at : at + SIDE, :]

    def columns_forward(images):
        for i in images:
            for c in range(3):
                at = EDGE + i * BLOCK + c - 1
                PC[PAD + i * BLOCK : PAD + (i + 1) * BLOCK, 256 * c : 256 * (c + 1)] = P0[at : at + BLOCK, :].astype(BF16)

    lax.fori_loop(0, 2, act_first, 0)
    to_padded((0,))
    columns_forward((0,))

    arrived(W2T.at[near], w_recv.at[8])
    arrived(W2T.at[last_one], w_recv.at[9])
    h1x = [remote(h1b, h1o, x_send.at[1], x_recv.at[10], across)]

    def conv(first, rows):
        taps = [PC[PAD * r + first : PAD * r + first + rows, :] for r in range(3)]
        weights = [W2T[:, k].reshape(256, 256) for k in range(9)]
        padded[first : first + rows, :] = mm_nt(jnp.concatenate(taps, axis=1), jnp.concatenate(weights, axis=1))

    def sum_second(t, carry):
        s, q = carry
        h = H2[pl.ds(pl.multiple_of(t * ROWS, 16), ROWS), :]
        h2s[t] = h.astype(BF16)
        vh = spread(V[t], 256) * h
        return s + fold8(vh), q + fold8(vh * h)

    def start_all(kind, src, dst, first, last):
        for t in range(first, last):
            xcopy(kind, src, dst, t).start()

    early = 3
    pieces = (
        (PAD, 8 * PAD, ((0, 0, 8),), 1),
        (9 * PAD, 2 * BLOCK - 10 * PAD, ((0, 8, SIDE), (1, 0, SIDE)), 3),
        (2 * BLOCK + PAD, 2 * BLOCK - 2 * PAD, ((2, 0, SIDE), (3, 0, SIDE)), OWN),
    )
    carry, done = (zero, zero), 0
    for first, rows, images, now in pieces:
        conv(first, rows)
        for image, y0, y1 in images:
            from_padded(H2, image, y0, y1)
        carry = lax.fori_loop(done, now, sum_second, carry)
        start_all(1, h2s, h2r, min(done, early), min(now, early))
        if done == 0:
            lax.fori_loop(2, OWN, act_first, 0)
            to_padded((1, 2, 3))
            columns_forward((1, 2, 3))
        done = now
    s, q = carry
    ar_start(1, pair_first(0, pack2(fold1(s), fold1(q))), "core")
    start_all(1, h2s, h2r, early, OWN)
    arrived(w3_piece(W3X.at[far], g_lo, 0), w_recv.at[14])
    w3y_flip[0].start()
    s, q = unpack2(ar_finish(1, "core", 4))
    avg2 = s * inv_n2
    scale2 = lax.rsqrt(q * inv_n2 - avg2 * avg2 + EPS)
    a2_gain = g2 * scale2
    a2_shift = b2 - avg2 * a2_gain

    arrived(w3_piece(W3X.at[far], flip, 0), w_recv.at[15])
    for cp in w3y_four:
        cp.start()
    w3y[1].start()
    arrived(W3.at[near], w_recv.at[12])
    arrived(W3.at[last_one], w_recv.at[13])

    def act_second(t, h, carry):
        s, q, d, e = carry
        v = spread(V[t], 256)
        act, slope = silu_and_slope(v * (h * (0.5 * a2_gain) + 0.5 * a2_shift))
        slope = spread(0.5 * V[t], 256) * slope
        far_slope = slope * (h - avg2)
        D2[t] = slope
        D2b[t] = slope.astype(BF16)
        D2h[t] = far_slope.astype(BF16)
        act = act.astype(BF16)
        A2[t] = act
        h3 = mm(act, W3[...].reshape(256, 512))
        H3[t] = h3
        return s + fold8(h3), q + fold8(h3 * h3), d + fold8(slope), e + fold8(far_slope)

    def own_second(t, carry):
        return act_second(t, H2[pl.ds(pl.multiple_of(t * ROWS, 16), ROWS), :], carry)

    def other_second(t, carry):
        return act_second(t + OWN, h2r[t].astype(F32), carry)

    wide_zero = jnp.zeros((8, 512), F32)
    carry = lax.fori_loop(0, OWN, own_second, (wide_zero, wide_zero, zero, zero))
    for cp in h1x:
        cp.start()
    for k, (first, last) in enumerate(((0, 3), (3, 5), (5, OWN))):
        arrived(h2r.at[pl.ds(first, last - first)], x_recv.at[3 + k])
        carry = lax.fori_loop(first, last, other_second, carry)
    s, q, slopes, far_slopes = carry
    ar_start(2, pack3(fold1(s), fold1(q)), "half")
    arrived(C.at[lo], ld_sem.at[4])
    arrived(C.at[1 - lo], fx_recv.at[2])
    def half_of(ref, part):
        return ref[OWN * part : OWN * (part + 1)].reshape(OWN * ROWS, ref.shape[2])

    cross_d = mm_tn(half_of(A2, 0), half_of(D2b, 0)) + mm_tn(half_of(A2, 1), half_of(D2b, 1))
    cross_h = mm_tn(half_of(A2, 0), half_of(D2h, 0)) + mm_tn(half_of(A2, 1), half_of(D2h, 1))
    slopes, far_slopes = fold1(slopes), fold1(far_slopes)
    arrived(A2.at[0, pl.ds(0, 96)], w_recv.at[21])
    w3y[2].start()

    s, q = unpack3(ar_finish(2, "half", 8))
    avg3 = s * inv_n
    scale3 = lax.rsqrt(q * inv_n - avg3 * avg3 + EPS)
    a3_gain = g3 * scale3
    a3_shift = b3 - avg3 * a3_gain
    half_gain, half_shift = 0.5 * a3_gain, 0.5 * a3_shift

    def put_out(ref, t, out):
        first, second = out[:, 0:256].astype(BF16), out[:, 256:512].astype(BF16)
        ref[mine + jnp.where(t < OWN, part0 + t, part1 + t - OWN)] = jnp.where(lo == 0, first, second)
        RES[t] = jnp.where(lo == 0, second, first)

    def last(t, carry):
        s, q = carry
        v = spread(V[t], 512)
        h3 = H3[t]
        wide = jnp.concatenate([F[0, t], F[1, t]], axis=1).astype(F32)
        out, slope = silu_and_slope(v * (h3 * half_gain + half_shift) + 0.5 * wide)
        put_out(res_out, t, out)
        given = jnp.concatenate([C[0, t], C[1, t]], axis=1).astype(F32)
        gs = given * slope
        GS[t] = gs
        return s + fold8(v * gs), q + fold8(gs * h3)

    def product(t, h, carry):
        s, q = carry
        given = (spread(V[t], 512) * (half_gain * GS[t])).astype(BF16)
        e = mm_nt(given, W3[...].reshape(256, 512)) * D2[t]
        return e, (s + fold8(e), q + fold8(e * (h - avg2)))

    def other_product(t, carry):
        e, carry = product(t + OWN, h2r[t].astype(F32), carry)
        e2s[t] = e.astype(BF16)
        return carry

    def last_and_product(t, carry):
        sums = last(t + OWN, carry[0])
        prods = other_product(t, carry[1])
        xcopy(2, e2s, e2r, t).start()
        return sums, prods

    def own_product(t, carry):
        e, carry = product(t, H2[pl.ds(pl.multiple_of(t * ROWS, 16), ROWS), :], carry)
        E2[t] = e
        return carry

    sums, prods = lax.fori_loop(0, 3, last_and_product, ((wide_zero, wide_zero), (zero, zero)))
    sums = lax.fori_loop(OWN + 3, BOTH, last, sums)
    s, q = lax.fori_loop(0, OWN, last, sums)
    s, q = 0.5 * fold1(s), 0.5 * fold1(q)
    ar_start(3, pack3(s, (q - avg3 * s) * scale3), "half")
    prods = lax.fori_loop(3, OWN, other_product, prods)
    start_all(2, e2s, e2r, 3, 5)
    prods = lax.fori_loop(0, OWN, own_product, prods)
    def beside_out(ref, k):
        return [
            remote(RES.at[pl.ds(OWN * s, OWN)], ref.at[pl.ds(mine + part, OWN)], o_send.at[k], o_recv.at[k], beside)
            for s, part in halves
        ]

    res_there, ig_there = beside_out(res_out, 0), beside_out(ig_out, 1)
    shift3, gain3 = unpack3(ar_finish(3, "half", 8))
    k3_h = -a3_gain * gain3 * scale3 * inv_n
    k3_0 = -a3_gain * shift3 * inv_n - k3_h * avg3

    def low_high(v):
        high = v.astype(BF16)
        return high, (v - high.astype(F32)).astype(BF16)

    def corrections(by_h, by_0, weights):
        flat = weights[...].reshape(256, 512)
        high, low = low_high(flat.astype(F32) * by_h)
        square = mm_nt(high, flat) + mm_nt(low, flat)
        high, low = low_high(by_0)
        rows = mm_nt(jnp.concatenate([high.astype(F32), low.astype(F32)] * 4, axis=0).astype(BF16), flat)
        return square, rows[0:1] + rows[1:2]

    kb[...] = jnp.concatenate([k3_h, k3_0, jnp.zeros((6, 512), F32)], axis=0)
    kx = remote(kb, kr, w_send.at[6], w_recv.at[18], across)
    kx.start()
    square, line = corrections(k3_h, k3_0, W3)
    s = fold1(prods[0]) + fold1(square * cross_d) + line * slopes
    q = fold1(prods[1]) + fold1(square * cross_h) + line * far_slopes
    ar_start(4, pack2(s, q * scale2), "all")
    start_all(2, e2s, e2r, 5, OWN)
    for cp in res_there:
        cp.start()

    def back_third(t, carry):
        v = spread(V[t], 512)
        G3[t] = (v * (half_gain * GS[t] + k3_h * H3[t] + k3_0)).astype(BF16)
        return carry

    lax.fori_loop(0, BOTH, back_third, 0)

    def group_at(t, up=False):
        return (g_hi * n_lo + (1 - top if up else top) * 4 + lax.rem(quad + t, 4), me_c)

    def over_groups(total, level, sems):
        if n_hi == 1:
            return total
        level[g_hi] = total.astype(BF16)

        def swap(t):
            q = lax.rem(g_hi + t, n_hi)
            return remote(level.at[g_hi], level.at[g_hi], sems[0].at[t], sems[1].at[t], (q * n_lo + g_lo, me_c))

        for t in range(1, n_hi):
            swap(t).start()
        for t in range(1, n_hi):
            swap(t).wait()
        total = level[0].astype(F32)
        for t in range(1, n_hi):
            total = total + level[t].astype(F32)
        return total

    def lanes_of(k):
        return pl.ds(0, 512 if k == 0 else 256)

    def pair_copies(k):
        at = lanes_of(k)
        return [remote(wp.at[k, h, :, at], wc.at[k, h, :, at], g_send.at[k], g_recv.at[k, 0], beside) for h in range(2)]

    def four_copies(k):
        return [
            remote(
                wb.at[k, lax.rem(quad + t, 4), :, :, lanes_of(k)],
                wr.at[k, quad, :, :, lanes_of(k)],
                g_send.at[k],
                g_recv.at[k, 1],
                group_at(t),
            )
            for t in range(1, 4)
        ]

    def swap_copy(k):
        at = lanes_of(k)
        return remote(wq.at[k, :, :, at], wu.at[k, :, :, at], g_send.at[k], g_recv.at[k, 2], group_at(0, True))

    def give_copies(k):
        at = lanes_of(k)
        spot = wfin.at[k, hi, quad, :, at]
        copies = []
        for t in range(4):
            group, place = group_at(t)
            if t > 0:
                copies.append(remote(wf.at[k, hi, :, at], spot, g_send.at[k], g_recv.at[k, 3], (group, place)))
            copies.append(
                remote(wf.at[k, 1 - hi, :, at], spot, g_send.at[k], g_recv.at[k, 3], (group, (1 - hi) * 2 + lo))
            )
        return copies

    def pair_start(k):
        width = 512 if k == 0 else 256
        for h in range(2):
            wp[k, h, :, 0:width] = acc_w[k, h, 1 - lo, :, 0:width].astype(BF16)
        for cp in pair_copies(k):
            cp.start()

    def pair_add(k):
        width = 512 if k == 0 else 256
        arrived(wc.at[k, :, :, lanes_of(k)], g_recv.at[k, 0])
        for h in range(2):
            both = acc_w[k, h, lo, :, 0:width] + wc[k, h, :, 0:width].astype(F32)
            both = both.reshape(4, 16, width)
            wa[k, h, :, :, 0:width] = both
            for q in range(4):
                wb[k, q, h, :, 0:width] = both[q].astype(BF16)
        for cp in four_copies(k):
            cp.start()

    def four_add(k):
        width = 512 if k == 0 else 256
        arrived(wr.at[k, pl.ds(0, 3), :, :, lanes_of(k)], g_recv.at[k, 1])
        total = wa[k, :, quad, :, 0:width]
        for t in range(1, 4):
            total = total + wr[k, lax.rem(quad + t, 4), :, :, 0:width].astype(F32)
        wq[k, :, :, 0:width] = total.astype(BF16)
        swap_copy(k).start()

    def swap_add(k):
        width = 512 if k == 0 else 256
        arrived(wu.at[k, :, :, lanes_of(k)], g_recv.at[k, 2])
        total = wq[k, :, :, 0:width].astype(F32) + wu[k, :, :, 0:width].astype(F32)
        total = over_groups(total, wh.at[k, :, :, :, lanes_of(k)], (h_send.at[k], h_recv.at[k])).astype(BF16)
        wf[k, :, :, 0:width] = total
        wfin[k, hi, quad, :, 0:width] = wf[k, hi, :, 0:width]
        for cp in give_copies(k):
            cp.start()

    def wide_take(k, out):
        arrived(A2.at[pl.ds(0, 2)] if k == 0 else A2.at[0], g_recv.at[k, 3])
        width, first = (512, 0) if k == 0 else (256, 256 * (k - 1))
        for h in range(2):
            out[:, 512 * h + first : 512 * h + first + width] = wfin[k, h, :, :, 0:width].astype(F32).reshape(64, width)

    def wide_close(k):
        arrived(Q.at[0, pl.ds(0, 736 if k == 0 else 368)], g_send.at[k])

    acc_w[0] = (mm_tn(half_of(A2, 0), half_of(G3, 0)) + mm_tn(half_of(A2, 1), half_of(G3, 1))).reshape(2, 2, 64, 512)
    pair_start(0)
    arrived(kr, w_recv.at[18])
    arrived(W3X.at[near], w_recv.at[16])
    arrived(W3X.at[last_one], w_recv.at[17])
    square_x, line_x = corrections(kr[0:1], kr[1:2], W3X)
    square_both = jnp.concatenate(low_high(square + square_x), axis=1)
    line = line + line_x

    def correct(t, carry):
        both = mm(A2[t], square_both)
        E2[t] += D2[t] * (both[:, 0:256] + both[:, 256:512] + line)
        return carry

    lax.fori_loop(0, OWN, correct, 0)
    pair_add(0)

    shift2, gain2 = unpack2(ar_finish(4, "all", 4))
    k2_h = -a2_gain * gain2 * scale2 * inv_n2
    k2_0 = -a2_gain * shift2 * inv_n2 - k2_h * avg2

    def s_pair(r):
        return [remote(sp.at[r, h], sc.at[r, h], s_send.at[0], s_recv.at[r, 0], beside) for h in range(2)]

    def s_four(r):
        copies = []
        for t in range(1, 4):
            q = lax.rem(quad + t, 4)
            copies.append(
                remote(
                    sb.at[r, lax.rem(q, 2), q // 2], sr.at[r, low, high], s_send.at[0], s_recv.at[r, 1], group_at(t)
                )
            )
        return copies

    def s_low(r):
        return remote(sb.at[r, 1 - low], sr.at[r, 0], s_send.at[0], s_recv.at[r, 1], next_group)

    def s_high(r):
        to = (g_hi * n_lo + top * 4 + (1 - high) * 2 + low, me_c)
        return remote(sr.at[r, 1, 0], sz.at[r], s_send.at[0], s_recv.at[r, 2], to)

    def s_swap(r):
        up = group_at(0, True)[0]
        aside = (1 - hi) * 2 + lo
        return [
            remote(sq.at[r, 1 - hi], sx.at[r, 0], s_send.at[0], s_recv.at[r, 3], (me_p, aside)),
            remote(sq.at[r, hi], sx.at[r, 1], s_send.at[0], s_recv.at[r, 3], (up, me_c)),
            remote(sq.at[r, 1 - hi], sx.at[r, 2], s_send.at[0], s_recv.at[r, 3], (up, aside)),
        ]

    def s_give(r):
        spot = sfin.at[r, quad]
        return [remote(spot, spot, s_send.at[0], s_recv.at[r, 4], group_at(t)) for t in range(1, 4)]

    def s_make(r):
        taps = mm(QT[...], PC[PAD * r : PAD * r + FLAT, :])
        acc_s[r] = taps.reshape(2, 2, 64, 768)
        for h in range(2):
            sp[r, h] = acc_s[r, h, 1 - lo].astype(BF16)
        for cp in s_pair(r):
            cp.start()

    def s_pair_add(r):
        arrived(sc.at[r], s_recv.at[r, 0])
        for h in range(2):
            both = (acc_s[r, h, lo] + sc[r, h].astype(F32)).reshape(4, 16, 768)
            s1[r, h] = both
            for q in range(4):
                sb[r, q % 2, q // 2, h] = both[q].astype(BF16)
        for cp in s_four(r) if r in (0, 1, 2) else [s_low(r)]:
            cp.start()

    def s_low_add(r):
        arrived(sr.at[r, 0], s_recv.at[r, 1])
        for z in range(2):
            st[r, z] = s1[r, :, 2 * z + low] + sr[r, 0, z].astype(F32)
        sr[r, 1, 0] = st[r, 1 - high].astype(BF16)
        s_high(r).start()

    def s_four_add(r):
        if r in (0, 1, 2):
            arrived(PC.at[pl.ds(0, 96)], s_recv.at[r, 1])
            total = s1[r, :, quad]
            for t in range(1, 4):
                q = lax.rem(quad + t, 4)
                total = total + sr[r, lax.rem(q, 2), q // 2].astype(F32)
        else:
            arrived(sz.at[r], s_recv.at[r, 2])
            total = st[r, high] + sz[r].astype(F32)
        sq[r] = total.astype(BF16)
        for cp in s_swap(r):
            cp.start()

    def s_swap_add(r):
        arrived(sx.at[r], s_recv.at[r, 3])
        here = sq[r, hi].astype(F32) + sx[r, 0].astype(F32)
        there = sx[r, 1].astype(F32) + sx[r, 2].astype(F32)
        total = over_groups(here + there, sh.at[r], (h_send.at[3 + r], h_recv.at[3 + r]))
        sfin[r, quad] = total.astype(BF16)
        for cp in s_give(r):
            cp.start()

    def s_take(r):
        arrived(sfin.at[r, pl.ds(0, 3)], s_recv.at[r, 4])
        rows = sfin[r].astype(F32).reshape(64, 768)
        for c in range(3):
            sg_out[3 * r + c] = rows[:, 256 * c : 256 * (c + 1)]

    def s_close():
        arrived(PC.at[pl.ds(0, 960)], s_send.at[0])

    def back_second(t, carry):
        at = pl.ds(pl.multiple_of(t * ROWS, 16), ROWS)
        e = E2[t] + e2r[t].astype(F32)
        comp[at, :] = spread(V[t], 256) * (a2_gain * e + k2_h * H2[at, :] + k2_0)
        return carry

    def columns_back(images):
        for i in images:
            for c in range(3):
                at = EDGE + i * BLOCK - (c - 1)
                Q[c, i * BLOCK : (i + 1) * BLOCK, :] = P0[at : at + BLOCK, :].astype(BF16)

    def conv_back(first, rows):
        taps = []
        for r in range(3):
            at = first + PAD * (1 - r)
            taps += [Q[c, at : at + rows, :] for c in range(3)]
        weights = [W2T[:, k].reshape(256, 256) for k in range(9)]
        padded[first : first + rows, :] = mm(jnp.concatenate(taps, axis=1), jnp.concatenate(weights, axis=0))

    arrived(e2r.at[pl.ds(0, 2)], x_recv.at[6])
    lax.fori_loop(0, 2, back_second, 0)
    to_padded((0,))
    columns_back((0,))

    def sum_back_first(t, carry):
        s, q = carry
        e = comp[pl.ds(pl.multiple_of(t * ROWS, 16), ROWS), :] * D1[t]
        E1[t] = e
        e1s[t] = e.astype(BF16)
        return s + fold8(e), q + fold8(e * (H1[t] - avg1))

    carry, done = (zero, zero), 0
    for first, rows, images, now in pieces:
        if done == 3:
            for i in range(IMAGES):
                QT[:, i * BLOCK : (i + 1) * BLOCK] = P0[EDGE + i * BLOCK : EDGE + (i + 1) * BLOCK, :].T.astype(BF16)
            s_make(0)
        conv_back(first, rows)
        for image, y0, y1 in images:
            from_padded(comp, image, y0, y1)
        carry = lax.fori_loop(done, now, sum_back_first, carry)
        start_all(3, e1s, e1r, min(done, early), min(now, early))
        if done == 0:
            arrived(e2r.at[pl.ds(2, OWN - 2)], x_recv.at[7])
            lax.fori_loop(2, OWN, back_second, 0)
            to_padded((1, 2, 3))
            columns_back((1, 2, 3))
        done = now
    s, q = carry
    ar_start(5, pack2(fold1(s), fold1(q * scale1)), "all")
    start_all(3, e1s, e1r, early, OWN)
    four_add(0)

    s_pair_add(0)
    s_make(1)
    s_make(2)
    s_pair_add(1)
    s_pair_add(2)

    shift1, gain1 = unpack2(ar_finish(5, "all", 4))
    k1_h = -a1_gain * gain1 * scale1 * inv_n2
    k1_0 = -a1_gain * shift1 * inv_n2 - k1_h * avg1

    def back_first(t, e, h):
        G1[t] = (spread(V[t], 256) * (a1_gain * e + k1_h * h + k1_0)).astype(BF16)

    def input_term(t, carry):
        out = mm(G1[t], W1T[...].reshape(256, 512)) + 0.5 * GS[t]
        put_out(ig_out, t, out)
        return carry

    arrived(RES, o_send.at[0])

    def own_back_first(t, carry):
        back_first(t, E1[t], H1[t])
        return carry

    def reduce_rows(first, chunks, w):
        left = G1[first : first + chunks].reshape(chunks * ROWS, 256)
        right = F[w, first : first + chunks].reshape(chunks * ROWS, 256)
        return mm_tn(left, right).reshape(2, 2, 64, 256)

    lax.fori_loop(0, OWN, own_back_first, 0)
    for w in range(2):
        acc_w[1 + w, :, :, :, 0:256] = reduce_rows(0, OWN, w)
    swap_add(0)
    lax.fori_loop(0, OWN, input_term, 0)
    ig_there[0].start()
    for cp in h1x:
        cp.wait_recv()

    def other_back_first(t, carry):
        back_first(t + OWN, e1r[t].astype(F32), h1o[t].astype(F32))
        return carry

    arrived(e1r.at[pl.ds(0, 4)], x_recv.at[8])
    arrived(e1r.at[pl.ds(4, OWN - 4)], x_recv.at[9])
    lax.fori_loop(0, OWN, other_back_first, 0)
    for w in range(2):
        acc_w[1 + w, :, :, :, 0:256] += reduce_rows(OWN, OWN, w)
        pair_start(1 + w)
    s_four_add(0)
    lax.fori_loop(OWN, BOTH, input_term, 0)
    ig_there[1].start()
    pair_add(1)
    pair_add(2)
    s_four_add(1)
    s_four_add(2)
    s_swap_add(0)
    four_add(1)
    four_add(2)
    s_swap_add(1)
    s_swap_add(2)
    swap_add(1)
    swap_add(2)

    def own64(v):
        half = jnp.where(hi == 0, v[:, 0:128], v[:, 128:256])
        swapped = jnp.concatenate([half[:, 64:128], half[:, 0:64]], axis=1)
        return jnp.concatenate([jnp.where(lo == 0, half, swapped), jnp.zeros((1, 128), F32)], axis=1)

    def own256(v):
        return jnp.where(lo == 0, v[:, 0:256], v[:, 256:512])

    st_out[...] = jnp.concatenate(
        [
            own64(gain1),
            own64(shift1),
            own64(gain2),
            own64(shift2),
            own256(gain3),
            own256(shift3),
            jnp.zeros((2, 256), F32),
        ],
        axis=0,
    )

    wide_take(0, eg_out)
    for r in range(3):
        s_take(r)
    wide_take(1, rg_out)
    wide_take(2, rg_out)

    wide_close(0)
    wide_close(1)
    wide_close(2)
    s_close()
    arrived(RES, o_send.at[1])
    for k, ref in enumerate((res_out, ig_out)):
        arrived(ref.at[pl.ds(theirs, BOTH)], o_recv.at[k])
    arrived(F, fx_send.at[0])
    for k, ref in enumerate((W1T.at[pl.ds(0, 3)], W2T.at[pl.ds(0, 2)], W3, W2T.at[0], W3.at[pl.ds(0, 2)], pk.at[pl.ds(0, 3)], kb)):
        arrived(ref, w_send.at[k])
    arrived(F, x_send.at[0])
    arrived(h1b, x_send.at[1])
    for k, kind, rows in (
        (0, "all", 4),
        (1, "core", 4),
        (2, "half", 8),
        (3, "half", 8),
        (4, "all", 4),
        (5, "all", 4),
        (6, "pix", 8),
    ):
        ar_close(k, kind, rows)


def block(n_pix, n_ch, *args):
    feat, cot, mask, w1, w2, w3 = args[:6]
    rows, lanes = feat.shape
    n_lo = 8
    n_hi = n_pix // n_lo
    chunks = rows // ROWS
    any_space = pl.BlockSpec(memory_space=pl.ANY)
    vmem = pl.BlockSpec(memory_space=pltpu.VMEM)
    V = pltpu.VMEM
    DMA = pltpu.SemaphoreType.DMA
    scratch = [
        V((rows,), jnp.int32),
        *[V((64,), BF16)] * 4,
        *[V((256,), BF16)] * 2,
        V((2, BOTH, ROWS, 256), BF16),
        V((2, BOTH, ROWS, 256), BF16),
        V((BOTH, ROWS, 128), F32),
        V((4, 64, 512), BF16),
        V((4, 9, 64, 256), BF16),
        V((4, 64, 512), BF16),
        V((4, 64, 512), BF16),
        V((4, 8, 256), F32),
        V((7, 8, 128), F32),
        V((7, n_pix * n_ch, 8, 128), F32),
        V((2, 2, 4, 128), F32),
        V((2, OWN, ROWS, 128), BF16),
        V((2, OWN, ROWS, 128), BF16),
        V((OWN, ROWS, 256), F32),
        V((OWN, ROWS, 256), BF16),
        V((OWN, ROWS, 256), BF16),
        V((OWN, ROWS, 256), F32),
        V((OWN * ROWS, 256), F32),
        V((FLAT + 2 * EDGE, 256), F32),
        V((FLAT + 2 * PAD, 768), BF16),
        V((3, FLAT, 256), BF16),
        V((FLAT, 256), F32),
        V((OWN * ROWS, 256), F32),
        V((OWN, ROWS, 256), BF16),
        V((OWN, ROWS, 256), BF16),
        V((BOTH, ROWS, 256), BF16),
        V((BOTH, ROWS, 256), F32),
        V((BOTH, ROWS, 256), BF16),
        V((BOTH, ROWS, 256), BF16),
        V((BOTH, ROWS, 512), F32),
        V((BOTH, ROWS, 512), F32),
        V((BOTH, ROWS, 256), BF16),
        V((BOTH, ROWS, 512), BF16),
        V((8, 512), F32),
        V((8, 512), F32),
        V((OWN, ROWS, 256), F32),
        V((OWN, ROWS, 256), BF16),
        V((OWN, ROWS, 256), BF16),
        V((OWN, ROWS, 256), F32),
        V((OWN, ROWS, 256), BF16),
        V((OWN, ROWS, 256), BF16),
        V((BOTH, ROWS, 256), BF16),
        V((256, FLAT), BF16),
        V((chunks, ROWS), F32),
        V((3, 2, 2, 64, 512), F32),
        V((3, 2, 64, 512), BF16),
        V((3, 2, 64, 512), BF16),
        V((3, 2, 4, 16, 512), F32),
        V((3, 4, 2, 16, 512), BF16),
        V((3, 4, 2, 16, 512), BF16),
        V((3, 2, 16, 512), BF16),
        V((3, 2, 16, 512), BF16),
        V((3, n_hi, 2, 16, 512), BF16),
        V((3, 2, 16, 512), BF16),
        V((3, 2, 4, 16, 512), BF16),
        V((3, 2, 2, 64, 768), F32),
        V((3, 2, 64, 768), BF16),
        V((3, 2, 64, 768), BF16),
        V((3, 2, 4, 16, 768), F32),
        V((3, 2, 2, 2, 16, 768), BF16),
        V((3, 2, 2, 2, 16, 768), BF16),
        V((2, 2, 2, 16, 768), F32),
        V((2, 2, 16, 768), BF16),
        V((3, 2, 16, 768), BF16),
        V((3, 3, 16, 768), BF16),
        V((3, n_hi, 16, 768), BF16),
        V((3, 4, 16, 768), BF16),
        DMA((13,)),
        DMA((1,)),
        DMA((3,)),
        DMA((7,)),
        DMA((22,)),
        DMA((7,)),
        DMA((7,)),
        DMA((1,)),
        DMA((1,)),
        DMA((2,)),
        DMA((11,)),
        DMA((2,)),
        DMA((2,)),
        DMA((3,)),
        DMA((3, 4)),
        DMA((1,)),
        DMA((3, 5)),
        DMA((6, n_hi) if n_hi > 1 else (1, 1)),
        DMA((6, n_hi) if n_hi > 1 else (1, 1)),
    ]
    wide = V((chunks, ROWS, lanes), BF16)
    made = pl.pallas_call(
        functools.partial(kernel, n_pix, n_ch),
        out_shape=(
            wide,
            wide,
            V((64, 1024), F32),
            V((9, 64, 256), F32),
            V((64, 1024), F32),
            V((8, 256), F32),
        ),
        in_specs=[any_space] * 12,
        out_specs=(vmem,) * 6,
        scratch_shapes=scratch,
        compiler_params=pltpu.CompilerParams(
            collective_id=0, has_side_effects=True, vmem_limit_bytes=56 * 2**20
        ),
        name="bottleneck",
    )(
        feat.reshape(chunks, ROWS, lanes),
        cot.reshape(chunks, ROWS, lanes),
        mask,
        w1.T,
        w2.transpose(0, 1, 3, 2).reshape(9, 64, 256),
        w3,
        *args[6:],
    )
    narrow = jax.ShapeDtypeStruct((64,), F32)
    broad = jax.ShapeDtypeStruct((256,), F32)
    return pl.pallas_call(
        finish,
        out_shape=tuple(jax.ShapeDtypeStruct(v.shape, v.dtype) for v in made[:5]) + (narrow,) * 4 + (broad,) * 2,
        in_specs=[any_space] * 6,
        out_specs=(any_space,) * 11,
        scratch_shapes=[V((8, 256), F32)] + [V(v.shape, F32) for v in (narrow,) * 4 + (broad,) * 2] + [DMA((12,))],
        compiler_params=pltpu.CompilerParams(vmem_limit_bytes=2**20),
        name="outputs",
    )(*[pltpu.with_memory_space_constraint(v, pltpu.VMEM) for v in made])


def finish(*refs):
    made, outs, stats, small, sems = refs[:6], refs[6:17], refs[17], refs[18:24], refs[24]
    copies = [pltpu.make_async_copy(a, b, sems.at[i]) for i, (a, b) in enumerate(zip(made[:5], outs[:5]))]
    got = pltpu.make_async_copy(made[5], stats, sems.at[5])
    got.start()
    for cp in copies:
        cp.start()
    got.wait()
    for i, (one, out) in enumerate(zip(small, outs[5:])):
        one[...] = stats[i : i + 1, 0 : one.shape[0]].reshape(one.shape)
        copies.append(pltpu.make_async_copy(one, out, sems.at[6 + i]))
        copies[-1].start()
    for cp in copies:
        cp.wait()


def solution(mesh):
    n_pix, n_ch = mesh.shape["pix"], mesh.shape["ch"]

    def body(feat, mask, w1, w2, w3, g1, b1, g2, b2, g3, b3, cot):
        made = block(n_pix, n_ch, feat, cot, mask, w1, w2, w3, g1, b1, g2, b2, g3, b3)
        res, ig, rg, sg, eg = made[:5]
        return (
            res.reshape(feat.shape),
            ig.reshape(feat.shape),
            rg.T,
            sg.reshape(3, 3, 64, 256).transpose(0, 1, 3, 2),
            eg,
        ) + tuple(made[5:])

    wide = P("pix", "ch")
    return jax.shard_map(
        body,
        mesh=mesh,
        in_specs=(wide, P("pix"), P(None, "ch"), P(None, None, None, "ch"), P("ch", None)) + (P("ch"),) * 6 + (wide,),
        out_specs=(wide, wide, P(None, "ch"), P(None, None, None, "ch"), P("ch", None)) + (P("ch"),) * 6,
        check_vma=False,
    )
```
